128 devices in a mesh: section: 4 (over z), space: 16 (over y, x), batch: 2 (over core).
Axes of the slice: x: 4, y: 4, z: 4, core: 2. Of those that a mesh axis runs over, the one named last changes fastest.
Arguments:
- frames: bfloat16 [2, 2, 64, 32, 256], P(None, 'batch', 'space'), may hold values from -6 to 6
- cotangent: bfloat16 [2, 2, 64, 32, 256], P(None, 'batch', 'space'), may hold values from -6 to 6
- first_hidden: bfloat16 [4, 2, 64, 32, 256], P('section', 'batch', 'space'), may hold values from -0.8984375 to 0.8984375
- first_cell: float32 [4, 2, 64, 32, 256], P('section', 'batch', 'space'), may hold values from -5 to 5
- gate_bias: float32 [4, 1024], P('section'), may hold values from -4 to 4
- gate_weight: bfloat16 [4, 4608, 1024], P('section'), may hold values from -0.09375 to 0.09375
Outputs:
- weight_grad: float32 [4, 4608, 1024], P('section', ('space', 'batch'))
The draws below stay inside these ranges and needn't reach their ends.
All inputs are finite; a program needn't handle non-finite values.
Results may differ from the reference program's by a relative error of at most 0.0035.
Values may be sent and summed in bfloat16 or wider, within the bound.
A program may use at most 128 MiB of HBM per device.

```python
import jax
import jax.numpy as jnp
from jax import lax

HID = 256
COLS = 32
TSTEPS = 2
LAYERS = 4
SAMPLES = 2
ROWS = 64


def shard_levels(stream_key, extent, cuts, low, high):
    loudness = 1.0
    for axis_at, shards_of in cuts:
        draws = jax.random.uniform(jax.random.fold_in(jax.random.fold_in(stream_key, 6), axis_at), (shards_of,), jnp.float32, low / len(cuts), high / len(cuts))
        loudness = loudness * jnp.repeat(jnp.exp(draws), extent[axis_at] // shards_of).reshape((-1,) + (1,) * (len(extent) - 1 - axis_at))
    return loudness


def scatter_about(rng, dims, width, limit, shards=(), dtype=jnp.bfloat16):
    entries = width * jax.random.normal(rng, dims, jnp.float32)
    if shards:
        entries = entries * shard_levels(rng, dims, shards, -0.22, 0.18)
    return jnp.clip(entries, -limit, limit).astype(dtype)


def setup_inputs(seed: int = 0) -> dict:
    keys = jax.random.split(jax.random.key(seed), 7)
    frames = scatter_about(keys[0], (TSTEPS, SAMPLES, ROWS, COLS, HID), 1.0, 6.0, ((1, 2), (2, 16)))
    cotangent = scatter_about(keys[1], (TSTEPS, SAMPLES, ROWS, COLS, HID), 1.0, 6.0, ((1, 2), (2, 16)))
    first_hidden = jnp.clip(jax.random.uniform(keys[2], (LAYERS, SAMPLES, ROWS, COLS, HID), jnp.float32, -0.8984375, 0.8984375) * shard_levels(keys[2], (LAYERS, SAMPLES, ROWS, COLS, HID), ((0, 4), (1, 2), (2, 16)), -0.4, 0.0), -0.8984375, 0.8984375).astype(jnp.bfloat16)
    first_cell = scatter_about(keys[3], (LAYERS, SAMPLES, ROWS, COLS, HID), 1.0, 5.0, ((0, 4), (1, 2), (2, 16)), jnp.float32)
    gate_bias = scatter_about(keys[4], (LAYERS, 4 * HID), 1.0, 4.0, ((0, 4),), jnp.float32)
    gate_weight = scatter_about(keys[5], (LAYERS, 18 * HID, 4 * HID), (18 * HID) ** -0.5, 0.09375, ((0, 4),))
    return {"frames": frames, "cotangent": cotangent, "first_hidden": first_hidden, "first_cell": first_cell, "gate_bias": gate_bias, "gate_weight": gate_weight}


def gate_patches(padded, out_rows, out_cols):
    pieces = [padded[..., row_off:row_off + out_rows, col_off:col_off + out_cols, :] for row_off in range(3) for col_off in range(3)]
    return jnp.concatenate(pieces, axis=-1)


def adjoint_conv(grad_pad, weight, out_rows, out_cols):
    channels = weight.shape[0] // 9
    gate_count = weight.shape[1]
    kernel = weight.reshape(3, 3, channels, gate_count)
    total_sum = None
    for row_off in range(3):
        for col_off in range(3):
            window = grad_pad[..., 2 - row_off:2 - row_off + out_rows, 2 - col_off:2 - col_off + out_cols, :]
            flat_rows = window.reshape(-1, gate_count)
            product = lax.dot_general(flat_rows, kernel[row_off, col_off], (((1,), (1,)), ((), ())), preferred_element_type=jnp.float32)
            total_sum = product if total_sum is None else total_sum + product
    return total_sum


def activate(preact, unit_count):
    return jnp.concatenate([jax.nn.sigmoid(preact[:, :3 * unit_count]), jnp.tanh(preact[:, 3 * unit_count:])], axis=-1)


def cell_backward(grad_h, grad_cell_next, gate_values, cell_state, new_cell, unit_count):
    input_gate = gate_values[:, :unit_count]
    forget_gate = gate_values[:, unit_count:2 * unit_count]
    output_gate = gate_values[:, 2 * unit_count:3 * unit_count]
    candidate = gate_values[:, 3 * unit_count:]
    squash = jnp.tanh(new_cell)
    grad_cell_now = grad_cell_next + grad_h * output_gate * (1.0 - squash * squash)
    grad_pre = jnp.concatenate([
        grad_cell_now * candidate * input_gate * (1.0 - input_gate),
        grad_cell_now * cell_state * forget_gate * (1.0 - forget_gate),
        grad_h * squash * output_gate * (1.0 - output_gate),
        grad_cell_now * input_gate * (1.0 - candidate * candidate)], axis=-1).astype(jnp.bfloat16)
    return grad_pre, grad_cell_now * forget_gate


def reference(frames, cotangent, first_hidden, first_cell, gate_bias, gate_weight):
    steps_count = frames.shape[0]
    layer_count = gate_weight.shape[0]
    samples, height, grid_cols, unit_count = frames.shape[1:]
    inputs = [frames[moment] for moment in range(steps_count)]
    saved = []
    for layer_index in range(layer_count):
        hidden = first_hidden[layer_index]
        cell_state = first_cell[layer_index].reshape(-1, unit_count)
        outputs = []
        layer_saved = []
        for moment in range(steps_count):
            joined = jnp.concatenate([inputs[moment], hidden], axis=-1)
            padded = jnp.pad(joined, ((0, 0), (1, 1), (1, 1), (0, 0)))
            patches = gate_patches(padded, height, grid_cols).reshape(-1, 18 * unit_count)
            preact = jnp.dot(patches, gate_weight[layer_index], preferred_element_type=jnp.float32) + gate_bias[layer_index]
            gate_values = activate(preact, unit_count)
            new_cell = gate_values[:, unit_count:2 * unit_count] * cell_state + gate_values[:, :unit_count] * gate_values[:, 3 * unit_count:]
            hidden = (gate_values[:, 2 * unit_count:3 * unit_count] * jnp.tanh(new_cell)).astype(jnp.bfloat16).reshape(samples, height, grid_cols, unit_count)
            layer_saved.append((padded, gate_values, cell_state, new_cell))
            cell_state = new_cell
            outputs.append(hidden)
        saved.append(layer_saved)
        inputs = outputs
    grads = []
    above = None
    for layer_index in reversed(range(layer_count)):
        grad_hidden = jnp.zeros((samples, height, grid_cols, unit_count), jnp.bfloat16)
        grad_cell = jnp.zeros((samples * height * grid_cols, unit_count), jnp.float32)
        weight_sum = jnp.zeros((18 * unit_count, 4 * unit_count), jnp.float32)
        below_grads = [None] * steps_count
        for moment in reversed(range(steps_count)):
            padded, gate_values, cell_state, new_cell = saved[layer_index][moment]
            arriving = cotangent[moment] if layer_index == layer_count - 1 else above[moment]
            grad_h = (arriving.astype(jnp.float32) + grad_hidden.astype(jnp.float32)).reshape(-1, unit_count)
            grad_pre, grad_cell = cell_backward(grad_h, grad_cell, gate_values, cell_state, new_cell, unit_count)
            patches = gate_patches(padded, height, grid_cols).reshape(-1, 18 * unit_count)
            weight_sum = weight_sum + lax.dot_general(patches, grad_pre, (((0,), (0,)), ((), ())), preferred_element_type=jnp.float32)
            grad_pad = jnp.pad(grad_pre.reshape(samples, height, grid_cols, 4 * unit_count), ((0, 0), (1, 1), (1, 1), (0, 0)))
            grad_joined = adjoint_conv(grad_pad, gate_weight[layer_index], height, grid_cols).astype(jnp.bfloat16).reshape(samples, height, grid_cols, 2 * unit_count)
            below_grads[moment] = grad_joined[..., :unit_count]
            grad_hidden = grad_joined[..., unit_count:]
        grads.insert(0, weight_sum)
        above = below_grads
    return jnp.stack(grads)
```

```python
import functools

import jax
import jax.numpy as jnp
from jax import lax
from jax.experimental import pallas as pl
from jax.experimental.pallas import tpu as pltpu
from jax.sharding import PartitionSpec as P

F32 = jnp.float32
BF16 = jnp.bfloat16
MESH = pl.DeviceIdType.MESH
LINE = 4


def dot(left, right):
    return jnp.dot(left, right, preferred_element_type=F32)


def kernel(
    frames, cotangent, first_hidden, first_cell, bias, weight, out,
    wx, wh, wxt, wht, sx, sh, sg, top_hidden, preact, gates, cells, coef, gin, gx_out, ghid,
    turned, turned_all, grads_all, acc, leaving, landed,
    w_sem, sx_r, sh_r, sg_r, gx_r, pt_r, ga_r, rv_r,
    fr_s, fh_s, sx_s, sh_s, sg_s, gx_s, pt_s, ga_s, rv_s,
):
    z, s, k = lax.axis_index("section"), lax.axis_index("space"), lax.axis_index("batch")
    y, x = s // LINE, s % LINE
    sections, tiles = lax.axis_size("section"), lax.axis_size("space")
    cols = 32
    n = first_cell.shape[0]
    hid = first_cell.shape[1]
    half = hid // 2
    gate_half = 4 * half
    mid = slice(cols, cols + n)
    high, low = slice(0, cols), slice(cols + n, 2 * cols + n)
    first_row, last_row = slice(cols, 2 * cols), slice(n, cols + n)
    centre = slice(hid, 2 * hid)
    gcentre = slice(4 * hid, 8 * hid)
    top, bottom, base, roof = s == 0, s == tiles - 1, z == 0, z == sections - 1
    pending = []

    def send(pred, make):
        if pred is None:
            make().start()
            pending.append(lambda: make().wait_send())
        else:
            pl.when(pred)(lambda: make().start())
            pending.append(lambda: pl.when(pred)(lambda: make().wait_send()))

    def remote(src, dst, send_sem, recv_sem, device):
        return pltpu.make_async_remote_copy(
            src_ref=src, dst_ref=dst, send_sem=send_sem, recv_sem=recv_sem,
            device_id=device, device_id_type=MESH,
        )

    def arrived(dst, recv_sem):
        remote(dst, dst, recv_sem, recv_sem, (z, s, 1 - k)).wait_recv()

    loads = {}
    for part, buffer in ((0, wx), (1, wh)):
        for c in range(2):
            for g in range(4):
                loads[part, c, g] = pltpu.make_async_copy(
                    weight.at[:, :, part * hid:(part + 1) * hid, pl.ds(g * hid + c * half, half)],
                    buffer.at[c, :, :, :, g * half:(g + 1) * half],
                    w_sem.at[part, c, g],
                )
    for part in (1, 0):
        for c in range(2):
            for g in range(4):
                loads[part, c, g].start()

    def weights_here(part):
        for c in range(2):
            for g in range(4):
                loads[part, c, g].wait()

    partners = [(jnp.logical_not(top), (z, s - 1, k)), (jnp.logical_not(bottom), (z, s + 1, k))]
    for step, ok in ((-1, z > 0), (1, z < sections - 1)):
        partners.append((ok, (z + step, s, k)))
        partners.append((ok & (s > 0), (z + step, s - 1, k)))
        partners.append((ok & (s < tiles - 1), (z + step, s + 1, k)))
    partners.append((None, (z, s, 1 - k)))
    for d in range(1, LINE):
        for core in range(2):
            partners.append((None, (z, y * LINE + (x + d) % LINE, core)))
            partners.append((None, (z, ((y + d) % LINE) * LINE + x, core)))
    barrier = pltpu.get_barrier_semaphore()
    expected = 0
    for pred, device in partners:
        greet = functools.partial(
            pl.semaphore_signal, barrier, inc=1, device_id=device, device_id_type=MESH
        )
        if pred is None:
            greet()
            expected = expected + 1
        else:
            pl.when(pred)(greet)
            expected = expected + jnp.where(pred, 1, 0)

    sh[0, mid, centre] = first_hidden[...]

    @pl.when(base)
    def _():
        for t in range(2):
            sx[t, mid, centre] = frames[t]

    @pl.when(roof)
    def _():
        for t in range(2):
            gin[t] = cotangent[t]

    @pl.when(top)
    def _():
        for t in range(2):
            sx[t, high, :] = jnp.zeros((cols, 3 * hid), BF16)
            sh[t, high, :] = jnp.zeros((cols, 3 * hid), BF16)
            sg[t, high, :] = jnp.zeros((cols, 12 * hid), BF16)

    @pl.when(bottom)
    def _():
        for t in range(2):
            sx[t, low, :] = jnp.zeros((cols, 3 * hid), BF16)
            sh[t, low, :] = jnp.zeros((cols, 3 * hid), BF16)
            sg[t, low, :] = jnp.zeros((cols, 12 * hid), BF16)

    pl.semaphore_wait(barrier, expected)

    def send_edges(src, dst, send_sems, recv_sems, section, pred):
        up, down = s > 0, s < tiles - 1
        if pred is not None:
            up, down = up & pred, down & pred
        send(up, lambda: remote(src[0], dst[1], send_sems.at[0], recv_sems.at[1], (section, s - 1, k)))
        send(down, lambda: remote(src[1], dst[0], send_sems.at[1], recv_sems.at[0], (section, s + 1, k)))

    for t in range(2):
        send_edges(
            (sx.at[t, first_row, centre], sx.at[t, last_row, centre]),
            (sx.at[t, high, centre], sx.at[t, low, centre]),
            fr_s.at[t], sx_r.at[t], z, base,
        )
        if t == 0:
            send_edges(
                (sh.at[t, first_row, centre], sh.at[t, last_row, centre]),
                (sh.at[t, high, centre], sh.at[t, low, centre]),
                fh_s, sh_r.at[t], z, None,
            )

    def spread(buffer, t, rows, width):
        count = rows.stop - rows.start
        value = buffer[t, rows, width:2 * width].astype(F32)
        column = lax.broadcasted_iota(jnp.int32, (count, width), 0) % cols
        buffer[t, rows, 0:width] = jnp.where(
            column == 0, 0.0, pltpu.roll(value, 1, 0)
        ).astype(BF16)
        buffer[t, rows, 2 * width:3 * width] = jnp.where(
            column == cols - 1, 0.0, pltpu.roll(value, count - 1, 0)
        ).astype(BF16)

    def edges_here(buffer, t, recv_sems, width):
        @pl.when(jnp.logical_not(top))
        def _():
            arrived(buffer.at[t, high, width:2 * width], recv_sems.at[0])
            spread(buffer, t, high, width)

        @pl.when(jnp.logical_not(bottom))
        def _():
            arrived(buffer.at[t, low, width:2 * width], recv_sems.at[1])
            spread(buffer, t, low, width)

    def conv(buffer, t, weights, c):
        total = None
        for a in range(3):
            term = dot(
                buffer[t, cols * a:cols * a + n, :],
                weights[c, a].reshape(3 * hid, gate_half),
            )
            total = term if total is None else total + term
        return total

    def turn_weights(source, target):
        def one(a, carry):
            for b in range(3):
                for c in range(2):
                    start = (2 - b) * 4 * hid + c * gate_half
                    target[a, start:start + gate_half, :] = source[c, a, b].T
            return carry

        lax.fori_loop(0, 3, one, 0)

    def turn_all_weights():
        turn_weights(wh, wht)
        pl.when(jnp.logical_not(base))(lambda: turn_weights(wx, wxt))

    def turn_patches():
        block = turned.shape[3]
        for t in range(2):
            for piece in range(18):
                window, part = piece // 2, piece % 2
                a, b = window // 3, window % 3
                buffer = sh if part else sx
                flipped = buffer[t, cols * a:cols * a + n, b * hid:(b + 1) * hid].T
                at, end = piece * hid, (piece + 1) * hid
                while at < end:
                    number = at // block
                    stop = min(end, (number + 1) * block)
                    turned[t, number // LINE, number % LINE, at - number * block:stop - number * block, :] = (
                        flipped[at - piece * hid:stop - piece * hid]
                    )
                    at = stop

    def spread_to_group(pred, views, send_sems, recv_sems):
        for d in (0, 1, 3, 2):
            for c in range(2):
                there = ((x if c == 0 else y) + d) % LINE
                chip = y * LINE + there if c == 0 else there * LINE + x
                slot = 2 * (x if c == 0 else y) + k
                src, dst = views(c, there, slot)
                make = functools.partial(
                    remote, src, dst, send_sems.at[c * LINE + d], recv_sems.at[slot], (z, chip, c)
                )
                ok = pred
                if d == 0:
                    ok = (k != c) if pred is None else pred & (k != c)
                    own = (k == c) if pred is None else pred & (k == c)
                    pl.when(own)(
                        functools.partial(
                            lambda src, dst, sem: pltpu.make_async_copy(src, dst, sem).start(),
                            src, dst, recv_sems.at[slot],
                        )
                    )
                send(ok, make)

    def lanes(slot, width):
        return pl.ds(pl.multiple_of(slot * width, width), width)

    def send_patches(pred):
        for t in range(2):
            def views(c, there, slot):
                src = turned.at[t, :, there] if c == 0 else turned.at[t, there]
                return src, turned_all.at[t, :, :, lanes(slot, n)]

            spread_to_group(pred, views, pt_s.at[t], pt_r.at[t])

    def send_grads(t, pred):
        def views(c, there, slot):
            src = sg.at[t, mid, 4 * hid + c * gate_half:4 * hid + (c + 1) * gate_half]
            return src, grads_all.at[t, lanes(slot, n), :]

        spread_to_group(pred, views, ga_s.at[t], ga_r.at[t])

    @pl.when(z >= 2)
    def _():
        weights_here(1)
        weights_here(0)
        turn_all_weights()

    for t in range(2):
        spread(sh, t, mid, hid)
        edges_here(sh, t, sh_r.at[t], hid)
        if t == 0:
            pl.when(z < 2)(lambda: weights_here(1))
        for c in range(2):
            start = jnp.concatenate(
                [bias[0:1, g * hid + c * half:g * hid + (c + 1) * half] for g in range(4)], axis=1
            )
            preact[:, c * gate_half:(c + 1) * gate_half] = conv(sh, t, wh, c) + start
        pl.when(jnp.logical_not(base))(
            lambda t=t: arrived(sx.at[t, mid, centre], sx_r.at[t, 2])
        )
        spread(sx, t, mid, hid)
        edges_here(sx, t, sx_r.at[t], hid)
        if t == 0:
            pl.when(z < 2)(lambda: weights_here(0))
        for c in range(2):
            chan = slice(c * half, (c + 1) * half)
            now = preact[:, c * gate_half:(c + 1) * gate_half] + conv(sx, t, wx, c)
            i_gate = jax.nn.sigmoid(now[:, 0:half])
            f_gate = jax.nn.sigmoid(now[:, half:2 * half])
            o_gate = jax.nn.sigmoid(now[:, 2 * half:3 * half])
            cand = jnp.tanh(now[:, 3 * half:])
            old = first_cell[:, chan] if t == 0 else cells[0, :, chan]
            new = f_gate * old + i_gate * cand
            squash = jnp.tanh(new)
            hidden = (o_gate * squash).astype(BF16)
            if t == 0:
                sh[1, mid, hid + c * half:hid + (c + 1) * half] = hidden
            else:
                top_hidden[:, chan] = hidden
            cells[t, :, chan] = new
            for index, value in enumerate((i_gate, f_gate, o_gate, cand, squash)):
                gates[index, :, chan] = value
        if t == 0:
            whole = sh.at[1, mid, centre]
            ends = (sh.at[1, first_row, centre], sh.at[1, last_row, centre])
            send_edges(
                ends, (sh.at[1, high, centre], sh.at[1, low, centre]), sh_s, sh_r.at[1], z, None
            )
        else:
            whole = top_hidden
            ends = (top_hidden.at[0:cols], top_hidden.at[n - cols:n])
        send_edges(
            ends, (sx.at[t, high, centre], sx.at[t, low, centre]),
            sx_s.at[t], sx_r.at[t], z + 1, z < sections - 1,
        )
        send(
            z < sections - 1,
            lambda whole=whole, t=t: remote(
                whole, sx.at[t, mid, centre], sx_s.at[t, 2], sx_r.at[t, 2], (z + 1, s, k)
            ),
        )
        for c in range(2):
            chan = slice(c * half, (c + 1) * half)
            i_gate, f_gate, o_gate, cand, squash = (gates[index, :, chan] for index in range(5))
            old = first_cell[:, chan] if t == 0 else cells[0, :, chan]
            coef[t, 0, :, chan] = o_gate * (1.0 - squash * squash)
            coef[t, 1, :, chan] = cand * i_gate * (1.0 - i_gate)
            coef[t, 2, :, chan] = old * f_gate * (1.0 - f_gate)
            coef[t, 3, :, chan] = squash * o_gate * (1.0 - o_gate)
            coef[t, 4, :, chan] = i_gate * (1.0 - cand * cand)
            coef[t, 5, :, chan] = f_gate

    pl.when(z < 2)(turn_all_weights)
    pl.when(jnp.logical_not(roof))(turn_patches)
    send_patches(jnp.logical_not(roof))

    def back_conv(t, weights):
        total = None
        for a in (1, 0, 2):
            term = dot(sg[t, cols * (2 - a):cols * (2 - a) + n, :], weights[a])
            total = term if total is None else total + term
        return total.astype(BF16)

    for t in (1, 0):
        pl.when(jnp.logical_not(roof))(lambda t=t: arrived(gin.at[t], gx_r.at[t]))
        for c in range(2):
            chan = slice(c * half, (c + 1) * half)
            grad_h = gin[t, :, chan].astype(F32)
            if t == 0:
                grad_h = grad_h + ghid[:, chan].astype(F32)
            grad_c = grad_h * coef[t, 0, :, chan]
            if t == 0:
                grad_c = grad_c + cells[1, :, chan]
            for g, value in enumerate((
                grad_c * coef[t, 1, :, chan],
                grad_c * coef[t, 2, :, chan],
                grad_h * coef[t, 3, :, chan],
                grad_c * coef[t, 4, :, chan],
            )):
                at = 4 * hid + c * gate_half + g * half
                sg[t, mid, at:at + half] = value.astype(BF16)
            if t == 1:
                cells[1, :, chan] = grad_c * coef[t, 5, :, chan]
        send_edges(
            (sg.at[t, first_row, gcentre], sg.at[t, last_row, gcentre]),
            (sg.at[t, high, gcentre], sg.at[t, low, gcentre]),
            sg_s.at[t], sg_r.at[t], z, None if t == 1 else jnp.logical_not(base),
        )
        if t == 0:
            send_grads(t, base)

        def input_grad(t=t):
            gx_out[t] = back_conv(t, wxt)

        def widen(t=t):
            spread(sg, t, mid, 4 * hid)
            edges_here(sg, t, sg_r.at[t], 4 * hid)

        if t == 1:
            widen()
            pl.when(jnp.logical_not(base))(input_grad)
        else:
            @pl.when(jnp.logical_not(base))
            def _():
                widen()
                input_grad()

        send(
            jnp.logical_not(base),
            lambda t=t: remote(gx_out.at[t], gin.at[t], gx_s.at[t], gx_r.at[t], (z - 1, s, k)),
        )
        if t == 1:
            ghid[...] = back_conv(t, wht)
            send_grads(t, None)
        else:
            send_grads(t, jnp.logical_not(base))

    pl.when(roof)(turn_patches)
    send_patches(roof)

    rows = out.shape[0]
    me = jnp.where(k == 0, y, x)
    for t in (1, 0):
        for slot in range(2 * LINE):
            arrived(turned_all.at[t, :, :, slot * n:(slot + 1) * n], pt_r.at[t, slot])
            arrived(grads_all.at[t, slot * n:(slot + 1) * n], ga_r.at[t, slot])
        if t == 1:
            for j in range(LINE):
                acc[j] = dot(turned_all[t, j], grads_all[t])
        else:
            for d in (1, 3, 2, 0):
                j = (me + d) % LINE
                leaving[d] = (acc[j] + dot(turned_all[t, j], grads_all[t])).astype(BF16)
                chip = jnp.where(k == 0, j * LINE + x, y * LINE + j)
                for q in range(2):
                    src, dst = leaving.at[d, q * rows:(q + 1) * rows], landed.at[k, me]
                    make = functools.partial(
                        remote, src, dst, rv_s.at[d * 2 + q], rv_r.at[k, me], (z, chip, q)
                    )
                    if d == 0:
                        pl.when(k == q)(
                            lambda src=src, dst=dst: pltpu.make_async_copy(
                                src, dst, rv_r.at[k, me]
                            ).start()
                        )
                    send(k != q if d == 0 else None, make)
    for c in range(2):
        for i in range(LINE):
            arrived(landed.at[c, i], rv_r.at[c, i])
        for g in range(4):
            total = landed[c, 0, :, g * half:(g + 1) * half].astype(F32)
            for i in range(1, LINE):
                total = total + landed[c, i, :, g * half:(g + 1) * half].astype(F32)
            out[:, g * hid + c * half:g * hid + (c + 1) * half] = total
    for wait in pending:
        wait()


def on_device(frames, cotangent, first_hidden, first_cell, gate_bias, gate_weight):
    steps, _, tile_rows, cols, hid = frames.shape
    n = tile_rows * cols
    pad = n + 2 * cols
    half = hid // 2
    gates = 4 * hid
    share = 18 * hid // (lax.axis_size("space") * lax.axis_size("batch"))
    block = 2 * share
    vmem = pl.BlockSpec(memory_space=pltpu.VMEM)
    dma = pltpu.SemaphoreType.DMA
    scratch = [
        pltpu.VMEM((2, 3, 3, hid, gates // 2), BF16),
        pltpu.VMEM((2, 3, 3, hid, gates // 2), BF16),
        pltpu.VMEM((3, 3 * gates, hid), BF16),
        pltpu.VMEM((3, 3 * gates, hid), BF16),
        pltpu.VMEM((steps, pad, 3 * hid), BF16),
        pltpu.VMEM((steps, pad, 3 * hid), BF16),
        pltpu.VMEM((steps, pad, 3 * gates), BF16),
        pltpu.VMEM((n, hid), BF16),
        pltpu.VMEM((n, gates), F32),
        pltpu.VMEM((5, n, hid), F32),
        pltpu.VMEM((steps, n, hid), F32),
        pltpu.VMEM((steps, 6, n, hid), F32),
        pltpu.VMEM((steps, n, hid), BF16),
        pltpu.VMEM((steps, n, hid), BF16),
        pltpu.VMEM((n, hid), BF16),
        pltpu.VMEM((steps, LINE, LINE, block, n), BF16),
        pltpu.VMEM((steps, LINE, block, 2 * LINE * n), BF16),
        pltpu.VMEM((steps, 2 * LINE * n, gates // 2), BF16),
        pltpu.VMEM((LINE, block, gates // 2), F32),
        pltpu.VMEM((LINE, block, gates // 2), BF16),
        pltpu.VMEM((2, LINE, share, gates // 2), BF16),
        dma((2, 2, 4)),
        dma((steps, 3)), dma((steps, 2)), dma((steps, 2)), dma((steps,)),
        dma((steps, 2 * LINE)), dma((steps, 2 * LINE)), dma((2, LINE)),
        dma((steps, 2)), dma((2,)), dma((steps, 3)), dma((2,)), dma((steps, 2)), dma((steps,)),
        dma((steps, 2 * LINE)), dma((steps, 2 * LINE)), dma((2 * LINE,)),
    ]
    result = pl.pallas_call(
        kernel,
        out_shape=jax.ShapeDtypeStruct((share, gates), F32),
        in_specs=[vmem] * 5 + [pl.BlockSpec(memory_space=pl.ANY)],
        out_specs=vmem,
        scratch_shapes=scratch,
        compiler_params=pltpu.CompilerParams(
            collective_id=0, has_side_effects=True, vmem_limit_bytes=56 * 2**20
        ),
    )(
        frames.reshape(steps, n, hid),
        cotangent.reshape(steps, n, hid),
        first_hidden.reshape(n, hid),
        first_cell.reshape(n, hid),
        gate_bias,
        gate_weight.reshape(3, 3, 2 * hid, gates),
    )
    return result[None]


def solution(mesh):
    return jax.shard_map(
        on_device,
        mesh=mesh,
        in_specs=(
            P(None, "batch", "space", None, None),
            P(None, "batch", "space", None, None),
            P("section", "batch", "space", None, None),
            P("section", "batch", "space", None, None),
            P("section", None),
            P("section", None, None),
        ),
        out_specs=P("section", ("space", "batch"), None),
        check_vma=False,
    )
```

```python
import functools

import jax
import jax.numpy as jnp
from jax import lax
from jax.experimental import pallas as pl
from jax.experimental.pallas import tpu as pltpu
from jax.sharding import PartitionSpec as P

F32 = jnp.float32
BF16 = jnp.bfloat16
MESH = pl.DeviceIdType.MESH
LINE = 4


def dot(left, right):
    return jnp.dot(left, right, preferred_element_type=F32)


def kernel(
    frames, cotangent, first_hidden, first_cell, bias, weight, out,
    wx, wh, wxt, wht, sx, sh, sg, top_hidden, preact, gates, cells, carry, coef, gin, gx_out, ghid,
    tiles_all, flipped, turned, grads_all, acc, leaving, landed,
    w_sem, sx_r, sh_r, c_r, gx_r, gh_r, ti_r, ga_r, rv_r,
    fr_s, fh_s, fc_s, ct_s, sx_s, sh_s, gx_s, gh_s, ti_s, ga_s, rv_s,
):
    z, s, k = lax.axis_index("section"), lax.axis_index("space"), lax.axis_index("batch")
    y, x = s // LINE, s % LINE
    sections, tiles = lax.axis_size("section"), lax.axis_size("space")
    cols = 32
    n = first_cell.shape[0]
    hid = first_cell.shape[1]
    half = hid // 2
    gate_half = 4 * half
    own2, above2, below2 = slice(2 * cols, 2 * cols + n), slice(0, 2 * cols), slice(2 * cols + n, 4 * cols + n)
    own1, above1, below1 = slice(cols, cols + n), slice(0, cols), slice(cols + n, 2 * cols + n)
    centre = slice(hid, 2 * hid)
    top, bottom, base, roof = s == 0, s == tiles - 1, z == 0, z == sections - 1
    inner = jnp.logical_not(base)
    pending = []

    def send(pred, make):
        if pred is None:
            make().start()
            pending.append(lambda: make().wait_send())
        else:
            pl.when(pred)(lambda: make().start())
            pending.append(lambda: pl.when(pred)(lambda: make().wait_send()))

    def remote(src, dst, send_sem, recv_sem, device):
        return pltpu.make_async_remote_copy(
            src_ref=src, dst_ref=dst, send_sem=send_sem, recv_sem=recv_sem,
            device_id=device, device_id_type=MESH,
        )

    def arrived(dst, recv_sem):
        remote(dst, dst, recv_sem, recv_sem, (z, s, 1 - k)).wait_recv()

    loads = {}
    for part, buffer in ((0, wx), (1, wh)):
        for c in range(2):
            for g in range(4):
                loads[part, c, g] = pltpu.make_async_copy(
                    weight.at[:, :, part * hid:(part + 1) * hid, pl.ds(g * hid + c * half, half)],
                    buffer.at[c, :, :, :, g * half:(g + 1) * half],
                    w_sem.at[part, c, g],
                )
    for part in (1, 0):
        for c in range(2):
            for g in range(4):
                loads[part, c, g].start()

    def weights_here(part):
        for c in range(2):
            for g in range(4):
                loads[part, c, g].wait()

    partners = [(jnp.logical_not(top), (z, s - 1, k)), (jnp.logical_not(bottom), (z, s + 1, k))]
    for step, ok in ((-1, z > 0), (1, z < sections - 1)):
        partners.append((ok, (z + step, s, k)))
        partners.append((ok & (s > 0), (z + step, s - 1, k)))
        partners.append((ok & (s < tiles - 1), (z + step, s + 1, k)))
    partners.append((None, (z, s, 1 - k)))
    for d in range(1, LINE):
        for core in range(2):
            partners.append((None, (z, y * LINE + (x + d) % LINE, core)))
            partners.append((None, (z, ((y + d) % LINE) * LINE + x, core)))
    barrier = pltpu.get_barrier_semaphore()
    expected = 0
    for pred, device in partners:
        greet = functools.partial(
            pl.semaphore_signal, barrier, inc=1, device_id=device, device_id_type=MESH
        )
        if pred is None:
            greet()
            expected = expected + 1
        else:
            pl.when(pred)(greet)
            expected = expected + jnp.where(pred, 1, 0)

    sh[0, own2, centre] = first_hidden[...]
    cells[0, own1] = first_cell[...]

    @pl.when(base)
    def _():
        for t in range(2):
            sx[t, own2, centre] = frames[t]

    @pl.when(roof)
    def _():
        for t in range(2):
            gin[t, own1] = cotangent[t]

    def clear(wide, narrow):
        for t in range(2):
            sx[t, wide, :] = jnp.zeros((2 * cols, 3 * hid), BF16)
            sh[t, wide, :] = jnp.zeros((2 * cols, 3 * hid), BF16)
            gin[t, narrow] = jnp.zeros((cols, hid), BF16)
        cells[0, narrow] = jnp.zeros((cols, hid), F32)
        ghid[narrow] = jnp.zeros((cols, hid), BF16)

    pl.when(top)(lambda: clear(above2, above1))
    pl.when(bottom)(lambda: clear(below2, below1))

    pl.semaphore_wait(barrier, expected)

    def send_edges(src, dst, send_sems, recv_sems, section, pred):
        up, down = s > 0, s < tiles - 1
        if pred is not None:
            up, down = up & pred, down & pred
        send(up, lambda: remote(src[0], dst[1], send_sems.at[0], recv_sems.at[1], (section, s - 1, k)))
        send(down, lambda: remote(src[1], dst[0], send_sems.at[1], recv_sems.at[0], (section, s + 1, k)))

    def wide(buffer, t):
        return buffer.at[t, above2, centre], buffer.at[t, below2, centre]

    def outer(ref, width):
        return ref.at[0:width], ref.at[n - width:n]

    def narrow(ref):
        return ref.at[above1], ref.at[below1]

    send_edges(outer(first_hidden, 2 * cols), wide(sh, 0), fh_s, sh_r.at[0], z, None)
    for t in range(2):
        send_edges(outer(frames.at[t], 2 * cols), wide(sx, t), fr_s.at[t], sx_r.at[t], z, base)
    send_edges(outer(first_cell, cols), narrow(cells.at[0]), fc_s, c_r, z, None)
    for t in range(2):
        send_edges(outer(cotangent.at[t], cols), narrow(gin.at[t]), ct_s.at[t], gx_r.at[t], z, roof)

    def spread_value(value, width):
        count = value.shape[0]
        column = lax.broadcasted_iota(jnp.int32, (count, width), 0) % cols
        left = jnp.where(column == 0, 0.0, pltpu.roll(value, 1, 0)).astype(BF16)
        right = jnp.where(column == cols - 1, 0.0, pltpu.roll(value, count - 1, 0)).astype(BF16)
        return left, right

    def spread(buffer, t, rows, width):
        left, right = spread_value(buffer[t, rows, width:2 * width].astype(F32), width)
        buffer[t, rows, 0:width] = left
        buffer[t, rows, 2 * width:3 * width] = right

    def when_edges(first, second):
        pl.when(jnp.logical_not(top))(first)
        pl.when(jnp.logical_not(bottom))(second)

    def wide_here(buffer, t, recv_sems):
        def here(rows, index):
            arrived(buffer.at[t, rows, centre], recv_sems.at[index])
            spread(buffer, t, rows, hid)

        when_edges(lambda: here(above2, 0), lambda: here(below2, 1))

    def narrow_here(ref, recv_sems):
        when_edges(
            lambda: arrived(ref.at[above1], recv_sems.at[0]),
            lambda: arrived(ref.at[below1], recv_sems.at[1]),
        )

    def conv(buffer, t, weights, c, offsets):
        total = None
        for a in offsets:
            term = dot(
                buffer[t, cols * (a + 1):cols * (a + 1) + n, :],
                weights[c, a].reshape(3 * hid, gate_half),
            )
            total = term if total is None else total + term
        return total

    def conv_beside(t, c):
        total = None
        for buffer, weights in ((sh, wh), (sx, wx)):
            for a in range(3):
                low = cols * (a + 1) + n
                cells_in = jnp.concatenate(
                    [buffer[t, cols * a:cols * (a + 1), :], buffer[t, low:low + cols, :]], axis=0
                )
                term = dot(cells_in, weights[c, a].reshape(3 * hid, gate_half))
                total = term if total is None else total + term
        return total

    def bias_of(c):
        return jnp.concatenate(
            [bias[0:1, g * hid + c * half:g * hid + (c + 1) * half] for g in range(4)], axis=1
        )

    def activate(now, old):
        i_gate = jax.nn.sigmoid(now[:, 0:half])
        f_gate = jax.nn.sigmoid(now[:, half:2 * half])
        o_gate = jax.nn.sigmoid(now[:, 2 * half:3 * half])
        cand = jnp.tanh(now[:, 3 * half:])
        new = f_gate * old + i_gate * cand
        return i_gate, f_gate, o_gate, cand, new, jnp.tanh(new)

    def factors(i_gate, f_gate, o_gate, cand, squash, old):
        return (
            o_gate * (1.0 - squash * squash),
            cand * i_gate * (1.0 - i_gate),
            old * f_gate * (1.0 - f_gate),
            squash * o_gate * (1.0 - o_gate),
            i_gate * (1.0 - cand * cand),
            f_gate,
        )

    def turn_weights(source, target):
        def one(a, carried):
            for b in range(3):
                for c in range(2):
                    start = (2 - b) * 4 * hid + c * gate_half
                    target[a, start:start + gate_half, :] = source[c, a, b].T
            return carried

        lax.fori_loop(0, 3, one, 0)

    def turn_all_weights():
        turn_weights(wh, wht)
        pl.when(inner)(lambda: turn_weights(wx, wxt))

    def spread_to_group(pred, view, send_sems, recv_sems):
        for d in (0, 1, 3, 2):
            for c in range(2):
                there = ((x if c == 0 else y) + d) % LINE
                chip = y * LINE + there if c == 0 else there * LINE + x
                slot = 2 * (x if c == 0 else y) + k
                src, dst = view(c, slot)
                make = functools.partial(
                    remote, src, dst, send_sems.at[c * LINE + d], recv_sems.at[slot], (z, chip, c)
                )
                ok = pred
                if d == 0:
                    ok = (k != c) if pred is None else pred & (k != c)
                    own = (k == c) if pred is None else pred & (k == c)
                    pl.when(own)(
                        functools.partial(
                            lambda src, dst, sem: pltpu.make_async_copy(src, dst, sem).start(),
                            src, dst, recv_sems.at[slot],
                        )
                    )
                send(ok, make)

    def send_tile(t, part, pred):
        src = (sh if part else sx).at[t, cols:3 * cols + n, centre]
        spread_to_group(
            pred, lambda c, slot: (src, tiles_all.at[t, part, slot]), ti_s.at[t, part], ti_r.at[t, part]
        )

    def send_grads(t, pred):
        def view(c, slot):
            src = sg.at[t, own1, 4 * hid + c * gate_half:4 * hid + (c + 1) * gate_half]
            return src, grads_all.at[t, pl.ds(pl.multiple_of(slot * n, n), n), :]

        spread_to_group(pred, view, ga_s.at[t], ga_r.at[t])

    rows = out.shape[0]
    block = 2 * rows
    me = jnp.where(k == 0, y, x)

    def turn_patches():
        for t in range(2):
            for part in range(2):
                for slot in range(2 * LINE):
                    arrived(tiles_all.at[t, part, slot], ti_r.at[t, part, slot])

            def one(slot, carried):
                for part in range(2):
                    tile = tiles_all[t, part, slot]
                    left, right = spread_value(tile.astype(F32), hid)
                    for b, moved in enumerate((left, tile, right)):
                        for a in range(3):
                            at = (a * 3 + b) * 2 * hid + part * hid
                            flipped[at:at + hid, :] = moved[cols * a:cols * a + n, :].T
                for j in range(LINE):
                    chip = jnp.where(k == 0, j * LINE + x, y * LINE + j)
                    turned[t, j, :, pl.ds(pl.multiple_of(slot * n, n), n)] = flipped[
                        pl.ds(pl.multiple_of(chip * block, 32), block), :
                    ]
                return carried

            lax.fori_loop(0, 2 * LINE, one, 0)

    @pl.when(z >= 2)
    def _():
        weights_here(1)
        weights_here(0)
        turn_all_weights()

    for t in range(2):
        spread(sh, t, own2, hid)
        if t == 0:
            pl.when(z < 2)(lambda: weights_here(1))
        part_sums = [conv(sh, t, wh, c, (1,)) + bias_of(c) for c in range(2)]
        for c in range(2):
            preact[:, c * gate_half:(c + 1) * gate_half] = part_sums[c]
        wide_here(sh, t, sh_r.at[t])
        if t == 0:
            send_tile(0, 1, inner)
        for c in range(2):
            preact[:, c * gate_half:(c + 1) * gate_half] += conv(sh, t, wh, c, (0, 2))
        pl.when(inner)(lambda t=t: arrived(sx.at[t, own2, centre], sx_r.at[t, 2]))
        spread(sx, t, own2, hid)
        if t == 0:
            pl.when(z < 2)(lambda: weights_here(0))
        for c in range(2):
            preact[:, c * gate_half:(c + 1) * gate_half] += conv(sx, t, wx, c, (1,))
        wide_here(sx, t, sx_r.at[t])
        for c in range(2):
            chan = slice(c * half, (c + 1) * half)
            now = preact[:, c * gate_half:(c + 1) * gate_half] + conv(sx, t, wx, c, (0, 2))
            i_gate, f_gate, o_gate, cand, new, squash = activate(now, cells[t, own1, chan])
            hidden = (o_gate * squash).astype(BF16)
            if t == 0:
                sh[1, own2, hid + c * half:hid + (c + 1) * half] = hidden
                cells[1, own1, chan] = new
            else:
                top_hidden[:, chan] = hidden
            for index, value in enumerate((i_gate, f_gate, o_gate, cand, squash)):
                gates[index, :, chan] = value
        whole = sh.at[1, own2, centre] if t == 0 else top_hidden
        send(
            z < sections - 1,
            lambda whole=whole, t=t: remote(
                whole, sx.at[t, own2, centre], sx_s.at[t, 2], sx_r.at[t, 2], (z + 1, s, k)
            ),
        )
        if t == 0:
            ends = sh.at[1, 2 * cols:4 * cols, centre], sh.at[1, n:n + 2 * cols, centre]
            send_edges(ends, wide(sh, 1), sh_s, sh_r.at[1], z, None)
        else:
            ends = outer(top_hidden, 2 * cols)
        send_edges(ends, wide(sx, t), sx_s.at[t], sx_r.at[t], z + 1, z < sections - 1)
        if t == 0:
            narrow_here(cells.at[0], c_r)
        for c in range(2):
            chan = slice(c * half, (c + 1) * half)
            beside = jnp.concatenate([cells[t, above1, chan], cells[t, below1, chan]], axis=0)
            values = activate(conv_beside(t, c) + bias_of(c), beside)
            i_gate, f_gate, o_gate, cand, new, squash = values
            if t == 0:
                cells[1, above1, chan] = new[0:cols]
                cells[1, below1, chan] = new[cols:]
            for index, value in enumerate(factors(i_gate, f_gate, o_gate, cand, squash, beside)):
                coef[t, index, above1, chan] = value[0:cols]
                coef[t, index, below1, chan] = value[cols:]
            i_gate, f_gate, o_gate, cand, squash = (gates[index, :, chan] for index in range(5))
            for index, value in enumerate(
                factors(i_gate, f_gate, o_gate, cand, squash, cells[t, own1, chan])
            ):
                coef[t, index, own1, chan] = value

    pl.when(z < 2)(turn_all_weights)
    send_tile(0, 1, base)
    for t, part in ((0, 0), (1, 1), (1, 0)):
        send_tile(t, part, jnp.logical_not(roof))
    pl.when(z < 2)(turn_patches)

    def back_conv(t, weights):
        total = None
        for a in range(3):
            term = dot(sg[t, cols * (2 - a):cols * (2 - a) + n, :], weights[a])
            total = term if total is None else total + term
        return total.astype(BF16)

    for t in (1, 0):
        pl.when(jnp.logical_not(roof))(lambda t=t: arrived(gin.at[t, own1], gx_r.at[t, 2]))
        if t == 1:
            narrow_here(gin.at[t], gx_r.at[t])
        else:
            @pl.when(inner)
            def _():
                narrow_here(gin.at[0], gx_r.at[0])
                narrow_here(ghid, gh_r)
        for c in range(2):
            chan = slice(c * half, (c + 1) * half)
            grad_h = gin[t, :, chan].astype(F32)
            if t == 0:
                grad_h = grad_h + ghid[:, chan].astype(F32)
            grad_c = grad_h * coef[t, 0, :, chan]
            if t == 0:
                grad_c = grad_c + carry[:, chan]
            for g, value in enumerate((
                grad_c * coef[t, 1, :, chan],
                grad_c * coef[t, 2, :, chan],
                grad_h * coef[t, 3, :, chan],
                grad_c * coef[t, 4, :, chan],
            )):
                at = 4 * hid + c * gate_half + g * half
                sg[t, :, at:at + half] = value.astype(BF16)
            if t == 1:
                carry[:, chan] = grad_c * coef[t, 5, :, chan]
        send_grads(t, base)

        def widen(t=t):
            spread(sg, t, slice(0, 2 * cols + n), 4 * hid)

            @pl.when(top)
            def _():
                sg[t, above1, :] = jnp.zeros((cols, 12 * hid), BF16)

            @pl.when(bottom)
            def _():
                sg[t, below1, :] = jnp.zeros((cols, 12 * hid), BF16)

        def input_grad(t=t):
            gx_out[t] = back_conv(t, wxt)

        if t == 1:
            widen()
            pl.when(inner)(input_grad)
        else:
            @pl.when(inner)
            def _():
                widen()
                input_grad()

        send(
            inner,
            lambda t=t: remote(gx_out.at[t], gin.at[t, own1], gx_s.at[t, 2], gx_r.at[t, 2], (z - 1, s, k)),
        )
        send_edges(
            outer(gx_out.at[t], cols), narrow(gin.at[t]), gx_s.at[t], gx_r.at[t], z - 1,
            inner if t == 1 else z >= 2,
        )
        if t == 1:
            ghid[own1] = back_conv(t, wht)
            send_edges(
                (ghid.at[cols:2 * cols], ghid.at[n:n + cols]), narrow(ghid), gh_s, gh_r, z, inner
            )
        send_grads(t, inner)

    for t, part in ((0, 0), (1, 1), (1, 0)):
        send_tile(t, part, roof)
    pl.when(z >= 2)(turn_patches)

    for t in (1, 0):
        for slot in range(2 * LINE):
            arrived(grads_all.at[t, slot * n:(slot + 1) * n], ga_r.at[t, slot])
        if t == 1:
            for j in range(LINE):
                acc[j] = dot(turned[t, j], grads_all[t])
        else:
            for d in (1, 3, 2, 0):
                j = (me + d) % LINE
                leaving[d] = (acc[j] + dot(turned[t, j], grads_all[t])).astype(BF16)
                chip = jnp.where(k == 0, j * LINE + x, y * LINE + j)
                for q in range(2):
                    src, dst = leaving.at[d, q * rows:(q + 1) * rows], landed.at[k, me]
                    make = functools.partial(
                        remote, src, dst, rv_s.at[d * 2 + q], rv_r.at[k, me], (z, chip, q)
                    )
                    if d == 0:
                        pl.when(k == q)(
                            lambda src=src, dst=dst: pltpu.make_async_copy(
                                src, dst, rv_r.at[k, me]
                            ).start()
                        )
                    send(k != q if d == 0 else None, make)
    for c in range(2):
        for i in range(LINE):
            arrived(landed.at[c, i], rv_r.at[c, i])
        for g in range(4):
            total = landed[c, 0, :, g * half:(g + 1) * half].astype(F32)
            for i in range(1, LINE):
                total = total + landed[c, i, :, g * half:(g + 1) * half].astype(F32)
            out[:, g * hid + c * half:g * hid + (c + 1) * half] = total
    for wait in pending:
        wait()


def on_device(frames, cotangent, first_hidden, first_cell, gate_bias, gate_weight):
    steps, _, tile_rows, cols, hid = frames.shape
    n = tile_rows * cols
    pad = n + 2 * cols
    half = hid // 2
    gates = 4 * hid
    share = 18 * hid // (lax.axis_size("space") * lax.axis_size("batch"))
    block = 2 * share
    vmem = pl.BlockSpec(memory_space=pltpu.VMEM)
    dma = pltpu.SemaphoreType.DMA
    scratch = [
        pltpu.VMEM((2, 3, 3, hid, gates // 2), BF16),
        pltpu.VMEM((2, 3, 3, hid, gates // 2), BF16),
        pltpu.VMEM((3, 3 * gates, hid), BF16),
        pltpu.VMEM((3, 3 * gates, hid), BF16),
        pltpu.VMEM((steps, pad + 2 * cols, 3 * hid), BF16),
        pltpu.VMEM((steps, pad + 2 * cols, 3 * hid), BF16),
        pltpu.VMEM((steps, pad, 3 * gates), BF16),
        pltpu.VMEM((n, hid), BF16),
        pltpu.VMEM((n, gates), F32),
        pltpu.VMEM((5, n, hid), F32),
        pltpu.VMEM((steps, pad, hid), F32),
        pltpu.VMEM((pad, hid), F32),
        pltpu.VMEM((steps, 6, pad, hid), F32),
        pltpu.VMEM((steps, pad, hid), BF16),
        pltpu.VMEM((steps, n, hid), BF16),
        pltpu.VMEM((pad, hid), BF16),
        pltpu.VMEM((steps, 2, 2 * LINE, pad, hid), BF16),
        pltpu.VMEM((18 * hid, n), BF16),
        pltpu.VMEM((steps, LINE, block, 2 * LINE * n), BF16),
        pltpu.VMEM((steps, 2 * LINE * n, gates // 2), BF16),
        pltpu.VMEM((LINE, block, gates // 2), F32),
        pltpu.VMEM((LINE, block, gates // 2), BF16),
        pltpu.VMEM((2, LINE, share, gates // 2), BF16),
        dma((2, 2, 4)),
        dma((steps, 3)), dma((steps, 2)), dma((2,)), dma((steps, 3)), dma((2,)),
        dma((steps, 2, 2 * LINE)), dma((steps, 2 * LINE)), dma((2, LINE)),
        dma((steps, 2)), dma((2,)), dma((2,)), dma((steps, 2)),
        dma((steps, 3)), dma((2,)), dma((steps, 3)), dma((2,)),
        dma((steps, 2, 2 * LINE)), dma((steps, 2 * LINE)), dma((2 * LINE,)),
    ]
    result = pl.pallas_call(
        kernel,
        out_shape=jax.ShapeDtypeStruct((share, gates), F32),
        in_specs=[vmem] * 5 + [pl.BlockSpec(memory_space=pl.ANY)],
        out_specs=vmem,
        scratch_shapes=scratch,
        compiler_params=pltpu.CompilerParams(
            collective_id=0, has_side_effects=True, vmem_limit_bytes=56 * 2**20
        ),
    )(
        frames.reshape(steps, n, hid),
        cotangent.reshape(steps, n, hid),
        first_hidden.reshape(n, hid),
        first_cell.reshape(n, hid),
        gate_bias,
        gate_weight.reshape(3, 3, 2 * hid, gates),
    )
    return result[None]


def solution(mesh):
    return jax.shard_map(
        on_device,
        mesh=mesh,
        in_specs=(
            P(None, "batch", "space", None, None),
            P(None, "batch", "space", None, None),
            P("section", "batch", "space", None, None),
            P("section", "batch", "space", None, None),
            P("section", None),
            P("section", None, None),
        ),
        out_specs=P("section", ("space", "batch"), None),
        check_vma=False,
    )
```

```python
import functools

import jax
import jax.numpy as jnp
from jax import lax
from jax.experimental import pallas as pl
from jax.experimental.pallas import tpu as pltpu
from jax.sharding import PartitionSpec as P

F32 = jnp.float32
BF16 = jnp.bfloat16
MESH = pl.DeviceIdType.MESH
LINE = 4


def dot(left, right):
    return jnp.dot(left, right, preferred_element_type=F32)


def kernel(
    frames, cotangent, first_hidden, first_cell, bias, weight, out,
    wx, wh, wxt, wht, sx, sh, sg, top_hidden, preact, gates, cells, carry, coef, gin, gx_out, ghid,
    tiles_all, flipped, turned, grads_all, acc, leaving, landed,
    w_sem, in_sem, sx_r, sx_f, sh_r, sh_f, c_r, gx_r, gh_r, ti_r, ga_r, rv_r,
    fr_s, fr_f, fh_s, fh_f, fc_s, ct_s, sx_s, sx_fs, sh_s, sh_fs, gx_s, gh_s, ti_s, ga_s, rv_s,
):
    z, s, k = lax.axis_index("section"), lax.axis_index("space"), lax.axis_index("batch")
    y, x = s // LINE, s % LINE
    sections, tiles = lax.axis_size("section"), lax.axis_size("space")
    cols = 32
    n = first_cell.shape[0]
    hid = first_cell.shape[1]
    half = hid // 2
    gate_half = 4 * half
    own2, above2, below2 = slice(2 * cols, 2 * cols + n), slice(0, 2 * cols), slice(2 * cols + n, 4 * cols + n)
    near = slice(cols, 2 * cols), slice(2 * cols + n, 3 * cols + n)
    far = slice(0, cols), slice(3 * cols + n, 4 * cols + n)
    own1, above1, below1 = slice(cols, cols + n), slice(0, cols), slice(cols + n, 2 * cols + n)
    centre = slice(hid, 2 * hid)
    top, bottom, base, roof = s == 0, s == tiles - 1, z == 0, z == sections - 1
    inner = jnp.logical_not(base)
    pending = []

    def send(pred, make):
        if pred is None:
            make().start()
            pending.append(lambda: make().wait_send())
        else:
            ask = pred if callable(pred) else lambda: pred
            pl.when(ask())(lambda: make().start())
            pending.append(lambda: pl.when(ask())(lambda: make().wait_send()))

    def remote(src, dst, send_sem, recv_sem, device):
        return pltpu.make_async_remote_copy(
            src_ref=src, dst_ref=dst, send_sem=send_sem, recv_sem=recv_sem,
            device_id=device, device_id_type=MESH,
        )

    def arrived(dst, recv_sem):
        remote(dst, dst, recv_sem, recv_sem, (z, s, 1 - k)).wait_recv()

    loads = {}
    for part, buffer in ((0, wx), (1, wh)):
        for c in range(2):
            for g in range(4):
                loads[part, c, g] = pltpu.make_async_copy(
                    weight.at[:, :, part * hid:(part + 1) * hid, pl.ds(g * hid + c * half, half)],
                    buffer.at[c, :, :, :, g * half:(g + 1) * half],
                    w_sem.at[part, c, g],
                )

    def weights_here(part):
        for c in range(2):
            for g in range(4):
                loads[part, c, g].wait()

    partners = [(jnp.logical_not(top), (z, s - 1, k)), (jnp.logical_not(bottom), (z, s + 1, k))]
    for step, ok in ((-1, z > 0), (1, z < sections - 1)):
        partners.append((ok, (z + step, s, k)))
        partners.append((ok & (s > 0), (z + step, s - 1, k)))
        partners.append((ok & (s < tiles - 1), (z + step, s + 1, k)))
    partners.append((None, (z, s, 1 - k)))
    for d in range(1, LINE):
        for core in range(2):
            partners.append((None, (z, y * LINE + (x + d) % LINE, core)))
            partners.append((None, (z, ((y + d) % LINE) * LINE + x, core)))
    barrier = pltpu.get_barrier_semaphore()
    expected = 0
    for pred, device in partners:
        greet = functools.partial(
            pl.semaphore_signal, barrier, inc=1, device_id=device, device_id_type=MESH
        )
        if pred is None:
            greet()
            expected = expected + 1
        else:
            pl.when(pred)(greet)
            expected = expected + jnp.where(pred, 1, 0)

    half_lanes = [slice(hid + c * half, hid + (c + 1) * half) for c in range(2)]
    own_hidden = pltpu.make_async_copy(first_hidden, sh.at[0, own2, centre], in_sem.at[0])
    own_cell = pltpu.make_async_copy(first_cell, cells.at[0, own1], in_sem.at[1])
    own_hidden.start()

    @pl.when(base)
    def _():
        for t in range(2):
            for c in range(2):
                pltpu.make_async_copy(
                    frames.at[t, :, pl.ds(c * half, half)], sx.at[t, own2, half_lanes[c]], sx_r.at[t, c, 2]
                ).start()

    own_cell.start()

    @pl.when(roof)
    def _():
        for t in range(2):
            pltpu.make_async_copy(cotangent.at[t], gin.at[t, own1], gx_r.at[t, 2]).start()

    for part in (1, 0):
        for c in range(2):
            for g in range(4):
                loads[part, c, g].start()

    def clear(wide, narrow):
        for t in range(2):
            sx[t, wide, :] = jnp.zeros((2 * cols, 3 * hid), BF16)
            sh[t, wide, :] = jnp.zeros((2 * cols, 3 * hid), BF16)
            gin[t, narrow] = jnp.zeros((cols, hid), BF16)
        cells[0, narrow] = jnp.zeros((cols, hid), F32)
        ghid[narrow] = jnp.zeros((cols, hid), BF16)

    pl.when(top)(lambda: clear(above2, above1))
    pl.when(bottom)(lambda: clear(below2, below1))

    pl.semaphore_wait(barrier, expected)

    def send_edges(src, dst, send_sems, recv_sems, section, pred):
        edges(lambda: (src, dst, send_sems, recv_sems), section, pred)

    def edges(parts, section, pred):
        def up():
            return s > 0 if pred is None else (s > 0) & pred

        def down():
            return s < tiles - 1 if pred is None else (s < tiles - 1) & pred

        def make(end, device):
            src, dst, send_sems, recv_sems = parts()
            return remote(src[end], dst[1 - end], send_sems.at[end], recv_sems.at[1 - end], device)

        send(up, lambda: make(0, (section, s - 1, k)))
        send(down, lambda: make(1, (section, s + 1, k)))

    def outer(ref, width):
        return ref.at[0:width], ref.at[n - width:n]

    def beyond(ref):
        return ref.at[cols:2 * cols], ref.at[n - 2 * cols:n - cols]

    def narrow(ref):
        return ref.at[above1], ref.at[below1]

    def at_rows(buffer, t, rows, lanes):
        return buffer.at[t, rows[0], lanes], buffer.at[t, rows[1], lanes]

    def halves(ref, c):
        return ref.at[0:cols, pl.ds(c * half, half)], ref.at[n - cols:n, pl.ds(c * half, half)]

    send_edges(outer(first_hidden, cols), at_rows(sh, 0, near, centre), fh_s, sh_r.at[0, 0], z, None)

    def send_frames(t):
        for c in range(2):
            send_edges(
                halves(frames.at[t], c), at_rows(sx, t, near, half_lanes[c]),
                fr_s.at[t, c], sx_r.at[t, c], z, base,
            )

    send_frames(0)
    send_edges(beyond(first_hidden), at_rows(sh, 0, far, centre), fh_f, sh_f.at[0], z, None)
    send_edges(outer(first_cell, cols), narrow(cells.at[0]), fc_s, c_r, z, None)
    send_edges(beyond(frames.at[0]), at_rows(sx, 0, far, centre), fr_f.at[0], sx_f.at[0], z, base)
    send_frames(1)
    send_edges(beyond(frames.at[1]), at_rows(sx, 1, far, centre), fr_f.at[1], sx_f.at[1], z, base)
    for t in range(2):
        send_edges(outer(cotangent.at[t], cols), narrow(gin.at[t]), ct_s.at[t], gx_r.at[t], z, roof)

    def spread_value(value, width):
        count = value.shape[0]
        column = lax.broadcasted_iota(jnp.int32, (count, width), 0) % cols
        left = jnp.where(column == 0, 0.0, pltpu.roll(value, 1, 0)).astype(BF16)
        right = jnp.where(column == cols - 1, 0.0, pltpu.roll(value, count - 1, 0)).astype(BF16)
        return left, right

    def spread(buffer, t, rows, width):
        left, right = spread_value(buffer[t, rows, width:2 * width].astype(F32), width)
        buffer[t, rows, 0:width] = left
        buffer[t, rows, 2 * width:3 * width] = right

    def when_edges(first, second):
        pl.when(jnp.logical_not(top))(first)
        pl.when(jnp.logical_not(bottom))(second)

    def near_here(buffer, t, recv_sems, lanes):
        def here(index):
            for c, part in enumerate(lanes):
                arrived(buffer.at[t, near[index], part], recv_sems.at[c, index])
            spread(buffer, t, near[index], hid)

        when_edges(lambda: here(0), lambda: here(1))

    def far_here(buffer, t, recv_sems):
        def here(index):
            arrived(buffer.at[t, far[index], centre], recv_sems.at[index])
            spread(buffer, t, far[index], hid)

        when_edges(lambda: here(0), lambda: here(1))

    def narrow_here(ref, recv_sems):
        when_edges(
            lambda: arrived(ref.at[above1], recv_sems.at[0]),
            lambda: arrived(ref.at[below1], recv_sems.at[1]),
        )

    def conv(buffer, t, weights, c, offsets):
        total = None
        for a in offsets:
            term = dot(
                buffer[t, cols * (a + 1):cols * (a + 1) + n, :],
                weights[c, a].reshape(3 * hid, gate_half),
            )
            total = term if total is None else total + term
        return total

    def conv_all(buffer, t, weights, c):
        total = None
        for a in range(3):
            term = dot(
                buffer[t, cols * a:cols * (a + 2) + n, :],
                weights[c, a].reshape(3 * hid, gate_half),
            )
            total = term if total is None else total + term
        return total

    def conv_beside(t, c):
        total = None
        for buffer, weights in ((sh, wh), (sx, wx)):
            for a in range(3):
                low = cols * (a + 1) + n
                cells_in = jnp.concatenate(
                    [buffer[t, cols * a:cols * (a + 1), :], buffer[t, low:low + cols, :]], axis=0
                )
                term = dot(cells_in, weights[c, a].reshape(3 * hid, gate_half))
                total = term if total is None else total + term
        return total

    def bias_of(c):
        return jnp.concatenate(
            [bias[0:1, g * hid + c * half:g * hid + (c + 1) * half] for g in range(4)], axis=1
        )

    def activate(now, old):
        i_gate = jax.nn.sigmoid(now[:, 0:half])
        f_gate = jax.nn.sigmoid(now[:, half:2 * half])
        o_gate = jax.nn.sigmoid(now[:, 2 * half:3 * half])
        cand = jnp.tanh(now[:, 3 * half:])
        new = f_gate * old + i_gate * cand
        return i_gate, f_gate, o_gate, cand, new, jnp.tanh(new)

    def factors(i_gate, f_gate, o_gate, cand, squash, old):
        return (
            o_gate * (1.0 - squash * squash),
            cand * i_gate * (1.0 - i_gate),
            old * f_gate * (1.0 - f_gate),
            squash * o_gate * (1.0 - o_gate),
            i_gate * (1.0 - cand * cand),
            f_gate,
        )

    def turn_weights(source, target):
        def one(a, carried):
            for b in range(3):
                for c in range(2):
                    start = (2 - b) * 4 * hid + c * gate_half
                    target[a, start:start + gate_half, :] = source[c, a, b].T
            return carried

        lax.fori_loop(0, 3, one, 0)

    def turn_all_weights():
        turn_weights(wh, wht)
        pl.when(inner)(lambda: turn_weights(wx, wxt))

    def spread_to_group(pred, view, send_sems, recv_sems):
        for d in (0, 1, 3, 2):
            for c in range(2):
                there = ((x if c == 0 else y) + d) % LINE
                chip = y * LINE + there if c == 0 else there * LINE + x
                slot = 2 * (x if c == 0 else y) + k
                src, dst = view(c, slot)
                make = functools.partial(
                    remote, src, dst, send_sems.at[c * LINE + d], recv_sems.at[slot], (z, chip, c)
                )
                ok = pred
                if d == 0:
                    ok = (k != c) if pred is None else pred & (k != c)
                    own = (k == c) if pred is None else pred & (k == c)
                    pl.when(own)(
                        functools.partial(
                            lambda src, dst, sem: pltpu.make_async_copy(src, dst, sem).start(),
                            src, dst, recv_sems.at[slot],
                        )
                    )
                send(ok, make)

    def send_tile(t, part, pred):
        src = (sh if part else sx).at[t, cols:3 * cols + n, centre]
        spread_to_group(
            pred, lambda c, slot: (src, tiles_all.at[t, part, slot]), ti_s.at[t, part], ti_r.at[t, part]
        )

    pairs = [slice(p * 2 * half, (p + 1) * 2 * half) for p in range(2)]

    def send_grads(t, pred):
        for p, lanes in enumerate(pairs):
            def view(c, slot):
                at = 4 * hid + c * gate_half
                src = sg.at[t, own1, at + lanes.start:at + lanes.stop]
                return src, grads_all.at[t, pl.ds(pl.multiple_of(slot * n, n), n), lanes]

            spread_to_group(pred, view, ga_s.at[t, p], ga_r.at[t, p])

    rows = out.shape[0]
    block = 2 * rows
    me = jnp.where(k == 0, y, x)

    def turn_patches():
        for t in range(2):
            for part in range(2):
                for slot in range(2 * LINE):
                    arrived(tiles_all.at[t, part, slot], ti_r.at[t, part, slot])

            def one(slot, carried):
                for part in range(2):
                    tile = tiles_all[t, part, slot]
                    left, right = spread_value(tile.astype(F32), hid)
                    for b, moved in enumerate((left, tile, right)):
                        for a in range(3):
                            at = (a * 3 + b) * 2 * hid + part * hid
                            flipped[at:at + hid, :] = moved[cols * a:cols * a + n, :].T
                for j in range(LINE):
                    chip = jnp.where(k == 0, j * LINE + x, y * LINE + j)
                    turned[t, j, :, pl.ds(pl.multiple_of(slot * n, n), n)] = flipped[
                        pl.ds(pl.multiple_of(chip * block, 32), block), :
                    ]
                return carried

            lax.fori_loop(0, 2 * LINE, one, 0)

    @pl.when(z >= 2)
    def _():
        weights_here(1)
        weights_here(0)
        turn_all_weights()

    not_roof = jnp.logical_not(roof)
    z_up = z + 1

    def save(t, into, values, old, chan):
        i_gate, f_gate, o_gate, cand, squash = values
        for index, value in enumerate(factors(i_gate, f_gate, o_gate, cand, squash, old)):
            for cells_to, cells_from in into:
                coef[t, index, cells_to, chan] = value[cells_from]

    def x_here(t):
        for c in range(2):
            arrived(sx.at[t, own2, half_lanes[c]], sx_r.at[t, c, 2])
        spread(sx, t, own2, hid)

    def own_rows(t):
        part_sums = [conv(sh, t, wh, c, (1,)) + bias_of(c) for c in range(2)]
        for c in range(2):
            preact[0:n, c * gate_half:(c + 1) * gate_half] = part_sums[c]
        near_here(sh, t, sh_r.at[t], (centre,) if t == 0 else half_lanes)
        if t == 0:
            send_tile(0, 1, inner)
        for c in range(2):
            preact[0:n, c * gate_half:(c + 1) * gate_half] += conv(sh, t, wh, c, (0, 2))
        if t == 0:
            pl.when(z < 2)(lambda: weights_here(0))
        x_here(t)
        for c in range(2):
            preact[0:n, c * gate_half:(c + 1) * gate_half] += conv(sx, t, wx, c, (1,))
        near_here(sx, t, sx_r.at[t], half_lanes)
        if t == 0:
            own_cell.wait()
        for c in range(2):
            chan, lanes = slice(c * half, (c + 1) * half), half_lanes[c]
            now = preact[0:n, c * gate_half:(c + 1) * gate_half] + conv(sx, t, wx, c, (0, 2))
            i_gate, f_gate, o_gate, cand, new, squash = activate(now, cells[t, own1, chan])
            hidden = (o_gate * squash).astype(BF16)
            if t == 0:
                sh[1, own2, lanes] = hidden
                cells[1, own1, chan] = new
                whole = sh.at[1, own2, lanes]
                ends = sh.at[1, 2 * cols:3 * cols, lanes], sh.at[1, n + cols:n + 2 * cols, lanes]
            else:
                top_hidden[:, chan] = hidden
                whole = top_hidden.at[:, chan]
                ends = top_hidden.at[0:cols, chan], top_hidden.at[n - cols:n, chan]
            send(
                not_roof,
                lambda whole=whole, lanes=lanes, c=c: remote(
                    whole, sx.at[t, own2, lanes], sx_s.at[t, c, 2], sx_r.at[t, c, 2], (z_up, s, k)
                ),
            )
            if t == 0:
                send_edges(ends, at_rows(sh, 1, near, lanes), sh_s.at[c], sh_r.at[1, c], z, None)
            edges(
                lambda ends=ends, lanes=lanes, c=c: (
                    ends, at_rows(sx, t, near, lanes), sx_s.at[t, c], sx_r.at[t, c]
                ),
                z_up, not_roof,
            )
            for index, value in enumerate((i_gate, f_gate, o_gate, cand, squash)):
                gates[index, :, chan] = value
        if t == 0:
            ends = sh.at[1, 3 * cols:4 * cols, centre], sh.at[1, n:n + cols, centre]
            send_edges(ends, at_rows(sh, 1, far, centre), sh_fs, sh_f.at[1], z, None)
        else:
            ends = beyond(top_hidden)
        last = ends
        edges(
            lambda: (last, at_rows(sx, t, far, centre), sx_fs.at[t], sx_f.at[t]), z_up, not_roof
        )
        if t == 0:
            narrow_here(cells.at[0], c_r)

        far_here(sh, t, sh_f.at[t])
        far_here(sx, t, sx_f.at[t])
        for c in range(2):
            chan = slice(c * half, (c + 1) * half)
            beside = jnp.concatenate([cells[t, above1, chan], cells[t, below1, chan]], axis=0)
            i_gate, f_gate, o_gate, cand, new, squash = activate(conv_beside(t, c) + bias_of(c), beside)
            if t == 0:
                cells[1, above1, chan] = new[0:cols]
                cells[1, below1, chan] = new[cols:]
            save(
                t, ((above1, slice(0, cols)), (below1, slice(cols, 2 * cols))),
                (i_gate, f_gate, o_gate, cand, squash), beside, chan,
            )
            save(
                t, ((own1, slice(0, n)),),
                tuple(gates[index, :, chan] for index in range(5)), cells[t, own1, chan], chan,
            )

    def all_rows():
        near_here(sh, 1, sh_r.at[1], half_lanes)
        far_here(sh, 1, sh_f.at[1])
        for c in range(2):
            preact[:, c * gate_half:(c + 1) * gate_half] = conv_all(sh, 1, wh, c) + bias_of(c)
        x_here(1)
        near_here(sx, 1, sx_r.at[1], half_lanes)
        far_here(sx, 1, sx_f.at[1])
        for c in range(2):
            chan = slice(c * half, (c + 1) * half)
            now = preact[:, c * gate_half:(c + 1) * gate_half] + conv_all(sx, 1, wx, c)
            old = cells[1, :, chan]
            i_gate, f_gate, o_gate, cand, new, squash = activate(now, old)
            save(
                1, ((slice(0, n + 2 * cols), slice(0, n + 2 * cols)),),
                (i_gate, f_gate, o_gate, cand, squash), old, chan,
            )

    own_hidden.wait()
    spread(sh, 0, own2, hid)
    pl.when(z < 2)(lambda: weights_here(1))
    own_rows(0)
    spread(sh, 1, own2, hid)
    pl.when(not_roof)(lambda: own_rows(1))
    pl.when(roof)(all_rows)

    pl.when(z < 2)(turn_all_weights)
    send_tile(0, 1, base)
    for t, part in ((0, 0), (1, 1), (1, 0)):
        send_tile(t, part, not_roof)
    pl.when(z < 2)(turn_patches)

    def back_conv(t, weights):
        total = None
        for a in range(3):
            term = dot(sg[t, cols * (2 - a):cols * (2 - a) + n, :], weights[a])
            total = term if total is None else total + term
        return total.astype(BF16)

    for t in (1, 0):
        arrived(gin.at[t, own1], gx_r.at[t, 2])
        if t == 1:
            narrow_here(gin.at[t], gx_r.at[t])
        else:
            @pl.when(inner)
            def _():
                narrow_here(gin.at[0], gx_r.at[0])
                narrow_here(ghid, gh_r)
        for c in range(2):
            chan = slice(c * half, (c + 1) * half)
            grad_h = gin[t, :, chan].astype(F32)
            if t == 0:
                grad_h = grad_h + ghid[:, chan].astype(F32)
            grad_c = grad_h * coef[t, 0, :, chan]
            if t == 0:
                grad_c = grad_c + carry[:, chan]
            for g, value in enumerate((
                grad_c * coef[t, 1, :, chan],
                grad_c * coef[t, 2, :, chan],
                grad_h * coef[t, 3, :, chan],
                grad_c * coef[t, 4, :, chan],
            )):
                at = 4 * hid + c * gate_half + g * half
                sg[t, :, at:at + half] = value.astype(BF16)
            if t == 1:
                carry[:, chan] = grad_c * coef[t, 5, :, chan]
        send_grads(t, base)

        def widen(t=t):
            spread(sg, t, slice(0, 2 * cols + n), 4 * hid)

            @pl.when(top)
            def _():
                sg[t, above1, :] = jnp.zeros((cols, 12 * hid), BF16)

            @pl.when(bottom)
            def _():
                sg[t, below1, :] = jnp.zeros((cols, 12 * hid), BF16)

        def input_grad(t=t):
            gx_out[t] = back_conv(t, wxt)

        if t == 1:
            widen()
            pl.when(inner)(input_grad)
        else:
            @pl.when(inner)
            def _():
                widen()
                input_grad()

        send(
            inner,
            lambda t=t: remote(gx_out.at[t], gin.at[t, own1], gx_s.at[t, 2], gx_r.at[t, 2], (z - 1, s, k)),
        )
        send_edges(
            outer(gx_out.at[t], cols), narrow(gin.at[t]), gx_s.at[t], gx_r.at[t], z - 1,
            inner if t == 1 else z >= 2,
        )
        if t == 1:
            ghid[own1] = back_conv(t, wht)
            send_edges(
                (ghid.at[cols:2 * cols], ghid.at[n:n + cols]), narrow(ghid), gh_s, gh_r, z, inner
            )
            for step, part in ((0, 0), (1, 1), (1, 0)):
                send_tile(step, part, roof)
        send_grads(t, inner)

    pl.when(z >= 2)(turn_patches)

    def grads_here(t, p):
        for slot in range(2 * LINE):
            arrived(grads_all.at[t, slot * n:(slot + 1) * n, pairs[p]], ga_r.at[t, p, slot])

    grads_here(1, 0)
    grads_here(1, 1)
    for j in range(LINE):
        acc[j] = dot(turned[1, j], grads_all[1])
    for p, lanes in enumerate(pairs):
        grads_here(0, p)
        for d in (1, 3, 2, 0):
            j = (me + d) % LINE
            leaving[d, :, lanes] = (
                acc[j, :, lanes] + dot(turned[0, j], grads_all[0, :, lanes])
            ).astype(BF16)
            chip = jnp.where(k == 0, j * LINE + x, y * LINE + j)
            for q in range(2):
                src, dst = leaving.at[d, q * rows:(q + 1) * rows, lanes], landed.at[k, me, :, lanes]
                make = functools.partial(
                    remote, src, dst, rv_s.at[p, d * 2 + q], rv_r.at[p, k, me], (z, chip, q)
                )
                if d == 0:
                    pl.when(k == q)(
                        functools.partial(
                            lambda src, dst, sem: pltpu.make_async_copy(src, dst, sem).start(),
                            src, dst, rv_r.at[p, k, me],
                        )
                    )
                send(k != q if d == 0 else None, make)
    for p, lanes in enumerate(pairs):
        for c in range(2):
            for i in range(LINE):
                arrived(landed.at[c, i, :, lanes], rv_r.at[p, c, i])
            for g in (2 * p, 2 * p + 1):
                total = landed[c, 0, :, g * half:(g + 1) * half].astype(F32)
                for i in range(1, LINE):
                    total = total + landed[c, i, :, g * half:(g + 1) * half].astype(F32)
                out[:, g * hid + c * half:g * hid + (c + 1) * half] = total
    for wait in pending:
        wait()


def on_device(frames, cotangent, first_hidden, first_cell, gate_bias, gate_weight):
    steps, _, tile_rows, cols, hid = frames.shape
    n = tile_rows * cols
    pad = n + 2 * cols
    half = hid // 2
    gates = 4 * hid
    share = 18 * hid // (lax.axis_size("space") * lax.axis_size("batch"))
    block = 2 * share
    vmem = pl.BlockSpec(memory_space=pltpu.VMEM)
    anywhere = pl.BlockSpec(memory_space=pl.ANY)
    dma = pltpu.SemaphoreType.DMA
    scratch = [
        pltpu.VMEM((2, 3, 3, hid, gates // 2), BF16),
        pltpu.VMEM((2, 3, 3, hid, gates // 2), BF16),
        pltpu.VMEM((3, 3 * gates, hid), BF16),
        pltpu.VMEM((3, 3 * gates, hid), BF16),
        pltpu.VMEM((steps, pad + 2 * cols, 3 * hid), BF16),
        pltpu.VMEM((steps, pad + 2 * cols, 3 * hid), BF16),
        pltpu.VMEM((steps, pad, 3 * gates), BF16),
        pltpu.VMEM((n, hid), BF16),
        pltpu.VMEM((pad, gates), F32),
        pltpu.VMEM((5, n, hid), F32),
        pltpu.VMEM((steps, pad, hid), F32),
        pltpu.VMEM((pad, hid), F32),
        pltpu.VMEM((steps, 6, pad, hid), F32),
        pltpu.VMEM((steps, pad, hid), BF16),
        pltpu.VMEM((steps, n, hid), BF16),
        pltpu.VMEM((pad, hid), BF16),
        pltpu.VMEM((steps, 2, 2 * LINE, pad, hid), BF16),
        pltpu.VMEM((18 * hid, n), BF16),
        pltpu.VMEM((steps, LINE, block, 2 * LINE * n), BF16),
        pltpu.VMEM((steps, 2 * LINE * n, gates // 2), BF16),
        pltpu.VMEM((LINE, block, gates // 2), F32),
        pltpu.VMEM((LINE, block, gates // 2), BF16),
        pltpu.VMEM((2, LINE, share, gates // 2), BF16),
        dma((2, 2, 4)), dma((2,)),
        dma((steps, 2, 3)), dma((steps, 2)), dma((steps, 2, 2)), dma((steps, 2)),
        dma((2,)), dma((steps, 3)), dma((2,)),
        dma((steps, 2, 2 * LINE)), dma((steps, 2, 2 * LINE)), dma((2, 2, LINE)),
        dma((steps, 2, 2)), dma((steps, 2)), dma((2,)), dma((2,)), dma((2,)), dma((steps, 2)),
        dma((steps, 2, 3)), dma((steps, 2)), dma((2, 2)), dma((2,)), dma((steps, 3)), dma((2,)),
        dma((steps, 2, 2 * LINE)), dma((steps, 2, 2 * LINE)), dma((2, 2 * LINE)),
    ]
    result = pl.pallas_call(
        kernel,
        out_shape=jax.ShapeDtypeStruct((share, gates), F32),
        in_specs=[anywhere] * 4 + [vmem, anywhere],
        out_specs=vmem,
        scratch_shapes=scratch,
        compiler_params=pltpu.CompilerParams(
            collective_id=0, has_side_effects=True, vmem_limit_bytes=56 * 2**20
        ),
    )(
        frames.reshape(steps, n, hid),
        cotangent.reshape(steps, n, hid),
        first_hidden.reshape(n, hid),
        first_cell.reshape(n, hid),
        gate_bias,
        gate_weight.reshape(3, 3, 2 * hid, gates),
    )
    return result[None]


def solution(mesh):
    return jax.shard_map(
        on_device,
        mesh=mesh,
        in_specs=(
            P(None, "batch", "space", None, None),
            P(None, "batch", "space", None, None),
            P("section", "batch", "space", None, None),
            P("section", "batch", "space", None, None),
            P("section", None),
            P("section", None, None),
        ),
        out_specs=P("section", ("space", "batch"), None),
        check_vma=False,
    )
```

```python
import functools

import jax
import jax.numpy as jnp
from jax import lax
from jax.experimental import pallas as pl
from jax.experimental.pallas import tpu as pltpu
from jax.sharding import PartitionSpec as P

F32 = jnp.float32
BF16 = jnp.bfloat16
MESH = pl.DeviceIdType.MESH
LINE = 4


def dot(left, right):
    return jnp.dot(left, right, preferred_element_type=F32)


def kernel(
    frames, cotangent, first_hidden, first_cell, bias, weight, out,
    wx, wh, wxt, wht, sx, sh, sg, top_hidden, preact, gates, cells, carry, coef, gin, gx_out, ghid,
    tiles_all, flipped, turned, grads_all, acc, leaving, landed,
    w_sem, in_sem, sx_r, sx_f, sh_r, sh_f, c_r, gx_r, gh_r, ti_r, ga_r, rv_r,
    fr_s, fr_f, fh_s, fh_f, fc_s, ct_s, sx_s, sx_fs, sh_s, sh_fs, gx_s, gh_s, ti_s, ga_s, rv_s,
):
    z, s, k = lax.axis_index("section"), lax.axis_index("space"), lax.axis_index("batch")
    y, x = s // LINE, s % LINE
    sections, tiles = lax.axis_size("section"), lax.axis_size("space")
    cols = 32
    n = first_cell.shape[0]
    hid = first_cell.shape[1]
    half = hid // 2
    gate_half = 4 * half
    own2, above2, below2 = slice(2 * cols, 2 * cols + n), slice(0, 2 * cols), slice(2 * cols + n, 4 * cols + n)
    near = slice(cols, 2 * cols), slice(2 * cols + n, 3 * cols + n)
    far = slice(0, cols), slice(3 * cols + n, 4 * cols + n)
    own1, above1, below1 = slice(cols, cols + n), slice(0, cols), slice(cols + n, 2 * cols + n)
    centre = slice(hid, 2 * hid)
    top, bottom, base, roof = s == 0, s == tiles - 1, z == 0, z == sections - 1
    inner = jnp.logical_not(base)
    pending = []

    def send(pred, make):
        if pred is None:
            make().start()
            pending.append(lambda: make().wait_send())
        else:
            ask = pred if callable(pred) else lambda: pred
            pl.when(ask())(lambda: make().start())
            pending.append(lambda: pl.when(ask())(lambda: make().wait_send()))

    def remote(src, dst, send_sem, recv_sem, device):
        return pltpu.make_async_remote_copy(
            src_ref=src, dst_ref=dst, send_sem=send_sem, recv_sem=recv_sem,
            device_id=device, device_id_type=MESH,
        )

    def arrived(dst, recv_sem):
        remote(dst, dst, recv_sem, recv_sem, (z, s, 1 - k)).wait_recv()

    loads = {}
    for part, buffer in ((0, wx), (1, wh)):
        for c in range(2):
            for g in range(4):
                loads[part, c, g] = pltpu.make_async_copy(
                    weight.at[:, :, part * hid:(part + 1) * hid, pl.ds(g * hid + c * half, half)],
                    buffer.at[c, :, :, :, g * half:(g + 1) * half],
                    w_sem.at[part, c, g],
                )

    def weights_here(part):
        for c in range(2):
            for g in range(4):
                loads[part, c, g].wait()

    partners = [(jnp.logical_not(top), (z, s - 1, k)), (jnp.logical_not(bottom), (z, s + 1, k))]
    for step, ok in ((-1, z > 0), (1, z < sections - 1)):
        partners.append((ok, (z + step, s, k)))
        partners.append((ok & (s > 0), (z + step, s - 1, k)))
        partners.append((ok & (s < tiles - 1), (z + step, s + 1, k)))
    partners.append((None, (z, s, 1 - k)))
    for d in range(1, LINE):
        for core in range(2):
            partners.append((None, (z, y * LINE + (x + d) % LINE, core)))
            partners.append((None, (z, ((y + d) % LINE) * LINE + x, core)))
    barrier = pltpu.get_barrier_semaphore()
    expected = 0
    for pred, device in partners:
        greet = functools.partial(
            pl.semaphore_signal, barrier, inc=1, device_id=device, device_id_type=MESH
        )
        if pred is None:
            greet()
            expected = expected + 1
        else:
            pl.when(pred)(greet)
            expected = expected + jnp.where(pred, 1, 0)

    half_lanes = [slice(hid + c * half, hid + (c + 1) * half) for c in range(2)]
    own_hidden = pltpu.make_async_copy(first_hidden, sh.at[0, own2, centre], in_sem.at[0])
    own_cell = pltpu.make_async_copy(first_cell, cells.at[0, own1], in_sem.at[1])
    own_hidden.start()

    @pl.when(base)
    def _():
        for t in range(2):
            for c in range(2):
                pltpu.make_async_copy(
                    frames.at[t, :, pl.ds(c * half, half)], sx.at[t, own2, half_lanes[c]], sx_r.at[t, c, 2]
                ).start()

    own_cell.start()

    @pl.when(roof)
    def _():
        for t in range(2):
            pltpu.make_async_copy(cotangent.at[t], gin.at[t, own1], gx_r.at[t, 2]).start()

    for part in (1, 0):
        for c in range(2):
            for g in range(4):
                loads[part, c, g].start()

    def clear(wide, narrow):
        for t in range(2):
            sx[t, wide, :] = jnp.zeros((2 * cols, 3 * hid), BF16)
            sh[t, wide, :] = jnp.zeros((2 * cols, 3 * hid), BF16)
            gin[t, narrow] = jnp.zeros((cols, hid), BF16)
        cells[0, narrow] = jnp.zeros((cols, hid), F32)
        ghid[narrow] = jnp.zeros((cols, hid), BF16)

    pl.when(top)(lambda: clear(above2, above1))
    pl.when(bottom)(lambda: clear(below2, below1))

    pl.semaphore_wait(barrier, expected)

    def send_edges(src, dst, send_sems, recv_sems, section, pred):
        edges(lambda: (src, dst, send_sems, recv_sems), section, pred)

    def edges(parts, section, pred):
        def up():
            return s > 0 if pred is None else (s > 0) & pred

        def down():
            return s < tiles - 1 if pred is None else (s < tiles - 1) & pred

        def make(end, device):
            src, dst, send_sems, recv_sems = parts()
            return remote(src[end], dst[1 - end], send_sems.at[end], recv_sems.at[1 - end], device)

        send(up, lambda: make(0, (section, s - 1, k)))
        send(down, lambda: make(1, (section, s + 1, k)))

    def outer(ref, width):
        return ref.at[0:width], ref.at[n - width:n]

    def beyond(ref):
        return ref.at[cols:2 * cols], ref.at[n - 2 * cols:n - cols]

    def narrow(ref):
        return ref.at[above1], ref.at[below1]

    def at_rows(buffer, t, rows, lanes):
        return buffer.at[t, rows[0], lanes], buffer.at[t, rows[1], lanes]

    def halves(ref, c):
        return ref.at[0:cols, pl.ds(c * half, half)], ref.at[n - cols:n, pl.ds(c * half, half)]

    send_edges(outer(first_hidden, cols), at_rows(sh, 0, near, centre), fh_s, sh_r.at[0, 0], z, None)

    def send_frames(t):
        for c in range(2):
            send_edges(
                halves(frames.at[t], c), at_rows(sx, t, near, half_lanes[c]),
                fr_s.at[t, c], sx_r.at[t, c], z, base,
            )

    send_frames(0)
    send_edges(beyond(first_hidden), at_rows(sh, 0, far, centre), fh_f, sh_f.at[0], z, None)
    send_edges(outer(first_cell, cols), narrow(cells.at[0]), fc_s, c_r, z, None)
    send_edges(beyond(frames.at[0]), at_rows(sx, 0, far, centre), fr_f.at[0], sx_f.at[0], z, base)
    send_frames(1)
    send_edges(beyond(frames.at[1]), at_rows(sx, 1, far, centre), fr_f.at[1], sx_f.at[1], z, base)
    for t in range(2):
        send_edges(outer(cotangent.at[t], cols), narrow(gin.at[t]), ct_s.at[t], gx_r.at[t], z, roof)

    def spread_value(value, width):
        count = value.shape[0]
        column = lax.broadcasted_iota(jnp.int32, (count, width), 0) % cols
        left = jnp.where(column == 0, 0.0, pltpu.roll(value, 1, 0)).astype(BF16)
        right = jnp.where(column == cols - 1, 0.0, pltpu.roll(value, count - 1, 0)).astype(BF16)
        return left, right

    def spread(buffer, t, rows, width):
        left, right = spread_value(buffer[t, rows, width:2 * width].astype(F32), width)
        buffer[t, rows, 0:width] = left
        buffer[t, rows, 2 * width:3 * width] = right

    def when_edges(first, second):
        pl.when(jnp.logical_not(top))(first)
        pl.when(jnp.logical_not(bottom))(second)

    def near_here(buffer, t, recv_sems, lanes):
        def here(index):
            for c, part in enumerate(lanes):
                arrived(buffer.at[t, near[index], part], recv_sems.at[c, index])
            spread(buffer, t, near[index], hid)

        when_edges(lambda: here(0), lambda: here(1))

    def far_here(buffer, t, recv_sems):
        def here(index):
            arrived(buffer.at[t, far[index], centre], recv_sems.at[index])
            spread(buffer, t, far[index], hid)

        when_edges(lambda: here(0), lambda: here(1))

    def narrow_here(ref, recv_sems):
        when_edges(
            lambda: arrived(ref.at[above1], recv_sems.at[0]),
            lambda: arrived(ref.at[below1], recv_sems.at[1]),
        )

    def conv(buffer, t, weights, c, offsets):
        total = None
        for a in offsets:
            term = dot(
                buffer[t, cols * (a + 1):cols * (a + 1) + n, :],
                weights[c, a].reshape(3 * hid, gate_half),
            )
            total = term if total is None else total + term
        return total

    def conv_all(buffer, t, weights, c):
        total = None
        for a in range(3):
            term = dot(
                buffer[t, cols * a:cols * (a + 2) + n, :],
                weights[c, a].reshape(3 * hid, gate_half),
            )
            total = term if total is None else total + term
        return total

    def conv_beside(t, c):
        total = None
        for buffer, weights in ((sh, wh), (sx, wx)):
            for a in range(3):
                low = cols * (a + 1) + n
                cells_in = jnp.concatenate(
                    [buffer[t, cols * a:cols * (a + 1), :], buffer[t, low:low + cols, :]], axis=0
                )
                term = dot(cells_in, weights[c, a].reshape(3 * hid, gate_half))
                total = term if total is None else total + term
        return total

    def bias_of(c):
        return jnp.concatenate(
            [bias[0:1, g * hid + c * half:g * hid + (c + 1) * half] for g in range(4)], axis=1
        )

    def activate(now, old):
        i_gate = jax.nn.sigmoid(now[:, 0:half])
        f_gate = jax.nn.sigmoid(now[:, half:2 * half])
        o_gate = jax.nn.sigmoid(now[:, 2 * half:3 * half])
        cand = jnp.tanh(now[:, 3 * half:])
        new = f_gate * old + i_gate * cand
        return i_gate, f_gate, o_gate, cand, new, jnp.tanh(new)

    def factors(i_gate, f_gate, o_gate, cand, squash, old):
        return (
            o_gate * (1.0 - squash * squash),
            cand * i_gate * (1.0 - i_gate),
            old * f_gate * (1.0 - f_gate),
            squash * o_gate * (1.0 - o_gate),
            i_gate * (1.0 - cand * cand),
            f_gate,
        )

    def turn_weights(source, target):
        def one(a, carried):
            for b in range(3):
                for c in range(2):
                    start = (2 - b) * 4 * hid + c * gate_half
                    target[a, start:start + gate_half, :] = source[c, a, b].T
            return carried

        lax.fori_loop(0, 3, one, 0)

    def turn_all_weights():
        turn_weights(wh, wht)
        pl.when(inner)(lambda: turn_weights(wx, wxt))

    def spread_to_group(pred, view, send_sems, recv_sems):
        for d in (0, 1, 3, 2):
            for c in range(2):
                there = ((x if c == 0 else y) + d) % LINE
                chip = y * LINE + there if c == 0 else there * LINE + x
                slot = 2 * (x if c == 0 else y) + k
                src, dst = view(c, slot)
                make = functools.partial(
                    remote, src, dst, send_sems.at[c * LINE + d], recv_sems.at[slot], (z, chip, c)
                )
                ok = pred
                if d == 0:
                    ok = (k != c) if pred is None else pred & (k != c)
                    own = (k == c) if pred is None else pred & (k == c)
                    pl.when(own)(
                        functools.partial(
                            lambda src, dst, sem: pltpu.make_async_copy(src, dst, sem).start(),
                            src, dst, recv_sems.at[slot],
                        )
                    )
                send(ok, make)

    def send_tile(t, part, pred):
        src = (sh if part else sx).at[t, cols:3 * cols + n, centre]
        spread_to_group(
            pred, lambda c, slot: (src, tiles_all.at[t, part, slot]), ti_s.at[t, part], ti_r.at[t, part]
        )

    pairs = [slice(p * 2 * half, (p + 1) * 2 * half) for p in range(2)]

    def send_grads(t, pred):
        for p, lanes in enumerate(pairs if t == 0 else [slice(0, gate_half)]):
            def view(c, slot):
                at = 4 * hid + c * gate_half
                src = sg.at[t, own1, at + lanes.start:at + lanes.stop]
                return src, grads_all.at[t, pl.ds(pl.multiple_of(slot * n, n), n), lanes]

            spread_to_group(pred, view, ga_s.at[t, p], ga_r.at[t, p])

    rows = out.shape[0]
    block = 2 * rows
    me = jnp.where(k == 0, y, x)

    def turn_patches():
        for t in range(2):
            for part in range(2):
                for slot in range(2 * LINE):
                    arrived(tiles_all.at[t, part, slot], ti_r.at[t, part, slot])

            def one(slot, carried):
                for part in range(2):
                    tile = tiles_all[t, part, slot]
                    left, right = spread_value(tile.astype(F32), hid)
                    for b, moved in enumerate((left, tile, right)):
                        for a in range(3):
                            at = (a * 3 + b) * 2 * hid + part * hid
                            flipped[at:at + hid, :] = moved[cols * a:cols * a + n, :].T
                for j in range(LINE):
                    chip = jnp.where(k == 0, j * LINE + x, y * LINE + j)
                    turned[t, j, :, pl.ds(pl.multiple_of(slot * n, n), n)] = flipped[
                        pl.ds(pl.multiple_of(chip * block, 32), block), :
                    ]
                return carried

            lax.fori_loop(0, 2 * LINE, one, 0)

    @pl.when(z >= 2)
    def _():
        weights_here(1)
        weights_here(0)
        turn_all_weights()

    not_roof = jnp.logical_not(roof)
    z_up = z + 1

    def save(t, into, values, old, chan):
        i_gate, f_gate, o_gate, cand, squash = values
        for index, value in enumerate(factors(i_gate, f_gate, o_gate, cand, squash, old)):
            for cells_to, cells_from in into:
                coef[t, index, cells_to, chan] = value[cells_from]

    def x_here(t):
        for c in range(2):
            arrived(sx.at[t, own2, half_lanes[c]], sx_r.at[t, c, 2])
        spread(sx, t, own2, hid)

    def add(c, term):
        preact[0:n, c * gate_half:(c + 1) * gate_half] += term

    def own_rows(t):
        hidden_lanes = (centre,) if t == 0 else half_lanes
        part_sums = [conv(sh, t, wh, c, (1,)) + bias_of(c) for c in range(2)]
        for c in range(2):
            preact[0:n, c * gate_half:(c + 1) * gate_half] = part_sums[c]

        def x_middle():
            x_here(t)
            for c in range(2):
                add(c, conv(sx, t, wx, c, (1,)))

        def x_edges():
            near_here(sx, t, sx_r.at[t], half_lanes)

        def h_edges():
            near_here(sh, t, sh_r.at[t], hidden_lanes)

        def h_outer():
            for c in range(2):
                add(c, conv(sh, t, wh, c, (0, 2)))

        @pl.when(base)
        def _():
            if t == 0:
                weights_here(0)
            x_middle()
            if t == 1:
                x_edges()
                for c in range(2):
                    add(c, conv(sx, t, wx, c, (0, 2)))
                h_edges()

        if t == 0:
            h_edges()
            h_outer()
            send_tile(0, 1, inner)
            pl.when(z == 1)(lambda: weights_here(0))

        @pl.when(inner)
        def _():
            if t == 1:
                h_edges()
                h_outer()
            x_middle()
            if t == 1:
                x_edges()

        if t == 0:
            x_edges()
            own_cell.wait()

        def finish(buffer, weights, c):
            chan, lanes = slice(c * half, (c + 1) * half), half_lanes[c]
            now = preact[0:n, c * gate_half:(c + 1) * gate_half] + conv(buffer, t, weights, c, (0, 2))
            i_gate, f_gate, o_gate, cand, new, squash = activate(now, cells[t, own1, chan])
            hidden = (o_gate * squash).astype(BF16)
            if t == 0:
                sh[1, own2, lanes] = hidden
                cells[1, own1, chan] = new
            else:
                top_hidden[:, chan] = hidden
            for index, value in enumerate((i_gate, f_gate, o_gate, cand, squash)):
                gates[index, :, chan] = value

        for c in range(2):
            chan, lanes = slice(c * half, (c + 1) * half), half_lanes[c]
            if t == 0:
                finish(sx, wx, c)
                whole = sh.at[1, own2, lanes]
                ends = sh.at[1, 2 * cols:3 * cols, lanes], sh.at[1, n + cols:n + 2 * cols, lanes]
            else:
                pl.when(base)(lambda c=c: finish(sh, wh, c))
                pl.when(inner)(lambda c=c: finish(sx, wx, c))
                whole = top_hidden.at[:, chan]
                ends = top_hidden.at[0:cols, chan], top_hidden.at[n - cols:n, chan]
            send(
                not_roof,
                lambda whole=whole, lanes=lanes, c=c: remote(
                    whole, sx.at[t, own2, lanes], sx_s.at[t, c, 2], sx_r.at[t, c, 2], (z_up, s, k)
                ),
            )
            if t == 0:
                send_edges(ends, at_rows(sh, 1, near, lanes), sh_s.at[c], sh_r.at[1, c], z, None)
            edges(
                lambda ends=ends, lanes=lanes, c=c: (
                    ends, at_rows(sx, t, near, lanes), sx_s.at[t, c], sx_r.at[t, c]
                ),
                z_up, not_roof,
            )
        if t == 0:
            ends = sh.at[1, 3 * cols:4 * cols, centre], sh.at[1, n:n + cols, centre]
            send_edges(ends, at_rows(sh, 1, far, centre), sh_fs, sh_f.at[1], z, None)
        else:
            ends = beyond(top_hidden)
        last = ends
        edges(
            lambda: (last, at_rows(sx, t, far, centre), sx_fs.at[t], sx_f.at[t]), z_up, not_roof
        )
        for c in range(2):
            chan = slice(c * half, (c + 1) * half)
            save(
                t, ((own1, slice(0, n)),),
                tuple(gates[index, :, chan] for index in range(5)), cells[t, own1, chan], chan,
            )

    def beside_rows(t):
        if t == 0:
            narrow_here(cells.at[0], c_r)
        far_here(sh, t, sh_f.at[t])
        far_here(sx, t, sx_f.at[t])
        for c in range(2):
            chan = slice(c * half, (c + 1) * half)
            old = jnp.concatenate([cells[t, above1, chan], cells[t, below1, chan]], axis=0)
            i_gate, f_gate, o_gate, cand, new, squash = activate(conv_beside(t, c) + bias_of(c), old)
            if t == 0:
                cells[1, above1, chan] = new[0:cols]
                cells[1, below1, chan] = new[cols:]
            save(
                t, ((above1, slice(0, cols)), (below1, slice(cols, 2 * cols))),
                (i_gate, f_gate, o_gate, cand, squash), old, chan,
            )

    def all_rows():
        far_here(sh, 1, sh_f.at[1])
        for c in range(2):
            preact[:, c * gate_half:(c + 1) * gate_half] = conv_all(sh, 1, wh, c) + bias_of(c)
        x_here(1)
        near_here(sx, 1, sx_r.at[1], half_lanes)
        far_here(sx, 1, sx_f.at[1])
        for c in range(2):
            chan = slice(c * half, (c + 1) * half)
            now = preact[:, c * gate_half:(c + 1) * gate_half] + conv_all(sx, 1, wx, c)
            old = cells[1, :, chan]
            i_gate, f_gate, o_gate, cand, new, squash = activate(now, old)
            save(
                1, ((slice(0, n + 2 * cols), slice(0, n + 2 * cols)),),
                (i_gate, f_gate, o_gate, cand, squash), old, chan,
            )

    own_hidden.wait()
    spread(sh, 0, own2, hid)
    pl.when(z < 2)(lambda: weights_here(1))
    own_rows(0)
    send_tile(0, 0, roof)
    spread(sh, 1, own2, hid)

    @pl.when(not_roof)
    def _():
        own_rows(1)
        beside_rows(0)
        beside_rows(1)

    @pl.when(roof)
    def _():
        beside_rows(0)
        near_here(sh, 1, sh_r.at[1], half_lanes)

    send_tile(1, 1, roof)
    pl.when(roof)(all_rows)

    def blank(outside):
        coef[:, :, outside, :] = jnp.zeros((2, 6, cols, hid), F32)

    pl.when(top)(lambda: blank(above1))
    pl.when(bottom)(lambda: blank(below1))

    pl.when(z < 2)(turn_all_weights)
    send_tile(0, 1, base)
    for t, part in ((0, 0), (1, 1), (1, 0)):
        send_tile(t, part, not_roof)
    pl.when(z < 2)(turn_patches)

    def back_conv(t, weights):
        total = None
        for a in range(3):
            term = dot(sg[t, cols * (2 - a):cols * (2 - a) + n, :], weights[a])
            total = term if total is None else total + term
        return total.astype(BF16)

    for t in (1, 0):
        arrived(gin.at[t, own1], gx_r.at[t, 2])
        if t == 1:
            narrow_here(gin.at[t], gx_r.at[t])
        else:
            @pl.when(inner)
            def _():
                narrow_here(gin.at[0], gx_r.at[0])
                narrow_here(ghid, gh_r)
        for c in range(2):
            chan = slice(c * half, (c + 1) * half)
            grad_h = gin[t, :, chan].astype(F32)
            if t == 0:
                grad_h = grad_h + ghid[:, chan].astype(F32)
            grad_c = grad_h * coef[t, 0, :, chan]
            if t == 0:
                grad_c = grad_c + carry[:, chan]
            for g, value in enumerate((
                grad_c * coef[t, 1, :, chan],
                grad_c * coef[t, 2, :, chan],
                grad_h * coef[t, 3, :, chan],
                grad_c * coef[t, 4, :, chan],
            )):
                at = 4 * hid + c * gate_half + g * half
                sg[t, :, at:at + half] = value.astype(BF16)
            if t == 1:
                carry[:, chan] = grad_c * coef[t, 5, :, chan]
        send_grads(t, base)

        def widen(t=t):
            spread(sg, t, slice(0, 2 * cols + n), 4 * hid)

        def input_grad(t=t):
            gx_out[t] = back_conv(t, wxt)

        if t == 1:
            widen()
            pl.when(inner)(input_grad)
        else:
            @pl.when(inner)
            def _():
                widen()
                input_grad()

        send(
            inner,
            lambda t=t: remote(gx_out.at[t], gin.at[t, own1], gx_s.at[t, 2], gx_r.at[t, 2], (z - 1, s, k)),
        )
        send_edges(
            outer(gx_out.at[t], cols), narrow(gin.at[t]), gx_s.at[t], gx_r.at[t], z - 1,
            inner if t == 1 else z >= 2,
        )
        if t == 1:
            ghid[own1] = back_conv(t, wht)
            send_edges(
                (ghid.at[cols:2 * cols], ghid.at[n:n + cols]), narrow(ghid), gh_s, gh_r, z, inner
            )
            send_tile(1, 0, roof)
        else:
            send_grads(1, inner)
            send_grads(0, inner)

    pl.when(z >= 2)(turn_patches)

    def grads_here(t, p, lanes):
        for slot in range(2 * LINE):
            arrived(grads_all.at[t, slot * n:(slot + 1) * n, lanes], ga_r.at[t, p, slot])

    grads_here(1, 0, slice(0, gate_half))
    for j in range(LINE):
        acc[j] = dot(turned[1, j], grads_all[1])
    for p, lanes in enumerate(pairs):
        grads_here(0, p, lanes)
        for d in (1, 3, 2, 0):
            j = (me + d) % LINE
            leaving[d, :, lanes] = (
                acc[j, :, lanes] + dot(turned[0, j], grads_all[0, :, lanes])
            ).astype(BF16)
            chip = jnp.where(k == 0, j * LINE + x, y * LINE + j)
            for q in range(2):
                src, dst = leaving.at[d, q * rows:(q + 1) * rows, lanes], landed.at[k, me, :, lanes]
                make = functools.partial(
                    remote, src, dst, rv_s.at[p, d * 2 + q], rv_r.at[p, k, me], (z, chip, q)
                )
                if d == 0:
                    pl.when(k == q)(
                        functools.partial(
                            lambda src, dst, sem: pltpu.make_async_copy(src, dst, sem).start(),
                            src, dst, rv_r.at[p, k, me],
                        )
                    )
                send(k != q if d == 0 else None, make)
    for p, lanes in enumerate(pairs):
        for c in range(2):
            for i in range(LINE):
                arrived(landed.at[c, i, :, lanes], rv_r.at[p, c, i])
            for g in (2 * p, 2 * p + 1):
                total = landed[c, 0, :, g * half:(g + 1) * half].astype(F32)
                for i in range(1, LINE):
                    total = total + landed[c, i, :, g * half:(g + 1) * half].astype(F32)
                out[:, g * hid + c * half:g * hid + (c + 1) * half] = total
    for wait in pending:
        wait()


def on_device(frames, cotangent, first_hidden, first_cell, gate_bias, gate_weight):
    steps, _, tile_rows, cols, hid = frames.shape
    n = tile_rows * cols
    pad = n + 2 * cols
    half = hid // 2
    gates = 4 * hid
    share = 18 * hid // (lax.axis_size("space") * lax.axis_size("batch"))
    block = 2 * share
    vmem = pl.BlockSpec(memory_space=pltpu.VMEM)
    anywhere = pl.BlockSpec(memory_space=pl.ANY)
    dma = pltpu.SemaphoreType.DMA
    scratch = [
        pltpu.VMEM((2, 3, 3, hid, gates // 2), BF16),
        pltpu.VMEM((2, 3, 3, hid, gates // 2), BF16),
        pltpu.VMEM((3, 3 * gates, hid), BF16),
        pltpu.VMEM((3, 3 * gates, hid), BF16),
        pltpu.VMEM((steps, pad + 2 * cols, 3 * hid), BF16),
        pltpu.VMEM((steps, pad + 2 * cols, 3 * hid), BF16),
        pltpu.VMEM((steps, pad, 3 * gates), BF16),
        pltpu.VMEM((n, hid), BF16),
        pltpu.VMEM((pad, gates), F32),
        pltpu.VMEM((5, n, hid), F32),
        pltpu.VMEM((steps, pad, hid), F32),
        pltpu.VMEM((pad, hid), F32),
        pltpu.VMEM((steps, 6, pad, hid), F32),
        pltpu.VMEM((steps, pad, hid), BF16),
        pltpu.VMEM((steps, n, hid), BF16),
        pltpu.VMEM((pad, hid), BF16),
        pltpu.VMEM((steps, 2, 2 * LINE, pad, hid), BF16),
        pltpu.VMEM((18 * hid, n), BF16),
        pltpu.VMEM((steps, LINE, block, 2 * LINE * n), BF16),
        pltpu.VMEM((steps, 2 * LINE * n, gates // 2), BF16),
        pltpu.VMEM((LINE, block, gates // 2), F32),
        pltpu.VMEM((LINE, block, gates // 2), BF16),
        pltpu.VMEM((2, LINE, share, gates // 2), BF16),
        dma((2, 2, 4)), dma((2,)),
        dma((steps, 2, 3)), dma((steps, 2)), dma((steps, 2, 2)), dma((steps, 2)),
        dma((2,)), dma((steps, 3)), dma((2,)),
        dma((steps, 2, 2 * LINE)), dma((steps, 2, 2 * LINE)), dma((2, 2, LINE)),
        dma((steps, 2, 2)), dma((steps, 2)), dma((2,)), dma((2,)), dma((2,)), dma((steps, 2)),
        dma((steps, 2, 3)), dma((steps, 2)), dma((2, 2)), dma((2,)), dma((steps, 3)), dma((2,)),
        dma((steps, 2, 2 * LINE)), dma((steps, 2, 2 * LINE)), dma((2, 2 * LINE)),
    ]
    result = pl.pallas_call(
        kernel,
        out_shape=jax.ShapeDtypeStruct((share, gates), F32),
        in_specs=[anywhere] * 4 + [vmem, anywhere],
        out_specs=vmem,
        scratch_shapes=scratch,
        compiler_params=pltpu.CompilerParams(
            collective_id=0, has_side_effects=True, vmem_limit_bytes=56 * 2**20
        ),
    )(
        frames.reshape(steps, n, hid),
        cotangent.reshape(steps, n, hid),
        first_hidden.reshape(n, hid),
        first_cell.reshape(n, hid),
        gate_bias,
        gate_weight.reshape(3, 3, 2 * hid, gates),
    )
    return result[None]


def solution(mesh):
    return jax.shard_map(
        on_device,
        mesh=mesh,
        in_specs=(
            P(None, "batch", "space", None, None),
            P(None, "batch", "space", None, None),
            P("section", "batch", "space", None, None),
            P("section", "batch", "space", None, None),
            P("section", None),
            P("section", None, None),
        ),
        out_specs=P("section", ("space", "batch"), None),
        check_vma=False,
    )
```

```python
import functools

import jax
import jax.numpy as jnp
from jax import lax
from jax.experimental import pallas as pl
from jax.experimental.pallas import tpu as pltpu
from jax.sharding import PartitionSpec as P

F32 = jnp.float32
BF16 = jnp.bfloat16
MESH = pl.DeviceIdType.MESH
LINE = 4


def dot(left, right):
    return jnp.dot(left, right, preferred_element_type=F32)


def kernel(
    frames, cotangent, first_hidden, first_cell, bias, weight, out,
    wx, wh, wxt, wht, sx, sh, sg, top_hidden, preact, gates, cells, carry, coef, gin, gx_out, ghid,
    tiles_all, flipped, turned, grads_all, acc, leaving, landed,
    w_sem, in_sem, sx_r, sx_f, sh_r, sh_f, c_r, gx_r, gh_r, ti_r, ga_r, rv_r,
    fr_s, fr_f, fh_s, fh_f, fc_s, ct_s, sx_s, sx_fs, sh_s, sh_fs, gx_s, gh_s, ti_s, ga_s, rv_s,
):
    z, s, k = lax.axis_index("section"), lax.axis_index("space"), lax.axis_index("batch")
    y, x = s // LINE, s % LINE
    sections, tiles = lax.axis_size("section"), lax.axis_size("space")
    cols = 32
    n = first_cell.shape[0]
    hid = first_cell.shape[1]
    half = hid // 2
    gate_half = 4 * half
    own2, above2, below2 = slice(2 * cols, 2 * cols + n), slice(0, 2 * cols), slice(2 * cols + n, 4 * cols + n)
    near = slice(cols, 2 * cols), slice(2 * cols + n, 3 * cols + n)
    far = slice(0, cols), slice(3 * cols + n, 4 * cols + n)
    own1, above1, below1 = slice(cols, cols + n), slice(0, cols), slice(cols + n, 2 * cols + n)
    centre = slice(hid, 2 * hid)
    top, bottom, base, roof = s == 0, s == tiles - 1, z == 0, z == sections - 1
    inner = jnp.logical_not(base)
    pending = []

    def send(pred, make):
        if pred is None:
            make().start()
            pending.append(lambda: make().wait_send())
        else:
            ask = pred if callable(pred) else lambda: pred
            pl.when(ask())(lambda: make().start())
            pending.append(lambda: pl.when(ask())(lambda: make().wait_send()))

    def remote(src, dst, send_sem, recv_sem, device):
        return pltpu.make_async_remote_copy(
            src_ref=src, dst_ref=dst, send_sem=send_sem, recv_sem=recv_sem,
            device_id=device, device_id_type=MESH,
        )

    def arrived(dst, recv_sem):
        remote(dst, dst, recv_sem, recv_sem, (z, s, 1 - k)).wait_recv()

    loads = {}
    for part, buffer in ((0, wx), (1, wh)):
        for c in range(2):
            for g in range(4):
                loads[part, c, g] = pltpu.make_async_copy(
                    weight.at[:, :, part * hid:(part + 1) * hid, pl.ds(g * hid + c * half, half)],
                    buffer.at[c, :, :, :, g * half:(g + 1) * half],
                    w_sem.at[part, c, g],
                )

    def weights_here(part):
        for c in range(2):
            for g in range(4):
                loads[part, c, g].wait()

    barrier = pltpu.get_barrier_semaphore()

    def greet(partners):
        for pred, device in partners:
            call = functools.partial(
                pl.semaphore_signal, barrier, inc=1, device_id=device, device_id_type=MESH
            )
            if pred is None:
                call()
            else:
                pl.when(pred)(call)

    def count(partners):
        total = 0
        for pred, _ in partners:
            total = total + (1 if pred is None else jnp.where(pred, 1, 0))
        return total

    plane = [(jnp.logical_not(top), (z, s - 1, k)), (jnp.logical_not(bottom), (z, s + 1, k))]
    plane.append((None, (z, s, 1 - k)))
    for d in range(1, LINE):
        for core in range(2):
            plane.append((None, (z, y * LINE + (x + d) % LINE, core)))
            plane.append((None, (z, ((y + d) % LINE) * LINE + x, core)))

    def section_at(step, ok):
        return [
            (ok, (z + step, s, k)),
            (ok & (s > 0), (z + step, s - 1, k)),
            (ok & (s < tiles - 1), (z + step, s + 1, k)),
        ]

    below, above = section_at(-1, z > 0), section_at(1, z < sections - 1)
    greet(plane)

    half_lanes = [slice(hid + c * half, hid + (c + 1) * half) for c in range(2)]
    own_hidden = pltpu.make_async_copy(first_hidden, sh.at[0, own2, centre], in_sem.at[0])
    own_cell = pltpu.make_async_copy(first_cell, cells.at[0, own1], in_sem.at[1])
    own_hidden.start()

    @pl.when(base)
    def _():
        for t in range(2):
            for c in range(2):
                pltpu.make_async_copy(
                    frames.at[t, :, pl.ds(c * half, half)], sx.at[t, own2, half_lanes[c]], sx_r.at[t, c, 2]
                ).start()

    own_cell.start()

    @pl.when(roof)
    def _():
        for t in range(2):
            pltpu.make_async_copy(cotangent.at[t], gin.at[t, own1], gx_r.at[t, 2]).start()

    for part in (1, 0):
        for c in range(2):
            for g in range(4):
                loads[part, c, g].start()

    def clear(wide, narrow):
        for t in range(2):
            sx[t, wide, :] = jnp.zeros((2 * cols, 3 * hid), BF16)
            sh[t, wide, :] = jnp.zeros((2 * cols, 3 * hid), BF16)
            gin[t, narrow] = jnp.zeros((cols, hid), BF16)
        cells[0, narrow] = jnp.zeros((cols, hid), F32)
        ghid[narrow] = jnp.zeros((cols, hid), BF16)

    pl.when(top)(lambda: clear(above2, above1))
    pl.when(bottom)(lambda: clear(below2, below1))

    pl.semaphore_wait(barrier, count(plane) + count(below))

    def send_edges(src, dst, send_sems, recv_sems, section, pred):
        edges(lambda: (src, dst, send_sems, recv_sems), section, pred)

    def edges(parts, section, pred):
        def up():
            return s > 0 if pred is None else (s > 0) & pred

        def down():
            return s < tiles - 1 if pred is None else (s < tiles - 1) & pred

        def make(end, device):
            src, dst, send_sems, recv_sems = parts()
            return remote(src[end], dst[1 - end], send_sems.at[end], recv_sems.at[1 - end], device)

        send(up, lambda: make(0, (section, s - 1, k)))
        send(down, lambda: make(1, (section, s + 1, k)))

    def outer(ref, width):
        return ref.at[0:width], ref.at[n - width:n]

    def beyond(ref):
        return ref.at[cols:2 * cols], ref.at[n - 2 * cols:n - cols]

    def narrow(ref):
        return ref.at[above1], ref.at[below1]

    def at_rows(buffer, t, rows, lanes):
        return buffer.at[t, rows[0], lanes], buffer.at[t, rows[1], lanes]

    def halves(ref, c):
        return ref.at[0:cols, pl.ds(c * half, half)], ref.at[n - cols:n, pl.ds(c * half, half)]

    send_edges(outer(first_hidden, cols), at_rows(sh, 0, near, centre), fh_s, sh_r.at[0, 0], z, None)

    def send_frames(t):
        for c in range(2):
            send_edges(
                halves(frames.at[t], c), at_rows(sx, t, near, half_lanes[c]),
                fr_s.at[t, c], sx_r.at[t, c], z, base,
            )

    send_frames(0)
    greet(above)
    greet(below)
    send_edges(beyond(first_hidden), at_rows(sh, 0, far, centre), fh_f, sh_f.at[0], z, None)
    send_edges(outer(first_cell, cols), narrow(cells.at[0]), fc_s, c_r, z, None)
    send_edges(beyond(frames.at[0]), at_rows(sx, 0, far, centre), fr_f.at[0], sx_f.at[0], z, base)
    send_frames(1)
    send_edges(beyond(frames.at[1]), at_rows(sx, 1, far, centre), fr_f.at[1], sx_f.at[1], z, base)
    for t in range(2):
        send_edges(outer(cotangent.at[t], cols), narrow(gin.at[t]), ct_s.at[t], gx_r.at[t], z, roof)

    def spread_value(value, width):
        count = value.shape[0]
        column = lax.broadcasted_iota(jnp.int32, (count, width), 0) % cols
        left = jnp.where(column == 0, 0.0, pltpu.roll(value, 1, 0)).astype(BF16)
        right = jnp.where(column == cols - 1, 0.0, pltpu.roll(value, count - 1, 0)).astype(BF16)
        return left, right

    def spread(buffer, t, rows, width):
        left, right = spread_value(buffer[t, rows, width:2 * width].astype(F32), width)
        buffer[t, rows, 0:width] = left
        buffer[t, rows, 2 * width:3 * width] = right

    def when_edges(first, second):
        pl.when(jnp.logical_not(top))(first)
        pl.when(jnp.logical_not(bottom))(second)

    def near_here(buffer, t, recv_sems, lanes):
        def here(index):
            for c, part in enumerate(lanes):
                arrived(buffer.at[t, near[index], part], recv_sems.at[c, index])
            spread(buffer, t, near[index], hid)

        when_edges(lambda: here(0), lambda: here(1))

    def far_here(buffer, t, recv_sems):
        def here(index):
            arrived(buffer.at[t, far[index], centre], recv_sems.at[index])
            spread(buffer, t, far[index], hid)

        when_edges(lambda: here(0), lambda: here(1))

    def narrow_here(ref, recv_sems):
        when_edges(
            lambda: arrived(ref.at[above1], recv_sems.at[0]),
            lambda: arrived(ref.at[below1], recv_sems.at[1]),
        )

    def conv(buffer, t, weights, c, offsets):
        total = None
        for a in offsets:
            term = dot(
                buffer[t, cols * (a + 1):cols * (a + 1) + n, :],
                weights[c, a].reshape(3 * hid, gate_half),
            )
            total = term if total is None else total + term
        return total

    def conv_all(buffer, t, weights, c):
        total = None
        for a in range(3):
            term = dot(
                buffer[t, cols * a:cols * (a + 2) + n, :],
                weights[c, a].reshape(3 * hid, gate_half),
            )
            total = term if total is None else total + term
        return total

    def conv_beside(t, c):
        total = None
        for buffer, weights in ((sh, wh), (sx, wx)):
            for a in range(3):
                low = cols * (a + 1) + n
                cells_in = jnp.concatenate(
                    [buffer[t, cols * a:cols * (a + 1), :], buffer[t, low:low + cols, :]], axis=0
                )
                term = dot(cells_in, weights[c, a].reshape(3 * hid, gate_half))
                total = term if total is None else total + term
        return total

    def bias_of(c):
        return jnp.concatenate(
            [bias[0:1, g * hid + c * half:g * hid + (c + 1) * half] for g in range(4)], axis=1
        )

    def activate(now, old):
        i_gate = jax.nn.sigmoid(now[:, 0:half])
        f_gate = jax.nn.sigmoid(now[:, half:2 * half])
        o_gate = jax.nn.sigmoid(now[:, 2 * half:3 * half])
        cand = jnp.tanh(now[:, 3 * half:])
        new = f_gate * old + i_gate * cand
        return i_gate, f_gate, o_gate, cand, new, jnp.tanh(new)

    def factors(i_gate, f_gate, o_gate, cand, squash, old):
        return (
            o_gate * (1.0 - squash * squash),
            cand * i_gate * (1.0 - i_gate),
            old * f_gate * (1.0 - f_gate),
            squash * o_gate * (1.0 - o_gate),
            i_gate * (1.0 - cand * cand),
            f_gate,
        )

    def turn_weights(source, target):
        def one(a, carried):
            for b in range(3):
                for c in range(2):
                    start = (2 - b) * 4 * hid + c * gate_half
                    target[a, start:start + gate_half, :] = source[c, a, b].T
            return carried

        lax.fori_loop(0, 3, one, 0)

    def turn_all_weights():
        turn_weights(wh, wht)
        pl.when(inner)(lambda: turn_weights(wx, wxt))

    def spread_to_group(pred, view, send_sems, recv_sems):
        for d in (0, 1, 3, 2):
            for c in range(2):
                there = ((x if c == 0 else y) + d) % LINE
                chip = y * LINE + there if c == 0 else there * LINE + x
                slot = 2 * (x if c == 0 else y) + k
                src, dst = view(c, slot)
                make = functools.partial(
                    remote, src, dst, send_sems.at[c * LINE + d], recv_sems.at[slot], (z, chip, c)
                )
                ok = pred
                if d == 0:
                    ok = (k != c) if pred is None else pred & (k != c)
                    own = (k == c) if pred is None else pred & (k == c)
                    pl.when(own)(
                        functools.partial(
                            lambda src, dst, sem: pltpu.make_async_copy(src, dst, sem).start(),
                            src, dst, recv_sems.at[slot],
                        )
                    )
                send(ok, make)

    def send_tile(t, part, pred):
        src = (sh if part else sx).at[t, cols:3 * cols + n, centre]
        spread_to_group(
            pred, lambda c, slot: (src, tiles_all.at[t, part, slot]), ti_s.at[t, part], ti_r.at[t, part]
        )

    pairs = [slice(p * 2 * half, (p + 1) * 2 * half) for p in range(2)]

    def send_grads(t, pred):
        for p, lanes in enumerate(pairs if t == 0 else [slice(0, gate_half)]):
            def view(c, slot):
                at = 4 * hid + c * gate_half
                src = sg.at[t, own1, at + lanes.start:at + lanes.stop]
                return src, grads_all.at[t, pl.ds(pl.multiple_of(slot * n, n), n), lanes]

            spread_to_group(pred, view, ga_s.at[t, p], ga_r.at[t, p])

    rows = out.shape[0]
    block = 2 * rows
    me = jnp.where(k == 0, y, x)

    def turn_patches():
        for t in range(2):
            for part in range(2):
                for slot in range(2 * LINE):
                    arrived(tiles_all.at[t, part, slot], ti_r.at[t, part, slot])

            def one(slot, carried):
                for part in range(2):
                    tile = tiles_all[t, part, slot]
                    left, right = spread_value(tile.astype(F32), hid)
                    for b, moved in enumerate((left, tile, right)):
                        for a in range(3):
                            at = (a * 3 + b) * 2 * hid + part * hid
                            flipped[at:at + hid, :] = moved[cols * a:cols * a + n, :].T
                for j in range(LINE):
                    chip = jnp.where(k == 0, j * LINE + x, y * LINE + j)
                    turned[t, j, :, pl.ds(pl.multiple_of(slot * n, n), n)] = flipped[
                        pl.ds(pl.multiple_of(chip * block, 32), block), :
                    ]
                return carried

            lax.fori_loop(0, 2 * LINE, one, 0)

    @pl.when(z >= 2)
    def _():
        weights_here(1)
        weights_here(0)
        turn_all_weights()

    not_roof = jnp.logical_not(roof)
    z_up = z + 1

    def save(t, into, values, old, chan):
        i_gate, f_gate, o_gate, cand, squash = values
        for index, value in enumerate(factors(i_gate, f_gate, o_gate, cand, squash, old)):
            for cells_to, cells_from in into:
                coef[t, index, cells_to, chan] = value[cells_from]

    def x_here(t):
        for c in range(2):
            arrived(sx.at[t, own2, half_lanes[c]], sx_r.at[t, c, 2])
        spread(sx, t, own2, hid)

    def add(c, term):
        preact[0:n, c * gate_half:(c + 1) * gate_half] += term

    def own_rows(t):
        hidden_lanes = (centre,) if t == 0 else half_lanes
        part_sums = [conv(sh, t, wh, c, (1,)) + bias_of(c) for c in range(2)]
        for c in range(2):
            preact[0:n, c * gate_half:(c + 1) * gate_half] = part_sums[c]

        def x_middle():
            x_here(t)
            for c in range(2):
                add(c, conv(sx, t, wx, c, (1,)))

        def x_edges():
            near_here(sx, t, sx_r.at[t], half_lanes)

        def h_edges():
            near_here(sh, t, sh_r.at[t], hidden_lanes)

        def h_outer():
            for c in range(2):
                add(c, conv(sh, t, wh, c, (0, 2)))

        @pl.when(base)
        def _():
            if t == 0:
                weights_here(0)
            x_middle()
            if t == 1:
                x_edges()
                for c in range(2):
                    add(c, conv(sx, t, wx, c, (0, 2)))
                h_edges()

        if t == 0:
            h_edges()
            h_outer()
            send_tile(0, 1, inner)
            pl.when(z == 1)(lambda: weights_here(0))

        @pl.when(inner)
        def _():
            if t == 1:
                h_edges()
                h_outer()
            x_middle()
            if t == 1:
                x_edges()

        if t == 0:
            x_edges()
            own_cell.wait()
            pl.when(not_roof)(lambda: pl.semaphore_wait(barrier, count(above)))

        def finish(buffer, weights, c):
            chan, lanes = slice(c * half, (c + 1) * half), half_lanes[c]
            now = preact[0:n, c * gate_half:(c + 1) * gate_half] + conv(buffer, t, weights, c, (0, 2))
            i_gate, f_gate, o_gate, cand, new, squash = activate(now, cells[t, own1, chan])
            hidden = (o_gate * squash).astype(BF16)
            if t == 0:
                sh[1, own2, lanes] = hidden
                cells[1, own1, chan] = new
            else:
                top_hidden[:, chan] = hidden
            for index, value in enumerate((i_gate, f_gate, o_gate, cand, squash)):
                gates[index, :, chan] = value

        for c in range(2):
            chan, lanes = slice(c * half, (c + 1) * half), half_lanes[c]
            if t == 0:
                finish(sx, wx, c)
                whole = sh.at[1, own2, lanes]
                ends = sh.at[1, 2 * cols:3 * cols, lanes], sh.at[1, n + cols:n + 2 * cols, lanes]
            else:
                pl.when(base)(lambda c=c: finish(sh, wh, c))
                pl.when(inner)(lambda c=c: finish(sx, wx, c))
                whole = top_hidden.at[:, chan]
                ends = top_hidden.at[0:cols, chan], top_hidden.at[n - cols:n, chan]
            send(
                not_roof,
                lambda whole=whole, lanes=lanes, c=c: remote(
                    whole, sx.at[t, own2, lanes], sx_s.at[t, c, 2], sx_r.at[t, c, 2], (z_up, s, k)
                ),
            )
            if t == 0:
                send_edges(ends, at_rows(sh, 1, near, lanes), sh_s.at[c], sh_r.at[1, c], z, None)
            edges(
                lambda ends=ends, lanes=lanes, c=c: (
                    ends, at_rows(sx, t, near, lanes), sx_s.at[t, c], sx_r.at[t, c]
                ),
                z_up, not_roof,
            )
        if t == 0:
            ends = sh.at[1, 3 * cols:4 * cols, centre], sh.at[1, n:n + cols, centre]
            send_edges(ends, at_rows(sh, 1, far, centre), sh_fs, sh_f.at[1], z, None)
        else:
            ends = beyond(top_hidden)
        last = ends
        edges(
            lambda: (last, at_rows(sx, t, far, centre), sx_fs.at[t], sx_f.at[t]), z_up, not_roof
        )
        for c in range(2):
            chan = slice(c * half, (c + 1) * half)
            save(
                t, ((own1, slice(0, n)),),
                tuple(gates[index, :, chan] for index in range(5)), cells[t, own1, chan], chan,
            )

    def beside_rows(t):
        if t == 0:
            narrow_here(cells.at[0], c_r)
        far_here(sh, t, sh_f.at[t])
        far_here(sx, t, sx_f.at[t])
        for c in range(2):
            chan = slice(c * half, (c + 1) * half)
            old = jnp.concatenate([cells[t, above1, chan], cells[t, below1, chan]], axis=0)
            i_gate, f_gate, o_gate, cand, new, squash = activate(conv_beside(t, c) + bias_of(c), old)
            if t == 0:
                cells[1, above1, chan] = new[0:cols]
                cells[1, below1, chan] = new[cols:]
            save(
                t, ((above1, slice(0, cols)), (below1, slice(cols, 2 * cols))),
                (i_gate, f_gate, o_gate, cand, squash), old, chan,
            )

    def all_rows():
        far_here(sh, 1, sh_f.at[1])
        for c in range(2):
            preact[:, c * gate_half:(c + 1) * gate_half] = conv_all(sh, 1, wh, c) + bias_of(c)
        x_here(1)
        near_here(sx, 1, sx_r.at[1], half_lanes)
        far_here(sx, 1, sx_f.at[1])
        for c in range(2):
            chan = slice(c * half, (c + 1) * half)
            now = preact[:, c * gate_half:(c + 1) * gate_half] + conv_all(sx, 1, wx, c)
            old = cells[1, :, chan]
            i_gate, f_gate, o_gate, cand, new, squash = activate(now, old)
            save(
                1, ((slice(0, n + 2 * cols), slice(0, n + 2 * cols)),),
                (i_gate, f_gate, o_gate, cand, squash), old, chan,
            )

    own_hidden.wait()
    spread(sh, 0, own2, hid)
    pl.when(z < 2)(lambda: weights_here(1))
    own_rows(0)
    send_tile(0, 0, roof)
    spread(sh, 1, own2, hid)

    @pl.when(not_roof)
    def _():
        own_rows(1)
        beside_rows(0)
        beside_rows(1)

    @pl.when(roof)
    def _():
        beside_rows(0)
        near_here(sh, 1, sh_r.at[1], half_lanes)

    send_tile(1, 1, roof)
    pl.when(roof)(all_rows)

    def blank(outside):
        coef[:, :, outside, :] = jnp.zeros((2, 6, cols, hid), F32)

    pl.when(top)(lambda: blank(above1))
    pl.when(bottom)(lambda: blank(below1))

    pl.when(z < 2)(turn_all_weights)
    send_tile(0, 1, base)
    for t, part in ((0, 0), (1, 1), (1, 0)):
        send_tile(t, part, not_roof)
    pl.when(z < 2)(turn_patches)

    def back_conv(t, weights):
        total = None
        for a in range(3):
            term = dot(sg[t, cols * (2 - a):cols * (2 - a) + n, :], weights[a])
            total = term if total is None else total + term
        return total.astype(BF16)

    for t in (1, 0):
        arrived(gin.at[t, own1], gx_r.at[t, 2])
        if t == 1:
            narrow_here(gin.at[t], gx_r.at[t])
        else:
            @pl.when(inner)
            def _():
                narrow_here(gin.at[0], gx_r.at[0])
                narrow_here(ghid, gh_r)
        for c in range(2):
            chan = slice(c * half, (c + 1) * half)
            grad_h = gin[t, :, chan].astype(F32)
            if t == 0:
                grad_h = grad_h + ghid[:, chan].astype(F32)
            grad_c = grad_h * coef[t, 0, :, chan]
            if t == 0:
                grad_c = grad_c + carry[:, chan]
            for g, value in enumerate((
                grad_c * coef[t, 1, :, chan],
                grad_c * coef[t, 2, :, chan],
                grad_h * coef[t, 3, :, chan],
                grad_c * coef[t, 4, :, chan],
            )):
                at = 4 * hid + c * gate_half + g * half
                sg[t, :, at:at + half] = value.astype(BF16)
            if t == 1:
                carry[:, chan] = grad_c * coef[t, 5, :, chan]
        send_grads(t, base)

        def widen(t=t):
            spread(sg, t, slice(0, 2 * cols + n), 4 * hid)

        def input_grad(t=t):
            gx_out[t] = back_conv(t, wxt)

        if t == 1:
            widen()
            pl.when(inner)(input_grad)
        else:
            @pl.when(inner)
            def _():
                widen()
                input_grad()

        send(
            inner,
            lambda t=t: remote(gx_out.at[t], gin.at[t, own1], gx_s.at[t, 2], gx_r.at[t, 2], (z - 1, s, k)),
        )
        send_edges(
            outer(gx_out.at[t], cols), narrow(gin.at[t]), gx_s.at[t], gx_r.at[t], z - 1,
            inner if t == 1 else z >= 2,
        )
        if t == 1:
            ghid[own1] = back_conv(t, wht)
            send_edges(
                (ghid.at[cols:2 * cols], ghid.at[n:n + cols]), narrow(ghid), gh_s, gh_r, z, inner
            )
            send_tile(1, 0, roof)
            send_grads(1, z == 1)
        else:
            send_grads(1, z >= 2)
            send_grads(0, inner)

    pl.when(z >= 2)(turn_patches)

    def grads_here(t, p, lanes):
        for slot in range(2 * LINE):
            arrived(grads_all.at[t, slot * n:(slot + 1) * n, lanes], ga_r.at[t, p, slot])

    grads_here(1, 0, slice(0, gate_half))
    for j in range(LINE):
        acc[j] = dot(turned[1, j], grads_all[1])
    earlier = list(pending)
    pending.clear()
    for p, lanes in enumerate(pairs):
        grads_here(0, p, lanes)
        for d in (1, 3, 2, 0):
            j = (me + d) % LINE
            leaving[d, :, lanes] = (
                acc[j, :, lanes] + dot(turned[0, j], grads_all[0, :, lanes])
            ).astype(BF16)
            chip = jnp.where(k == 0, j * LINE + x, y * LINE + j)
            for q in range(2):
                src, dst = leaving.at[d, q * rows:(q + 1) * rows, lanes], landed.at[k, me, :, lanes]
                make = functools.partial(
                    remote, src, dst, rv_s.at[p, d * 2 + q], rv_r.at[p, k, me], (z, chip, q)
                )
                if d == 0:
                    pl.when(k == q)(
                        functools.partial(
                            lambda src, dst, sem: pltpu.make_async_copy(src, dst, sem).start(),
                            src, dst, rv_r.at[p, k, me],
                        )
                    )
                send(k != q if d == 0 else None, make)
    for wait in earlier:
        wait()
    for p, lanes in enumerate(pairs):
        for c in range(2):
            for i in range(LINE):
                arrived(landed.at[c, i, :, lanes], rv_r.at[p, c, i])
            for g in (2 * p, 2 * p + 1):
                total = landed[c, 0, :, g * half:(g + 1) * half].astype(F32)
                for i in range(1, LINE):
                    total = total + landed[c, i, :, g * half:(g + 1) * half].astype(F32)
                out[:, g * hid + c * half:g * hid + (c + 1) * half] = total
    for wait in pending:
        wait()


def on_device(frames, cotangent, first_hidden, first_cell, gate_bias, gate_weight):
    steps, _, tile_rows, cols, hid = frames.shape
    n = tile_rows * cols
    pad = n + 2 * cols
    half = hid // 2
    gates = 4 * hid
    share = 18 * hid // (lax.axis_size("space") * lax.axis_size("batch"))
    block = 2 * share
    vmem = pl.BlockSpec(memory_space=pltpu.VMEM)
    anywhere = pl.BlockSpec(memory_space=pl.ANY)
    dma = pltpu.SemaphoreType.DMA
    scratch = [
        pltpu.VMEM((2, 3, 3, hid, gates // 2), BF16),
        pltpu.VMEM((2, 3, 3, hid, gates // 2), BF16),
        pltpu.VMEM((3, 3 * gates, hid), BF16),
        pltpu.VMEM((3, 3 * gates, hid), BF16),
        pltpu.VMEM((steps, pad + 2 * cols, 3 * hid), BF16),
        pltpu.VMEM((steps, pad + 2 * cols, 3 * hid), BF16),
        pltpu.VMEM((steps, pad, 3 * gates), BF16),
        pltpu.VMEM((n, hid), BF16),
        pltpu.VMEM((pad, gates), F32),
        pltpu.VMEM((5, n, hid), F32),
        pltpu.VMEM((steps, pad, hid), F32),
        pltpu.VMEM((pad, hid), F32),
        pltpu.VMEM((steps, 6, pad, hid), F32),
        pltpu.VMEM((steps, pad, hid), BF16),
        pltpu.VMEM((steps, n, hid), BF16),
        pltpu.VMEM((pad, hid), BF16),
        pltpu.VMEM((steps, 2, 2 * LINE, pad, hid), BF16),
        pltpu.VMEM((18 * hid, n), BF16),
        pltpu.VMEM((steps, LINE, block, 2 * LINE * n), BF16),
        pltpu.VMEM((steps, 2 * LINE * n, gates // 2), BF16),
        pltpu.VMEM((LINE, block, gates // 2), F32),
        pltpu.VMEM((LINE, block, gates // 2), BF16),
        pltpu.VMEM((2, LINE, share, gates // 2), BF16),
        dma((2, 2, 4)), dma((2,)),
        dma((steps, 2, 3)), dma((steps, 2)), dma((steps, 2, 2)), dma((steps, 2)),
        dma((2,)), dma((steps, 3)), dma((2,)),
        dma((steps, 2, 2 * LINE)), dma((steps, 2, 2 * LINE)), dma((2, 2, LINE)),
        dma((steps, 2, 2)), dma((steps, 2)), dma((2,)), dma((2,)), dma((2,)), dma((steps, 2)),
        dma((steps, 2, 3)), dma((steps, 2)), dma((2, 2)), dma((2,)), dma((steps, 3)), dma((2,)),
        dma((steps, 2, 2 * LINE)), dma((steps, 2, 2 * LINE)), dma((2, 2 * LINE)),
    ]
    result = pl.pallas_call(
        kernel,
        out_shape=jax.ShapeDtypeStruct((share, gates), F32),
        in_specs=[anywhere] * 4 + [vmem, anywhere],
        out_specs=vmem,
        scratch_shapes=scratch,
        compiler_params=pltpu.CompilerParams(
            collective_id=0, has_side_effects=True, vmem_limit_bytes=56 * 2**20
        ),
    )(
        frames.reshape(steps, n, hid),
        cotangent.reshape(steps, n, hid),
        first_hidden.reshape(n, hid),
        first_cell.reshape(n, hid),
        gate_bias,
        gate_weight.reshape(3, 3, 2 * hid, gates),
    )
    return result[None]


def solution(mesh):
    return jax.shard_map(
        on_device,
        mesh=mesh,
        in_specs=(
            P(None, "batch", "space", None, None),
            P(None, "batch", "space", None, None),
            P("section", "batch", "space", None, None),
            P("section", "batch", "space", None, None),
            P("section", None),
            P("section", None, None),
        ),
        out_specs=P("section", ("space", "batch"), None),
        check_vma=False,
    )
```

```python
import functools

import jax
import jax.numpy as jnp
from jax import lax
from jax.experimental import pallas as pl
from jax.experimental.pallas import tpu as pltpu
from jax.sharding import PartitionSpec as P

F32 = jnp.float32
BF16 = jnp.bfloat16
MESH = pl.DeviceIdType.MESH
LINE = 4


def dot(left, right):
    return jnp.dot(left, right, preferred_element_type=F32)


def kernel(
    frames, cotangent, first_hidden, first_cell, bias, weight, out,
    wx, wh, wxt, wht, sx, sh, sg, top_hidden, preact, gates, cells, carry, coef, gin, gx_out, ghid,
    tiles_all, flipped, turned, grads_all, packed, packed_all, vec, vec_all, acc, leaving, landed,
    w_sem, in_sem, sx_r, sx_f, sh_r, sh_f, c_r, gx_r, gh_r, ti_r, ga_r, co_r, ve_r, rv_r,
    fr_s, fr_f, fh_s, fh_f, fc_s, ct_s, sx_s, sx_fs, sh_s, sh_fs, gx_s, gh_s, ti_s, ga_s, co_s, ve_s, rv_s,
):
    z, s, k = lax.axis_index("section"), lax.axis_index("space"), lax.axis_index("batch")
    y, x = s // LINE, s % LINE
    sections, tiles = lax.axis_size("section"), lax.axis_size("space")
    cols = 32
    n = first_cell.shape[0]
    hid = first_cell.shape[1]
    half = hid // 2
    gate_half = 4 * half
    own2, above2, below2 = slice(2 * cols, 2 * cols + n), slice(0, 2 * cols), slice(2 * cols + n, 4 * cols + n)
    near = slice(cols, 2 * cols), slice(2 * cols + n, 3 * cols + n)
    far = slice(0, cols), slice(3 * cols + n, 4 * cols + n)
    own1, above1, below1 = slice(cols, cols + n), slice(0, cols), slice(cols + n, 2 * cols + n)
    centre = slice(hid, 2 * hid)
    top, bottom, base, roof = s == 0, s == tiles - 1, z == 0, z == sections - 1
    inner = jnp.logical_not(base)
    pending = []

    def send(pred, make):
        if pred is None:
            make().start()
            pending.append(lambda: make().wait_send())
        else:
            ask = pred if callable(pred) else lambda: pred
            pl.when(ask())(lambda: make().start())
            pending.append(lambda: pl.when(ask())(lambda: make().wait_send()))

    def remote(src, dst, send_sem, recv_sem, device):
        return pltpu.make_async_remote_copy(
            src_ref=src, dst_ref=dst, send_sem=send_sem, recv_sem=recv_sem,
            device_id=device, device_id_type=MESH,
        )

    def arrived(dst, recv_sem):
        remote(dst, dst, recv_sem, recv_sem, (z, s, 1 - k)).wait_recv()

    loads = {}
    for part, buffer in ((0, wx), (1, wh)):
        for c in range(2):
            for g in range(4):
                loads[part, c, g] = pltpu.make_async_copy(
                    weight.at[:, :, part * hid:(part + 1) * hid, pl.ds(g * hid + c * half, half)],
                    buffer.at[c, :, :, :, g * half:(g + 1) * half],
                    w_sem.at[part, c, g],
                )

    def weights_here(part):
        for c in range(2):
            for g in range(4):
                loads[part, c, g].wait()

    barrier = pltpu.get_barrier_semaphore()

    def greet(partners):
        for pred, device in partners:
            call = functools.partial(
                pl.semaphore_signal, barrier, inc=1, device_id=device, device_id_type=MESH
            )
            if pred is None:
                call()
            else:
                pl.when(pred)(call)

    def count(partners):
        total = 0
        for pred, _ in partners:
            total = total + (1 if pred is None else jnp.where(pred, 1, 0))
        return total

    plane = [(jnp.logical_not(top), (z, s - 1, k)), (jnp.logical_not(bottom), (z, s + 1, k))]
    plane.append((None, (z, s, 1 - k)))
    for d in range(1, LINE):
        for core in range(2):
            plane.append((None, (z, y * LINE + (x + d) % LINE, core)))
            plane.append((None, (z, ((y + d) % LINE) * LINE + x, core)))

    def section_at(step, ok):
        return [
            (ok, (z + step, s, k)),
            (ok & (s > 0), (z + step, s - 1, k)),
            (ok & (s < tiles - 1), (z + step, s + 1, k)),
        ]

    below, above = section_at(-1, z > 0), section_at(1, z < sections - 1)
    greet(plane)

    half_lanes = [slice(hid + c * half, hid + (c + 1) * half) for c in range(2)]
    own_hidden = pltpu.make_async_copy(first_hidden, sh.at[0, own2, centre], in_sem.at[0])
    own_cell = pltpu.make_async_copy(first_cell, cells.at[0, own1], in_sem.at[1])
    own_hidden.start()

    @pl.when(base)
    def _():
        for t in range(2):
            for c in range(2):
                pltpu.make_async_copy(
                    frames.at[t, :, pl.ds(c * half, half)], sx.at[t, own2, half_lanes[c]], sx_r.at[t, c, 2]
                ).start()

    own_cell.start()

    @pl.when(roof)
    def _():
        for t in range(2):
            pltpu.make_async_copy(cotangent.at[t], gin.at[t, own1], gx_r.at[t, 2]).start()

    for part in (1, 0):
        for c in range(2):
            for g in range(4):
                loads[part, c, g].start()

    def clear(wide, narrow):
        for t in range(2):
            sx[t, wide, :] = jnp.zeros((2 * cols, 3 * hid), BF16)
            sh[t, wide, :] = jnp.zeros((2 * cols, 3 * hid), BF16)
            gin[t, narrow] = jnp.zeros((cols, hid), BF16)
        cells[0, narrow] = jnp.zeros((cols, hid), F32)
        ghid[narrow] = jnp.zeros((cols, hid), BF16)

    pl.when(top)(lambda: clear(above2, above1))
    pl.when(bottom)(lambda: clear(below2, below1))

    pl.semaphore_wait(barrier, count(plane) + count(below))

    def send_edges(src, dst, send_sems, recv_sems, section, pred):
        edges(lambda: (src, dst, send_sems, recv_sems), section, pred)

    def edges(parts, section, pred):
        def up():
            return s > 0 if pred is None else (s > 0) & pred

        def down():
            return s < tiles - 1 if pred is None else (s < tiles - 1) & pred

        def make(end, device):
            src, dst, send_sems, recv_sems = parts()
            return remote(src[end], dst[1 - end], send_sems.at[end], recv_sems.at[1 - end], device)

        send(up, lambda: make(0, (section, s - 1, k)))
        send(down, lambda: make(1, (section, s + 1, k)))

    def outer(ref, width):
        return ref.at[0:width], ref.at[n - width:n]

    def beyond(ref):
        return ref.at[cols:2 * cols], ref.at[n - 2 * cols:n - cols]

    def narrow(ref):
        return ref.at[above1], ref.at[below1]

    def at_rows(buffer, t, rows, lanes):
        return buffer.at[t, rows[0], lanes], buffer.at[t, rows[1], lanes]

    def halves(ref, c):
        return ref.at[0:cols, pl.ds(c * half, half)], ref.at[n - cols:n, pl.ds(c * half, half)]

    send_edges(outer(first_hidden, cols), at_rows(sh, 0, near, centre), fh_s, sh_r.at[0, 0], z, None)

    def send_frames(t):
        for c in range(2):
            send_edges(
                halves(frames.at[t], c), at_rows(sx, t, near, half_lanes[c]),
                fr_s.at[t, c], sx_r.at[t, c], z, base,
            )

    send_frames(0)
    greet(above)
    greet(below)
    send_edges(beyond(first_hidden), at_rows(sh, 0, far, centre), fh_f, sh_f.at[0], z, None)
    send_edges(outer(first_cell, cols), narrow(cells.at[0]), fc_s, c_r, z, None)
    send_edges(beyond(frames.at[0]), at_rows(sx, 0, far, centre), fr_f.at[0], sx_f.at[0], z, base)
    send_frames(1)
    send_edges(beyond(frames.at[1]), at_rows(sx, 1, far, centre), fr_f.at[1], sx_f.at[1], z, base)
    for t in range(2):
        send_edges(outer(cotangent.at[t], cols), narrow(gin.at[t]), ct_s.at[t], gx_r.at[t], z, roof)

    def spread_value(value, width):
        count = value.shape[0]
        column = lax.broadcasted_iota(jnp.int32, (count, width), 0) % cols
        left = jnp.where(column == 0, 0.0, pltpu.roll(value, 1, 0)).astype(BF16)
        right = jnp.where(column == cols - 1, 0.0, pltpu.roll(value, count - 1, 0)).astype(BF16)
        return left, right

    def spread(buffer, t, rows, width):
        left, right = spread_value(buffer[t, rows, width:2 * width].astype(F32), width)
        buffer[t, rows, 0:width] = left
        buffer[t, rows, 2 * width:3 * width] = right

    def when_edges(first, second):
        pl.when(jnp.logical_not(top))(first)
        pl.when(jnp.logical_not(bottom))(second)

    def near_here(buffer, t, recv_sems, lanes):
        def here(index):
            for c, part in enumerate(lanes):
                arrived(buffer.at[t, near[index], part], recv_sems.at[c, index])
            spread(buffer, t, near[index], hid)

        when_edges(lambda: here(0), lambda: here(1))

    def far_here(buffer, t, recv_sems):
        def here(index):
            arrived(buffer.at[t, far[index], centre], recv_sems.at[index])
            spread(buffer, t, far[index], hid)

        when_edges(lambda: here(0), lambda: here(1))

    def narrow_here(ref, recv_sems):
        when_edges(
            lambda: arrived(ref.at[above1], recv_sems.at[0]),
            lambda: arrived(ref.at[below1], recv_sems.at[1]),
        )

    def conv(buffer, t, weights, c, offsets):
        total = None
        for a in offsets:
            term = dot(
                buffer[t, cols * (a + 1):cols * (a + 1) + n, :],
                weights[c, a].reshape(3 * hid, gate_half),
            )
            total = term if total is None else total + term
        return total

    def conv_all(buffer, t, weights, c):
        total = None
        for a in range(3):
            term = dot(
                buffer[t, cols * a:cols * (a + 2) + n, :],
                weights[c, a].reshape(3 * hid, gate_half),
            )
            total = term if total is None else total + term
        return total

    def conv_beside(t, c):
        total = None
        for buffer, weights in ((sh, wh), (sx, wx)):
            for a in range(3):
                low = cols * (a + 1) + n
                cells_in = jnp.concatenate(
                    [buffer[t, cols * a:cols * (a + 1), :], buffer[t, low:low + cols, :]], axis=0
                )
                term = dot(cells_in, weights[c, a].reshape(3 * hid, gate_half))
                total = term if total is None else total + term
        return total

    def bias_of(c):
        return jnp.concatenate(
            [bias[0:1, g * hid + c * half:g * hid + (c + 1) * half] for g in range(4)], axis=1
        )

    def activate(now, old):
        i_gate = jax.nn.sigmoid(now[:, 0:half])
        f_gate = jax.nn.sigmoid(now[:, half:2 * half])
        o_gate = jax.nn.sigmoid(now[:, 2 * half:3 * half])
        cand = jnp.tanh(now[:, 3 * half:])
        new = f_gate * old + i_gate * cand
        return i_gate, f_gate, o_gate, cand, new, jnp.tanh(new)

    def factors(i_gate, f_gate, o_gate, cand, squash, old):
        return (
            o_gate * (1.0 - squash * squash),
            cand * i_gate * (1.0 - i_gate),
            old * f_gate * (1.0 - f_gate),
            squash * o_gate * (1.0 - o_gate),
            i_gate * (1.0 - cand * cand),
            f_gate,
        )

    def turn_weights(source, target):
        def one(a, carried):
            for b in range(3):
                for c in range(2):
                    start = (2 - b) * 4 * hid + c * gate_half
                    target[a, start:start + gate_half, :] = source[c, a, b].T
            return carried

        lax.fori_loop(0, 3, one, 0)

    def turn_all_weights():
        turn_weights(wh, wht)
        pl.when(inner)(lambda: turn_weights(wx, wxt))

    def spread_to_group(pred, view, send_sems, recv_sems):
        for d in (0, 1, 3, 2):
            for c in range(2):
                there = ((x if c == 0 else y) + d) % LINE
                chip = y * LINE + there if c == 0 else there * LINE + x
                slot = 2 * (x if c == 0 else y) + k
                src, dst = view(c, slot)
                make = functools.partial(
                    remote, src, dst, send_sems.at[c * LINE + d], recv_sems.at[slot], (z, chip, c)
                )
                ok = pred
                if d == 0:
                    ok = (k != c) if pred is None else pred & (k != c)
                    own = (k == c) if pred is None else pred & (k == c)
                    pl.when(own)(
                        functools.partial(
                            lambda src, dst, sem: pltpu.make_async_copy(src, dst, sem).start(),
                            src, dst, recv_sems.at[slot],
                        )
                    )
                send(ok, make)

    def send_tile(t, part, pred):
        src = (sh if part else sx).at[t, cols:3 * cols + n, centre]
        spread_to_group(
            pred, lambda c, slot: (src, tiles_all.at[t, part, slot]), ti_s.at[t, part], ti_r.at[t, part]
        )

    pairs = [slice(p * 2 * half, (p + 1) * 2 * half) for p in range(2)]

    def send_grads(t, pred):
        for p, lanes in enumerate(pairs if t == 0 else [slice(0, gate_half)]):
            def view(c, slot):
                at = 4 * hid + c * gate_half
                src = sg.at[t, own1, at + lanes.start:at + lanes.stop]
                return src, grads_all.at[t, pl.ds(pl.multiple_of(slot * n, n), n), lanes]

            spread_to_group(pred, view, ga_s.at[t, p], ga_r.at[t, p])

    early = z < 2

    def send_factors(t):
        def view(c, slot):
            src = packed.at[t, :, c * gate_half:(c + 1) * gate_half]
            return src, packed_all.at[t, pl.ds(pl.multiple_of(slot * n, n), n), :]

        spread_to_group(early, view, co_s.at[t], co_r.at[t])

    def pack_factors():
        for c in range(2):
            chan = slice(c * half, (c + 1) * half)
            for t in range(2):
                for g in range(4):
                    value = coef[t, 1 + g, own1, chan]
                    if t == 1 and g != 2:
                        value = value * coef[t, 0, own1, chan]
                    at = c * gate_half + g * half
                    packed[t, :, at:at + half] = value.astype(BF16)

    def send_vec(index, pred):
        def view(c, slot):
            chan = slice(c * half, (c + 1) * half)
            src = gin.at[1, own1, chan] if index == 0 else vec.at[index - 1, :, chan]
            return src, vec_all.at[index, pl.ds(pl.multiple_of(slot * n, n), n), :]

        spread_to_group(pred, view, ve_s.at[index], ve_r.at[index])

    rows = out.shape[0]
    block = 2 * rows
    me = jnp.where(k == 0, y, x)

    def turn_patches():
        for t in range(2):
            for part in range(2):
                for slot in range(2 * LINE):
                    arrived(tiles_all.at[t, part, slot], ti_r.at[t, part, slot])

            def one(slot, carried):
                for part in range(2):
                    tile = tiles_all[t, part, slot]
                    left, right = spread_value(tile.astype(F32), hid)
                    for b, moved in enumerate((left, tile, right)):
                        for a in range(3):
                            at = (a * 3 + b) * 2 * hid + part * hid
                            flipped[at:at + hid, :] = moved[cols * a:cols * a + n, :].T
                for j in range(LINE):
                    chip = jnp.where(k == 0, j * LINE + x, y * LINE + j)
                    turned[t, j, :, pl.ds(pl.multiple_of(slot * n, n), n)] = flipped[
                        pl.ds(pl.multiple_of(chip * block, 32), block), :
                    ]
                return carried

            lax.fori_loop(0, 2 * LINE, one, 0)

    @pl.when(z >= 2)
    def _():
        weights_here(1)
        weights_here(0)
        turn_all_weights()

    not_roof = jnp.logical_not(roof)
    z_up = z + 1

    def save(t, into, values, old, chan):
        i_gate, f_gate, o_gate, cand, squash = values
        for index, value in enumerate(factors(i_gate, f_gate, o_gate, cand, squash, old)):
            for cells_to, cells_from in into:
                coef[t, index, cells_to, chan] = value[cells_from]

    def x_here(t):
        for c in range(2):
            arrived(sx.at[t, own2, half_lanes[c]], sx_r.at[t, c, 2])
        spread(sx, t, own2, hid)

    def add(c, term):
        preact[0:n, c * gate_half:(c + 1) * gate_half] += term

    def own_rows(t):
        hidden_lanes = (centre,) if t == 0 else half_lanes
        part_sums = [conv(sh, t, wh, c, (1,)) + bias_of(c) for c in range(2)]
        for c in range(2):
            preact[0:n, c * gate_half:(c + 1) * gate_half] = part_sums[c]

        def x_middle():
            x_here(t)
            for c in range(2):
                add(c, conv(sx, t, wx, c, (1,)))

        def x_edges():
            near_here(sx, t, sx_r.at[t], half_lanes)

        def h_edges():
            near_here(sh, t, sh_r.at[t], hidden_lanes)

        def h_outer():
            for c in range(2):
                add(c, conv(sh, t, wh, c, (0, 2)))

        @pl.when(base)
        def _():
            if t == 0:
                weights_here(0)
            x_middle()
            if t == 1:
                x_edges()
                for c in range(2):
                    add(c, conv(sx, t, wx, c, (0, 2)))
                h_edges()

        if t == 0:
            h_edges()
            h_outer()
            send_tile(0, 1, inner)
            pl.when(z == 1)(lambda: weights_here(0))

        @pl.when(inner)
        def _():
            if t == 1:
                h_edges()
                h_outer()
            x_middle()
            if t == 1:
                x_edges()

        if t == 0:
            x_edges()
            own_cell.wait()
            pl.when(not_roof)(lambda: pl.semaphore_wait(barrier, count(above)))

        def finish(buffer, weights, c):
            chan, lanes = slice(c * half, (c + 1) * half), half_lanes[c]
            now = preact[0:n, c * gate_half:(c + 1) * gate_half] + conv(buffer, t, weights, c, (0, 2))
            i_gate, f_gate, o_gate, cand, new, squash = activate(now, cells[t, own1, chan])
            hidden = (o_gate * squash).astype(BF16)
            if t == 0:
                sh[1, own2, lanes] = hidden
                cells[1, own1, chan] = new
            else:
                top_hidden[:, chan] = hidden
            for index, value in enumerate((i_gate, f_gate, o_gate, cand, squash)):
                gates[index, :, chan] = value

        for c in range(2):
            chan, lanes = slice(c * half, (c + 1) * half), half_lanes[c]
            if t == 0:
                finish(sx, wx, c)
                whole = sh.at[1, own2, lanes]
                ends = sh.at[1, 2 * cols:3 * cols, lanes], sh.at[1, n + cols:n + 2 * cols, lanes]
            else:
                pl.when(base)(lambda c=c: finish(sh, wh, c))
                pl.when(inner)(lambda c=c: finish(sx, wx, c))
                whole = top_hidden.at[:, chan]
                ends = top_hidden.at[0:cols, chan], top_hidden.at[n - cols:n, chan]
            send(
                not_roof,
                lambda whole=whole, lanes=lanes, c=c: remote(
                    whole, sx.at[t, own2, lanes], sx_s.at[t, c, 2], sx_r.at[t, c, 2], (z_up, s, k)
                ),
            )
            if t == 0:
                send_edges(ends, at_rows(sh, 1, near, lanes), sh_s.at[c], sh_r.at[1, c], z, None)
            edges(
                lambda ends=ends, lanes=lanes, c=c: (
                    ends, at_rows(sx, t, near, lanes), sx_s.at[t, c], sx_r.at[t, c]
                ),
                z_up, not_roof,
            )
        if t == 0:
            ends = sh.at[1, 3 * cols:4 * cols, centre], sh.at[1, n:n + cols, centre]
            send_edges(ends, at_rows(sh, 1, far, centre), sh_fs, sh_f.at[1], z, None)
        else:
            ends = beyond(top_hidden)
        last = ends
        edges(
            lambda: (last, at_rows(sx, t, far, centre), sx_fs.at[t], sx_f.at[t]), z_up, not_roof
        )
        for c in range(2):
            chan = slice(c * half, (c + 1) * half)
            save(
                t, ((own1, slice(0, n)),),
                tuple(gates[index, :, chan] for index in range(5)), cells[t, own1, chan], chan,
            )

    def beside_rows(t):
        if t == 0:
            narrow_here(cells.at[0], c_r)
        far_here(sh, t, sh_f.at[t])
        far_here(sx, t, sx_f.at[t])
        for c in range(2):
            chan = slice(c * half, (c + 1) * half)
            old = jnp.concatenate([cells[t, above1, chan], cells[t, below1, chan]], axis=0)
            i_gate, f_gate, o_gate, cand, new, squash = activate(conv_beside(t, c) + bias_of(c), old)
            if t == 0:
                cells[1, above1, chan] = new[0:cols]
                cells[1, below1, chan] = new[cols:]
            save(
                t, ((above1, slice(0, cols)), (below1, slice(cols, 2 * cols))),
                (i_gate, f_gate, o_gate, cand, squash), old, chan,
            )

    def all_rows():
        far_here(sh, 1, sh_f.at[1])
        for c in range(2):
            preact[:, c * gate_half:(c + 1) * gate_half] = conv_all(sh, 1, wh, c) + bias_of(c)
        x_here(1)
        near_here(sx, 1, sx_r.at[1], half_lanes)
        far_here(sx, 1, sx_f.at[1])
        for c in range(2):
            chan = slice(c * half, (c + 1) * half)
            now = preact[:, c * gate_half:(c + 1) * gate_half] + conv_all(sx, 1, wx, c)
            old = cells[1, :, chan]
            i_gate, f_gate, o_gate, cand, new, squash = activate(now, old)
            save(
                1, ((slice(0, n + 2 * cols), slice(0, n + 2 * cols)),),
                (i_gate, f_gate, o_gate, cand, squash), old, chan,
            )

    own_hidden.wait()
    spread(sh, 0, own2, hid)
    pl.when(z < 2)(lambda: weights_here(1))
    own_rows(0)
    send_tile(0, 0, inner)
    spread(sh, 1, own2, hid)

    @pl.when(not_roof)
    def _():
        own_rows(1)
        beside_rows(0)
        beside_rows(1)

    @pl.when(roof)
    def _():
        beside_rows(0)
        near_here(sh, 1, sh_r.at[1], half_lanes)

    send_tile(1, 1, roof)
    pl.when(roof)(all_rows)

    def blank(outside):
        coef[:, :, outside, :] = jnp.zeros((2, 6, cols, hid), F32)

    pl.when(top)(lambda: blank(above1))
    pl.when(bottom)(lambda: blank(below1))

    pl.when(z < 2)(turn_all_weights)
    pl.when(early)(pack_factors)
    send_tile(0, 1, base)
    send_tile(0, 0, base)
    send_tile(1, 1, not_roof)
    send_tile(1, 0, not_roof)
    send_factors(1)
    send_factors(0)
    pl.when(z < 2)(turn_patches)

    def back_conv(t, weights):
        total = None
        for a in range(3):
            term = dot(sg[t, cols * (2 - a):cols * (2 - a) + n, :], weights[a])
            total = term if total is None else total + term
        return total.astype(BF16)

    for t in (1, 0):
        arrived(gin.at[t, own1], gx_r.at[t, 2])
        if t == 1:
            send_vec(0, base)
        if t == 1:
            narrow_here(gin.at[t], gx_r.at[t])
        else:
            @pl.when(inner)
            def _():
                narrow_here(gin.at[0], gx_r.at[0])
                narrow_here(ghid, gh_r)
        for c in range(2):
            chan = slice(c * half, (c + 1) * half)
            grad_h = gin[t, :, chan].astype(F32)
            if t == 0:
                grad_h = grad_h + ghid[:, chan].astype(F32)
            grad_c = grad_h * coef[t, 0, :, chan]
            if t == 0:
                grad_c = grad_c + carry[:, chan]
            for g, value in enumerate((
                grad_c * coef[t, 1, :, chan],
                grad_c * coef[t, 2, :, chan],
                grad_h * coef[t, 3, :, chan],
                grad_c * coef[t, 4, :, chan],
            )):
                at = 4 * hid + c * gate_half + g * half
                sg[t, :, at:at + half] = value.astype(BF16)
            if t == 0:
                vec[0, :, chan] = grad_c[cols:cols + n].astype(BF16)
                vec[1, :, chan] = grad_h[cols:cols + n].astype(BF16)
            if t == 1:
                carry[:, chan] = grad_c * coef[t, 5, :, chan]
        if t == 0:
            send_vec(1, early)
            send_vec(2, early)

        def widen(t=t):
            spread(sg, t, slice(0, 2 * cols + n), 4 * hid)

        def input_grad(t=t):
            gx_out[t] = back_conv(t, wxt)

        if t == 1:
            widen()
            pl.when(inner)(input_grad)
        else:
            @pl.when(inner)
            def _():
                widen()
                input_grad()

        send(
            inner,
            lambda t=t: remote(gx_out.at[t], gin.at[t, own1], gx_s.at[t, 2], gx_r.at[t, 2], (z - 1, s, k)),
        )
        send_edges(
            outer(gx_out.at[t], cols), narrow(gin.at[t]), gx_s.at[t], gx_r.at[t], z - 1,
            inner if t == 1 else z >= 2,
        )
        if t == 1:
            ghid[own1] = back_conv(t, wht)
            send_edges(
                (ghid.at[cols:2 * cols], ghid.at[n:n + cols]), narrow(ghid), gh_s, gh_r, z, inner
            )
            send_tile(1, 0, roof)
            send_vec(0, z == 1)
        else:
            send_grads(1, z >= 2)
            send_grads(0, z >= 2)

    pl.when(z >= 2)(turn_patches)

    def grads_here(t, p, lanes):
        for slot in range(2 * LINE):
            arrived(grads_all.at[t, slot * n:(slot + 1) * n, lanes], ga_r.at[t, p, slot])

    def vec_here(index):
        for slot in range(2 * LINE):
            arrived(vec_all.at[index, slot * n:(slot + 1) * n], ve_r.at[index, slot])

    def factors_here(t):
        for slot in range(2 * LINE):
            arrived(packed_all.at[t, slot * n:(slot + 1) * n], co_r.at[t, slot])

    def form(t, gates_of, index):
        for g in gates_of:
            lanes = slice(g * half, (g + 1) * half)
            grads_all[t, :, lanes] = (
                packed_all[t, :, lanes].astype(F32) * vec_all[index].astype(F32)
            ).astype(BF16)

    @pl.when(early)
    def _():
        factors_here(1)
        factors_here(0)
        vec_here(0)
        form(1, range(4), 0)

    pl.when(z >= 2)(lambda: grads_here(1, 0, slice(0, gate_half)))
    for j in range(LINE):
        acc[j] = dot(turned[1, j], grads_all[1])
    earlier = list(pending)
    pending.clear()
    for p, lanes in enumerate(pairs):
        @pl.when(early)
        def _():
            vec_here(1 + p)
            if p == 0:
                form(0, (0, 1), 1)
            else:
                form(0, (2,), 2)
                form(0, (3,), 1)

        pl.when(z >= 2)(lambda: grads_here(0, p, lanes))
        for d in (1, 3, 2, 0):
            j = (me + d) % LINE
            leaving[d, :, lanes] = (
                acc[j, :, lanes] + dot(turned[0, j], grads_all[0, :, lanes])
            ).astype(BF16)
            chip = jnp.where(k == 0, j * LINE + x, y * LINE + j)
            for q in range(2):
                src, dst = leaving.at[d, q * rows:(q + 1) * rows, lanes], landed.at[k, me, :, lanes]
                make = functools.partial(
                    remote, src, dst, rv_s.at[p, d * 2 + q], rv_r.at[p, k, me], (z, chip, q)
                )
                if d == 0:
                    pl.when(k == q)(
                        functools.partial(
                            lambda src, dst, sem: pltpu.make_async_copy(src, dst, sem).start(),
                            src, dst, rv_r.at[p, k, me],
                        )
                    )
                send(k != q if d == 0 else None, make)
    for wait in earlier:
        wait()
    for p, lanes in enumerate(pairs):
        for c in range(2):
            for i in range(LINE):
                arrived(landed.at[c, i, :, lanes], rv_r.at[p, c, i])
            for g in (2 * p, 2 * p + 1):
                total = landed[c, 0, :, g * half:(g + 1) * half].astype(F32)
                for i in range(1, LINE):
                    total = total + landed[c, i, :, g * half:(g + 1) * half].astype(F32)
                out[:, g * hid + c * half:g * hid + (c + 1) * half] = total
    for wait in pending:
        wait()


def on_device(frames, cotangent, first_hidden, first_cell, gate_bias, gate_weight):
    steps, _, tile_rows, cols, hid = frames.shape
    n = tile_rows * cols
    pad = n + 2 * cols
    half = hid // 2
    gates = 4 * hid
    share = 18 * hid // (lax.axis_size("space") * lax.axis_size("batch"))
    block = 2 * share
    vmem = pl.BlockSpec(memory_space=pltpu.VMEM)
    anywhere = pl.BlockSpec(memory_space=pl.ANY)
    dma = pltpu.SemaphoreType.DMA
    scratch = [
        pltpu.VMEM((2, 3, 3, hid, gates // 2), BF16),
        pltpu.VMEM((2, 3, 3, hid, gates // 2), BF16),
        pltpu.VMEM((3, 3 * gates, hid), BF16),
        pltpu.VMEM((3, 3 * gates, hid), BF16),
        pltpu.VMEM((steps, pad + 2 * cols, 3 * hid), BF16),
        pltpu.VMEM((steps, pad + 2 * cols, 3 * hid), BF16),
        pltpu.VMEM((steps, pad, 3 * gates), BF16),
        pltpu.VMEM((n, hid), BF16),
        pltpu.VMEM((pad, gates), F32),
        pltpu.VMEM((5, n, hid), F32),
        pltpu.VMEM((steps, pad, hid), F32),
        pltpu.VMEM((pad, hid), F32),
        pltpu.VMEM((steps, 6, pad, hid), F32),
        pltpu.VMEM((steps, pad, hid), BF16),
        pltpu.VMEM((steps, n, hid), BF16),
        pltpu.VMEM((pad, hid), BF16),
        pltpu.VMEM((steps, 2, 2 * LINE, pad, hid), BF16),
        pltpu.VMEM((18 * hid, n), BF16),
        pltpu.VMEM((steps, LINE, block, 2 * LINE * n), BF16),
        pltpu.VMEM((steps, 2 * LINE * n, gates // 2), BF16),
        pltpu.VMEM((steps, n, gates), BF16),
        pltpu.VMEM((steps, 2 * LINE * n, gates // 2), BF16),
        pltpu.VMEM((2, n, hid), BF16),
        pltpu.VMEM((3, 2 * LINE * n, half), BF16),
        pltpu.VMEM((LINE, block, gates // 2), F32),
        pltpu.VMEM((LINE, block, gates // 2), BF16),
        pltpu.VMEM((2, LINE, share, gates // 2), BF16),
        dma((2, 2, 4)), dma((2,)),
        dma((steps, 2, 3)), dma((steps, 2)), dma((steps, 2, 2)), dma((steps, 2)),
        dma((2,)), dma((steps, 3)), dma((2,)),
        dma((steps, 2, 2 * LINE)), dma((steps, 2, 2 * LINE)), dma((steps, 2 * LINE)), dma((3, 2 * LINE)),
        dma((2, 2, LINE)),
        dma((steps, 2, 2)), dma((steps, 2)), dma((2,)), dma((2,)), dma((2,)), dma((steps, 2)),
        dma((steps, 2, 3)), dma((steps, 2)), dma((2, 2)), dma((2,)), dma((steps, 3)), dma((2,)),
        dma((steps, 2, 2 * LINE)), dma((steps, 2, 2 * LINE)), dma((steps, 2 * LINE)), dma((3, 2 * LINE)),
        dma((2, 2 * LINE)),
    ]
    result = pl.pallas_call(
        kernel,
        out_shape=jax.ShapeDtypeStruct((share, gates), F32),
        in_specs=[anywhere] * 4 + [vmem, anywhere],
        out_specs=vmem,
        scratch_shapes=scratch,
        compiler_params=pltpu.CompilerParams(
            collective_id=0, has_side_effects=True, vmem_limit_bytes=56 * 2**20
        ),
    )(
        frames.reshape(steps, n, hid),
        cotangent.reshape(steps, n, hid),
        first_hidden.reshape(n, hid),
        first_cell.reshape(n, hid),
        gate_bias,
        gate_weight.reshape(3, 3, 2 * hid, gates),
    )
    return result[None]


def solution(mesh):
    return jax.shard_map(
        on_device,
        mesh=mesh,
        in_specs=(
            P(None, "batch", "space", None, None),
            P(None, "batch", "space", None, None),
            P("section", "batch", "space", None, None),
            P("section", "batch", "space", None, None),
            P("section", None),
            P("section", None, None),
        ),
        out_specs=P("section", ("space", "batch"), None),
        check_vma=False,
    )
```

```python
import functools

import jax
import jax.numpy as jnp
from jax import lax
from jax.experimental import pallas as pl
from jax.experimental.pallas import tpu as pltpu
from jax.sharding import PartitionSpec as P

F32 = jnp.float32
BF16 = jnp.bfloat16
MESH = pl.DeviceIdType.MESH
LINE = 4


def dot(left, right):
    return jnp.dot(left, right, preferred_element_type=F32)


def kernel(
    frames, cotangent, first_hidden, first_cell, bias, weight, out,
    wx, wh, wxt, wht, sx, sh, sg, top_hidden, preact, gates, cells, carry, coef, gin, gx_out, ghid,
    tiles_all, flipped, turned, grads_all, packed, packed_all, vec, vec_all, acc, leaving, landed,
    w_sem, in_sem, sx_r, sx_f, sh_r, sh_f, c_r, gx_r, gh_r, ti_r, ga_r, co_r, ve_r, rv_r,
    fr_s, fr_f, fh_s, fh_f, fc_s, ct_s, sx_s, sx_fs, sh_s, sh_fs, gx_s, gh_s, ti_s, ga_s, co_s, ve_s, rv_s,
):
    z, s, k = lax.axis_index("section"), lax.axis_index("space"), lax.axis_index("batch")
    y, x = s // LINE, s % LINE
    sections, tiles = lax.axis_size("section"), lax.axis_size("space")
    cols = 32
    n = first_cell.shape[0]
    hid = first_cell.shape[1]
    half = hid // 2
    gate_half = 4 * half
    own2, above2, below2 = slice(2 * cols, 2 * cols + n), slice(0, 2 * cols), slice(2 * cols + n, 4 * cols + n)
    near = slice(cols, 2 * cols), slice(2 * cols + n, 3 * cols + n)
    far = slice(0, cols), slice(3 * cols + n, 4 * cols + n)
    own1, above1, below1 = slice(cols, cols + n), slice(0, cols), slice(cols + n, 2 * cols + n)
    centre = slice(hid, 2 * hid)
    top, bottom, base, roof = s == 0, s == tiles - 1, z == 0, z == sections - 1
    inner = jnp.logical_not(base)
    pending = []

    def send(pred, make):
        if pred is None:
            make().start()
            pending.append(lambda: make().wait_send())
        else:
            ask = pred if callable(pred) else lambda: pred
            pl.when(ask())(lambda: make().start())
            pending.append(lambda: pl.when(ask())(lambda: make().wait_send()))

    def remote(src, dst, send_sem, recv_sem, device):
        return pltpu.make_async_remote_copy(
            src_ref=src, dst_ref=dst, send_sem=send_sem, recv_sem=recv_sem,
            device_id=device, device_id_type=MESH,
        )

    def arrived(dst, recv_sem):
        remote(dst, dst, recv_sem, recv_sem, (z, s, 1 - k)).wait_recv()

    loads = {}
    for part, buffer in ((0, wx), (1, wh)):
        for c in range(2):
            for g in range(4):
                loads[part, c, g] = pltpu.make_async_copy(
                    weight.at[:, :, part * hid:(part + 1) * hid, pl.ds(g * hid + c * half, half)],
                    buffer.at[c, :, :, :, g * half:(g + 1) * half],
                    w_sem.at[part, c, g],
                )

    def weights_here(part):
        for c in range(2):
            for g in range(4):
                loads[part, c, g].wait()

    barrier = pltpu.get_barrier_semaphore()

    def greet(partners):
        for pred, device in partners:
            call = functools.partial(
                pl.semaphore_signal, barrier, inc=1, device_id=device, device_id_type=MESH
            )
            if pred is None:
                call()
            else:
                pl.when(pred)(call)

    def count(partners):
        total = 0
        for pred, _ in partners:
            total = total + (1 if pred is None else jnp.where(pred, 1, 0))
        return total

    plane = [(jnp.logical_not(top), (z, s - 1, k)), (jnp.logical_not(bottom), (z, s + 1, k))]
    plane.append((None, (z, s, 1 - k)))
    for d in range(1, LINE):
        for core in range(2):
            plane.append((None, (z, y * LINE + (x + d) % LINE, core)))
            plane.append((None, (z, ((y + d) % LINE) * LINE + x, core)))

    def section_at(step, ok):
        return [
            (ok, (z + step, s, k)),
            (ok & (s > 0), (z + step, s - 1, k)),
            (ok & (s < tiles - 1), (z + step, s + 1, k)),
        ]

    below, above = section_at(-1, z > 0), section_at(1, z < sections - 1)
    greet(plane)

    half_lanes = [slice(hid + c * half, hid + (c + 1) * half) for c in range(2)]
    own_hidden = pltpu.make_async_copy(first_hidden, sh.at[0, own2, centre], in_sem.at[0])
    own_cell = pltpu.make_async_copy(first_cell, cells.at[0, own1], in_sem.at[1])
    own_hidden.start()

    @pl.when(base)
    def _():
        for t in range(2):
            for c in range(2):
                pltpu.make_async_copy(
                    frames.at[t, :, pl.ds(c * half, half)], sx.at[t, own2, half_lanes[c]], sx_r.at[t, c, 2]
                ).start()

    own_cell.start()

    @pl.when(roof)
    def _():
        for t in range(2):
            pltpu.make_async_copy(cotangent.at[t], gin.at[t, own1], gx_r.at[t, 2]).start()

    for part in (1, 0):
        for c in range(2):
            for g in range(4):
                loads[part, c, g].start()

    def clear(wide, narrow):
        for t in range(2):
            sx[t, wide, :] = jnp.zeros((2 * cols, 3 * hid), BF16)
            sh[t, wide, :] = jnp.zeros((2 * cols, 3 * hid), BF16)
            gin[t, narrow] = jnp.zeros((cols, hid), BF16)
        cells[0, narrow] = jnp.zeros((cols, hid), F32)
        ghid[narrow] = jnp.zeros((cols, hid), BF16)

    pl.when(top)(lambda: clear(above2, above1))
    pl.when(bottom)(lambda: clear(below2, below1))

    pl.semaphore_wait(barrier, count(plane) + count(below))

    def send_edges(src, dst, send_sems, recv_sems, section, pred):
        edges(lambda: (src, dst, send_sems, recv_sems), section, pred)

    def edges(parts, section, pred):
        def up():
            return s > 0 if pred is None else (s > 0) & pred

        def down():
            return s < tiles - 1 if pred is None else (s < tiles - 1) & pred

        def make(end, device):
            src, dst, send_sems, recv_sems = parts()
            return remote(src[end], dst[1 - end], send_sems.at[end], recv_sems.at[1 - end], device)

        send(up, lambda: make(0, (section, s - 1, k)))
        send(down, lambda: make(1, (section, s + 1, k)))

    def outer(ref, width):
        return ref.at[0:width], ref.at[n - width:n]

    def beyond(ref):
        return ref.at[cols:2 * cols], ref.at[n - 2 * cols:n - cols]

    def narrow(ref):
        return ref.at[above1], ref.at[below1]

    def at_rows(buffer, t, rows, lanes):
        return buffer.at[t, rows[0], lanes], buffer.at[t, rows[1], lanes]

    def halves(ref, c):
        return ref.at[0:cols, pl.ds(c * half, half)], ref.at[n - cols:n, pl.ds(c * half, half)]

    send_edges(outer(first_hidden, cols), at_rows(sh, 0, near, centre), fh_s, sh_r.at[0, 0], z, None)

    def send_frames(t):
        for c in range(2):
            send_edges(
                halves(frames.at[t], c), at_rows(sx, t, near, half_lanes[c]),
                fr_s.at[t, c], sx_r.at[t, c], z, base,
            )

    send_frames(0)
    greet(above)
    greet(below)
    send_edges(beyond(first_hidden), at_rows(sh, 0, far, centre), fh_f, sh_f.at[0], z, None)
    send_edges(outer(first_cell, cols), narrow(cells.at[0]), fc_s, c_r, z, None)
    send_edges(beyond(frames.at[0]), at_rows(sx, 0, far, centre), fr_f.at[0], sx_f.at[0], z, base)
    send_frames(1)
    send_edges(beyond(frames.at[1]), at_rows(sx, 1, far, centre), fr_f.at[1], sx_f.at[1], z, base)
    for t in range(2):
        send_edges(outer(cotangent.at[t], cols), narrow(gin.at[t]), ct_s.at[t], gx_r.at[t], z, roof)

    def spread_value(value, width):
        count = value.shape[0]
        column = lax.broadcasted_iota(jnp.int32, (count, width), 0) % cols
        left = jnp.where(column == 0, 0.0, pltpu.roll(value, 1, 0)).astype(BF16)
        right = jnp.where(column == cols - 1, 0.0, pltpu.roll(value, count - 1, 0)).astype(BF16)
        return left, right

    def spread(buffer, t, rows, width):
        left, right = spread_value(buffer[t, rows, width:2 * width].astype(F32), width)
        buffer[t, rows, 0:width] = left
        buffer[t, rows, 2 * width:3 * width] = right

    def when_edges(first, second):
        pl.when(jnp.logical_not(top))(first)
        pl.when(jnp.logical_not(bottom))(second)

    def near_here(buffer, t, recv_sems, lanes):
        def here(index):
            for c, part in enumerate(lanes):
                arrived(buffer.at[t, near[index], part], recv_sems.at[c, index])
            spread(buffer, t, near[index], hid)

        when_edges(lambda: here(0), lambda: here(1))

    def far_here(buffer, t, recv_sems):
        def here(index):
            arrived(buffer.at[t, far[index], centre], recv_sems.at[index])
            spread(buffer, t, far[index], hid)

        when_edges(lambda: here(0), lambda: here(1))

    def narrow_here(ref, recv_sems):
        when_edges(
            lambda: arrived(ref.at[above1], recv_sems.at[0]),
            lambda: arrived(ref.at[below1], recv_sems.at[1]),
        )

    def conv(buffer, t, weights, c, offsets):
        total = None
        for a in offsets:
            term = dot(
                buffer[t, cols * (a + 1):cols * (a + 1) + n, :],
                weights[c, a].reshape(3 * hid, gate_half),
            )
            total = term if total is None else total + term
        return total

    def conv_all(buffer, t, weights, c):
        total = None
        for a in range(3):
            term = dot(
                buffer[t, cols * a:cols * (a + 2) + n, :],
                weights[c, a].reshape(3 * hid, gate_half),
            )
            total = term if total is None else total + term
        return total

    def conv_beside(t, c):
        total = None
        for buffer, weights in ((sh, wh), (sx, wx)):
            for a in range(3):
                low = cols * (a + 1) + n
                cells_in = jnp.concatenate(
                    [buffer[t, cols * a:cols * (a + 1), :], buffer[t, low:low + cols, :]], axis=0
                )
                term = dot(cells_in, weights[c, a].reshape(3 * hid, gate_half))
                total = term if total is None else total + term
        return total

    def bias_of(c):
        return jnp.concatenate(
            [bias[0:1, g * hid + c * half:g * hid + (c + 1) * half] for g in range(4)], axis=1
        )

    def activate(now, old):
        i_gate = jax.nn.sigmoid(now[:, 0:half])
        f_gate = jax.nn.sigmoid(now[:, half:2 * half])
        o_gate = jax.nn.sigmoid(now[:, 2 * half:3 * half])
        cand = jnp.tanh(now[:, 3 * half:])
        new = f_gate * old + i_gate * cand
        return i_gate, f_gate, o_gate, cand, new, jnp.tanh(new)

    def factors(i_gate, f_gate, o_gate, cand, squash, old):
        return (
            o_gate * (1.0 - squash * squash),
            cand * i_gate * (1.0 - i_gate),
            old * f_gate * (1.0 - f_gate),
            squash * o_gate * (1.0 - o_gate),
            i_gate * (1.0 - cand * cand),
            f_gate,
        )

    def turn_weights(source, target):
        def one(a, carried):
            for b in range(3):
                for c in range(2):
                    start = (2 - b) * 4 * hid + c * gate_half
                    target[a, start:start + gate_half, :] = source[c, a, b].T
            return carried

        lax.fori_loop(0, 3, one, 0)

    def turn_all_weights():
        turn_weights(wh, wht)
        pl.when(inner)(lambda: turn_weights(wx, wxt))

    def spread_to_group(pred, view, seven, send_sem, recv_sem):
        def go():
            for d in (0, 1, 3, 2):
                for c in range(2):
                    there = ((x if c == 0 else y) + d) % LINE
                    chip = y * LINE + there if c == 0 else there * LINE + x
                    src, dst = view(c, 2 * (x if c == 0 else y) + k)
                    copy = functools.partial(remote, src, dst, send_sem(), recv_sem(), (z, chip, c))
                    if d == 0:
                        pl.when(k == c)(lambda: pltpu.make_async_copy(src, dst, recv_sem()).start())
                        pl.when(k != c)(lambda: copy().start())
                    else:
                        copy().start()

        def done():
            remote(seven(), seven(), send_sem(), recv_sem(), (z, s, 1 - k)).wait_send()

        pl.when(pred)(go)
        pending.append(lambda: pl.when(pred)(done))

    def rows_of(slot):
        return pl.ds(pl.multiple_of(slot * n, n), n)

    most = slice(0, 7 * n)

    def send_tile(t, part, pred):
        spread_to_group(
            pred,
            lambda c, slot: (
                (sh if part else sx).at[t, cols:3 * cols + n, centre], tiles_all.at[t, part, slot]
            ),
            lambda: tiles_all.at[t, part, 0:7],
            lambda: ti_s.at[t, part], lambda: ti_r.at[t, part],
        )

    pairs = [slice(p * 2 * half, (p + 1) * 2 * half) for p in range(2)]

    def send_grads(t, pred):
        for p, lanes in enumerate(pairs if t == 0 else [slice(0, gate_half)]):
            def view(c, slot, lanes=lanes):
                at = 4 * hid + c * gate_half
                src = sg.at[t, own1, at + lanes.start:at + lanes.stop]
                return src, grads_all.at[t, rows_of(slot), lanes]

            spread_to_group(
                pred, view, lambda lanes=lanes: grads_all.at[t, most, lanes],
                lambda p=p: ga_s.at[t, p], lambda p=p: ga_r.at[t, p],
            )

    early = z < 2

    def send_factors(t):
        def view(c, slot):
            src = packed.at[t, :, c * gate_half:(c + 1) * gate_half]
            return src, packed_all.at[t, rows_of(slot), :]

        spread_to_group(
            early, view, lambda: packed_all.at[t, most], lambda: co_s.at[t], lambda: co_r.at[t]
        )

    def pack_factors():
        for c in range(2):
            chan = slice(c * half, (c + 1) * half)
            for t in range(2):
                for g in range(4):
                    value = coef[t, 1 + g, own1, chan]
                    if t == 1 and g != 2:
                        value = value * coef[t, 0, own1, chan]
                    at = c * gate_half + g * half
                    packed[t, :, at:at + half] = value.astype(BF16)

    def send_vec(index, pred):
        def view(c, slot):
            chan = slice(c * half, (c + 1) * half)
            src = gin.at[1, own1, chan] if index == 0 else vec.at[index - 1, :, chan]
            return src, vec_all.at[index, rows_of(slot), :]

        spread_to_group(
            pred, view, lambda: vec_all.at[index, most], lambda: ve_s.at[index], lambda: ve_r.at[index]
        )

    rows = out.shape[0]
    block = 2 * rows
    me = jnp.where(k == 0, y, x)

    def turn_patches():
        for t in range(2):
            for part in range(2):
                arrived(tiles_all.at[t, part], ti_r.at[t, part])

            def one(slot, carried):
                for part in range(2):
                    tile = tiles_all[t, part, slot]
                    left, right = spread_value(tile.astype(F32), hid)
                    for b, moved in enumerate((left, tile, right)):
                        for a in range(3):
                            at = (a * 3 + b) * 2 * hid + part * hid
                            flipped[at:at + hid, :] = moved[cols * a:cols * a + n, :].T
                for j in range(LINE):
                    chip = jnp.where(k == 0, j * LINE + x, y * LINE + j)
                    turned[t, j, :, pl.ds(pl.multiple_of(slot * n, n), n)] = flipped[
                        pl.ds(pl.multiple_of(chip * block, 32), block), :
                    ]
                return carried

            lax.fori_loop(0, 2 * LINE, one, 0)

    @pl.when(z >= 2)
    def _():
        weights_here(1)
        weights_here(0)
        turn_all_weights()

    not_roof = jnp.logical_not(roof)
    z_up = z + 1

    def save(t, into, values, old, chan):
        i_gate, f_gate, o_gate, cand, squash = values
        for index, value in enumerate(factors(i_gate, f_gate, o_gate, cand, squash, old)):
            for cells_to, cells_from in into:
                coef[t, index, cells_to, chan] = value[cells_from]

    def x_here(t):
        for c in range(2):
            arrived(sx.at[t, own2, half_lanes[c]], sx_r.at[t, c, 2])
        spread(sx, t, own2, hid)

    def add(c, term):
        preact[0:n, c * gate_half:(c + 1) * gate_half] += term

    def own_rows(t):
        hidden_lanes = (centre,) if t == 0 else half_lanes
        part_sums = [conv(sh, t, wh, c, (1,)) + bias_of(c) for c in range(2)]
        for c in range(2):
            preact[0:n, c * gate_half:(c + 1) * gate_half] = part_sums[c]

        def x_middle():
            x_here(t)
            for c in range(2):
                add(c, conv(sx, t, wx, c, (1,)))

        def x_edges():
            near_here(sx, t, sx_r.at[t], half_lanes)

        def h_edges():
            near_here(sh, t, sh_r.at[t], hidden_lanes)

        def h_outer():
            for c in range(2):
                add(c, conv(sh, t, wh, c, (0, 2)))

        @pl.when(base)
        def _():
            if t == 0:
                weights_here(0)
            x_middle()
            if t == 1:
                x_edges()
                for c in range(2):
                    add(c, conv(sx, t, wx, c, (0, 2)))
                h_edges()

        if t == 0:
            h_edges()
            h_outer()
            send_tile(0, 1, inner)
            pl.when(z == 1)(lambda: weights_here(0))

        @pl.when(inner)
        def _():
            if t == 1:
                h_edges()
                h_outer()
            x_middle()
            if t == 1:
                x_edges()

        if t == 0:
            x_edges()
            own_cell.wait()
            pl.when(not_roof)(lambda: pl.semaphore_wait(barrier, count(above)))

        def finish(buffer, weights, c):
            chan, lanes = slice(c * half, (c + 1) * half), half_lanes[c]
            now = preact[0:n, c * gate_half:(c + 1) * gate_half] + conv(buffer, t, weights, c, (0, 2))
            i_gate, f_gate, o_gate, cand, new, squash = activate(now, cells[t, own1, chan])
            hidden = (o_gate * squash).astype(BF16)
            if t == 0:
                sh[1, own2, lanes] = hidden
                cells[1, own1, chan] = new
            else:
                top_hidden[:, chan] = hidden
            for index, value in enumerate((i_gate, f_gate, o_gate, cand, squash)):
                gates[index, :, chan] = value

        for c in range(2):
            chan, lanes = slice(c * half, (c + 1) * half), half_lanes[c]
            if t == 0:
                finish(sx, wx, c)
                whole = sh.at[1, own2, lanes]
                ends = sh.at[1, 2 * cols:3 * cols, lanes], sh.at[1, n + cols:n + 2 * cols, lanes]
            else:
                pl.when(base)(lambda c=c: finish(sh, wh, c))
                pl.when(inner)(lambda c=c: finish(sx, wx, c))
                whole = top_hidden.at[:, chan]
                ends = top_hidden.at[0:cols, chan], top_hidden.at[n - cols:n, chan]
            send(
                not_roof,
                lambda whole=whole, lanes=lanes, c=c: remote(
                    whole, sx.at[t, own2, lanes], sx_s.at[t, c, 2], sx_r.at[t, c, 2], (z_up, s, k)
                ),
            )
            if t == 0:
                send_edges(ends, at_rows(sh, 1, near, lanes), sh_s.at[c], sh_r.at[1, c], z, None)
            edges(
                lambda ends=ends, lanes=lanes, c=c: (
                    ends, at_rows(sx, t, near, lanes), sx_s.at[t, c], sx_r.at[t, c]
                ),
                z_up, not_roof,
            )
        if t == 0:
            ends = sh.at[1, 3 * cols:4 * cols, centre], sh.at[1, n:n + cols, centre]
            send_edges(ends, at_rows(sh, 1, far, centre), sh_fs, sh_f.at[1], z, None)
        else:
            ends = beyond(top_hidden)
        last = ends
        edges(
            lambda: (last, at_rows(sx, t, far, centre), sx_fs.at[t], sx_f.at[t]), z_up, not_roof
        )
        for c in range(2):
            chan = slice(c * half, (c + 1) * half)
            save(
                t, ((own1, slice(0, n)),),
                tuple(gates[index, :, chan] for index in range(5)), cells[t, own1, chan], chan,
            )

    def beside_rows(t):
        if t == 0:
            narrow_here(cells.at[0], c_r)
        far_here(sh, t, sh_f.at[t])
        far_here(sx, t, sx_f.at[t])
        for c in range(2):
            chan = slice(c * half, (c + 1) * half)
            old = jnp.concatenate([cells[t, above1, chan], cells[t, below1, chan]], axis=0)
            i_gate, f_gate, o_gate, cand, new, squash = activate(conv_beside(t, c) + bias_of(c), old)
            if t == 0:
                cells[1, above1, chan] = new[0:cols]
                cells[1, below1, chan] = new[cols:]
            save(
                t, ((above1, slice(0, cols)), (below1, slice(cols, 2 * cols))),
                (i_gate, f_gate, o_gate, cand, squash), old, chan,
            )

    def all_rows():
        far_here(sh, 1, sh_f.at[1])
        for c in range(2):
            preact[:, c * gate_half:(c + 1) * gate_half] = conv_all(sh, 1, wh, c) + bias_of(c)
        x_here(1)
        near_here(sx, 1, sx_r.at[1], half_lanes)
        far_here(sx, 1, sx_f.at[1])
        for c in range(2):
            chan = slice(c * half, (c + 1) * half)
            now = preact[:, c * gate_half:(c + 1) * gate_half] + conv_all(sx, 1, wx, c)
            old = cells[1, :, chan]
            i_gate, f_gate, o_gate, cand, new, squash = activate(now, old)
            save(
                1, ((slice(0, n + 2 * cols), slice(0, n + 2 * cols)),),
                (i_gate, f_gate, o_gate, cand, squash), old, chan,
            )

    own_hidden.wait()
    spread(sh, 0, own2, hid)
    pl.when(z < 2)(lambda: weights_here(1))
    own_rows(0)
    send_tile(0, 0, inner)
    spread(sh, 1, own2, hid)

    @pl.when(not_roof)
    def _():
        own_rows(1)
        beside_rows(0)
        beside_rows(1)

    @pl.when(roof)
    def _():
        beside_rows(0)
        near_here(sh, 1, sh_r.at[1], half_lanes)

    send_tile(1, 1, roof)
    pl.when(roof)(all_rows)

    def blank(outside):
        coef[:, :, outside, :] = jnp.zeros((2, 6, cols, hid), F32)

    pl.when(top)(lambda: blank(above1))
    pl.when(bottom)(lambda: blank(below1))

    pl.when(z < 2)(turn_all_weights)
    pl.when(early)(pack_factors)
    send_tile(0, 1, base)
    send_tile(0, 0, base)
    send_tile(1, 1, not_roof)
    send_tile(1, 0, not_roof)
    send_factors(1)
    send_factors(0)
    pl.when(z < 2)(turn_patches)

    def back_conv(t, weights):
        total = None
        for a in range(3):
            term = dot(sg[t, cols * (2 - a):cols * (2 - a) + n, :], weights[a])
            total = term if total is None else total + term
        return total.astype(BF16)

    for t in (1, 0):
        arrived(gin.at[t, own1], gx_r.at[t, 2])
        if t == 1:
            send_vec(0, base)
        if t == 1:
            narrow_here(gin.at[t], gx_r.at[t])
        else:
            @pl.when(inner)
            def _():
                narrow_here(gin.at[0], gx_r.at[0])
                narrow_here(ghid, gh_r)
        for c in range(2):
            chan = slice(c * half, (c + 1) * half)
            grad_h = gin[t, :, chan].astype(F32)
            if t == 0:
                grad_h = grad_h + ghid[:, chan].astype(F32)
            grad_c = grad_h * coef[t, 0, :, chan]
            if t == 0:
                grad_c = grad_c + carry[:, chan]
            for g, value in enumerate((
                grad_c * coef[t, 1, :, chan],
                grad_c * coef[t, 2, :, chan],
                grad_h * coef[t, 3, :, chan],
                grad_c * coef[t, 4, :, chan],
            )):
                at = 4 * hid + c * gate_half + g * half
                sg[t, :, at:at + half] = value.astype(BF16)
            if t == 0:
                vec[0, :, chan] = grad_c[cols:cols + n].astype(BF16)
                vec[1, :, chan] = grad_h[cols:cols + n].astype(BF16)
            if t == 1:
                carry[:, chan] = grad_c * coef[t, 5, :, chan]
        if t == 0:
            send_vec(1, early)
            send_vec(2, early)

        def widen(t=t):
            spread(sg, t, slice(0, 2 * cols + n), 4 * hid)

        def input_grad(t=t):
            gx_out[t] = back_conv(t, wxt)

        if t == 1:
            widen()
            pl.when(inner)(input_grad)
        else:
            @pl.when(inner)
            def _():
                widen()
                input_grad()

        send(
            inner,
            lambda t=t: remote(gx_out.at[t], gin.at[t, own1], gx_s.at[t, 2], gx_r.at[t, 2], (z - 1, s, k)),
        )
        send_edges(
            outer(gx_out.at[t], cols), narrow(gin.at[t]), gx_s.at[t], gx_r.at[t], z - 1,
            inner if t == 1 else z >= 2,
        )
        if t == 1:
            ghid[own1] = back_conv(t, wht)
            send_edges(
                (ghid.at[cols:2 * cols], ghid.at[n:n + cols]), narrow(ghid), gh_s, gh_r, z, inner
            )
            send_tile(1, 0, roof)
            send_vec(0, z == 1)
        else:
            send_grads(1, z >= 2)
            send_grads(0, z >= 2)

    pl.when(z >= 2)(turn_patches)

    def grads_here(t, p, lanes):
        arrived(grads_all.at[t, :, lanes], ga_r.at[t, p])

    def vec_here(index):
        arrived(vec_all.at[index], ve_r.at[index])

    def factors_here(t):
        arrived(packed_all.at[t], co_r.at[t])

    def form(t, gates_of, index):
        for g in gates_of:
            lanes = slice(g * half, (g + 1) * half)
            grads_all[t, :, lanes] = (
                packed_all[t, :, lanes].astype(F32) * vec_all[index].astype(F32)
            ).astype(BF16)

    @pl.when(early)
    def _():
        factors_here(1)
        factors_here(0)
        vec_here(0)
        form(1, range(4), 0)

    pl.when(z >= 2)(lambda: grads_here(1, 0, slice(0, gate_half)))
    for j in range(LINE):
        acc[j] = dot(turned[1, j], grads_all[1])
    for p, lanes in enumerate(pairs):
        @pl.when(early)
        def _():
            vec_here(1 + p)
            if p == 0:
                form(0, (0, 1), 1)
            else:
                form(0, (2,), 2)
                form(0, (3,), 1)

        pl.when(z >= 2)(lambda: grads_here(0, p, lanes))
        for d in (1, 3, 2, 0):
            j = (me + d) % LINE
            leaving[d, :, lanes] = (
                acc[j, :, lanes] + dot(turned[0, j], grads_all[0, :, lanes])
            ).astype(BF16)
            chip = jnp.where(k == 0, j * LINE + x, y * LINE + j)
            for q in range(2):
                src, dst = leaving.at[d, q * rows:(q + 1) * rows, lanes], landed.at[k, me, :, lanes]
                copy = functools.partial(
                    remote, src, dst, rv_s.at[p, min(d, 1)], rv_r.at[p], (z, chip, q)
                )
                if d == 0:
                    pl.when(k == q)(
                        lambda: pltpu.make_async_copy(src, dst, rv_r.at[p]).start()
                    )
                    pl.when(k != q)(lambda: copy().start())
                else:
                    copy().start()
    for wait in pending:
        wait()
    for p, lanes in enumerate(pairs):
        arrived(landed.at[:, :, :, lanes], rv_r.at[p])
        for c in range(2):
            for g in (2 * p, 2 * p + 1):
                total = landed[c, 0, :, g * half:(g + 1) * half].astype(F32)
                for i in range(1, LINE):
                    total = total + landed[c, i, :, g * half:(g + 1) * half].astype(F32)
                out[:, g * hid + c * half:g * hid + (c + 1) * half] = total
    for p, lanes in enumerate(pairs):
        for ref, sem in ((leaving.at[0, 0:rows, lanes], rv_s.at[p, 0]), (leaving.at[1:4, :, lanes], rv_s.at[p, 1])):
            remote(ref, ref, sem, sem, (z, s, 1 - k)).wait_send()


def on_device(frames, cotangent, first_hidden, first_cell, gate_bias, gate_weight):
    steps, _, tile_rows, cols, hid = frames.shape
    n = tile_rows * cols
    pad = n + 2 * cols
    half = hid // 2
    gates = 4 * hid
    share = 18 * hid // (lax.axis_size("space") * lax.axis_size("batch"))
    block = 2 * share
    vmem = pl.BlockSpec(memory_space=pltpu.VMEM)
    anywhere = pl.BlockSpec(memory_space=pl.ANY)
    dma = pltpu.SemaphoreType.DMA
    scratch = [
        pltpu.VMEM((2, 3, 3, hid, gates // 2), BF16),
        pltpu.VMEM((2, 3, 3, hid, gates // 2), BF16),
        pltpu.VMEM((3, 3 * gates, hid), BF16),
        pltpu.VMEM((3, 3 * gates, hid), BF16),
        pltpu.VMEM((steps, pad + 2 * cols, 3 * hid), BF16),
        pltpu.VMEM((steps, pad + 2 * cols, 3 * hid), BF16),
        pltpu.VMEM((steps, pad, 3 * gates), BF16),
        pltpu.VMEM((n, hid), BF16),
        pltpu.VMEM((pad, gates), F32),
        pltpu.VMEM((5, n, hid), F32),
        pltpu.VMEM((steps, pad, hid), F32),
        pltpu.VMEM((pad, hid), F32),
        pltpu.VMEM((steps, 6, pad, hid), F32),
        pltpu.VMEM((steps, pad, hid), BF16),
        pltpu.VMEM((steps, n, hid), BF16),
        pltpu.VMEM((pad, hid), BF16),
        pltpu.VMEM((steps, 2, 2 * LINE, pad, hid), BF16),
        pltpu.VMEM((18 * hid, n), BF16),
        pltpu.VMEM((steps, LINE, block, 2 * LINE * n), BF16),
        pltpu.VMEM((steps, 2 * LINE * n, gates // 2), BF16),
        pltpu.VMEM((steps, n, gates), BF16),
        pltpu.VMEM((steps, 2 * LINE * n, gates // 2), BF16),
        pltpu.VMEM((2, n, hid), BF16),
        pltpu.VMEM((3, 2 * LINE * n, half), BF16),
        pltpu.VMEM((LINE, block, gates // 2), F32),
        pltpu.VMEM((LINE, block, gates // 2), BF16),
        pltpu.VMEM((2, LINE, share, gates // 2), BF16),
        dma((2, 2, 4)), dma((2,)),
        dma((steps, 2, 3)), dma((steps, 2)), dma((steps, 2, 2)), dma((steps, 2)),
        dma((2,)), dma((steps, 3)), dma((2,)),
        dma((steps, 2)), dma((steps, 2)), dma((steps,)), dma((3,)), dma((2,)),
        dma((steps, 2, 2)), dma((steps, 2)), dma((2,)), dma((2,)), dma((2,)), dma((steps, 2)),
        dma((steps, 2, 3)), dma((steps, 2)), dma((2, 2)), dma((2,)), dma((steps, 3)), dma((2,)),
        dma((steps, 2)), dma((steps, 2)), dma((steps,)), dma((3,)), dma((2, 2)),
    ]
    result = pl.pallas_call(
        kernel,
        out_shape=jax.ShapeDtypeStruct((share, gates), F32),
        in_specs=[anywhere] * 4 + [vmem, anywhere],
        out_specs=vmem,
        scratch_shapes=scratch,
        compiler_params=pltpu.CompilerParams(
            collective_id=0, has_side_effects=True, vmem_limit_bytes=56 * 2**20
        ),
    )(
        frames.reshape(steps, n, hid),
        cotangent.reshape(steps, n, hid),
        first_hidden.reshape(n, hid),
        first_cell.reshape(n, hid),
        gate_bias,
        gate_weight.reshape(3, 3, 2 * hid, gates),
    )
    return result[None]


def solution(mesh):
    return jax.shard_map(
        on_device,
        mesh=mesh,
        in_specs=(
            P(None, "batch", "space", None, None),
            P(None, "batch", "space", None, None),
            P("section", "batch", "space", None, None),
            P("section", "batch", "space", None, None),
            P("section", None),
            P("section", None, None),
        ),
        out_specs=P("section", ("space", "batch"), None),
        check_vma=False,
    )
```

```python
import functools

import jax
import jax.numpy as jnp
from jax import lax
from jax.experimental import pallas as pl
from jax.experimental.pallas import tpu as pltpu
from jax.sharding import PartitionSpec as P

F32 = jnp.float32
BF16 = jnp.bfloat16
MESH = pl.DeviceIdType.MESH
LINE = 4


def dot(left, right):
    return jnp.dot(left, right, preferred_element_type=F32)


def kernel(
    frames, cotangent, first_hidden, first_cell, bias, weight, out,
    wx, wh, wxt, wht, sx, sh, sg, top_hidden, preact, gates, cells, carry, coef, gin, gx_out, ghid,
    tiles_all, flipped, turned, grads_all, packed, packed_all, vec_all, acc, leaving, landed,
    w_sem, in_sem, sx_r, sx_f, sh_r, sh_f, c_r, gx_r, gh_r, ti_r, ga_r, co_r, ve_r, rv_r,
    fr_s, fr_f, fh_s, fh_f, fc_s, ct_s, sx_s, sx_fs, sh_s, sh_fs, gx_s, gh_s, ti_s, ga_s, co_s, ve_s, vd_s, rv_s,
):
    z, s, k = lax.axis_index("section"), lax.axis_index("space"), lax.axis_index("batch")
    y, x = s // LINE, s % LINE
    sections, tiles = lax.axis_size("section"), lax.axis_size("space")
    cols = 32
    n = first_cell.shape[0]
    hid = first_cell.shape[1]
    half = hid // 2
    gate_half = 4 * half
    own2, above2, below2 = slice(2 * cols, 2 * cols + n), slice(0, 2 * cols), slice(2 * cols + n, 4 * cols + n)
    near = slice(cols, 2 * cols), slice(2 * cols + n, 3 * cols + n)
    far = slice(0, cols), slice(3 * cols + n, 4 * cols + n)
    own1, above1, below1 = slice(cols, cols + n), slice(0, cols), slice(cols + n, 2 * cols + n)
    centre = slice(hid, 2 * hid)
    top, bottom, base, roof = s == 0, s == tiles - 1, z == 0, z == sections - 1
    inner = jnp.logical_not(base)
    pending = []

    def send(pred, make):
        if pred is None:
            make().start()
            pending.append(lambda: make().wait_send())
        else:
            ask = pred if callable(pred) else lambda: pred
            pl.when(ask())(lambda: make().start())
            pending.append(lambda: pl.when(ask())(lambda: make().wait_send()))

    def remote(src, dst, send_sem, recv_sem, device):
        return pltpu.make_async_remote_copy(
            src_ref=src, dst_ref=dst, send_sem=send_sem, recv_sem=recv_sem,
            device_id=device, device_id_type=MESH,
        )

    def arrived(dst, recv_sem):
        remote(dst, dst, recv_sem, recv_sem, (z, s, 1 - k)).wait_recv()

    loads = {}
    for part, buffer in ((0, wx), (1, wh)):
        for c in range(2):
            for g in range(4):
                loads[part, c, g] = pltpu.make_async_copy(
                    weight.at[:, :, part * hid:(part + 1) * hid, pl.ds(g * hid + c * half, half)],
                    buffer.at[c, :, :, :, g * half:(g + 1) * half],
                    w_sem.at[part, c, g],
                )

    def weights_here(part):
        for c in range(2):
            for g in range(4):
                loads[part, c, g].wait()

    barrier = pltpu.get_barrier_semaphore()

    def greet(partners):
        for pred, device in partners:
            call = functools.partial(
                pl.semaphore_signal, barrier, inc=1, device_id=device, device_id_type=MESH
            )
            if pred is None:
                call()
            else:
                pl.when(pred)(call)

    def count(partners):
        total = 0
        for pred, _ in partners:
            total = total + (1 if pred is None else jnp.where(pred, 1, 0))
        return total

    plane = [(jnp.logical_not(top), (z, s - 1, k)), (jnp.logical_not(bottom), (z, s + 1, k))]
    plane.append((None, (z, s, 1 - k)))
    for d in range(1, LINE):
        for core in range(2):
            plane.append((None, (z, y * LINE + (x + d) % LINE, core)))
            plane.append((None, (z, ((y + d) % LINE) * LINE + x, core)))

    def section_at(step, ok):
        return [
            (ok, (z + step, s, k)),
            (ok & (s > 0), (z + step, s - 1, k)),
            (ok & (s < tiles - 1), (z + step, s + 1, k)),
        ]

    below, above = section_at(-1, z > 0), section_at(1, z < sections - 1)
    group = [
        (base, (z + 1, jnp.where(k == 0, y * LINE + j, j * LINE + x), core))
        for j in range(LINE) for core in range(2)
    ]
    greet(plane)

    half_lanes = [slice(hid + c * half, hid + (c + 1) * half) for c in range(2)]
    own_hidden = pltpu.make_async_copy(first_hidden, sh.at[0, own2, centre], in_sem.at[0])
    own_cell = pltpu.make_async_copy(first_cell, cells.at[0, own1], in_sem.at[1])
    own_hidden.start()

    @pl.when(base)
    def _():
        for t in range(2):
            for c in range(2):
                pltpu.make_async_copy(
                    frames.at[t, :, pl.ds(c * half, half)], sx.at[t, own2, half_lanes[c]], sx_r.at[t, c, 2]
                ).start()

    own_cell.start()

    @pl.when(roof)
    def _():
        for t in range(2):
            pltpu.make_async_copy(cotangent.at[t], gin.at[t, own1], gx_r.at[t, 2]).start()

    for part in (1, 0):
        for c in range(2):
            for g in range(4):
                loads[part, c, g].start()

    def clear(wide, narrow):
        for t in range(2):
            sx[t, wide, :] = jnp.zeros((2 * cols, 3 * hid), BF16)
            sh[t, wide, :] = jnp.zeros((2 * cols, 3 * hid), BF16)
            gin[t, narrow] = jnp.zeros((cols, hid), BF16)
        cells[0, narrow] = jnp.zeros((cols, hid), F32)
        ghid[narrow] = jnp.zeros((cols, hid), BF16)

    pl.when(top)(lambda: clear(above2, above1))
    pl.when(bottom)(lambda: clear(below2, below1))

    pl.semaphore_wait(
        barrier, count(plane) + count(below) + jnp.where(z == 1, len(group), 0)
    )

    def send_edges(src, dst, send_sems, recv_sems, section, pred):
        edges(lambda: (src, dst, send_sems, recv_sems), section, pred)

    def edges(parts, section, pred):
        def up():
            return s > 0 if pred is None else (s > 0) & pred

        def down():
            return s < tiles - 1 if pred is None else (s < tiles - 1) & pred

        def make(end, device):
            src, dst, send_sems, recv_sems = parts()
            return remote(src[end], dst[1 - end], send_sems.at[end], recv_sems.at[1 - end], device)

        send(up, lambda: make(0, (section, s - 1, k)))
        send(down, lambda: make(1, (section, s + 1, k)))

    def outer(ref, width):
        return ref.at[0:width], ref.at[n - width:n]

    def beyond(ref):
        return ref.at[cols:2 * cols], ref.at[n - 2 * cols:n - cols]

    def narrow(ref):
        return ref.at[above1], ref.at[below1]

    def at_rows(buffer, t, rows, lanes):
        return buffer.at[t, rows[0], lanes], buffer.at[t, rows[1], lanes]

    def halves(ref, c):
        return ref.at[0:cols, pl.ds(c * half, half)], ref.at[n - cols:n, pl.ds(c * half, half)]

    send_edges(outer(first_hidden, cols), at_rows(sh, 0, near, centre), fh_s, sh_r.at[0, 0], z, None)

    def send_frames(t):
        for c in range(2):
            send_edges(
                halves(frames.at[t], c), at_rows(sx, t, near, half_lanes[c]),
                fr_s.at[t, c], sx_r.at[t, c], z, base,
            )

    send_frames(0)
    greet(above)
    greet(group)
    greet(below)
    send_edges(beyond(first_hidden), at_rows(sh, 0, far, centre), fh_f, sh_f.at[0], z, None)
    send_edges(outer(first_cell, cols), narrow(cells.at[0]), fc_s, c_r, z, None)
    send_edges(beyond(frames.at[0]), at_rows(sx, 0, far, centre), fr_f.at[0], sx_f.at[0], z, base)
    send_frames(1)
    send_edges(beyond(frames.at[1]), at_rows(sx, 1, far, centre), fr_f.at[1], sx_f.at[1], z, base)
    for t in range(2):
        send_edges(outer(cotangent.at[t], cols), narrow(gin.at[t]), ct_s.at[t], gx_r.at[t], z, roof)

    def spread_value(value, width):
        count = value.shape[0]
        column = lax.broadcasted_iota(jnp.int32, (count, width), 0) % cols
        left = jnp.where(column == 0, 0.0, pltpu.roll(value, 1, 0)).astype(BF16)
        right = jnp.where(column == cols - 1, 0.0, pltpu.roll(value, count - 1, 0)).astype(BF16)
        return left, right

    def spread(buffer, t, rows, width):
        left, right = spread_value(buffer[t, rows, width:2 * width].astype(F32), width)
        buffer[t, rows, 0:width] = left
        buffer[t, rows, 2 * width:3 * width] = right

    def when_edges(first, second):
        pl.when(jnp.logical_not(top))(first)
        pl.when(jnp.logical_not(bottom))(second)

    def near_here(buffer, t, recv_sems, lanes):
        def here(index):
            for c, part in enumerate(lanes):
                arrived(buffer.at[t, near[index], part], recv_sems.at[c, index])
            spread(buffer, t, near[index], hid)

        when_edges(lambda: here(0), lambda: here(1))

    def far_here(buffer, t, recv_sems):
        def here(index):
            arrived(buffer.at[t, far[index], centre], recv_sems.at[index])
            spread(buffer, t, far[index], hid)

        when_edges(lambda: here(0), lambda: here(1))

    def narrow_here(ref, recv_sems):
        when_edges(
            lambda: arrived(ref.at[above1], recv_sems.at[0]),
            lambda: arrived(ref.at[below1], recv_sems.at[1]),
        )

    def conv(buffer, t, weights, c, offsets):
        total = None
        for a in offsets:
            term = dot(
                buffer[t, cols * (a + 1):cols * (a + 1) + n, :],
                weights[c, a].reshape(3 * hid, gate_half),
            )
            total = term if total is None else total + term
        return total

    def conv_all(buffer, t, weights, c):
        total = None
        for a in range(3):
            term = dot(
                buffer[t, cols * a:cols * (a + 2) + n, :],
                weights[c, a].reshape(3 * hid, gate_half),
            )
            total = term if total is None else total + term
        return total

    def conv_beside(t, c):
        total = None
        for buffer, weights in ((sh, wh), (sx, wx)):
            for a in range(3):
                low = cols * (a + 1) + n
                cells_in = jnp.concatenate(
                    [buffer[t, cols * a:cols * (a + 1), :], buffer[t, low:low + cols, :]], axis=0
                )
                term = dot(cells_in, weights[c, a].reshape(3 * hid, gate_half))
                total = term if total is None else total + term
        return total

    def bias_of(c):
        return jnp.concatenate(
            [bias[0:1, g * hid + c * half:g * hid + (c + 1) * half] for g in range(4)], axis=1
        )

    def activate(now, old):
        i_gate = jax.nn.sigmoid(now[:, 0:half])
        f_gate = jax.nn.sigmoid(now[:, half:2 * half])
        o_gate = jax.nn.sigmoid(now[:, 2 * half:3 * half])
        cand = jnp.tanh(now[:, 3 * half:])
        new = f_gate * old + i_gate * cand
        return i_gate, f_gate, o_gate, cand, new, jnp.tanh(new)

    def factors(i_gate, f_gate, o_gate, cand, squash, old):
        return (
            o_gate * (1.0 - squash * squash),
            cand * i_gate * (1.0 - i_gate),
            old * f_gate * (1.0 - f_gate),
            squash * o_gate * (1.0 - o_gate),
            i_gate * (1.0 - cand * cand),
            f_gate,
        )

    def turn_weights(source, target):
        def one(a, carried):
            for b in range(3):
                for c in range(2):
                    start = (2 - b) * 4 * hid + c * gate_half
                    target[a, start:start + gate_half, :] = source[c, a, b].T
            return carried

        lax.fori_loop(0, 3, one, 0)

    def turn_all_weights():
        turn_weights(wh, wht)
        pl.when(inner)(lambda: turn_weights(wx, wxt))

    def spread_to_group(pred, view, seven, send_sem, recv_sem):
        def go():
            for d in (2, 1, 3, 0):
                for c in range(2):
                    there = ((x if c == 0 else y) + d) % LINE
                    chip = y * LINE + there if c == 0 else there * LINE + x
                    src, dst = view(c, 2 * (x if c == 0 else y) + k)
                    copy = functools.partial(remote, src, dst, send_sem(), recv_sem(), (z, chip, c))
                    if d == 0:
                        pl.when(k == c)(lambda: pltpu.make_async_copy(src, dst, recv_sem()).start())
                        pl.when(k != c)(lambda: copy().start())
                    else:
                        copy().start()

        def done():
            remote(seven(), seven(), send_sem(), recv_sem(), (z, s, 1 - k)).wait_send()

        pl.when(pred)(go)
        pending.append(lambda: pl.when(pred)(done))

    def rows_of(slot):
        return pl.ds(pl.multiple_of(slot * n, n), n)

    most = slice(0, 7 * n)

    def send_tile(t, part, pred):
        spread_to_group(
            pred,
            lambda c, slot: (
                (sh if part else sx).at[t, cols:3 * cols + n, centre], tiles_all.at[t, part, slot]
            ),
            lambda: tiles_all.at[t, part, 0:7],
            lambda: ti_s.at[t, part], lambda: ti_r.at[t, part],
        )

    pairs = [slice(p * 2 * half, (p + 1) * 2 * half) for p in range(2)]

    def send_grads(t, p, pred):
        lanes = pairs[p]

        def view(c, slot):
            at = 4 * hid + c * gate_half
            src = sg.at[t, own1, at + lanes.start:at + lanes.stop]
            return src, grads_all.at[t, rows_of(slot), lanes]

        spread_to_group(
            pred, view, lambda: grads_all.at[t, most, lanes],
            lambda: ga_s.at[t, p], lambda: ga_r.at[t, p],
        )

    early = z < 2

    def send_factors(t):
        def view(c, slot):
            src = packed.at[t, :, c * 5 * half:(c + 1) * 5 * half]
            return src, packed_all.at[t, rows_of(slot), :]

        spread_to_group(
            early, view, lambda: packed_all.at[t, most], lambda: co_s.at[t], lambda: co_r.at[t]
        )

    def pack_factors():
        for c in range(2):
            chan = slice(c * half, (c + 1) * half)
            for t in range(2):
                first = coef[t, 0, own1, chan]
                for g in range(5):
                    if g == 4:
                        value = first * coef[t, 5, own1, chan] if t == 1 else first
                    else:
                        value = coef[t, 1 + g, own1, chan]
                        if t == 1 and g != 2:
                            value = value * first
                    at = (c * 5 + g) * half
                    packed[t, :, at:at + half] = value.astype(BF16)

    def send_vec(index, pred):
        def view(c, slot):
            chan = slice(c * half, (c + 1) * half)
            src = ghid.at[own1, chan] if index == 2 else gin.at[1 - index, own1, chan]
            return src, vec_all.at[index, rows_of(slot), :]

        spread_to_group(
            pred, view, lambda: vec_all.at[index, most], lambda: ve_s.at[index], lambda: ve_r.at[index]
        )

    def send_down():
        def go():
            for d in (2, 1, 3, 0):
                for c in range(2):
                    there = ((x if c == 0 else y) + d) % LINE
                    chip = y * LINE + there if c == 0 else there * LINE + x
                    remote(
                        gx_out.at[0, :, c * half:(c + 1) * half],
                        vec_all.at[1, rows_of(2 * (x if c == 0 else y) + k), :],
                        vd_s.at[0], ve_r.at[1], (z - 1, chip, c),
                    ).start()

        def done():
            remote(vec_all.at[1], vec_all.at[1], vd_s.at[0], ve_r.at[1], (z, s, 1 - k)).wait_send()

        pl.when(z == 1)(go)
        pending.append(lambda: pl.when(z == 1)(done))

    rows = out.shape[0]
    block = 2 * rows
    me = jnp.where(k == 0, y, x)

    def turn_patches():
        for t in range(2):
            for part in range(2):
                arrived(tiles_all.at[t, part], ti_r.at[t, part])

            def one(slot, carried):
                for part in range(2):
                    tile = tiles_all[t, part, slot]
                    left, right = spread_value(tile.astype(F32), hid)
                    for b, moved in enumerate((left, tile, right)):
                        for a in range(3):
                            at = (a * 3 + b) * 2 * hid + part * hid
                            flipped[at:at + hid, :] = moved[cols * a:cols * a + n, :].T
                for j in range(LINE):
                    chip = jnp.where(k == 0, j * LINE + x, y * LINE + j)
                    turned[t, j, :, pl.ds(pl.multiple_of(slot * n, n), n)] = flipped[
                        pl.ds(pl.multiple_of(chip * block, 32), block), :
                    ]
                return carried

            lax.fori_loop(0, 2 * LINE, one, 0)

    @pl.when(z >= 2)
    def _():
        weights_here(1)
        weights_here(0)
        turn_all_weights()

    not_roof = jnp.logical_not(roof)
    z_up = z + 1

    def save(t, into, values, old, chan):
        i_gate, f_gate, o_gate, cand, squash = values
        for index, value in enumerate(factors(i_gate, f_gate, o_gate, cand, squash, old)):
            for cells_to, cells_from in into:
                coef[t, index, cells_to, chan] = value[cells_from]

    def x_here(t):
        for c in range(2):
            arrived(sx.at[t, own2, half_lanes[c]], sx_r.at[t, c, 2])
        spread(sx, t, own2, hid)

    def add(c, term):
        preact[0:n, c * gate_half:(c + 1) * gate_half] += term

    def own_rows(t):
        hidden_lanes = (centre,) if t == 0 else half_lanes
        part_sums = [conv(sh, t, wh, c, (1,)) + bias_of(c) for c in range(2)]
        for c in range(2):
            preact[0:n, c * gate_half:(c + 1) * gate_half] = part_sums[c]

        def x_middle():
            x_here(t)
            for c in range(2):
                add(c, conv(sx, t, wx, c, (1,)))

        def x_edges():
            near_here(sx, t, sx_r.at[t], half_lanes)

        def h_edges():
            near_here(sh, t, sh_r.at[t], hidden_lanes)

        def h_outer():
            for c in range(2):
                add(c, conv(sh, t, wh, c, (0, 2)))

        @pl.when(base)
        def _():
            if t == 0:
                weights_here(0)
            x_middle()
            if t == 1:
                x_edges()
                for c in range(2):
                    add(c, conv(sx, t, wx, c, (0, 2)))
                h_edges()

        if t == 0:
            h_edges()
            h_outer()
            send_tile(0, 1, inner)
            pl.when(z == 1)(lambda: weights_here(0))

        @pl.when(inner)
        def _():
            if t == 1:
                h_edges()
                h_outer()
            x_middle()
            if t == 1:
                x_edges()

        if t == 0:
            x_edges()
            own_cell.wait()
            pl.when(not_roof)(lambda: pl.semaphore_wait(barrier, count(above)))

        def finish(buffer, weights, c):
            chan, lanes = slice(c * half, (c + 1) * half), half_lanes[c]
            now = preact[0:n, c * gate_half:(c + 1) * gate_half] + conv(buffer, t, weights, c, (0, 2))
            i_gate, f_gate, o_gate, cand, new, squash = activate(now, cells[t, own1, chan])
            hidden = (o_gate * squash).astype(BF16)
            if t == 0:
                sh[1, own2, lanes] = hidden
                cells[1, own1, chan] = new
            else:
                top_hidden[:, chan] = hidden
            for index, value in enumerate((i_gate, f_gate, o_gate, cand, squash)):
                gates[index, :, chan] = value

        for c in range(2):
            chan, lanes = slice(c * half, (c + 1) * half), half_lanes[c]
            if t == 0:
                finish(sx, wx, c)
                whole = sh.at[1, own2, lanes]
                ends = sh.at[1, 2 * cols:3 * cols, lanes], sh.at[1, n + cols:n + 2 * cols, lanes]
            else:
                pl.when(base)(lambda c=c: finish(sh, wh, c))
                pl.when(inner)(lambda c=c: finish(sx, wx, c))
                whole = top_hidden.at[:, chan]
                ends = top_hidden.at[0:cols, chan], top_hidden.at[n - cols:n, chan]
            send(
                not_roof,
                lambda whole=whole, lanes=lanes, c=c: remote(
                    whole, sx.at[t, own2, lanes], sx_s.at[t, c, 2], sx_r.at[t, c, 2], (z_up, s, k)
                ),
            )
            if t == 0:
                send_edges(ends, at_rows(sh, 1, near, lanes), sh_s.at[c], sh_r.at[1, c], z, None)
            edges(
                lambda ends=ends, lanes=lanes, c=c: (
                    ends, at_rows(sx, t, near, lanes), sx_s.at[t, c], sx_r.at[t, c]
                ),
                z_up, not_roof,
            )
        if t == 0:
            ends = sh.at[1, 3 * cols:4 * cols, centre], sh.at[1, n:n + cols, centre]
            send_edges(ends, at_rows(sh, 1, far, centre), sh_fs, sh_f.at[1], z, None)
        else:
            ends = beyond(top_hidden)
        last = ends
        edges(
            lambda: (last, at_rows(sx, t, far, centre), sx_fs.at[t], sx_f.at[t]), z_up, not_roof
        )
        for c in range(2):
            chan = slice(c * half, (c + 1) * half)
            save(
                t, ((own1, slice(0, n)),),
                tuple(gates[index, :, chan] for index in range(5)), cells[t, own1, chan], chan,
            )

    def beside_rows(t):
        if t == 0:
            narrow_here(cells.at[0], c_r)
        far_here(sh, t, sh_f.at[t])
        far_here(sx, t, sx_f.at[t])
        for c in range(2):
            chan = slice(c * half, (c + 1) * half)
            old = jnp.concatenate([cells[t, above1, chan], cells[t, below1, chan]], axis=0)
            i_gate, f_gate, o_gate, cand, new, squash = activate(conv_beside(t, c) + bias_of(c), old)
            if t == 0:
                cells[1, above1, chan] = new[0:cols]
                cells[1, below1, chan] = new[cols:]
            save(
                t, ((above1, slice(0, cols)), (below1, slice(cols, 2 * cols))),
                (i_gate, f_gate, o_gate, cand, squash), old, chan,
            )

    def all_rows():
        far_here(sh, 1, sh_f.at[1])
        for c in range(2):
            preact[:, c * gate_half:(c + 1) * gate_half] = conv_all(sh, 1, wh, c) + bias_of(c)
        x_here(1)
        near_here(sx, 1, sx_r.at[1], half_lanes)
        far_here(sx, 1, sx_f.at[1])
        for c in range(2):
            chan = slice(c * half, (c + 1) * half)
            now = preact[:, c * gate_half:(c + 1) * gate_half] + conv_all(sx, 1, wx, c)
            old = cells[1, :, chan]
            i_gate, f_gate, o_gate, cand, new, squash = activate(now, old)
            save(
                1, ((slice(0, n + 2 * cols), slice(0, n + 2 * cols)),),
                (i_gate, f_gate, o_gate, cand, squash), old, chan,
            )

    own_hidden.wait()
    spread(sh, 0, own2, hid)
    pl.when(z < 2)(lambda: weights_here(1))
    own_rows(0)
    send_tile(0, 0, inner)
    spread(sh, 1, own2, hid)

    @pl.when(not_roof)
    def _():
        own_rows(1)
        beside_rows(0)
        beside_rows(1)

    @pl.when(roof)
    def _():
        beside_rows(0)
        near_here(sh, 1, sh_r.at[1], half_lanes)

    send_tile(1, 1, roof)
    pl.when(roof)(all_rows)

    def blank(outside):
        coef[:, :, outside, :] = jnp.zeros((2, 6, cols, hid), F32)

    pl.when(top)(lambda: blank(above1))
    pl.when(bottom)(lambda: blank(below1))

    pl.when(z < 2)(turn_all_weights)
    pl.when(early)(pack_factors)
    send_tile(0, 1, base)
    send_tile(0, 0, base)
    send_tile(1, 1, not_roof)
    send_tile(1, 0, not_roof)
    send_factors(1)
    send_factors(0)
    pl.when(z < 2)(turn_patches)

    def back_conv(t, weights):
        total = None
        for a in range(3):
            term = dot(sg[t, cols * (2 - a):cols * (2 - a) + n, :], weights[a])
            total = term if total is None else total + term
        return total.astype(BF16)

    def gate_grads(t):
        for c in range(2):
            chan = slice(c * half, (c + 1) * half)
            grad_h = gin[t, :, chan].astype(F32)
            if t == 0:
                grad_h = grad_h + ghid[:, chan].astype(F32)
            grad_c = grad_h * coef[t, 0, :, chan]
            if t == 0:
                grad_c = grad_c + carry[:, chan]
            for g, value in enumerate((
                grad_c * coef[t, 1, :, chan],
                grad_c * coef[t, 2, :, chan],
                grad_h * coef[t, 3, :, chan],
                grad_c * coef[t, 4, :, chan],
            )):
                at = 4 * hid + c * gate_half + g * half
                sg[t, :, at:at + half] = value.astype(BF16)
            if t == 1:
                carry[:, chan] = grad_c * coef[t, 5, :, chan]
        spread(sg, t, slice(0, 2 * cols + n), 4 * hid)

    def send_input_grad(t, pred):
        send(
            pred,
            lambda: remote(gx_out.at[t], gin.at[t, own1], gx_s.at[t, 2], gx_r.at[t, 2], (z - 1, s, k)),
        )
        send_edges(outer(gx_out.at[t], cols), narrow(gin.at[t]), gx_s.at[t], gx_r.at[t], z - 1, pred)

    arrived(gin.at[1, own1], gx_r.at[1, 2])
    send_vec(0, base)
    narrow_here(gin.at[1], gx_r.at[1])
    gate_grads(1)

    @pl.when(inner)
    def _():
        gx_out[1] = back_conv(1, wxt)

    send_input_grad(1, inner)
    ghid[own1] = back_conv(1, wht)
    send_edges((ghid.at[cols:2 * cols], ghid.at[n:n + cols]), narrow(ghid), gh_s, gh_r, z, inner)
    send_vec(0, z == 1)
    send_vec(2, early)
    send_tile(1, 0, roof)
    send_grads(1, 0, z == 2)

    pl.when(inner)(lambda: arrived(gin.at[0, own1], gx_r.at[0, 2]))
    send_vec(1, z == 1)

    @pl.when(inner)
    def _():
        narrow_here(gin.at[0], gx_r.at[0])
        narrow_here(ghid, gh_r)
        gate_grads(0)
        gx_out[0] = back_conv(0, wxt)

    send_down()
    send_input_grad(0, z >= 2)
    send_grads(1, 0, roof)
    send_grads(1, 1, z >= 2)
    send_grads(0, 0, z >= 2)
    send_grads(0, 1, z >= 2)

    pl.when(z >= 2)(turn_patches)

    def grads_here(t, p, lanes):
        arrived(grads_all.at[t, :, lanes], ga_r.at[t, p])

    def vec_here(index):
        arrived(vec_all.at[index], ve_r.at[index])

    def factors_here(t):
        arrived(packed_all.at[t], co_r.at[t])

    def factor(t, g):
        return packed_all[t, :, g * half:(g + 1) * half].astype(F32)

    def put(t, g, value):
        grads_all[t, :, g * half:(g + 1) * half] = (factor(t, g) * value).astype(BF16)

    @pl.when(early)
    def _():
        factors_here(1)
        factors_here(0)
        vec_here(0)
        for g in range(4):
            put(1, g, vec_all[0].astype(F32))

    @pl.when(z >= 2)
    def _():
        grads_here(1, 0, pairs[0])
        grads_here(1, 1, pairs[1])

    for j in range(LINE):
        acc[j] = dot(turned[1, j], grads_all[1])
    for p, lanes in enumerate(pairs):
        @pl.when(early)
        def _():
            if p == 0:
                vec_here(2)
                vec_here(1)
            grad_h = vec_all[1].astype(F32) + vec_all[2].astype(F32)
            grad_c = vec_all[0].astype(F32) * factor(1, 4) + grad_h * factor(0, 4)
            put(0, 2 * p, grad_h if p else grad_c)
            put(0, 2 * p + 1, grad_c)

        pl.when(z >= 2)(lambda: grads_here(0, p, lanes))
        for d in (2, 1, 3, 0):
            j = (me + d) % LINE
            leaving[d, :, lanes] = (
                acc[j, :, lanes] + dot(turned[0, j], grads_all[0, :, lanes])
            ).astype(BF16)
            chip = jnp.where(k == 0, j * LINE + x, y * LINE + j)
            for q in range(2):
                src, dst = leaving.at[d, q * rows:(q + 1) * rows, lanes], landed.at[k, me, :, lanes]
                copy = functools.partial(
                    remote, src, dst, rv_s.at[p, min(d, 1)], rv_r.at[p], (z, chip, q)
                )
                if d == 0:
                    pl.when(k == q)(
                        lambda: pltpu.make_async_copy(src, dst, rv_r.at[p]).start()
                    )
                    pl.when(k != q)(lambda: copy().start())
                else:
                    copy().start()
    for wait in pending:
        wait()
    for p, lanes in enumerate(pairs):
        arrived(landed.at[:, :, :, lanes], rv_r.at[p])
        for c in range(2):
            for g in (2 * p, 2 * p + 1):
                total = landed[c, 0, :, g * half:(g + 1) * half].astype(F32)
                for i in range(1, LINE):
                    total = total + landed[c, i, :, g * half:(g + 1) * half].astype(F32)
                out[:, g * hid + c * half:g * hid + (c + 1) * half] = total
    for p, lanes in enumerate(pairs):
        for ref, sem in ((leaving.at[0, 0:rows, lanes], rv_s.at[p, 0]), (leaving.at[1:4, :, lanes], rv_s.at[p, 1])):
            remote(ref, ref, sem, sem, (z, s, 1 - k)).wait_send()


def on_device(frames, cotangent, first_hidden, first_cell, gate_bias, gate_weight):
    steps, _, tile_rows, cols, hid = frames.shape
    n = tile_rows * cols
    pad = n + 2 * cols
    half = hid // 2
    gates = 4 * hid
    share = 18 * hid // (lax.axis_size("space") * lax.axis_size("batch"))
    block = 2 * share
    vmem = pl.BlockSpec(memory_space=pltpu.VMEM)
    anywhere = pl.BlockSpec(memory_space=pl.ANY)
    dma = pltpu.SemaphoreType.DMA
    scratch = [
        pltpu.VMEM((2, 3, 3, hid, gates // 2), BF16),
        pltpu.VMEM((2, 3, 3, hid, gates // 2), BF16),
        pltpu.VMEM((3, 3 * gates, hid), BF16),
        pltpu.VMEM((3, 3 * gates, hid), BF16),
        pltpu.VMEM((steps, pad + 2 * cols, 3 * hid), BF16),
        pltpu.VMEM((steps, pad + 2 * cols, 3 * hid), BF16),
        pltpu.VMEM((steps, pad, 3 * gates), BF16),
        pltpu.VMEM((n, hid), BF16),
        pltpu.VMEM((pad, gates), F32),
        pltpu.VMEM((5, n, hid), F32),
        pltpu.VMEM((steps, pad, hid), F32),
        pltpu.VMEM((pad, hid), F32),
        pltpu.VMEM((steps, 6, pad, hid), F32),
        pltpu.VMEM((steps, pad, hid), BF16),
        pltpu.VMEM((steps, n, hid), BF16),
        pltpu.VMEM((pad, hid), BF16),
        pltpu.VMEM((steps, 2, 2 * LINE, pad, hid), BF16),
        pltpu.VMEM((18 * hid, n), BF16),
        pltpu.VMEM((steps, LINE, block, 2 * LINE * n), BF16),
        pltpu.VMEM((steps, 2 * LINE * n, gates // 2), BF16),
        pltpu.VMEM((steps, n, 5 * hid), BF16),
        pltpu.VMEM((steps, 2 * LINE * n, 5 * half), BF16),
        pltpu.VMEM((3, 2 * LINE * n, half), BF16),
        pltpu.VMEM((LINE, block, gates // 2), F32),
        pltpu.VMEM((LINE, block, gates // 2), BF16),
        pltpu.VMEM((2, LINE, share, gates // 2), BF16),
        dma((2, 2, 4)), dma((2,)),
        dma((steps, 2, 3)), dma((steps, 2)), dma((steps, 2, 2)), dma((steps, 2)),
        dma((2,)), dma((steps, 3)), dma((2,)),
        dma((steps, 2)), dma((steps, 2)), dma((steps,)), dma((3,)), dma((2,)),
        dma((steps, 2, 2)), dma((steps, 2)), dma((2,)), dma((2,)), dma((2,)), dma((steps, 2)),
        dma((steps, 2, 3)), dma((steps, 2)), dma((2, 2)), dma((2,)), dma((steps, 3)), dma((2,)),
        dma((steps, 2)), dma((steps, 2)), dma((steps,)), dma((3,)), dma((1,)), dma((2, 2)),
    ]
    result = pl.pallas_call(
        kernel,
        out_shape=jax.ShapeDtypeStruct((share, gates), F32),
        in_specs=[anywhere] * 4 + [vmem, anywhere],
        out_specs=vmem,
        scratch_shapes=scratch,
        compiler_params=pltpu.CompilerParams(
            collective_id=0, has_side_effects=True, vmem_limit_bytes=56 * 2**20
        ),
    )(
        frames.reshape(steps, n, hid),
        cotangent.reshape(steps, n, hid),
        first_hidden.reshape(n, hid),
        first_cell.reshape(n, hid),
        gate_bias,
        gate_weight.reshape(3, 3, 2 * hid, gates),
    )
    return result[None]


def solution(mesh):
    return jax.shard_map(
        on_device,
        mesh=mesh,
        in_specs=(
            P(None, "batch", "space", None, None),
            P(None, "batch", "space", None, None),
            P("section", "batch", "space", None, None),
            P("section", "batch", "space", None, None),
            P("section", None),
            P("section", None, None),
        ),
        out_specs=P("section", ("space", "batch"), None),
        check_vma=False,
    )
```

```python
import functools

import jax
import jax.numpy as jnp
from jax import lax
from jax.experimental import pallas as pl
from jax.experimental.pallas import tpu as pltpu
from jax.sharding import PartitionSpec as P

F32 = jnp.float32
BF16 = jnp.bfloat16
MESH = pl.DeviceIdType.MESH
LINE = 4


def dot(left, right):
    return jnp.dot(left, right, preferred_element_type=F32)


def kernel(
    frames, cotangent, first_hidden, first_cell, bias, weight, out,
    wx, wh, wxt, wht, sx, sh, sg, top_hidden, preact, gates, cells, carry, coef, gin, gx_out, ghid,
    tiles_all, flipped, turned, grads_all, packed, packed_all, vec_all, acc, leaving, landed, result,
    w_sem, in_sem, sx_r, sx_f, sh_r, sh_f, c_r, gx_r, gh_r, ti_r, ga_r, co_r, ve_r, rv_r,
    fr_s, fr_f, fh_s, fh_f, fc_s, ct_s, sx_s, sx_fs, sh_s, sh_fs, gx_s, gh_s, ti_s, ga_s, co_s, ve_s, vd_s, rv_s, out_sem,
):
    z, s, k = lax.axis_index("section"), lax.axis_index("space"), lax.axis_index("batch")
    y, x = s // LINE, s % LINE
    sections, tiles = lax.axis_size("section"), lax.axis_size("space")
    cols = 32
    n = first_cell.shape[0]
    hid = first_cell.shape[1]
    half = hid // 2
    gate_half = 4 * half
    own2, above2, below2 = slice(2 * cols, 2 * cols + n), slice(0, 2 * cols), slice(2 * cols + n, 4 * cols + n)
    near = slice(cols, 2 * cols), slice(2 * cols + n, 3 * cols + n)
    far = slice(0, cols), slice(3 * cols + n, 4 * cols + n)
    own1, above1, below1 = slice(cols, cols + n), slice(0, cols), slice(cols + n, 2 * cols + n)
    centre = slice(hid, 2 * hid)
    top, bottom, base, roof = s == 0, s == tiles - 1, z == 0, z == sections - 1
    inner = jnp.logical_not(base)
    pending = []

    def send(pred, make):
        if pred is None:
            make().start()
            pending.append(lambda: make().wait_send())
        else:
            ask = pred if callable(pred) else lambda: pred
            pl.when(ask())(lambda: make().start())
            pending.append(lambda: pl.when(ask())(lambda: make().wait_send()))

    def remote(src, dst, send_sem, recv_sem, device):
        return pltpu.make_async_remote_copy(
            src_ref=src, dst_ref=dst, send_sem=send_sem, recv_sem=recv_sem,
            device_id=device, device_id_type=MESH,
        )

    def arrived(dst, recv_sem):
        remote(dst, dst, recv_sem, recv_sem, (z, s, 1 - k)).wait_recv()

    loads = {}
    for part, buffer in ((0, wx), (1, wh)):
        for c in range(2):
            for g in range(4):
                loads[part, c, g] = pltpu.make_async_copy(
                    weight.at[:, :, part * hid:(part + 1) * hid, pl.ds(g * hid + c * half, half)],
                    buffer.at[c, :, :, :, g * half:(g + 1) * half],
                    w_sem.at[part, c, g],
                )

    def weights_here(part):
        for c in range(2):
            for g in range(4):
                loads[part, c, g].wait()

    barrier = pltpu.get_barrier_semaphore()

    def greet(partners):
        for pred, device in partners:
            call = functools.partial(
                pl.semaphore_signal, barrier, inc=1, device_id=device, device_id_type=MESH
            )
            if pred is None:
                call()
            else:
                pl.when(pred)(call)

    def count(partners):
        total = 0
        for pred, _ in partners:
            total = total + (1 if pred is None else jnp.where(pred, 1, 0))
        return total

    plane = [(jnp.logical_not(top), (z, s - 1, k)), (jnp.logical_not(bottom), (z, s + 1, k))]
    plane.append((None, (z, s, 1 - k)))
    for d in range(1, LINE):
        for core in range(2):
            plane.append((None, (z, y * LINE + (x + d) % LINE, core)))
            plane.append((None, (z, ((y + d) % LINE) * LINE + x, core)))

    def section_at(step, ok):
        return [
            (ok, (z + step, s, k)),
            (ok & (s > 0), (z + step, s - 1, k)),
            (ok & (s < tiles - 1), (z + step, s + 1, k)),
        ]

    below, above = section_at(-1, z > 0), section_at(1, z < sections - 1)
    group = [
        (base, (z + 1, jnp.where(k == 0, y * LINE + j, j * LINE + x), core))
        for j in range(LINE) for core in range(2)
    ]
    greet(plane)

    half_lanes = [slice(hid + c * half, hid + (c + 1) * half) for c in range(2)]
    own_hidden = pltpu.make_async_copy(first_hidden, sh.at[0, own2, centre], in_sem.at[0])
    own_cell = pltpu.make_async_copy(first_cell, cells.at[0, own1], in_sem.at[1])
    own_hidden.start()

    @pl.when(base)
    def _():
        for t in range(2):
            for c in range(2):
                pltpu.make_async_copy(
                    frames.at[t, :, pl.ds(c * half, half)], sx.at[t, own2, half_lanes[c]], sx_r.at[t, c, 2]
                ).start()

    own_cell.start()

    @pl.when(roof)
    def _():
        for t in range(2):
            pltpu.make_async_copy(cotangent.at[t], gin.at[t, own1], gx_r.at[t, 2]).start()

    for part in (1, 0):
        for c in range(2):
            for g in range(4):
                loads[part, c, g].start()

    def clear(wide, narrow):
        for t in range(2):
            sx[t, wide, :] = jnp.zeros((2 * cols, 3 * hid), BF16)
            sh[t, wide, :] = jnp.zeros((2 * cols, 3 * hid), BF16)
            gin[t, narrow] = jnp.zeros((cols, hid), BF16)
        cells[0, narrow] = jnp.zeros((cols, hid), F32)
        ghid[narrow] = jnp.zeros((cols, hid), BF16)

    pl.when(top)(lambda: clear(above2, above1))
    pl.when(bottom)(lambda: clear(below2, below1))

    pl.semaphore_wait(
        barrier, count(plane) + count(below) + jnp.where(z == 1, len(group), 0)
    )

    def send_edges(src, dst, send_sems, recv_sems, section, pred):
        edges(lambda: (src, dst, send_sems, recv_sems), section, pred)

    def edges(parts, section, pred):
        def up():
            return s > 0 if pred is None else (s > 0) & pred

        def down():
            return s < tiles - 1 if pred is None else (s < tiles - 1) & pred

        def make(end, device):
            src, dst, send_sems, recv_sems = parts()
            return remote(src[end], dst[1 - end], send_sems.at[end], recv_sems.at[1 - end], device)

        send(up, lambda: make(0, (section, s - 1, k)))
        send(down, lambda: make(1, (section, s + 1, k)))

    def outer(ref, width):
        return ref.at[0:width], ref.at[n - width:n]

    def beyond(ref):
        return ref.at[cols:2 * cols], ref.at[n - 2 * cols:n - cols]

    def narrow(ref):
        return ref.at[above1], ref.at[below1]

    def at_rows(buffer, t, rows, lanes):
        return buffer.at[t, rows[0], lanes], buffer.at[t, rows[1], lanes]

    def halves(ref, c):
        return ref.at[0:cols, pl.ds(c * half, half)], ref.at[n - cols:n, pl.ds(c * half, half)]

    send_edges(outer(first_hidden, cols), at_rows(sh, 0, near, centre), fh_s, sh_r.at[0, 0], z, None)

    def send_frames(t):
        for c in range(2):
            send_edges(
                halves(frames.at[t], c), at_rows(sx, t, near, half_lanes[c]),
                fr_s.at[t, c], sx_r.at[t, c], z, base,
            )

    send_frames(0)
    greet(above)
    greet(group)
    greet(below)
    send_edges(beyond(first_hidden), at_rows(sh, 0, far, centre), fh_f, sh_f.at[0], z, None)
    send_edges(outer(first_cell, cols), narrow(cells.at[0]), fc_s, c_r, z, None)
    send_edges(beyond(frames.at[0]), at_rows(sx, 0, far, centre), fr_f.at[0], sx_f.at[0], z, base)
    send_frames(1)
    send_edges(beyond(frames.at[1]), at_rows(sx, 1, far, centre), fr_f.at[1], sx_f.at[1], z, base)
    for t in range(2):
        send_edges(outer(cotangent.at[t], cols), narrow(gin.at[t]), ct_s.at[t], gx_r.at[t], z, roof)

    def spread_value(value, width):
        count = value.shape[0]
        column = lax.broadcasted_iota(jnp.int32, (count, width), 0) % cols
        left = jnp.where(column == 0, 0.0, pltpu.roll(value, 1, 0)).astype(BF16)
        right = jnp.where(column == cols - 1, 0.0, pltpu.roll(value, count - 1, 0)).astype(BF16)
        return left, right

    def spread(buffer, t, rows, width):
        left, right = spread_value(buffer[t, rows, width:2 * width].astype(F32), width)
        buffer[t, rows, 0:width] = left
        buffer[t, rows, 2 * width:3 * width] = right

    def when_edges(first, second):
        pl.when(jnp.logical_not(top))(first)
        pl.when(jnp.logical_not(bottom))(second)

    def near_here(buffer, t, recv_sems, lanes):
        def here(index):
            for c, part in enumerate(lanes):
                arrived(buffer.at[t, near[index], part], recv_sems.at[c, index])
            spread(buffer, t, near[index], hid)

        when_edges(lambda: here(0), lambda: here(1))

    def far_here(buffer, t, recv_sems):
        def here(index):
            arrived(buffer.at[t, far[index], centre], recv_sems.at[index])
            spread(buffer, t, far[index], hid)

        when_edges(lambda: here(0), lambda: here(1))

    def narrow_here(ref, recv_sems):
        when_edges(
            lambda: arrived(ref.at[above1], recv_sems.at[0]),
            lambda: arrived(ref.at[below1], recv_sems.at[1]),
        )

    def conv(buffer, t, weights, c, offsets):
        total = None
        for a in offsets:
            term = dot(
                buffer[t, cols * (a + 1):cols * (a + 1) + n, :],
                weights[c, a].reshape(3 * hid, gate_half),
            )
            total = term if total is None else total + term
        return total

    def conv_all(buffer, t, weights, c):
        total = None
        for a in range(3):
            term = dot(
                buffer[t, cols * a:cols * (a + 2) + n, :],
                weights[c, a].reshape(3 * hid, gate_half),
            )
            total = term if total is None else total + term
        return total

    def conv_beside(t, c):
        total = None
        for buffer, weights in ((sh, wh), (sx, wx)):
            for a in range(3):
                low = cols * (a + 1) + n
                cells_in = jnp.concatenate(
                    [buffer[t, cols * a:cols * (a + 1), :], buffer[t, low:low + cols, :]], axis=0
                )
                term = dot(cells_in, weights[c, a].reshape(3 * hid, gate_half))
                total = term if total is None else total + term
        return total

    def bias_of(c):
        return jnp.concatenate(
            [bias[0:1, g * hid + c * half:g * hid + (c + 1) * half] for g in range(4)], axis=1
        )

    def activate(now, old):
        i_gate = jax.nn.sigmoid(now[:, 0:half])
        f_gate = jax.nn.sigmoid(now[:, half:2 * half])
        o_gate = jax.nn.sigmoid(now[:, 2 * half:3 * half])
        cand = jnp.tanh(now[:, 3 * half:])
        new = f_gate * old + i_gate * cand
        return i_gate, f_gate, o_gate, cand, new, jnp.tanh(new)

    def factors(i_gate, f_gate, o_gate, cand, squash, old):
        return (
            o_gate * (1.0 - squash * squash),
            cand * i_gate * (1.0 - i_gate),
            old * f_gate * (1.0 - f_gate),
            squash * o_gate * (1.0 - o_gate),
            i_gate * (1.0 - cand * cand),
            f_gate,
        )

    def turn_weights(source, target):
        def one(a, carried):
            for b in range(3):
                for c in range(2):
                    start = (2 - b) * 4 * hid + c * gate_half
                    target[a, start:start + gate_half, :] = source[c, a, b].T
            return carried

        lax.fori_loop(0, 3, one, 0)

    def turn_all_weights():
        turn_weights(wh, wht)
        pl.when(inner)(lambda: turn_weights(wx, wxt))

    def spread_to_group(pred, view, seven, send_sem, recv_sem):
        def go():
            for d in (2, 1, 3, 0):
                for c in range(2):
                    there = ((x if c == 0 else y) + d) % LINE
                    chip = y * LINE + there if c == 0 else there * LINE + x
                    src, dst = view(c, 2 * (x if c == 0 else y) + k)
                    copy = functools.partial(remote, src, dst, send_sem(), recv_sem(), (z, chip, c))
                    if d == 0:
                        pl.when(k == c)(lambda: pltpu.make_async_copy(src, dst, recv_sem()).start())
                        pl.when(k != c)(lambda: copy().start())
                    else:
                        copy().start()

        def done():
            remote(seven(), seven(), send_sem(), recv_sem(), (z, s, 1 - k)).wait_send()

        pl.when(pred)(go)
        pending.append(lambda: pl.when(pred)(done))

    def rows_of(slot):
        return pl.ds(pl.multiple_of(slot * n, n), n)

    most = slice(0, 7 * n)

    def send_tile(t, part, pred):
        spread_to_group(
            pred,
            lambda c, slot: (
                (sh if part else sx).at[t, cols:3 * cols + n, centre], tiles_all.at[t, part, slot]
            ),
            lambda: tiles_all.at[t, part, 0:7],
            lambda: ti_s.at[t, part], lambda: ti_r.at[t, part],
        )

    pairs = [slice(p * 2 * half, (p + 1) * 2 * half) for p in range(2)]

    def send_grads(t, p, pred):
        lanes = pairs[p]

        def view(c, slot):
            at = 4 * hid + c * gate_half
            src = sg.at[t, own1, at + lanes.start:at + lanes.stop]
            return src, grads_all.at[t, rows_of(slot), lanes]

        spread_to_group(
            pred, view, lambda: grads_all.at[t, most, lanes],
            lambda: ga_s.at[t, p], lambda: ga_r.at[t, p],
        )

    early = z < 2

    def send_factors(t):
        def view(c, slot):
            src = packed.at[t, :, c * 5 * half:(c + 1) * 5 * half]
            return src, packed_all.at[t, rows_of(slot), :]

        spread_to_group(
            early, view, lambda: packed_all.at[t, most], lambda: co_s.at[t], lambda: co_r.at[t]
        )

    def pack_factors():
        for c in range(2):
            chan = slice(c * half, (c + 1) * half)
            for t in range(2):
                first = coef[t, 0, own1, chan]
                for g in range(5):
                    if g == 4:
                        value = first * coef[t, 5, own1, chan] if t == 1 else first
                    else:
                        value = coef[t, 1 + g, own1, chan]
                        if t == 1 and g != 2:
                            value = value * first
                    at = (c * 5 + g) * half
                    packed[t, :, at:at + half] = value.astype(BF16)

    def send_vec(index, pred):
        def view(c, slot):
            chan = slice(c * half, (c + 1) * half)
            src = ghid.at[own1, chan] if index == 2 else gin.at[1 - index, own1, chan]
            return src, vec_all.at[index, rows_of(slot), :]

        spread_to_group(
            pred, view, lambda: vec_all.at[index, most], lambda: ve_s.at[index], lambda: ve_r.at[index]
        )

    def send_down():
        def go():
            for d in (2, 1, 3, 0):
                for c in range(2):
                    there = ((x if c == 0 else y) + d) % LINE
                    chip = y * LINE + there if c == 0 else there * LINE + x
                    remote(
                        gx_out.at[0, :, c * half:(c + 1) * half],
                        vec_all.at[1, rows_of(2 * (x if c == 0 else y) + k), :],
                        vd_s.at[0], ve_r.at[1], (z - 1, chip, c),
                    ).start()

        def done():
            remote(vec_all.at[1], vec_all.at[1], vd_s.at[0], ve_r.at[1], (z, s, 1 - k)).wait_send()

        pl.when(z == 1)(go)
        pending.append(lambda: pl.when(z == 1)(done))

    rows = out.shape[0]
    block = 2 * rows
    me = jnp.where(k == 0, y, x)

    def turn_patches():
        for t in range(2):
            for part in range(2):
                arrived(tiles_all.at[t, part], ti_r.at[t, part])

            def one(slot, carried):
                for part in range(2):
                    tile = tiles_all[t, part, slot]
                    left, right = spread_value(tile.astype(F32), hid)
                    for b, moved in enumerate((left, tile, right)):
                        for a in range(3):
                            at = (a * 3 + b) * 2 * hid + part * hid
                            flipped[at:at + hid, :] = moved[cols * a:cols * a + n, :].T
                for j in range(LINE):
                    chip = jnp.where(k == 0, j * LINE + x, y * LINE + j)
                    turned[t, j, :, pl.ds(pl.multiple_of(slot * n, n), n)] = flipped[
                        pl.ds(pl.multiple_of(chip * block, 32), block), :
                    ]
                return carried

            lax.fori_loop(0, 2 * LINE, one, 0)

    @pl.when(z >= 2)
    def _():
        weights_here(1)
        weights_here(0)
        turn_all_weights()

    not_roof = jnp.logical_not(roof)
    z_up = z + 1

    def save(t, into, values, old, chan):
        i_gate, f_gate, o_gate, cand, squash = values
        for index, value in enumerate(factors(i_gate, f_gate, o_gate, cand, squash, old)):
            for cells_to, cells_from in into:
                coef[t, index, cells_to, chan] = value[cells_from]

    def x_here(t):
        for c in range(2):
            arrived(sx.at[t, own2, half_lanes[c]], sx_r.at[t, c, 2])
        spread(sx, t, own2, hid)

    def add(c, term):
        preact[0:n, c * gate_half:(c + 1) * gate_half] += term

    def own_rows(t):
        hidden_lanes = (centre,) if t == 0 else half_lanes
        part_sums = [conv(sh, t, wh, c, (1,)) + bias_of(c) for c in range(2)]
        for c in range(2):
            preact[0:n, c * gate_half:(c + 1) * gate_half] = part_sums[c]

        def x_middle():
            x_here(t)
            for c in range(2):
                add(c, conv(sx, t, wx, c, (1,)))

        def x_edges():
            near_here(sx, t, sx_r.at[t], half_lanes)

        def h_edges():
            near_here(sh, t, sh_r.at[t], hidden_lanes)

        def h_outer():
            for c in range(2):
                add(c, conv(sh, t, wh, c, (0, 2)))

        @pl.when(base)
        def _():
            if t == 0:
                weights_here(0)
            x_middle()
            if t == 1:
                x_edges()
                for c in range(2):
                    add(c, conv(sx, t, wx, c, (0, 2)))
                h_edges()

        if t == 0:
            h_edges()
            h_outer()
            send_tile(0, 1, inner)
            pl.when(z == 1)(lambda: weights_here(0))

        @pl.when(inner)
        def _():
            if t == 1:
                h_edges()
                h_outer()
            x_middle()
            if t == 1:
                x_edges()

        if t == 0:
            x_edges()
            own_cell.wait()
            pl.when(not_roof)(lambda: pl.semaphore_wait(barrier, count(above)))

        def finish(buffer, weights, c):
            chan, lanes = slice(c * half, (c + 1) * half), half_lanes[c]
            now = preact[0:n, c * gate_half:(c + 1) * gate_half] + conv(buffer, t, weights, c, (0, 2))
            i_gate, f_gate, o_gate, cand, new, squash = activate(now, cells[t, own1, chan])
            hidden = (o_gate * squash).astype(BF16)
            if t == 0:
                sh[1, own2, lanes] = hidden
                cells[1, own1, chan] = new
            else:
                top_hidden[:, chan] = hidden
            for index, value in enumerate((i_gate, f_gate, o_gate, cand, squash)):
                gates[index, :, chan] = value

        for c in range(2):
            chan, lanes = slice(c * half, (c + 1) * half), half_lanes[c]
            if t == 0:
                finish(sx, wx, c)
                whole = sh.at[1, own2, lanes]
                ends = sh.at[1, 2 * cols:3 * cols, lanes], sh.at[1, n + cols:n + 2 * cols, lanes]
            else:
                pl.when(base)(lambda c=c: finish(sh, wh, c))
                pl.when(inner)(lambda c=c: finish(sx, wx, c))
                whole = top_hidden.at[:, chan]
                ends = top_hidden.at[0:cols, chan], top_hidden.at[n - cols:n, chan]
            edges(
                lambda ends=ends, lanes=lanes, c=c: (
                    ends, at_rows(sx, t, near, lanes), sx_s.at[t, c], sx_r.at[t, c]
                ),
                z_up, not_roof,
            )
            send(
                not_roof,
                lambda whole=whole, lanes=lanes, c=c: remote(
                    whole, sx.at[t, own2, lanes], sx_s.at[t, c, 2], sx_r.at[t, c, 2], (z_up, s, k)
                ),
            )
            if t == 0:
                send_edges(ends, at_rows(sh, 1, near, lanes), sh_s.at[c], sh_r.at[1, c], z, None)
        if t == 0:
            ends = sh.at[1, 3 * cols:4 * cols, centre], sh.at[1, n:n + cols, centre]
            send_edges(ends, at_rows(sh, 1, far, centre), sh_fs, sh_f.at[1], z, None)
        else:
            ends = beyond(top_hidden)
        last = ends
        edges(
            lambda: (last, at_rows(sx, t, far, centre), sx_fs.at[t], sx_f.at[t]), z_up, not_roof
        )
        for c in range(2):
            chan = slice(c * half, (c + 1) * half)
            save(
                t, ((own1, slice(0, n)),),
                tuple(gates[index, :, chan] for index in range(5)), cells[t, own1, chan], chan,
            )

    def beside_rows(t):
        if t == 0:
            narrow_here(cells.at[0], c_r)
        far_here(sh, t, sh_f.at[t])
        far_here(sx, t, sx_f.at[t])
        for c in range(2):
            chan = slice(c * half, (c + 1) * half)
            old = jnp.concatenate([cells[t, above1, chan], cells[t, below1, chan]], axis=0)
            i_gate, f_gate, o_gate, cand, new, squash = activate(conv_beside(t, c) + bias_of(c), old)
            if t == 0:
                cells[1, above1, chan] = new[0:cols]
                cells[1, below1, chan] = new[cols:]
            save(
                t, ((above1, slice(0, cols)), (below1, slice(cols, 2 * cols))),
                (i_gate, f_gate, o_gate, cand, squash), old, chan,
            )

    def all_rows():
        far_here(sh, 1, sh_f.at[1])
        for c in range(2):
            preact[:, c * gate_half:(c + 1) * gate_half] = conv_all(sh, 1, wh, c) + bias_of(c)
        x_here(1)
        near_here(sx, 1, sx_r.at[1], half_lanes)
        far_here(sx, 1, sx_f.at[1])
        for c in range(2):
            chan = slice(c * half, (c + 1) * half)
            now = preact[:, c * gate_half:(c + 1) * gate_half] + conv_all(sx, 1, wx, c)
            old = cells[1, :, chan]
            i_gate, f_gate, o_gate, cand, new, squash = activate(now, old)
            save(
                1, ((slice(0, n + 2 * cols), slice(0, n + 2 * cols)),),
                (i_gate, f_gate, o_gate, cand, squash), old, chan,
            )

    own_hidden.wait()
    spread(sh, 0, own2, hid)
    pl.when(z < 2)(lambda: weights_here(1))
    own_rows(0)
    send_tile(0, 0, inner)
    spread(sh, 1, own2, hid)

    @pl.when(not_roof)
    def _():
        own_rows(1)
        beside_rows(0)
        beside_rows(1)

    @pl.when(roof)
    def _():
        beside_rows(0)
        near_here(sh, 1, sh_r.at[1], half_lanes)

    send_tile(1, 1, roof)
    pl.when(roof)(all_rows)

    def blank(outside):
        coef[:, :, outside, :] = jnp.zeros((2, 6, cols, hid), F32)

    pl.when(top)(lambda: blank(above1))
    pl.when(bottom)(lambda: blank(below1))

    pl.when(z < 2)(turn_all_weights)
    pl.when(early)(pack_factors)
    send_tile(0, 1, base)
    send_tile(0, 0, base)
    send_tile(1, 1, not_roof)
    send_tile(1, 0, not_roof)
    send_factors(1)
    send_factors(0)
    pl.when(z < 2)(turn_patches)

    def back_conv(t, weights):
        total = None
        for a in range(3):
            term = dot(sg[t, cols * (2 - a):cols * (2 - a) + n, :], weights[a])
            total = term if total is None else total + term
        return total.astype(BF16)

    def gate_grads(t):
        for c in range(2):
            chan = slice(c * half, (c + 1) * half)
            grad_h = gin[t, :, chan].astype(F32)
            if t == 0:
                grad_h = grad_h + ghid[:, chan].astype(F32)
            grad_c = grad_h * coef[t, 0, :, chan]
            if t == 0:
                grad_c = grad_c + carry[:, chan]
            for g, value in enumerate((
                grad_c * coef[t, 1, :, chan],
                grad_c * coef[t, 2, :, chan],
                grad_h * coef[t, 3, :, chan],
                grad_c * coef[t, 4, :, chan],
            )):
                at = 4 * hid + c * gate_half + g * half
                sg[t, :, at:at + half] = value.astype(BF16)
            if t == 1:
                carry[:, chan] = grad_c * coef[t, 5, :, chan]

    def first_conv(t, weights):
        total = None
        for b in (1, 0, 2):
            lanes = slice(b * 4 * hid, (b + 1) * 4 * hid)
            if b == 0:
                spread(sg, t, slice(0, 2 * cols + n), 4 * hid)
            for a in range(3):
                low = cols * (2 - a)
                term = dot(sg[t, low:low + n, lanes], weights[a, lanes, :])
                total = term if total is None else total + term
        return total.astype(BF16)

    def send_input_grad(t, pred):
        send_edges(outer(gx_out.at[t], cols), narrow(gin.at[t]), gx_s.at[t], gx_r.at[t], z - 1, pred)
        send(
            pred,
            lambda: remote(gx_out.at[t], gin.at[t, own1], gx_s.at[t, 2], gx_r.at[t, 2], (z - 1, s, k)),
        )

    arrived(gin.at[1, own1], gx_r.at[1, 2])
    send_vec(0, base)
    narrow_here(gin.at[1], gx_r.at[1])

    @pl.when(inner)
    def _():
        gate_grads(1)
        gx_out[1] = first_conv(1, wxt)

    send_input_grad(1, inner)

    @pl.when(inner)
    def _():
        ghid[own1] = back_conv(1, wht)

    @pl.when(base)
    def _():
        gate_grads(1)
        ghid[own1] = first_conv(1, wht)

    send_edges((ghid.at[cols:2 * cols], ghid.at[n:n + cols]), narrow(ghid), gh_s, gh_r, z, inner)
    send_vec(0, z == 1)
    send_vec(2, early)
    send_tile(1, 0, roof)
    send_grads(1, 0, z == 2)

    pl.when(inner)(lambda: arrived(gin.at[0, own1], gx_r.at[0, 2]))
    send_vec(1, z == 1)

    @pl.when(inner)
    def _():
        narrow_here(gin.at[0], gx_r.at[0])
        narrow_here(ghid, gh_r)
        gate_grads(0)
        gx_out[0] = first_conv(0, wxt)

    send_down()
    send_input_grad(0, z >= 2)
    send_grads(1, 0, roof)
    send_grads(1, 1, z >= 2)
    send_grads(0, 0, z >= 2)
    send_grads(0, 1, z >= 2)

    pl.when(z >= 2)(turn_patches)

    def grads_here(t, p, lanes):
        arrived(grads_all.at[t, :, lanes], ga_r.at[t, p])

    def vec_here(index):
        arrived(vec_all.at[index], ve_r.at[index])

    def factors_here(t):
        arrived(packed_all.at[t], co_r.at[t])

    def factor(t, g):
        return packed_all[t, :, g * half:(g + 1) * half].astype(F32)

    def put(t, g, value):
        grads_all[t, :, g * half:(g + 1) * half] = (factor(t, g) * value).astype(BF16)

    @pl.when(early)
    def _():
        factors_here(1)
        factors_here(0)
        vec_here(0)
        for g in range(4):
            put(1, g, vec_all[0].astype(F32))

    @pl.when(z >= 2)
    def _():
        grads_here(1, 0, pairs[0])
        grads_here(1, 1, pairs[1])

    for j in range(LINE):
        acc[j] = dot(turned[1, j], grads_all[1])
    for p, lanes in enumerate(pairs):
        @pl.when(early)
        def _():
            if p == 0:
                vec_here(2)
                vec_here(1)
            grad_h = vec_all[1].astype(F32) + vec_all[2].astype(F32)
            grad_c = vec_all[0].astype(F32) * factor(1, 4) + grad_h * factor(0, 4)
            put(0, 2 * p, grad_h if p else grad_c)
            put(0, 2 * p + 1, grad_c)

        pl.when(z >= 2)(lambda: grads_here(0, p, lanes))
        for d in (2, 1, 3, 0):
            j = (me + d) % LINE
            leaving[d, :, lanes] = (
                acc[j, :, lanes] + dot(turned[0, j], grads_all[0, :, lanes])
            ).astype(BF16)
            chip = jnp.where(k == 0, j * LINE + x, y * LINE + j)
            for q in range(2):
                src, dst = leaving.at[d, q * rows:(q + 1) * rows, lanes], landed.at[k, me, :, lanes]
                copy = functools.partial(
                    remote, src, dst, rv_s.at[p, min(d, 1)], rv_r.at[p], (z, chip, q)
                )
                if d == 0:
                    pl.when(k == q)(
                        lambda: pltpu.make_async_copy(src, dst, rv_r.at[p]).start()
                    )
                    pl.when(k != q)(lambda: copy().start())
                else:
                    copy().start()
    for wait in pending:
        wait()
    def final(p):
        wide = slice(2 * p * hid, 2 * (p + 1) * hid)
        return pltpu.make_async_copy(result.at[:, wide], out.at[:, wide], out_sem.at[p])

    for p, lanes in enumerate(pairs):
        arrived(landed.at[:, :, :, lanes], rv_r.at[p])
        for c in range(2):
            for g in (2 * p, 2 * p + 1):
                total = landed[c, 0, :, g * half:(g + 1) * half].astype(F32)
                for i in range(1, LINE):
                    total = total + landed[c, i, :, g * half:(g + 1) * half].astype(F32)
                result[:, g * hid + c * half:g * hid + (c + 1) * half] = total
        final(p).start()
    for p, lanes in enumerate(pairs):
        for ref, sem in ((leaving.at[0, 0:rows, lanes], rv_s.at[p, 0]), (leaving.at[1:4, :, lanes], rv_s.at[p, 1])):
            remote(ref, ref, sem, sem, (z, s, 1 - k)).wait_send()
        final(p).wait()


def on_device(frames, cotangent, first_hidden, first_cell, gate_bias, gate_weight):
    steps, _, tile_rows, cols, hid = frames.shape
    n = tile_rows * cols
    pad = n + 2 * cols
    half = hid // 2
    gates = 4 * hid
    share = 18 * hid // (lax.axis_size("space") * lax.axis_size("batch"))
    block = 2 * share
    vmem = pl.BlockSpec(memory_space=pltpu.VMEM)
    anywhere = pl.BlockSpec(memory_space=pl.ANY)
    dma = pltpu.SemaphoreType.DMA
    scratch = [
        pltpu.VMEM((2, 3, 3, hid, gates // 2), BF16),
        pltpu.VMEM((2, 3, 3, hid, gates // 2), BF16),
        pltpu.VMEM((3, 3 * gates, hid), BF16),
        pltpu.VMEM((3, 3 * gates, hid), BF16),
        pltpu.VMEM((steps, pad + 2 * cols, 3 * hid), BF16),
        pltpu.VMEM((steps, pad + 2 * cols, 3 * hid), BF16),
        pltpu.VMEM((steps, pad, 3 * gates), BF16),
        pltpu.VMEM((n, hid), BF16),
        pltpu.VMEM((pad, gates), F32),
        pltpu.VMEM((5, n, hid), F32),
        pltpu.VMEM((steps, pad, hid), F32),
        pltpu.VMEM((pad, hid), F32),
        pltpu.VMEM((steps, 6, pad, hid), F32),
        pltpu.VMEM((steps, pad, hid), BF16),
        pltpu.VMEM((steps, n, hid), BF16),
        pltpu.VMEM((pad, hid), BF16),
        pltpu.VMEM((steps, 2, 2 * LINE, pad, hid), BF16),
        pltpu.VMEM((18 * hid, n), BF16),
        pltpu.VMEM((steps, LINE, block, 2 * LINE * n), BF16),
        pltpu.VMEM((steps, 2 * LINE * n, gates // 2), BF16),
        pltpu.VMEM((steps, n, 5 * hid), BF16),
        pltpu.VMEM((steps, 2 * LINE * n, 5 * half), BF16),
        pltpu.VMEM((3, 2 * LINE * n, half), BF16),
        pltpu.VMEM((LINE, block, gates // 2), F32),
        pltpu.VMEM((LINE, block, gates // 2), BF16),
        pltpu.VMEM((2, LINE, share, gates // 2), BF16),
        pltpu.VMEM((share, gates), F32),
        dma((2, 2, 4)), dma((2,)),
        dma((steps, 2, 3)), dma((steps, 2)), dma((steps, 2, 2)), dma((steps, 2)),
        dma((2,)), dma((steps, 3)), dma((2,)),
        dma((steps, 2)), dma((steps, 2)), dma((steps,)), dma((3,)), dma((2,)),
        dma((steps, 2, 2)), dma((steps, 2)), dma((2,)), dma((2,)), dma((2,)), dma((steps, 2)),
        dma((steps, 2, 3)), dma((steps, 2)), dma((2, 2)), dma((2,)), dma((steps, 3)), dma((2,)),
        dma((steps, 2)), dma((steps, 2)), dma((steps,)), dma((3,)), dma((1,)), dma((2, 2)), dma((2,)),
    ]
    result = pl.pallas_call(
        kernel,
        out_shape=jax.ShapeDtypeStruct((share, gates), F32),
        in_specs=[anywhere] * 4 + [vmem, anywhere],
        out_specs=anywhere,
        scratch_shapes=scratch,
        compiler_params=pltpu.CompilerParams(
            collective_id=0, has_side_effects=True, vmem_limit_bytes=56 * 2**20
        ),
    )(
        frames.reshape(steps, n, hid),
        cotangent.reshape(steps, n, hid),
        first_hidden.reshape(n, hid),
        first_cell.reshape(n, hid),
        gate_bias,
        gate_weight.reshape(3, 3, 2 * hid, gates),
    )
    return result[None]


def solution(mesh):
    return jax.shard_map(
        on_device,
        mesh=mesh,
        in_specs=(
            P(None, "batch", "space", None, None),
            P(None, "batch", "space", None, None),
            P("section", "batch", "space", None, None),
            P("section", "batch", "space", None, None),
            P("section", None),
            P("section", None, None),
        ),
        out_specs=P("section", ("space", "batch"), None),
        check_vma=False,
    )
```

```python
import functools

import jax
import jax.numpy as jnp
from jax import lax
from jax.experimental import pallas as pl
from jax.experimental.pallas import tpu as pltpu
from jax.sharding import PartitionSpec as P

F32 = jnp.float32
BF16 = jnp.bfloat16
MESH = pl.DeviceIdType.MESH
LINE = 4


def dot(left, right):
    return jnp.dot(left, right, preferred_element_type=F32)


def kernel(
    frames, cotangent, first_hidden, first_cell, bias, weight, out,
    wx, wh, wxt, wht, sx, sh, sg, top_hidden, preact, gates, cells, carry, coef, gin, gx_out, ghid,
    tiles_all, flipped, turned, grads_all, packed, packed_all, vec_all, acc, leaving, landed, result,
    w_sem, in_sem, sx_r, sx_f, sh_r, sh_f, c_r, gx_r, gh_r, ti_r, ga_r, co_r, ve_r, rv_r,
    fr_s, fr_f, fh_s, fh_f, fc_s, ct_s, sx_s, sx_fs, sh_s, sh_fs, gx_s, gh_s, ti_s, ga_s, co_s, ve_s, vd_s, rv_s, out_sem,
):
    z, s, k = lax.axis_index("section"), lax.axis_index("space"), lax.axis_index("batch")
    y, x = s // LINE, s % LINE
    sections, tiles = lax.axis_size("section"), lax.axis_size("space")
    cols = 32
    n = first_cell.shape[0]
    hid = first_cell.shape[1]
    half = hid // 2
    gate_half = 4 * half
    own2, above2, below2 = slice(2 * cols, 2 * cols + n), slice(0, 2 * cols), slice(2 * cols + n, 4 * cols + n)
    near = slice(cols, 2 * cols), slice(2 * cols + n, 3 * cols + n)
    far = slice(0, cols), slice(3 * cols + n, 4 * cols + n)
    own1, above1, below1 = slice(cols, cols + n), slice(0, cols), slice(cols + n, 2 * cols + n)
    centre = slice(hid, 2 * hid)
    top, bottom, base, roof = s == 0, s == tiles - 1, z == 0, z == sections - 1
    inner = jnp.logical_not(base)
    pending = []

    def send(pred, make):
        if pred is None:
            make().start()
            pending.append(lambda: make().wait_send())
        else:
            ask = pred if callable(pred) else lambda: pred
            pl.when(ask())(lambda: make().start())
            pending.append(lambda: pl.when(ask())(lambda: make().wait_send()))

    def remote(src, dst, send_sem, recv_sem, device):
        return pltpu.make_async_remote_copy(
            src_ref=src, dst_ref=dst, send_sem=send_sem, recv_sem=recv_sem,
            device_id=device, device_id_type=MESH,
        )

    def arrived(dst, recv_sem):
        remote(dst, dst, recv_sem, recv_sem, (z, s, 1 - k)).wait_recv()

    loads = {}
    for part, buffer in ((0, wx), (1, wh)):
        for c in range(2):
            for g in range(4):
                loads[part, c, g] = pltpu.make_async_copy(
                    weight.at[:, :, part * hid:(part + 1) * hid, pl.ds(g * hid + c * half, half)],
                    buffer.at[c, :, :, :, g * half:(g + 1) * half],
                    w_sem.at[part, c, g],
                )

    def weights_here(part):
        for c in range(2):
            for g in range(4):
                loads[part, c, g].wait()

    barrier = pltpu.get_barrier_semaphore()

    def greet(partners):
        for pred, device in partners:
            call = functools.partial(
                pl.semaphore_signal, barrier, inc=1, device_id=device, device_id_type=MESH
            )
            if pred is None:
                call()
            else:
                pl.when(pred)(call)

    def count(partners):
        total = 0
        for pred, _ in partners:
            total = total + (1 if pred is None else jnp.where(pred, 1, 0))
        return total

    plane = [(jnp.logical_not(top), (z, s - 1, k)), (jnp.logical_not(bottom), (z, s + 1, k))]
    plane.append((None, (z, s, 1 - k)))
    for d in range(1, LINE):
        for core in range(2):
            plane.append((None, (z, y * LINE + (x + d) % LINE, core)))
            plane.append((None, (z, ((y + d) % LINE) * LINE + x, core)))

    def section_at(step, ok):
        return [
            (ok, (z + step, s, k)),
            (ok & (s > 0), (z + step, s - 1, k)),
            (ok & (s < tiles - 1), (z + step, s + 1, k)),
        ]

    below, above = section_at(-1, z > 0), section_at(1, z < sections - 1)
    group = [
        (base, (z + 1, jnp.where(k == 0, y * LINE + j, j * LINE + x), core))
        for j in range(LINE) for core in range(2)
    ]
    greet(plane)

    half_lanes = [slice(hid + c * half, hid + (c + 1) * half) for c in range(2)]
    own_hidden = pltpu.make_async_copy(first_hidden, sh.at[0, own2, centre], in_sem.at[0])
    own_cell = pltpu.make_async_copy(first_cell, cells.at[0, own1], in_sem.at[1])
    own_hidden.start()

    @pl.when(base)
    def _():
        for t in range(2):
            for c in range(2):
                pltpu.make_async_copy(
                    frames.at[t, :, pl.ds(c * half, half)], sx.at[t, own2, half_lanes[c]], sx_r.at[t, c, 2]
                ).start()

    own_cell.start()

    @pl.when(roof)
    def _():
        for t in range(2):
            pltpu.make_async_copy(cotangent.at[t], gin.at[t, own1], gx_r.at[t, 2]).start()

    for part in (1, 0):
        for c in range(2):
            for g in range(4):
                loads[part, c, g].start()

    def clear(wide, narrow):
        for t in range(2):
            sx[t, wide, :] = jnp.zeros((2 * cols, 3 * hid), BF16)
            sh[t, wide, :] = jnp.zeros((2 * cols, 3 * hid), BF16)
            gin[t, narrow] = jnp.zeros((cols, hid), BF16)
        cells[0, narrow] = jnp.zeros((cols, hid), F32)
        ghid[narrow] = jnp.zeros((cols, hid), BF16)

    pl.when(top)(lambda: clear(above2, above1))
    pl.when(bottom)(lambda: clear(below2, below1))

    pl.semaphore_wait(
        barrier, count(plane) + count(below) + jnp.where(z == 1, len(group), 0)
    )

    def send_edges(src, dst, send_sems, recv_sems, section, pred):
        edges(lambda: (src, dst, send_sems, recv_sems), section, pred)

    def edges(parts, section, pred):
        def up():
            return s > 0 if pred is None else (s > 0) & pred

        def down():
            return s < tiles - 1 if pred is None else (s < tiles - 1) & pred

        def make(end, device):
            src, dst, send_sems, recv_sems = parts()
            return remote(src[end], dst[1 - end], send_sems.at[end], recv_sems.at[1 - end], device)

        send(up, lambda: make(0, (section, s - 1, k)))
        send(down, lambda: make(1, (section, s + 1, k)))

    def outer(ref, width):
        return ref.at[0:width], ref.at[n - width:n]

    def beyond(ref):
        return ref.at[cols:2 * cols], ref.at[n - 2 * cols:n - cols]

    def narrow(ref):
        return ref.at[above1], ref.at[below1]

    def at_rows(buffer, t, rows, lanes):
        return buffer.at[t, rows[0], lanes], buffer.at[t, rows[1], lanes]

    def halves(ref, c):
        return ref.at[0:cols, pl.ds(c * half, half)], ref.at[n - cols:n, pl.ds(c * half, half)]

    send_edges(outer(first_hidden, cols), at_rows(sh, 0, near, centre), fh_s, sh_r.at[0, 0], z, None)

    def send_frames(t):
        for c in range(2):
            send_edges(
                halves(frames.at[t], c), at_rows(sx, t, near, half_lanes[c]),
                fr_s.at[t, c], sx_r.at[t, c], z, base,
            )

    send_frames(0)
    greet(above)
    greet(group)
    greet(below)
    send_edges(beyond(first_hidden), at_rows(sh, 0, far, centre), fh_f, sh_f.at[0], z, None)
    send_edges(outer(first_cell, cols), narrow(cells.at[0]), fc_s, c_r, z, None)
    send_edges(beyond(frames.at[0]), at_rows(sx, 0, far, centre), fr_f.at[0], sx_f.at[0], z, base)
    send_frames(1)
    send_edges(beyond(frames.at[1]), at_rows(sx, 1, far, centre), fr_f.at[1], sx_f.at[1], z, base)
    for t in range(2):
        send_edges(outer(cotangent.at[t], cols), narrow(gin.at[t]), ct_s.at[t], gx_r.at[t], z, roof)

    def spread_value(value, width):
        count = value.shape[0]
        column = lax.broadcasted_iota(jnp.int32, (count, width), 0) % cols
        left = jnp.where(column == 0, 0.0, pltpu.roll(value, 1, 0)).astype(BF16)
        right = jnp.where(column == cols - 1, 0.0, pltpu.roll(value, count - 1, 0)).astype(BF16)
        return left, right

    def spread(buffer, t, rows, width):
        left, right = spread_value(buffer[t, rows, width:2 * width].astype(F32), width)
        buffer[t, rows, 0:width] = left
        buffer[t, rows, 2 * width:3 * width] = right

    def when_edges(first, second):
        pl.when(jnp.logical_not(top))(first)
        pl.when(jnp.logical_not(bottom))(second)

    def near_here(buffer, t, recv_sems, lanes):
        def here(index):
            for c, part in enumerate(lanes):
                arrived(buffer.at[t, near[index], part], recv_sems.at[c, index])
            spread(buffer, t, near[index], hid)

        when_edges(lambda: here(0), lambda: here(1))

    def far_here(buffer, t, recv_sems):
        def here(index):
            arrived(buffer.at[t, far[index], centre], recv_sems.at[index])
            spread(buffer, t, far[index], hid)

        when_edges(lambda: here(0), lambda: here(1))

    def narrow_here(ref, recv_sems):
        when_edges(
            lambda: arrived(ref.at[above1], recv_sems.at[0]),
            lambda: arrived(ref.at[below1], recv_sems.at[1]),
        )

    def conv(buffer, t, weights, c, offsets):
        total = None
        for a in offsets:
            term = dot(
                buffer[t, cols * (a + 1):cols * (a + 1) + n, :],
                weights[c, a].reshape(3 * hid, gate_half),
            )
            total = term if total is None else total + term
        return total

    def conv_all(buffer, t, weights, c):
        total = None
        for a in range(3):
            term = dot(
                buffer[t, cols * a:cols * (a + 2) + n, :],
                weights[c, a].reshape(3 * hid, gate_half),
            )
            total = term if total is None else total + term
        return total

    def conv_beside(t, c):
        total = None
        for buffer, weights in ((sh, wh), (sx, wx)):
            for a in range(3):
                low = cols * (a + 1) + n
                cells_in = jnp.concatenate(
                    [buffer[t, cols * a:cols * (a + 1), :], buffer[t, low:low + cols, :]], axis=0
                )
                term = dot(cells_in, weights[c, a].reshape(3 * hid, gate_half))
                total = term if total is None else total + term
        return total

    def bias_of(c):
        return jnp.concatenate(
            [bias[0:1, g * hid + c * half:g * hid + (c + 1) * half] for g in range(4)], axis=1
        )

    def activate(now, old):
        i_gate = jax.nn.sigmoid(now[:, 0:half])
        f_gate = jax.nn.sigmoid(now[:, half:2 * half])
        o_gate = jax.nn.sigmoid(now[:, 2 * half:3 * half])
        cand = jnp.tanh(now[:, 3 * half:])
        new = f_gate * old + i_gate * cand
        return i_gate, f_gate, o_gate, cand, new, jnp.tanh(new)

    def factors(i_gate, f_gate, o_gate, cand, squash, old):
        return (
            o_gate * (1.0 - squash * squash),
            cand * i_gate * (1.0 - i_gate),
            old * f_gate * (1.0 - f_gate),
            squash * o_gate * (1.0 - o_gate),
            i_gate * (1.0 - cand * cand),
            f_gate,
        )

    def turn_weights(source, target):
        def one(a, carried):
            for b in range(3):
                for c in range(2):
                    start = (2 - b) * 4 * hid + c * gate_half
                    target[a, start:start + gate_half, :] = source[c, a, b].T
            return carried

        lax.fori_loop(0, 3, one, 0)

    def turn_all_weights():
        turn_weights(wh, wht)
        pl.when(inner)(lambda: turn_weights(wx, wxt))

    def spread_to_group(pred, view, seven, send_sem, recv_sem):
        def go():
            for d in (2, 1, 3, 0):
                for c in range(2):
                    there = ((x if c == 0 else y) + d) % LINE
                    chip = y * LINE + there if c == 0 else there * LINE + x
                    src, dst = view(c, 2 * (x if c == 0 else y) + k)
                    copy = functools.partial(remote, src, dst, send_sem(), recv_sem(), (z, chip, c))
                    if d == 0:
                        pl.when(k == c)(lambda: pltpu.make_async_copy(src, dst, recv_sem()).start())
                        pl.when(k != c)(lambda: copy().start())
                    else:
                        copy().start()

        def done():
            remote(seven(), seven(), send_sem(), recv_sem(), (z, s, 1 - k)).wait_send()

        pl.when(pred)(go)
        pending.append(lambda: pl.when(pred)(done))

    def rows_of(slot):
        return pl.ds(pl.multiple_of(slot * n, n), n)

    most = slice(0, 7 * n)

    def send_tile(t, part, pred):
        spread_to_group(
            pred,
            lambda c, slot: (
                (sh if part else sx).at[t, cols:3 * cols + n, centre], tiles_all.at[t, part, slot]
            ),
            lambda: tiles_all.at[t, part, 0:7],
            lambda: ti_s.at[t, part], lambda: ti_r.at[t, part],
        )

    pairs = [slice(p * 2 * half, (p + 1) * 2 * half) for p in range(2)]

    def send_grads(t, p, pred):
        lanes = pairs[p]

        def view(c, slot):
            at = 4 * hid + c * gate_half
            src = sg.at[t, own1, at + lanes.start:at + lanes.stop]
            return src, grads_all.at[t, rows_of(slot), lanes]

        spread_to_group(
            pred, view, lambda: grads_all.at[t, most, lanes],
            lambda: ga_s.at[t, p], lambda: ga_r.at[t, p],
        )

    early = z < 2

    def send_factors(t):
        def view(c, slot):
            src = packed.at[t, :, c * 5 * half:(c + 1) * 5 * half]
            return src, packed_all.at[t, rows_of(slot), :]

        spread_to_group(
            early, view, lambda: packed_all.at[t, most], lambda: co_s.at[t], lambda: co_r.at[t]
        )

    def pack_factors():
        for c in range(2):
            chan = slice(c * half, (c + 1) * half)
            for t in range(2):
                first = coef[t, 0, own1, chan]
                for g in range(5):
                    if g == 4:
                        value = first * coef[t, 5, own1, chan] if t == 1 else first
                    else:
                        value = coef[t, 1 + g, own1, chan]
                        if t == 1 and g != 2:
                            value = value * first
                    at = (c * 5 + g) * half
                    packed[t, :, at:at + half] = value.astype(BF16)

    def send_vec(index, pred):
        def view(c, slot):
            chan = slice(c * half, (c + 1) * half)
            src = ghid.at[own1, chan] if index == 2 else gin.at[1 - index, own1, chan]
            return src, vec_all.at[index, rows_of(slot), :]

        spread_to_group(
            pred, view, lambda: vec_all.at[index, most], lambda: ve_s.at[index], lambda: ve_r.at[index]
        )

    def send_down():
        def go():
            for d in (2, 1, 3, 0):
                for c in range(2):
                    there = ((x if c == 0 else y) + d) % LINE
                    chip = y * LINE + there if c == 0 else there * LINE + x
                    remote(
                        gx_out.at[0, :, c * half:(c + 1) * half],
                        vec_all.at[1, rows_of(2 * (x if c == 0 else y) + k), :],
                        vd_s.at[0], ve_r.at[1], (z - 1, chip, c),
                    ).start()

        def done():
            remote(vec_all.at[1], vec_all.at[1], vd_s.at[0], ve_r.at[1], (z, s, 1 - k)).wait_send()

        pl.when(z == 1)(go)
        pending.append(lambda: pl.when(z == 1)(done))

    rows = out.shape[0]
    block = 2 * rows
    me = jnp.where(k == 0, y, x)

    def turn_patches():
        for t in range(2):
            for part in range(2):
                arrived(tiles_all.at[t, part], ti_r.at[t, part])

            def one(slot, carried):
                for part in range(2):
                    tile = tiles_all[t, part, slot]
                    left, right = spread_value(tile.astype(F32), hid)
                    for b, moved in enumerate((left, tile, right)):
                        for a in range(3):
                            at = (a * 3 + b) * 2 * hid + part * hid
                            flipped[at:at + hid, :] = moved[cols * a:cols * a + n, :].T
                for j in range(LINE):
                    chip = jnp.where(k == 0, j * LINE + x, y * LINE + j)
                    turned[t, j, :, pl.ds(pl.multiple_of(slot * n, n), n)] = flipped[
                        pl.ds(pl.multiple_of(chip * block, 32), block), :
                    ]
                return carried

            lax.fori_loop(0, 2 * LINE, one, 0)

    @pl.when(z >= 2)
    def _():
        weights_here(1)
        weights_here(0)
        turn_all_weights()

    not_roof = jnp.logical_not(roof)
    z_up = z + 1

    def save(t, into, values, old, chan):
        i_gate, f_gate, o_gate, cand, squash = values
        for index, value in enumerate(factors(i_gate, f_gate, o_gate, cand, squash, old)):
            for cells_to, cells_from in into:
                coef[t, index, cells_to, chan] = value[cells_from]

    def x_here(t):
        for c in range(2):
            arrived(sx.at[t, own2, half_lanes[c]], sx_r.at[t, c, 2])
        spread(sx, t, own2, hid)

    def add(c, term):
        preact[0:n, c * gate_half:(c + 1) * gate_half] += term

    def own_rows(t):
        hidden_lanes = (centre,) if t == 0 else half_lanes
        part_sums = [conv(sh, t, wh, c, (1,)) + bias_of(c) for c in range(2)]
        for c in range(2):
            preact[0:n, c * gate_half:(c + 1) * gate_half] = part_sums[c]

        def x_middle():
            x_here(t)
            for c in range(2):
                add(c, conv(sx, t, wx, c, (1,)))

        def x_edges():
            near_here(sx, t, sx_r.at[t], half_lanes)

        def h_edges():
            near_here(sh, t, sh_r.at[t], hidden_lanes)

        def h_outer():
            for c in range(2):
                add(c, conv(sh, t, wh, c, (0, 2)))

        @pl.when(base)
        def _():
            if t == 0:
                weights_here(0)
            x_middle()
            if t == 1:
                x_edges()
                for c in range(2):
                    add(c, conv(sx, t, wx, c, (0, 2)))
                h_edges()

        if t == 0:
            h_edges()
            h_outer()
            send_tile(0, 1, inner)
            pl.when(z == 1)(lambda: weights_here(0))

        @pl.when(inner)
        def _():
            if t == 1:
                h_edges()
                h_outer()
            x_middle()
            if t == 1:
                x_edges()

        if t == 0:
            x_edges()
            own_cell.wait()
            pl.when(not_roof)(lambda: pl.semaphore_wait(barrier, count(above)))

        def finish(buffer, weights, c):
            chan, lanes = slice(c * half, (c + 1) * half), half_lanes[c]
            now = preact[0:n, c * gate_half:(c + 1) * gate_half] + conv(buffer, t, weights, c, (0, 2))
            i_gate, f_gate, o_gate, cand, new, squash = activate(now, cells[t, own1, chan])
            hidden = (o_gate * squash).astype(BF16)
            if t == 0:
                sh[1, own2, lanes] = hidden
                cells[1, own1, chan] = new
            else:
                top_hidden[:, chan] = hidden
            for index, value in enumerate((i_gate, f_gate, o_gate, cand, squash)):
                gates[index, :, chan] = value

        for c in range(2):
            chan, lanes = slice(c * half, (c + 1) * half), half_lanes[c]
            if t == 0:
                finish(sx, wx, c)
                whole = sh.at[1, own2, lanes]
                ends = sh.at[1, 2 * cols:3 * cols, lanes], sh.at[1, n + cols:n + 2 * cols, lanes]
            else:
                pl.when(base)(lambda c=c: finish(sh, wh, c))
                pl.when(inner)(lambda c=c: finish(sx, wx, c))
                whole = top_hidden.at[:, chan]
                ends = top_hidden.at[0:cols, chan], top_hidden.at[n - cols:n, chan]
            edges(
                lambda ends=ends, lanes=lanes, c=c: (
                    ends, at_rows(sx, t, near, lanes), sx_s.at[t, c], sx_r.at[t, c]
                ),
                z_up, not_roof,
            )
            send(
                not_roof,
                lambda whole=whole, lanes=lanes, c=c: remote(
                    whole, sx.at[t, own2, lanes], sx_s.at[t, c, 2], sx_r.at[t, c, 2], (z_up, s, k)
                ),
            )
            if t == 0:
                send_edges(ends, at_rows(sh, 1, near, lanes), sh_s.at[c], sh_r.at[1, c], z, None)
        if t == 0:
            ends = sh.at[1, 3 * cols:4 * cols, centre], sh.at[1, n:n + cols, centre]
            send_edges(ends, at_rows(sh, 1, far, centre), sh_fs, sh_f.at[1], z, None)
        else:
            ends = beyond(top_hidden)
        last = ends
        edges(
            lambda: (last, at_rows(sx, t, far, centre), sx_fs.at[t], sx_f.at[t]), z_up, not_roof
        )
        for c in range(2):
            chan = slice(c * half, (c + 1) * half)
            save(
                t, ((own1, slice(0, n)),),
                tuple(gates[index, :, chan] for index in range(5)), cells[t, own1, chan], chan,
            )

    def beside_rows(t):
        if t == 0:
            narrow_here(cells.at[0], c_r)
        far_here(sh, t, sh_f.at[t])
        far_here(sx, t, sx_f.at[t])
        for c in range(2):
            chan = slice(c * half, (c + 1) * half)
            old = jnp.concatenate([cells[t, above1, chan], cells[t, below1, chan]], axis=0)
            i_gate, f_gate, o_gate, cand, new, squash = activate(conv_beside(t, c) + bias_of(c), old)
            if t == 0:
                cells[1, above1, chan] = new[0:cols]
                cells[1, below1, chan] = new[cols:]
            save(
                t, ((above1, slice(0, cols)), (below1, slice(cols, 2 * cols))),
                (i_gate, f_gate, o_gate, cand, squash), old, chan,
            )

    def all_rows():
        far_here(sh, 1, sh_f.at[1])
        for c in range(2):
            preact[:, c * gate_half:(c + 1) * gate_half] = conv_all(sh, 1, wh, c) + bias_of(c)
        x_here(1)
        near_here(sx, 1, sx_r.at[1], half_lanes)
        far_here(sx, 1, sx_f.at[1])
        for c in range(2):
            chan = slice(c * half, (c + 1) * half)
            now = preact[:, c * gate_half:(c + 1) * gate_half] + conv_all(sx, 1, wx, c)
            old = cells[1, :, chan]
            i_gate, f_gate, o_gate, cand, new, squash = activate(now, old)
            save(
                1, ((slice(0, n + 2 * cols), slice(0, n + 2 * cols)),),
                (i_gate, f_gate, o_gate, cand, squash), old, chan,
            )

    own_hidden.wait()
    spread(sh, 0, own2, hid)
    pl.when(z < 2)(lambda: weights_here(1))
    own_rows(0)
    send_tile(0, 0, inner)
    spread(sh, 1, own2, hid)

    pl.when(not_roof)(lambda: own_rows(1))
    pl.when(early)(pack_factors)
    send_tile(0, 1, base)
    send_tile(0, 0, base)
    send_tile(1, 1, not_roof)
    send_tile(1, 0, not_roof)
    send_factors(1)
    send_factors(0)

    @pl.when(not_roof)
    def _():
        beside_rows(0)
        beside_rows(1)

    @pl.when(roof)
    def _():
        beside_rows(0)
        near_here(sh, 1, sh_r.at[1], half_lanes)

    send_tile(1, 1, roof)
    pl.when(roof)(all_rows)

    def blank(outside):
        coef[:, :, outside, :] = jnp.zeros((2, 6, cols, hid), F32)

    pl.when(top)(lambda: blank(above1))
    pl.when(bottom)(lambda: blank(below1))

    pl.when(z < 2)(turn_all_weights)
    pl.when(z < 2)(turn_patches)

    def back_conv(t, weights):
        total = None
        for a in range(3):
            term = dot(sg[t, cols * (2 - a):cols * (2 - a) + n, :], weights[a])
            total = term if total is None else total + term
        return total.astype(BF16)

    def gate_grads(t):
        for c in range(2):
            chan = slice(c * half, (c + 1) * half)
            grad_h = gin[t, :, chan].astype(F32)
            if t == 0:
                grad_h = grad_h + ghid[:, chan].astype(F32)
            grad_c = grad_h * coef[t, 0, :, chan]
            if t == 0:
                grad_c = grad_c + carry[:, chan]
            for g, value in enumerate((
                grad_c * coef[t, 1, :, chan],
                grad_c * coef[t, 2, :, chan],
                grad_h * coef[t, 3, :, chan],
                grad_c * coef[t, 4, :, chan],
            )):
                at = 4 * hid + c * gate_half + g * half
                sg[t, :, at:at + half] = value.astype(BF16)
            if t == 1:
                carry[:, chan] = grad_c * coef[t, 5, :, chan]

    def first_conv(t, weights):
        total = None
        for b in (1, 0, 2):
            lanes = slice(b * 4 * hid, (b + 1) * 4 * hid)
            if b == 0:
                spread(sg, t, slice(0, 2 * cols + n), 4 * hid)
            for a in range(3):
                low = cols * (2 - a)
                term = dot(sg[t, low:low + n, lanes], weights[a, lanes, :])
                total = term if total is None else total + term
        return total.astype(BF16)

    def send_input_grad(t, pred):
        send_edges(outer(gx_out.at[t], cols), narrow(gin.at[t]), gx_s.at[t], gx_r.at[t], z - 1, pred)
        send(
            pred,
            lambda: remote(gx_out.at[t], gin.at[t, own1], gx_s.at[t, 2], gx_r.at[t, 2], (z - 1, s, k)),
        )

    arrived(gin.at[1, own1], gx_r.at[1, 2])
    send_vec(0, base)
    narrow_here(gin.at[1], gx_r.at[1])

    @pl.when(inner)
    def _():
        gate_grads(1)
        gx_out[1] = first_conv(1, wxt)

    send_input_grad(1, inner)

    @pl.when(inner)
    def _():
        ghid[own1] = back_conv(1, wht)

    @pl.when(base)
    def _():
        gate_grads(1)
        ghid[own1] = first_conv(1, wht)

    send_edges((ghid.at[cols:2 * cols], ghid.at[n:n + cols]), narrow(ghid), gh_s, gh_r, z, inner)
    send_vec(0, z == 1)
    send_vec(2, early)
    send_tile(1, 0, roof)
    send_grads(1, 0, z == 2)

    pl.when(inner)(lambda: arrived(gin.at[0, own1], gx_r.at[0, 2]))
    send_vec(1, z == 1)

    @pl.when(inner)
    def _():
        narrow_here(gin.at[0], gx_r.at[0])
        narrow_here(ghid, gh_r)
        gate_grads(0)
        gx_out[0] = first_conv(0, wxt)

    send_down()
    send_input_grad(0, z >= 2)
    send_grads(1, 0, roof)
    send_grads(1, 1, z >= 2)
    send_grads(0, 0, z >= 2)
    send_grads(0, 1, z >= 2)

    pl.when(z >= 2)(turn_patches)

    def grads_here(t, p, lanes):
        arrived(grads_all.at[t, :, lanes], ga_r.at[t, p])

    def vec_here(index):
        arrived(vec_all.at[index], ve_r.at[index])

    def factors_here(t):
        arrived(packed_all.at[t], co_r.at[t])

    def factor(t, g):
        return packed_all[t, :, g * half:(g + 1) * half].astype(F32)

    def put(t, g, value):
        grads_all[t, :, g * half:(g + 1) * half] = (factor(t, g) * value).astype(BF16)

    @pl.when(early)
    def _():
        factors_here(1)
        factors_here(0)
        vec_here(0)
        for g in range(4):
            put(1, g, vec_all[0].astype(F32))

    @pl.when(z >= 2)
    def _():
        grads_here(1, 0, pairs[0])
        grads_here(1, 1, pairs[1])

    for j in range(LINE):
        acc[j] = dot(turned[1, j], grads_all[1])
    for p, lanes in enumerate(pairs):
        @pl.when(early)
        def _():
            if p == 0:
                vec_here(2)
                vec_here(1)
            grad_h = vec_all[1].astype(F32) + vec_all[2].astype(F32)
            grad_c = vec_all[0].astype(F32) * factor(1, 4) + grad_h * factor(0, 4)
            put(0, 2 * p, grad_h if p else grad_c)
            put(0, 2 * p + 1, grad_c)

        pl.when(z >= 2)(lambda: grads_here(0, p, lanes))
        for d in (2, 1, 3, 0):
            j = (me + d) % LINE
            leaving[d, :, lanes] = (
                acc[j, :, lanes] + dot(turned[0, j], grads_all[0, :, lanes])
            ).astype(BF16)
            chip = jnp.where(k == 0, j * LINE + x, y * LINE + j)
            for q in range(2):
                src, dst = leaving.at[d, q * rows:(q + 1) * rows, lanes], landed.at[k, me, :, lanes]
                copy = functools.partial(
                    remote, src, dst, rv_s.at[p, min(d, 1)], rv_r.at[p], (z, chip, q)
                )
                if d == 0:
                    pl.when(k == q)(
                        lambda: pltpu.make_async_copy(src, dst, rv_r.at[p]).start()
                    )
                    pl.when(k != q)(lambda: copy().start())
                else:
                    copy().start()
    for wait in pending:
        wait()
    def final(p):
        wide = slice(2 * p * hid, 2 * (p + 1) * hid)
        return pltpu.make_async_copy(result.at[:, wide], out.at[:, wide], out_sem.at[p])

    for p, lanes in enumerate(pairs):
        arrived(landed.at[:, :, :, lanes], rv_r.at[p])
        for c in range(2):
            for g in (2 * p, 2 * p + 1):
                total = landed[c, 0, :, g * half:(g + 1) * half].astype(F32)
                for i in range(1, LINE):
                    total = total + landed[c, i, :, g * half:(g + 1) * half].astype(F32)
                result[:, g * hid + c * half:g * hid + (c + 1) * half] = total
        final(p).start()
    for p, lanes in enumerate(pairs):
        for ref, sem in ((leaving.at[0, 0:rows, lanes], rv_s.at[p, 0]), (leaving.at[1:4, :, lanes], rv_s.at[p, 1])):
            remote(ref, ref, sem, sem, (z, s, 1 - k)).wait_send()
        final(p).wait()


def on_device(frames, cotangent, first_hidden, first_cell, gate_bias, gate_weight):
    steps, _, tile_rows, cols, hid = frames.shape
    n = tile_rows * cols
    pad = n + 2 * cols
    half = hid // 2
    gates = 4 * hid
    share = 18 * hid // (lax.axis_size("space") * lax.axis_size("batch"))
    block = 2 * share
    vmem = pl.BlockSpec(memory_space=pltpu.VMEM)
    anywhere = pl.BlockSpec(memory_space=pl.ANY)
    dma = pltpu.SemaphoreType.DMA
    scratch = [
        pltpu.VMEM((2, 3, 3, hid, gates // 2), BF16),
        pltpu.VMEM((2, 3, 3, hid, gates // 2), BF16),
        pltpu.VMEM((3, 3 * gates, hid), BF16),
        pltpu.VMEM((3, 3 * gates, hid), BF16),
        pltpu.VMEM((steps, pad + 2 * cols, 3 * hid), BF16),
        pltpu.VMEM((steps, pad + 2 * cols, 3 * hid), BF16),
        pltpu.VMEM((steps, pad, 3 * gates), BF16),
        pltpu.VMEM((n, hid), BF16),
        pltpu.VMEM((pad, gates), F32),
        pltpu.VMEM((5, n, hid), F32),
        pltpu.VMEM((steps, pad, hid), F32),
        pltpu.VMEM((pad, hid), F32),
        pltpu.VMEM((steps, 6, pad, hid), F32),
        pltpu.VMEM((steps, pad, hid), BF16),
        pltpu.VMEM((steps, n, hid), BF16),
        pltpu.VMEM((pad, hid), BF16),
        pltpu.VMEM((steps, 2, 2 * LINE, pad, hid), BF16),
        pltpu.VMEM((18 * hid, n), BF16),
        pltpu.VMEM((steps, LINE, block, 2 * LINE * n), BF16),
        pltpu.VMEM((steps, 2 * LINE * n, gates // 2), BF16),
        pltpu.VMEM((steps, n, 5 * hid), BF16),
        pltpu.VMEM((steps, 2 * LINE * n, 5 * half), BF16),
        pltpu.VMEM((3, 2 * LINE * n, half), BF16),
        pltpu.VMEM((LINE, block, gates // 2), F32),
        pltpu.VMEM((LINE, block, gates // 2), BF16),
        pltpu.VMEM((2, LINE, share, gates // 2), BF16),
        pltpu.VMEM((share, gates), F32),
        dma((2, 2, 4)), dma((2,)),
        dma((steps, 2, 3)), dma((steps, 2)), dma((steps, 2, 2)), dma((steps, 2)),
        dma((2,)), dma((steps, 3)), dma((2,)),
        dma((steps, 2)), dma((steps, 2)), dma((steps,)), dma((3,)), dma((2,)),
        dma((steps, 2, 2)), dma((steps, 2)), dma((2,)), dma((2,)), dma((2,)), dma((steps, 2)),
        dma((steps, 2, 3)), dma((steps, 2)), dma((2, 2)), dma((2,)), dma((steps, 3)), dma((2,)),
        dma((steps, 2)), dma((steps, 2)), dma((steps,)), dma((3,)), dma((1,)), dma((2, 2)), dma((2,)),
    ]
    result = pl.pallas_call(
        kernel,
        out_shape=jax.ShapeDtypeStruct((share, gates), F32),
        in_specs=[anywhere] * 4 + [vmem, anywhere],
        out_specs=anywhere,
        scratch_shapes=scratch,
        compiler_params=pltpu.CompilerParams(
            collective_id=0, has_side_effects=True, vmem_limit_bytes=56 * 2**20
        ),
    )(
        frames.reshape(steps, n, hid),
        cotangent.reshape(steps, n, hid),
        first_hidden.reshape(n, hid),
        first_cell.reshape(n, hid),
        gate_bias,
        gate_weight.reshape(3, 3, 2 * hid, gates),
    )
    return result[None]


def solution(mesh):
    return jax.shard_map(
        on_device,
        mesh=mesh,
        in_specs=(
            P(None, "batch", "space", None, None),
            P(None, "batch", "space", None, None),
            P("section", "batch", "space", None, None),
            P("section", "batch", "space", None, None),
            P("section", None),
            P("section", None, None),
        ),
        out_specs=P("section", ("space", "batch"), None),
        check_vma=False,
    )
```

```python
import functools

import jax
import jax.numpy as jnp
from jax import lax
from jax.experimental import pallas as pl
from jax.experimental.pallas import tpu as pltpu
from jax.sharding import PartitionSpec as P

F32 = jnp.float32
BF16 = jnp.bfloat16
MESH = pl.DeviceIdType.MESH
LINE = 4


def dot(left, right):
    return jnp.dot(left, right, preferred_element_type=F32)


def kernel(
    frames, cotangent, first_hidden, first_cell, bias, weight, out,
    wx, wh, wxt, wht, sx, sh, sg, top_hidden, preact, gates, cells, carry, coef, gin, gx_out, ghid,
    tiles_all, flipped, turned, grads_all, packed, packed_all, vec_all, acc, leaving, landed, result,
    w_sem, in_sem, sx_r, sx_f, sh_r, sh_f, c_r, gx_r, gh_r, ti_r, ga_r, co_r, ve_r, rv_r,
    fr_s, fr_f, fh_s, fh_f, fc_s, ct_s, sx_s, sx_fs, sh_s, sh_fs, gx_s, gh_s, ti_s, ga_s, co_s, ve_s, vd_s, rv_s, out_sem,
):
    z, s, k = lax.axis_index("section"), lax.axis_index("space"), lax.axis_index("batch")
    y, x = s // LINE, s % LINE
    sections, tiles = lax.axis_size("section"), lax.axis_size("space")
    cols = 32
    n = first_cell.shape[0]
    hid = first_cell.shape[1]
    half = hid // 2
    gate_half = 4 * half
    own2, above2, below2 = slice(2 * cols, 2 * cols + n), slice(0, 2 * cols), slice(2 * cols + n, 4 * cols + n)
    near = slice(cols, 2 * cols), slice(2 * cols + n, 3 * cols + n)
    far = slice(0, cols), slice(3 * cols + n, 4 * cols + n)
    own1, above1, below1 = slice(cols, cols + n), slice(0, cols), slice(cols + n, 2 * cols + n)
    centre = slice(hid, 2 * hid)
    top, bottom, base, roof = s == 0, s == tiles - 1, z == 0, z == sections - 1
    inner = jnp.logical_not(base)
    pending = []

    def send(pred, make):
        if pred is None:
            make().start()
            pending.append(lambda: make().wait_send())
        else:
            ask = pred if callable(pred) else lambda: pred
            pl.when(ask())(lambda: make().start())
            pending.append(lambda: pl.when(ask())(lambda: make().wait_send()))

    def remote(src, dst, send_sem, recv_sem, device):
        return pltpu.make_async_remote_copy(
            src_ref=src, dst_ref=dst, send_sem=send_sem, recv_sem=recv_sem,
            device_id=device, device_id_type=MESH,
        )

    def arrived(dst, recv_sem):
        remote(dst, dst, recv_sem, recv_sem, (z, s, 1 - k)).wait_recv()

    loads = {}
    for part, buffer in ((0, wx), (1, wh)):
        for c in range(2):
            for g in range(4):
                loads[part, c, g] = pltpu.make_async_copy(
                    weight.at[:, :, part * hid:(part + 1) * hid, pl.ds(g * hid + c * half, half)],
                    buffer.at[c, :, :, :, g * half:(g + 1) * half],
                    w_sem.at[part, c, g],
                )

    def weights_here(part):
        for c in range(2):
            for g in range(4):
                loads[part, c, g].wait()

    barrier = pltpu.get_barrier_semaphore()

    def greet(partners):
        for pred, device in partners:
            call = functools.partial(
                pl.semaphore_signal, barrier, inc=1, device_id=device, device_id_type=MESH
            )
            if pred is None:
                call()
            else:
                pl.when(pred)(call)

    def count(partners):
        total = 0
        for pred, _ in partners:
            total = total + (1 if pred is None else jnp.where(pred, 1, 0))
        return total

    plane = [(jnp.logical_not(top), (z, s - 1, k)), (jnp.logical_not(bottom), (z, s + 1, k))]
    plane.append((None, (z, s, 1 - k)))
    for d in range(1, LINE):
        for core in range(2):
            plane.append((None, (z, y * LINE + (x + d) % LINE, core)))
            plane.append((None, (z, ((y + d) % LINE) * LINE + x, core)))

    def section_at(step, ok):
        return [
            (ok, (z + step, s, k)),
            (ok & (s > 0), (z + step, s - 1, k)),
            (ok & (s < tiles - 1), (z + step, s + 1, k)),
        ]

    below, above = section_at(-1, z > 0), section_at(1, z < sections - 1)
    group = [
        (base, (z + 1, jnp.where(k == 0, y * LINE + j, j * LINE + x), core))
        for j in range(LINE) for core in range(2)
    ]
    greet(plane)

    half_lanes = [slice(hid + c * half, hid + (c + 1) * half) for c in range(2)]
    own_hidden = pltpu.make_async_copy(first_hidden, sh.at[0, own2, centre], in_sem.at[0])
    own_cell = pltpu.make_async_copy(first_cell, cells.at[0, own1], in_sem.at[1])
    own_hidden.start()

    @pl.when(base)
    def _():
        for t in range(2):
            for c in range(2):
                pltpu.make_async_copy(
                    frames.at[t, :, pl.ds(c * half, half)], sx.at[t, own2, half_lanes[c]], sx_r.at[t, c, 2]
                ).start()

    own_cell.start()

    @pl.when(roof)
    def _():
        for t in range(2):
            pltpu.make_async_copy(cotangent.at[t], gin.at[t, own1], gx_r.at[t, 2]).start()

    for part in (1, 0):
        for c in range(2):
            for g in range(4):
                loads[part, c, g].start()

    def clear(wide, narrow):
        for t in range(2):
            sx[t, wide, :] = jnp.zeros((2 * cols, 3 * hid), BF16)
            sh[t, wide, :] = jnp.zeros((2 * cols, 3 * hid), BF16)
            gin[t, narrow] = jnp.zeros((cols, hid), BF16)
        cells[0, narrow] = jnp.zeros((cols, hid), F32)
        ghid[narrow] = jnp.zeros((cols, hid), BF16)

    pl.when(top)(lambda: clear(above2, above1))
    pl.when(bottom)(lambda: clear(below2, below1))

    pl.semaphore_wait(
        barrier, count(plane) + count(below) + jnp.where(z == 1, len(group), 0)
    )

    def send_edges(src, dst, send_sems, recv_sems, section, pred):
        edges(lambda: (src, dst, send_sems, recv_sems), section, pred)

    def edges(parts, section, pred):
        def up():
            return s > 0 if pred is None else (s > 0) & pred

        def down():
            return s < tiles - 1 if pred is None else (s < tiles - 1) & pred

        def make(end, device):
            src, dst, send_sems, recv_sems = parts()
            return remote(src[end], dst[1 - end], send_sems.at[end], recv_sems.at[1 - end], device)

        send(up, lambda: make(0, (section, s - 1, k)))
        send(down, lambda: make(1, (section, s + 1, k)))

    def outer(ref, width):
        return ref.at[0:width], ref.at[n - width:n]

    def beyond(ref):
        return ref.at[cols:2 * cols], ref.at[n - 2 * cols:n - cols]

    def narrow(ref):
        return ref.at[above1], ref.at[below1]

    def at_rows(buffer, t, rows, lanes):
        return buffer.at[t, rows[0], lanes], buffer.at[t, rows[1], lanes]

    def halves(ref, c):
        return ref.at[0:cols, pl.ds(c * half, half)], ref.at[n - cols:n, pl.ds(c * half, half)]

    send_edges(outer(first_hidden, cols), at_rows(sh, 0, near, centre), fh_s, sh_r.at[0, 0], z, None)

    def send_frames(t):
        for c in range(2):
            send_edges(
                halves(frames.at[t], c), at_rows(sx, t, near, half_lanes[c]),
                fr_s.at[t, c], sx_r.at[t, c], z, base,
            )

    send_frames(0)
    greet(above)
    greet(group)
    greet(below)
    send_edges(beyond(first_hidden), at_rows(sh, 0, far, centre), fh_f, sh_f.at[0], z, None)
    send_edges(outer(first_cell, cols), narrow(cells.at[0]), fc_s, c_r, z, None)
    send_edges(beyond(frames.at[0]), at_rows(sx, 0, far, centre), fr_f.at[0], sx_f.at[0], z, base)
    send_frames(1)
    send_edges(beyond(frames.at[1]), at_rows(sx, 1, far, centre), fr_f.at[1], sx_f.at[1], z, base)
    for t in range(2):
        send_edges(outer(cotangent.at[t], cols), narrow(gin.at[t]), ct_s.at[t], gx_r.at[t], z, roof)

    def spread_value(value, width):
        count = value.shape[0]
        column = lax.broadcasted_iota(jnp.int32, (count, width), 0) % cols
        left = jnp.where(column == 0, 0.0, pltpu.roll(value, 1, 0)).astype(BF16)
        right = jnp.where(column == cols - 1, 0.0, pltpu.roll(value, count - 1, 0)).astype(BF16)
        return left, right

    def spread(buffer, t, rows, width):
        left, right = spread_value(buffer[t, rows, width:2 * width].astype(F32), width)
        buffer[t, rows, 0:width] = left
        buffer[t, rows, 2 * width:3 * width] = right

    def when_edges(first, second):
        pl.when(jnp.logical_not(top))(first)
        pl.when(jnp.logical_not(bottom))(second)

    def near_here(buffer, t, recv_sems, lanes):
        def here(index):
            for c, part in enumerate(lanes):
                arrived(buffer.at[t, near[index], part], recv_sems.at[c, index])
            spread(buffer, t, near[index], hid)

        when_edges(lambda: here(0), lambda: here(1))

    def far_here(buffer, t, recv_sems):
        def here(index):
            arrived(buffer.at[t, far[index], centre], recv_sems.at[index])
            spread(buffer, t, far[index], hid)

        when_edges(lambda: here(0), lambda: here(1))

    def narrow_here(ref, recv_sems):
        when_edges(
            lambda: arrived(ref.at[above1], recv_sems.at[0]),
            lambda: arrived(ref.at[below1], recv_sems.at[1]),
        )

    def conv(buffer, t, weights, c, offsets):
        total = None
        for a in offsets:
            term = dot(
                buffer[t, cols * (a + 1):cols * (a + 1) + n, :],
                weights[c, a].reshape(3 * hid, gate_half),
            )
            total = term if total is None else total + term
        return total

    def conv_all(buffer, t, weights, c, offsets):
        total = None
        for a in offsets:
            term = dot(
                buffer[t, cols * a:cols * (a + 2) + n, :],
                weights[c, a].reshape(3 * hid, gate_half),
            )
            total = term if total is None else total + term
        return total

    def conv_beside(t, c):
        total = None
        for buffer, weights in ((sh, wh), (sx, wx)):
            for a in range(3):
                low = cols * (a + 1) + n
                cells_in = jnp.concatenate(
                    [buffer[t, cols * a:cols * (a + 1), :], buffer[t, low:low + cols, :]], axis=0
                )
                term = dot(cells_in, weights[c, a].reshape(3 * hid, gate_half))
                total = term if total is None else total + term
        return total

    def bias_of(c):
        return jnp.concatenate(
            [bias[0:1, g * hid + c * half:g * hid + (c + 1) * half] for g in range(4)], axis=1
        )

    def activate(now, old):
        i_gate = jax.nn.sigmoid(now[:, 0:half])
        f_gate = jax.nn.sigmoid(now[:, half:2 * half])
        o_gate = jax.nn.sigmoid(now[:, 2 * half:3 * half])
        cand = jnp.tanh(now[:, 3 * half:])
        new = f_gate * old + i_gate * cand
        return i_gate, f_gate, o_gate, cand, new, jnp.tanh(new)

    def factors(i_gate, f_gate, o_gate, cand, squash, old):
        return (
            o_gate * (1.0 - squash * squash),
            cand * i_gate * (1.0 - i_gate),
            old * f_gate * (1.0 - f_gate),
            squash * o_gate * (1.0 - o_gate),
            i_gate * (1.0 - cand * cand),
            f_gate,
        )

    def turn_weights(source, target):
        def one(a, carried):
            for b in range(3):
                for c in range(2):
                    start = (2 - b) * 4 * hid + c * gate_half
                    target[a, start:start + gate_half, :] = source[c, a, b].T
            return carried

        lax.fori_loop(0, 3, one, 0)

    def turn_all_weights():
        turn_weights(wh, wht)
        pl.when(inner)(lambda: turn_weights(wx, wxt))

    def spread_to_group(pred, view, seven, send_sem, recv_sem):
        def go():
            for d in (2, 1, 3, 0):
                for c in range(2):
                    there = ((x if c == 0 else y) + d) % LINE
                    chip = y * LINE + there if c == 0 else there * LINE + x
                    src, dst = view(c, 2 * (x if c == 0 else y) + k)
                    copy = functools.partial(remote, src, dst, send_sem(), recv_sem(), (z, chip, c))
                    if d == 0:
                        pl.when(k == c)(lambda: pltpu.make_async_copy(src, dst, recv_sem()).start())
                        pl.when(k != c)(lambda: copy().start())
                    else:
                        copy().start()

        def done():
            remote(seven(), seven(), send_sem(), recv_sem(), (z, s, 1 - k)).wait_send()

        pl.when(pred)(go)
        pending.append(lambda: pl.when(pred)(done))

    def rows_of(slot):
        return pl.ds(pl.multiple_of(slot * n, n), n)

    most = slice(0, 7 * n)

    def send_tile(t, part, pred):
        spread_to_group(
            pred,
            lambda c, slot: (
                (sh if part else sx).at[t, cols:3 * cols + n, centre], tiles_all.at[t, part, slot]
            ),
            lambda: tiles_all.at[t, part, 0:7],
            lambda: ti_s.at[t, part], lambda: ti_r.at[t, part],
        )

    pairs = [slice(p * 2 * half, (p + 1) * 2 * half) for p in range(2)]

    def send_grads(t, p, pred):
        lanes = pairs[p]

        def view(c, slot):
            at = 4 * hid + c * gate_half
            src = sg.at[t, own1, at + lanes.start:at + lanes.stop]
            return src, grads_all.at[t, rows_of(slot), lanes]

        spread_to_group(
            pred, view, lambda: grads_all.at[t, most, lanes],
            lambda: ga_s.at[t, p], lambda: ga_r.at[t, p],
        )

    early = z < 2

    def send_factors(t):
        def view(c, slot):
            src = packed.at[t, :, c * 5 * half:(c + 1) * 5 * half]
            return src, packed_all.at[t, rows_of(slot), :]

        spread_to_group(
            early, view, lambda: packed_all.at[t, most], lambda: co_s.at[t], lambda: co_r.at[t]
        )

    def pack_factors():
        for c in range(2):
            chan = slice(c * half, (c + 1) * half)
            for t in range(2):
                first = coef[t, 0, own1, chan]
                for g in range(5):
                    if g == 4:
                        value = first * coef[t, 5, own1, chan] if t == 1 else first
                    else:
                        value = coef[t, 1 + g, own1, chan]
                        if t == 1 and g != 2:
                            value = value * first
                    at = (c * 5 + g) * half
                    packed[t, :, at:at + half] = value.astype(BF16)

    def send_vec(index, pred):
        def view(c, slot):
            chan = slice(c * half, (c + 1) * half)
            src = ghid.at[own1, chan] if index == 2 else gin.at[1 - index, own1, chan]
            return src, vec_all.at[index, rows_of(slot), :]

        spread_to_group(
            pred, view, lambda: vec_all.at[index, most], lambda: ve_s.at[index], lambda: ve_r.at[index]
        )

    def send_down():
        def go():
            for d in (2, 1, 3, 0):
                for c in range(2):
                    there = ((x if c == 0 else y) + d) % LINE
                    chip = y * LINE + there if c == 0 else there * LINE + x
                    remote(
                        gx_out.at[0, :, c * half:(c + 1) * half],
                        vec_all.at[1, rows_of(2 * (x if c == 0 else y) + k), :],
                        vd_s.at[0], ve_r.at[1], (z - 1, chip, c),
                    ).start()

        def done():
            remote(vec_all.at[1], vec_all.at[1], vd_s.at[0], ve_r.at[1], (z, s, 1 - k)).wait_send()

        pl.when(z == 1)(go)
        pending.append(lambda: pl.when(z == 1)(done))

    rows = out.shape[0]
    block = 2 * rows
    me = jnp.where(k == 0, y, x)

    def turn_patches():
        for t in range(2):
            for part in range(2):
                arrived(tiles_all.at[t, part], ti_r.at[t, part])

            def one(slot, carried):
                for part in range(2):
                    tile = tiles_all[t, part, slot]
                    left, right = spread_value(tile.astype(F32), hid)
                    for b, moved in enumerate((left, tile, right)):
                        for a in range(3):
                            at = (a * 3 + b) * 2 * hid + part * hid
                            flipped[at:at + hid, :] = moved[cols * a:cols * a + n, :].T
                for j in range(LINE):
                    chip = jnp.where(k == 0, j * LINE + x, y * LINE + j)
                    turned[t, j, :, pl.ds(pl.multiple_of(slot * n, n), n)] = flipped[
                        pl.ds(pl.multiple_of(chip * block, 32), block), :
                    ]
                return carried

            lax.fori_loop(0, 2 * LINE, one, 0)

    @pl.when(z >= 2)
    def _():
        weights_here(1)
        weights_here(0)
        turn_all_weights()

    not_roof = jnp.logical_not(roof)
    z_up = z + 1

    def save(t, into, values, old, chan):
        i_gate, f_gate, o_gate, cand, squash = values
        for index, value in enumerate(factors(i_gate, f_gate, o_gate, cand, squash, old)):
            for cells_to, cells_from in into:
                coef[t, index, cells_to, chan] = value[cells_from]

    def x_here(t):
        for c in range(2):
            arrived(sx.at[t, own2, half_lanes[c]], sx_r.at[t, c, 2])
        spread(sx, t, own2, hid)

    def add(c, term):
        preact[0:n, c * gate_half:(c + 1) * gate_half] += term

    def own_rows(t):
        hidden_lanes = (centre,) if t == 0 else half_lanes
        part_sums = [conv(sh, t, wh, c, (1,)) + bias_of(c) for c in range(2)]
        for c in range(2):
            preact[0:n, c * gate_half:(c + 1) * gate_half] = part_sums[c]

        def x_middle():
            x_here(t)
            for c in range(2):
                add(c, conv(sx, t, wx, c, (1,)))

        def x_edges():
            near_here(sx, t, sx_r.at[t], half_lanes)

        def h_edges():
            near_here(sh, t, sh_r.at[t], hidden_lanes)

        def h_outer():
            for c in range(2):
                add(c, conv(sh, t, wh, c, (0, 2)))

        @pl.when(base)
        def _():
            if t == 0:
                weights_here(0)
            x_middle()
            if t == 1:
                x_edges()
                for c in range(2):
                    add(c, conv(sx, t, wx, c, (0, 2)))
                h_edges()

        if t == 0:
            h_edges()
            h_outer()
            send_tile(0, 1, inner)
            pl.when(z == 1)(lambda: weights_here(0))

        @pl.when(inner)
        def _():
            if t == 1:
                h_edges()
                h_outer()
            x_middle()
            if t == 1:
                x_edges()

        if t == 0:
            x_edges()
            own_cell.wait()
            pl.when(not_roof)(lambda: pl.semaphore_wait(barrier, count(above)))

        def finish(buffer, weights, c):
            chan, lanes = slice(c * half, (c + 1) * half), half_lanes[c]
            now = preact[0:n, c * gate_half:(c + 1) * gate_half] + conv(buffer, t, weights, c, (0, 2))
            i_gate, f_gate, o_gate, cand, new, squash = activate(now, cells[t, own1, chan])
            hidden = (o_gate * squash).astype(BF16)
            if t == 0:
                sh[1, own2, lanes] = hidden
                cells[1, own1, chan] = new
            else:
                top_hidden[:, chan] = hidden
            for index, value in enumerate((i_gate, f_gate, o_gate, cand, squash)):
                gates[index, :, chan] = value

        for c in range(2):
            chan, lanes = slice(c * half, (c + 1) * half), half_lanes[c]
            if t == 0:
                finish(sx, wx, c)
                whole = sh.at[1, own2, lanes]
                ends = sh.at[1, 2 * cols:3 * cols, lanes], sh.at[1, n + cols:n + 2 * cols, lanes]
            else:
                pl.when(base)(lambda c=c: finish(sh, wh, c))
                pl.when(inner)(lambda c=c: finish(sx, wx, c))
                whole = top_hidden.at[:, chan]
                ends = top_hidden.at[0:cols, chan], top_hidden.at[n - cols:n, chan]
            edges(
                lambda ends=ends, lanes=lanes, c=c: (
                    ends, at_rows(sx, t, near, lanes), sx_s.at[t, c], sx_r.at[t, c]
                ),
                z_up, not_roof,
            )
            send(
                not_roof,
                lambda whole=whole, lanes=lanes, c=c: remote(
                    whole, sx.at[t, own2, lanes], sx_s.at[t, c, 2], sx_r.at[t, c, 2], (z_up, s, k)
                ),
            )
            if t == 0:
                send_edges(ends, at_rows(sh, 1, near, lanes), sh_s.at[c], sh_r.at[1, c], z, None)
        if t == 0:
            ends = sh.at[1, 3 * cols:4 * cols, centre], sh.at[1, n:n + cols, centre]
            send_edges(ends, at_rows(sh, 1, far, centre), sh_fs, sh_f.at[1], z, None)
        else:
            ends = beyond(top_hidden)
        last = ends
        edges(
            lambda: (last, at_rows(sx, t, far, centre), sx_fs.at[t], sx_f.at[t]), z_up, not_roof
        )
        for c in range(2):
            chan = slice(c * half, (c + 1) * half)
            save(
                t, ((own1, slice(0, n)),),
                tuple(gates[index, :, chan] for index in range(5)), cells[t, own1, chan], chan,
            )

    def beside_rows(t):
        if t == 0:
            narrow_here(cells.at[0], c_r)
        far_here(sh, t, sh_f.at[t])
        far_here(sx, t, sx_f.at[t])
        for c in range(2):
            chan = slice(c * half, (c + 1) * half)
            old = jnp.concatenate([cells[t, above1, chan], cells[t, below1, chan]], axis=0)
            i_gate, f_gate, o_gate, cand, new, squash = activate(conv_beside(t, c) + bias_of(c), old)
            if t == 0:
                cells[1, above1, chan] = new[0:cols]
                cells[1, below1, chan] = new[cols:]
            save(
                t, ((above1, slice(0, cols)), (below1, slice(cols, 2 * cols))),
                (i_gate, f_gate, o_gate, cand, squash), old, chan,
            )

    def add_all(buffer, weights, offsets):
        for c in range(2):
            preact[:, c * gate_half:(c + 1) * gate_half] += conv_all(buffer, 1, weights, c, offsets)

    def all_rows_h():
        near_here(sh, 1, sh_r.at[1], half_lanes)
        for c in range(2):
            preact[:, c * gate_half:(c + 1) * gate_half] = conv_all(sh, 1, wh, c, (1,)) + bias_of(c)
        far_here(sh, 1, sh_f.at[1])
        add_all(sh, wh, (0, 2))

    def all_rows_x():
        x_here(1)
        near_here(sx, 1, sx_r.at[1], half_lanes)
        add_all(sx, wx, (1,))
        far_here(sx, 1, sx_f.at[1])
        for c in range(2):
            chan = slice(c * half, (c + 1) * half)
            now = preact[:, c * gate_half:(c + 1) * gate_half] + conv_all(sx, 1, wx, c, (0, 2))
            old = cells[1, :, chan]
            i_gate, f_gate, o_gate, cand, new, squash = activate(now, old)
            save(
                1, ((slice(0, n + 2 * cols), slice(0, n + 2 * cols)),),
                (i_gate, f_gate, o_gate, cand, squash), old, chan,
            )

    own_hidden.wait()
    spread(sh, 0, own2, hid)
    pl.when(z < 2)(lambda: weights_here(1))
    own_rows(0)
    send_tile(0, 0, inner)
    spread(sh, 1, own2, hid)

    pl.when(not_roof)(lambda: own_rows(1))
    pl.when(early)(pack_factors)
    send_tile(0, 1, base)
    send_tile(0, 0, base)
    send_tile(1, 1, not_roof)
    send_tile(1, 0, not_roof)
    send_factors(1)
    send_factors(0)

    @pl.when(not_roof)
    def _():
        beside_rows(0)
        beside_rows(1)

    @pl.when(roof)
    def _():
        beside_rows(0)
        all_rows_h()

    send_tile(1, 1, roof)
    pl.when(roof)(all_rows_x)

    def blank(outside):
        coef[:, :, outside, :] = jnp.zeros((2, 6, cols, hid), F32)

    pl.when(top)(lambda: blank(above1))
    pl.when(bottom)(lambda: blank(below1))

    pl.when(z < 2)(turn_all_weights)
    pl.when(z < 2)(turn_patches)

    def back_conv(t, weights):
        total = None
        for a in range(3):
            term = dot(sg[t, cols * (2 - a):cols * (2 - a) + n, :], weights[a])
            total = term if total is None else total + term
        return total.astype(BF16)

    def gate_grads(t):
        for c in range(2):
            chan = slice(c * half, (c + 1) * half)
            grad_h = gin[t, :, chan].astype(F32)
            if t == 0:
                grad_h = grad_h + ghid[:, chan].astype(F32)
            grad_c = grad_h * coef[t, 0, :, chan]
            if t == 0:
                grad_c = grad_c + carry[:, chan]
            for g, value in enumerate((
                grad_c * coef[t, 1, :, chan],
                grad_c * coef[t, 2, :, chan],
                grad_h * coef[t, 3, :, chan],
                grad_c * coef[t, 4, :, chan],
            )):
                at = 4 * hid + c * gate_half + g * half
                sg[t, :, at:at + half] = value.astype(BF16)
            if t == 1:
                carry[:, chan] = grad_c * coef[t, 5, :, chan]

    def first_conv(t, weights):
        total = None
        for b in (1, 0, 2):
            lanes = slice(b * 4 * hid, (b + 1) * 4 * hid)
            if b == 0:
                spread(sg, t, slice(0, 2 * cols + n), 4 * hid)
            for a in range(3):
                low = cols * (2 - a)
                term = dot(sg[t, low:low + n, lanes], weights[a, lanes, :])
                total = term if total is None else total + term
        return total.astype(BF16)

    def send_input_grad(t, pred):
        send_edges(outer(gx_out.at[t], cols), narrow(gin.at[t]), gx_s.at[t], gx_r.at[t], z - 1, pred)
        send(
            pred,
            lambda: remote(gx_out.at[t], gin.at[t, own1], gx_s.at[t, 2], gx_r.at[t, 2], (z - 1, s, k)),
        )

    arrived(gin.at[1, own1], gx_r.at[1, 2])
    send_vec(0, base)
    narrow_here(gin.at[1], gx_r.at[1])

    @pl.when(inner)
    def _():
        gate_grads(1)
        gx_out[1] = first_conv(1, wxt)

    send_input_grad(1, inner)

    @pl.when(inner)
    def _():
        ghid[own1] = back_conv(1, wht)

    @pl.when(base)
    def _():
        gate_grads(1)
        ghid[own1] = first_conv(1, wht)

    send_edges((ghid.at[cols:2 * cols], ghid.at[n:n + cols]), narrow(ghid), gh_s, gh_r, z, inner)
    send_vec(0, z == 1)
    send_vec(2, early)
    send_tile(1, 0, roof)
    send_grads(1, 0, z == 2)

    pl.when(inner)(lambda: arrived(gin.at[0, own1], gx_r.at[0, 2]))

    @pl.when(inner)
    def _():
        narrow_here(gin.at[0], gx_r.at[0])
        narrow_here(ghid, gh_r)
        gate_grads(0)
        gx_out[0] = first_conv(0, wxt)

    send_down()
    send_vec(1, z == 1)
    send_input_grad(0, z >= 2)
    send_grads(1, 0, roof)
    send_grads(1, 1, z >= 2)
    send_grads(0, 0, z >= 2)
    send_grads(0, 1, z >= 2)

    pl.when(z >= 2)(turn_patches)

    def grads_here(t, p, lanes):
        arrived(grads_all.at[t, :, lanes], ga_r.at[t, p])

    def vec_here(index):
        arrived(vec_all.at[index], ve_r.at[index])

    def factors_here(t):
        arrived(packed_all.at[t], co_r.at[t])

    def factor(t, g):
        return packed_all[t, :, g * half:(g + 1) * half].astype(F32)

    def put(t, g, value):
        grads_all[t, :, g * half:(g + 1) * half] = (factor(t, g) * value).astype(BF16)

    @pl.when(early)
    def _():
        factors_here(1)
        factors_here(0)
        vec_here(0)
        for g in range(4):
            put(1, g, vec_all[0].astype(F32))

    @pl.when(z >= 2)
    def _():
        grads_here(1, 0, pairs[0])
        grads_here(1, 1, pairs[1])

    for j in range(LINE):
        acc[j] = dot(turned[1, j], grads_all[1])
    for p, lanes in enumerate(pairs):
        @pl.when(early)
        def _():
            if p == 0:
                vec_here(2)
                vec_here(1)
            grad_h = vec_all[1].astype(F32) + vec_all[2].astype(F32)
            grad_c = vec_all[0].astype(F32) * factor(1, 4) + grad_h * factor(0, 4)
            put(0, 2 * p, grad_h if p else grad_c)
            put(0, 2 * p + 1, grad_c)

        pl.when(z >= 2)(lambda: grads_here(0, p, lanes))
        for d in (2, 1, 3, 0):
            j = (me + d) % LINE
            leaving[d, :, lanes] = (
                acc[j, :, lanes] + dot(turned[0, j], grads_all[0, :, lanes])
            ).astype(BF16)
            chip = jnp.where(k == 0, j * LINE + x, y * LINE + j)
            for q in range(2):
                src, dst = leaving.at[d, q * rows:(q + 1) * rows, lanes], landed.at[k, me, :, lanes]
                copy = functools.partial(
                    remote, src, dst, rv_s.at[p, min(d, 1)], rv_r.at[p], (z, chip, q)
                )
                if d == 0:
                    pl.when(k == q)(
                        lambda: pltpu.make_async_copy(src, dst, rv_r.at[p]).start()
                    )
                    pl.when(k != q)(lambda: copy().start())
                else:
                    copy().start()
    for wait in pending:
        wait()
    def final(p):
        wide = slice(2 * p * hid, 2 * (p + 1) * hid)
        return pltpu.make_async_copy(result.at[:, wide], out.at[:, wide], out_sem.at[p])

    for p, lanes in enumerate(pairs):
        arrived(landed.at[:, :, :, lanes], rv_r.at[p])
        for c in range(2):
            for g in (2 * p, 2 * p + 1):
                total = landed[c, 0, :, g * half:(g + 1) * half].astype(F32)
                for i in range(1, LINE):
                    total = total + landed[c, i, :, g * half:(g + 1) * half].astype(F32)
                result[:, g * hid + c * half:g * hid + (c + 1) * half] = total
        final(p).start()
    for p, lanes in enumerate(pairs):
        for ref, sem in ((leaving.at[0, 0:rows, lanes], rv_s.at[p, 0]), (leaving.at[1:4, :, lanes], rv_s.at[p, 1])):
            remote(ref, ref, sem, sem, (z, s, 1 - k)).wait_send()
        final(p).wait()


def on_device(frames, cotangent, first_hidden, first_cell, gate_bias, gate_weight):
    steps, _, tile_rows, cols, hid = frames.shape
    n = tile_rows * cols
    pad = n + 2 * cols
    half = hid // 2
    gates = 4 * hid
    share = 18 * hid // (lax.axis_size("space") * lax.axis_size("batch"))
    block = 2 * share
    vmem = pl.BlockSpec(memory_space=pltpu.VMEM)
    anywhere = pl.BlockSpec(memory_space=pl.ANY)
    dma = pltpu.SemaphoreType.DMA
    scratch = [
        pltpu.VMEM((2, 3, 3, hid, gates // 2), BF16),
        pltpu.VMEM((2, 3, 3, hid, gates // 2), BF16),
        pltpu.VMEM((3, 3 * gates, hid), BF16),
        pltpu.VMEM((3, 3 * gates, hid), BF16),
        pltpu.VMEM((steps, pad + 2 * cols, 3 * hid), BF16),
        pltpu.VMEM((steps, pad + 2 * cols, 3 * hid), BF16),
        pltpu.VMEM((steps, pad, 3 * gates), BF16),
        pltpu.VMEM((n, hid), BF16),
        pltpu.VMEM((pad, gates), F32),
        pltpu.VMEM((5, n, hid), F32),
        pltpu.VMEM((steps, pad, hid), F32),
        pltpu.VMEM((pad, hid), F32),
        pltpu.VMEM((steps, 6, pad, hid), F32),
        pltpu.VMEM((steps, pad, hid), BF16),
        pltpu.VMEM((steps, n, hid), BF16),
        pltpu.VMEM((pad, hid), BF16),
        pltpu.VMEM((steps, 2, 2 * LINE, pad, hid), BF16),
        pltpu.VMEM((18 * hid, n), BF16),
        pltpu.VMEM((steps, LINE, block, 2 * LINE * n), BF16),
        pltpu.VMEM((steps, 2 * LINE * n, gates // 2), BF16),
        pltpu.VMEM((steps, n, 5 * hid), BF16),
        pltpu.VMEM((steps, 2 * LINE * n, 5 * half), BF16),
        pltpu.VMEM((3, 2 * LINE * n, half), BF16),
        pltpu.VMEM((LINE, block, gates // 2), F32),
        pltpu.VMEM((LINE, block, gates // 2), BF16),
        pltpu.VMEM((2, LINE, share, gates // 2), BF16),
        pltpu.VMEM((share, gates), F32),
        dma((2, 2, 4)), dma((2,)),
        dma((steps, 2, 3)), dma((steps, 2)), dma((steps, 2, 2)), dma((steps, 2)),
        dma((2,)), dma((steps, 3)), dma((2,)),
        dma((steps, 2)), dma((steps, 2)), dma((steps,)), dma((3,)), dma((2,)),
        dma((steps, 2, 2)), dma((steps, 2)), dma((2,)), dma((2,)), dma((2,)), dma((steps, 2)),
        dma((steps, 2, 3)), dma((steps, 2)), dma((2, 2)), dma((2,)), dma((steps, 3)), dma((2,)),
        dma((steps, 2)), dma((steps, 2)), dma((steps,)), dma((3,)), dma((1,)), dma((2, 2)), dma((2,)),
    ]
    result = pl.pallas_call(
        kernel,
        out_shape=jax.ShapeDtypeStruct((share, gates), F32),
        in_specs=[anywhere] * 4 + [vmem, anywhere],
        out_specs=anywhere,
        scratch_shapes=scratch,
        compiler_params=pltpu.CompilerParams(
            collective_id=0, has_side_effects=True, vmem_limit_bytes=56 * 2**20
        ),
    )(
        frames.reshape(steps, n, hid),
        cotangent.reshape(steps, n, hid),
        first_hidden.reshape(n, hid),
        first_cell.reshape(n, hid),
        gate_bias,
        gate_weight.reshape(3, 3, 2 * hid, gates),
    )
    return result[None]


def solution(mesh):
    return jax.shard_map(
        on_device,
        mesh=mesh,
        in_specs=(
            P(None, "batch", "space", None, None),
            P(None, "batch", "space", None, None),
            P("section", "batch", "space", None, None),
            P("section", "batch", "space", None, None),
            P("section", None),
            P("section", None, None),
        ),
        out_specs=P("section", ("space", "batch"), None),
        check_vma=False,
    )
```

```python
import functools

import jax
import jax.numpy as jnp
from jax import lax
from jax.experimental import pallas as pl
from jax.experimental.pallas import tpu as pltpu
from jax.sharding import PartitionSpec as P

F32 = jnp.float32
BF16 = jnp.bfloat16
MESH = pl.DeviceIdType.MESH
LINE = 4


def dot(left, right):
    return jnp.dot(left, right, preferred_element_type=F32)


def kernel(
    frames, cotangent, first_hidden, first_cell, bias, weight, out,
    wx, wh, wxt, wht, sx, sh, sg, top_hidden, preact, gates, cells, carry, coef, gin, gx_out, ghid,
    tiles_all, flipped, turned, grads_all, packed, packed_all, vec_all, acc, leaving, landed, result,
    w_sem, in_sem, sx_r, sx_f, sh_r, sh_f, c_r, gx_r, gh_r, ti_r, ga_r, co_r, ve_r, rv_r,
    fr_s, fr_f, fh_s, fh_f, fc_s, ct_s, sx_s, sx_fs, sh_s, sh_fs, gx_s, gh_s, ti_s, ga_s, co_s, ve_s, vd_s, rv_s, out_sem,
):
    z, s, k = lax.axis_index("section"), lax.axis_index("space"), lax.axis_index("batch")
    y, x = s // LINE, s % LINE
    sections, tiles = lax.axis_size("section"), lax.axis_size("space")
    cols = 32
    n = first_cell.shape[0]
    hid = first_cell.shape[1]
    half = hid // 2
    gate_half = 4 * half
    own2, above2, below2 = slice(2 * cols, 2 * cols + n), slice(0, 2 * cols), slice(2 * cols + n, 4 * cols + n)
    near = slice(cols, 2 * cols), slice(2 * cols + n, 3 * cols + n)
    far = slice(0, cols), slice(3 * cols + n, 4 * cols + n)
    own1, above1, below1 = slice(cols, cols + n), slice(0, cols), slice(cols + n, 2 * cols + n)
    centre = slice(hid, 2 * hid)
    top, bottom, base, roof = s == 0, s == tiles - 1, z == 0, z == sections - 1
    inner = jnp.logical_not(base)
    pending = []

    def send(pred, make):
        if pred is None:
            make().start()
            pending.append(lambda: make().wait_send())
        else:
            ask = pred if callable(pred) else lambda: pred
            pl.when(ask())(lambda: make().start())
            pending.append(lambda: pl.when(ask())(lambda: make().wait_send()))

    def remote(src, dst, send_sem, recv_sem, device):
        return pltpu.make_async_remote_copy(
            src_ref=src, dst_ref=dst, send_sem=send_sem, recv_sem=recv_sem,
            device_id=device, device_id_type=MESH,
        )

    def arrived(dst, recv_sem):
        remote(dst, dst, recv_sem, recv_sem, (z, s, 1 - k)).wait_recv()

    loads = {}
    for part, buffer in ((0, wx), (1, wh)):
        for c in range(2):
            for g in range(4):
                loads[part, c, g] = pltpu.make_async_copy(
                    weight.at[:, :, part * hid:(part + 1) * hid, pl.ds(g * hid + c * half, half)],
                    buffer.at[c, :, :, :, g * half:(g + 1) * half],
                    w_sem.at[part, c, g],
                )

    def weights_here(part):
        for c in range(2):
            for g in range(4):
                loads[part, c, g].wait()

    barrier = pltpu.get_barrier_semaphore()

    def greet(partners):
        for pred, device in partners:
            call = functools.partial(
                pl.semaphore_signal, barrier, inc=1, device_id=device, device_id_type=MESH
            )
            if pred is None:
                call()
            else:
                pl.when(pred)(call)

    def count(partners):
        total = 0
        for pred, _ in partners:
            total = total + (1 if pred is None else jnp.where(pred, 1, 0))
        return total

    plane = [(jnp.logical_not(top), (z, s - 1, k)), (jnp.logical_not(bottom), (z, s + 1, k))]
    plane.append((None, (z, s, 1 - k)))
    for d in range(1, LINE):
        for core in range(2):
            plane.append((None, (z, y * LINE + (x + d) % LINE, core)))
            plane.append((None, (z, ((y + d) % LINE) * LINE + x, core)))

    def section_at(step, ok):
        return [
            (ok, (z + step, s, k)),
            (ok & (s > 0), (z + step, s - 1, k)),
            (ok & (s < tiles - 1), (z + step, s + 1, k)),
        ]

    below, above = section_at(-1, z > 0), section_at(1, z < sections - 1)
    group = [
        (base, (z + 1, jnp.where(k == 0, y * LINE + j, j * LINE + x), core))
        for j in range(LINE) for core in range(2)
    ]
    greet(plane)

    half_lanes = [slice(hid + c * half, hid + (c + 1) * half) for c in range(2)]
    own_hidden = pltpu.make_async_copy(first_hidden, sh.at[0, own2, centre], in_sem.at[0])
    own_cell = pltpu.make_async_copy(first_cell, cells.at[0, own1], in_sem.at[1])
    own_hidden.start()

    @pl.when(base)
    def _():
        for t in range(2):
            for c in range(2):
                pltpu.make_async_copy(
                    frames.at[t, :, pl.ds(c * half, half)], sx.at[t, own2, half_lanes[c]], sx_r.at[t, c, 2]
                ).start()

    own_cell.start()

    @pl.when(roof)
    def _():
        for t in range(2):
            pltpu.make_async_copy(cotangent.at[t], gin.at[t, own1], gx_r.at[t, 2]).start()

    for part in (1, 0):
        for c in range(2):
            for g in range(4):
                loads[part, c, g].start()

    def clear(wide, narrow):
        for t in range(2):
            sx[t, wide, :] = jnp.zeros((2 * cols, 3 * hid), BF16)
            sh[t, wide, :] = jnp.zeros((2 * cols, 3 * hid), BF16)
            gin[t, narrow] = jnp.zeros((cols, hid), BF16)
        cells[0, narrow] = jnp.zeros((cols, hid), F32)
        ghid[narrow] = jnp.zeros((cols, hid), BF16)

    pl.when(top)(lambda: clear(above2, above1))
    pl.when(bottom)(lambda: clear(below2, below1))

    pl.semaphore_wait(
        barrier, count(plane) + count(below) + jnp.where(z == 1, len(group), 0)
    )

    def send_edges(src, dst, send_sems, recv_sems, section, pred):
        edges(lambda: (src, dst, send_sems, recv_sems), section, pred)

    def edges(parts, section, pred):
        def up():
            return s > 0 if pred is None else (s > 0) & pred

        def down():
            return s < tiles - 1 if pred is None else (s < tiles - 1) & pred

        def make(end, device):
            src, dst, send_sems, recv_sems = parts()
            return remote(src[end], dst[1 - end], send_sems.at[end], recv_sems.at[1 - end], device)

        send(up, lambda: make(0, (section, s - 1, k)))
        send(down, lambda: make(1, (section, s + 1, k)))

    def outer(ref, width):
        return ref.at[0:width], ref.at[n - width:n]

    def beyond(ref):
        return ref.at[cols:2 * cols], ref.at[n - 2 * cols:n - cols]

    def narrow(ref):
        return ref.at[above1], ref.at[below1]

    def at_rows(buffer, t, rows, lanes):
        return buffer.at[t, rows[0], lanes], buffer.at[t, rows[1], lanes]

    def halves(ref, c):
        return ref.at[0:cols, pl.ds(c * half, half)], ref.at[n - cols:n, pl.ds(c * half, half)]

    send_edges(outer(first_hidden, cols), at_rows(sh, 0, near, centre), fh_s, sh_r.at[0, 0], z, None)

    def send_frames(t):
        for c in range(2):
            send_edges(
                halves(frames.at[t], c), at_rows(sx, t, near, half_lanes[c]),
                fr_s.at[t, c], sx_r.at[t, c], z, base,
            )

    send_frames(0)
    greet(above)
    greet(group)
    greet(below)
    send_edges(beyond(first_hidden), at_rows(sh, 0, far, centre), fh_f, sh_f.at[0], z, None)
    send_edges(outer(first_cell, cols), narrow(cells.at[0]), fc_s, c_r, z, None)
    send_edges(beyond(frames.at[0]), at_rows(sx, 0, far, centre), fr_f.at[0], sx_f.at[0], z, base)
    send_frames(1)
    send_edges(beyond(frames.at[1]), at_rows(sx, 1, far, centre), fr_f.at[1], sx_f.at[1], z, base)
    for t in range(2):
        send_edges(outer(cotangent.at[t], cols), narrow(gin.at[t]), ct_s.at[t], gx_r.at[t], z, roof)

    def spread_value(value, width):
        count = value.shape[0]
        column = lax.broadcasted_iota(jnp.int32, (count, width), 0) % cols
        left = jnp.where(column == 0, 0.0, pltpu.roll(value, 1, 0)).astype(BF16)
        right = jnp.where(column == cols - 1, 0.0, pltpu.roll(value, count - 1, 0)).astype(BF16)
        return left, right

    def spread(buffer, t, rows, width):
        left, right = spread_value(buffer[t, rows, width:2 * width].astype(F32), width)
        buffer[t, rows, 0:width] = left
        buffer[t, rows, 2 * width:3 * width] = right

    def when_edges(first, second):
        pl.when(jnp.logical_not(top))(first)
        pl.when(jnp.logical_not(bottom))(second)

    def near_here(buffer, t, recv_sems, lanes):
        def here(index):
            for c, part in enumerate(lanes):
                arrived(buffer.at[t, near[index], part], recv_sems.at[c, index])
            spread(buffer, t, near[index], hid)

        when_edges(lambda: here(0), lambda: here(1))

    def far_here(buffer, t, recv_sems):
        def here(index):
            arrived(buffer.at[t, far[index], centre], recv_sems.at[index])
            spread(buffer, t, far[index], hid)

        when_edges(lambda: here(0), lambda: here(1))

    def narrow_here(ref, recv_sems):
        when_edges(
            lambda: arrived(ref.at[above1], recv_sems.at[0]),
            lambda: arrived(ref.at[below1], recv_sems.at[1]),
        )

    def conv(buffer, t, weights, c, offsets):
        total = None
        for a in offsets:
            term = dot(
                buffer[t, cols * (a + 1):cols * (a + 1) + n, :],
                weights[c, a].reshape(3 * hid, gate_half),
            )
            total = term if total is None else total + term
        return total

    def conv_all(buffer, t, weights, c, offsets):
        total = None
        for a in offsets:
            term = dot(
                buffer[t, cols * a:cols * (a + 2) + n, :],
                weights[c, a].reshape(3 * hid, gate_half),
            )
            total = term if total is None else total + term
        return total

    def conv_beside(t, c):
        total = None
        for buffer, weights in ((sh, wh), (sx, wx)):
            for a in range(3):
                low = cols * (a + 1) + n
                cells_in = jnp.concatenate(
                    [buffer[t, cols * a:cols * (a + 1), :], buffer[t, low:low + cols, :]], axis=0
                )
                term = dot(cells_in, weights[c, a].reshape(3 * hid, gate_half))
                total = term if total is None else total + term
        return total

    def bias_of(c):
        return jnp.concatenate(
            [bias[0:1, g * hid + c * half:g * hid + (c + 1) * half] for g in range(4)], axis=1
        )

    def activate(now, old):
        i_gate = jax.nn.sigmoid(now[:, 0:half])
        f_gate = jax.nn.sigmoid(now[:, half:2 * half])
        o_gate = jax.nn.sigmoid(now[:, 2 * half:3 * half])
        cand = jnp.tanh(now[:, 3 * half:])
        new = f_gate * old + i_gate * cand
        return i_gate, f_gate, o_gate, cand, new, jnp.tanh(new)

    def factors(i_gate, f_gate, o_gate, cand, squash, old):
        return (
            o_gate * (1.0 - squash * squash),
            cand * i_gate * (1.0 - i_gate),
            old * f_gate * (1.0 - f_gate),
            squash * o_gate * (1.0 - o_gate),
            i_gate * (1.0 - cand * cand),
            f_gate,
        )

    def turn_weights(source, target):
        def one(a, carried):
            for b in range(3):
                for c in range(2):
                    start = (2 - b) * 4 * hid + c * gate_half
                    target[a, start:start + gate_half, :] = source[c, a, b].T
            return carried

        lax.fori_loop(0, 3, one, 0)

    def turn_all_weights():
        turn_weights(wh, wht)
        pl.when(inner)(lambda: turn_weights(wx, wxt))

    def spread_to_group(pred, view, seven, send_sem, recv_sem):
        def go():
            for d in (2, 1, 3, 0):
                for c in range(2):
                    there = ((x if c == 0 else y) + d) % LINE
                    chip = y * LINE + there if c == 0 else there * LINE + x
                    src, dst = view(c, 2 * (x if c == 0 else y) + k)
                    copy = functools.partial(remote, src, dst, send_sem(), recv_sem(), (z, chip, c))
                    if d == 0:
                        pl.when(k == c)(lambda: pltpu.make_async_copy(src, dst, recv_sem()).start())
                        pl.when(k != c)(lambda: copy().start())
                    else:
                        copy().start()

        def done():
            remote(seven(), seven(), send_sem(), recv_sem(), (z, s, 1 - k)).wait_send()

        pl.when(pred)(go)
        pending.append(lambda: pl.when(pred)(done))

    def rows_of(slot):
        return pl.ds(pl.multiple_of(slot * n, n), n)

    most = slice(0, 7 * n)

    def send_tile(t, part, pred):
        spread_to_group(
            pred,
            lambda c, slot: (
                (sh if part else sx).at[t, cols:3 * cols + n, centre], tiles_all.at[t, part, slot]
            ),
            lambda: tiles_all.at[t, part, 0:7],
            lambda: ti_s.at[t, part], lambda: ti_r.at[t, part],
        )

    pairs = [slice(p * 2 * half, (p + 1) * 2 * half) for p in range(2)]

    def send_grads(t, p, pred):
        lanes = pairs[p]

        def view(c, slot):
            at = 4 * hid + c * gate_half
            src = sg.at[t, own1, at + lanes.start:at + lanes.stop]
            return src, grads_all.at[t, rows_of(slot), lanes]

        spread_to_group(
            pred, view, lambda: grads_all.at[t, most, lanes],
            lambda: ga_s.at[t, p], lambda: ga_r.at[t, p],
        )

    early = z < 2

    def send_factors(t, pred):
        def view(c, slot):
            src = packed.at[t, :, c * 5 * half:(c + 1) * 5 * half]
            return src, packed_all.at[t, rows_of(slot), :]

        spread_to_group(
            pred, view, lambda: packed_all.at[t, most], lambda: co_s.at[t], lambda: co_r.at[t]
        )

    def pack_factors():
        for c in range(2):
            chan = slice(c * half, (c + 1) * half)
            for t in range(2):
                first = coef[t, 0, own1, chan]
                for g in range(5):
                    if g == 4:
                        value = first * coef[t, 5, own1, chan] if t == 1 else first
                    else:
                        value = coef[t, 1 + g, own1, chan]
                        if t == 1 and g != 2:
                            value = value * first
                    at = (c * 5 + g) * half
                    packed[t, :, at:at + half] = value.astype(BF16)

    def send_vec(index, pred):
        def view(c, slot):
            chan = slice(c * half, (c + 1) * half)
            src = ghid.at[own1, chan] if index == 2 else gin.at[1 - index, own1, chan]
            return src, vec_all.at[index, rows_of(slot), :]

        spread_to_group(
            pred, view, lambda: vec_all.at[index, most], lambda: ve_s.at[index], lambda: ve_r.at[index]
        )

    def send_down():
        def go():
            for d in (2, 1, 3, 0):
                for c in range(2):
                    there = ((x if c == 0 else y) + d) % LINE
                    chip = y * LINE + there if c == 0 else there * LINE + x
                    remote(
                        gx_out.at[0, :, c * half:(c + 1) * half],
                        vec_all.at[1, rows_of(2 * (x if c == 0 else y) + k), :],
                        vd_s.at[0], ve_r.at[1], (z - 1, chip, c),
                    ).start()

        def done():
            remote(vec_all.at[1], vec_all.at[1], vd_s.at[0], ve_r.at[1], (z, s, 1 - k)).wait_send()

        pl.when(z == 1)(go)
        pending.append(lambda: pl.when(z == 1)(done))

    rows = out.shape[0]
    block = 2 * rows
    me = jnp.where(k == 0, y, x)

    def turn_patches():
        for t in range(2):
            for part in range(2):
                arrived(tiles_all.at[t, part], ti_r.at[t, part])

            def one(slot, carried):
                for part in range(2):
                    tile = tiles_all[t, part, slot]
                    left, right = spread_value(tile.astype(F32), hid)
                    for b, moved in enumerate((left, tile, right)):
                        for a in range(3):
                            at = (a * 3 + b) * 2 * hid + part * hid
                            flipped[at:at + hid, :] = moved[cols * a:cols * a + n, :].T
                for j in range(LINE):
                    chip = jnp.where(k == 0, j * LINE + x, y * LINE + j)
                    turned[t, j, :, pl.ds(pl.multiple_of(slot * n, n), n)] = flipped[
                        pl.ds(pl.multiple_of(chip * block, 32), block), :
                    ]
                return carried

            lax.fori_loop(0, 2 * LINE, one, 0)

    @pl.when(z >= 2)
    def _():
        weights_here(1)
        weights_here(0)
        turn_all_weights()

    not_roof = jnp.logical_not(roof)
    z_up = z + 1

    def save(t, into, values, old, chan):
        i_gate, f_gate, o_gate, cand, squash = values
        for index, value in enumerate(factors(i_gate, f_gate, o_gate, cand, squash, old)):
            for cells_to, cells_from in into:
                coef[t, index, cells_to, chan] = value[cells_from]

    def x_here(t):
        for c in range(2):
            arrived(sx.at[t, own2, half_lanes[c]], sx_r.at[t, c, 2])
        spread(sx, t, own2, hid)

    def add(c, term):
        preact[0:n, c * gate_half:(c + 1) * gate_half] += term

    def own_rows(t):
        hidden_lanes = (centre,) if t == 0 else half_lanes
        part_sums = [conv(sh, t, wh, c, (1,)) + bias_of(c) for c in range(2)]
        for c in range(2):
            preact[0:n, c * gate_half:(c + 1) * gate_half] = part_sums[c]

        def x_middle():
            x_here(t)
            for c in range(2):
                add(c, conv(sx, t, wx, c, (1,)))

        def x_edges():
            near_here(sx, t, sx_r.at[t], half_lanes)

        def h_edges():
            near_here(sh, t, sh_r.at[t], hidden_lanes)

        def h_outer():
            for c in range(2):
                add(c, conv(sh, t, wh, c, (0, 2)))

        @pl.when(base)
        def _():
            if t == 0:
                weights_here(0)
            x_middle()
            if t == 1:
                x_edges()
                for c in range(2):
                    add(c, conv(sx, t, wx, c, (0, 2)))
                h_edges()

        if t == 0:
            h_edges()
            h_outer()
            send_tile(0, 1, inner)
            pl.when(z == 1)(lambda: weights_here(0))

        @pl.when(inner)
        def _():
            if t == 1:
                h_edges()
                h_outer()
            x_middle()
            if t == 1:
                x_edges()

        if t == 0:
            x_edges()
            own_cell.wait()
            pl.when(not_roof)(lambda: pl.semaphore_wait(barrier, count(above)))

        def finish(buffer, weights, c):
            chan, lanes = slice(c * half, (c + 1) * half), half_lanes[c]
            now = preact[0:n, c * gate_half:(c + 1) * gate_half] + conv(buffer, t, weights, c, (0, 2))
            i_gate, f_gate, o_gate, cand, new, squash = activate(now, cells[t, own1, chan])
            hidden = (o_gate * squash).astype(BF16)
            if t == 0:
                sh[1, own2, lanes] = hidden
                cells[1, own1, chan] = new
            else:
                top_hidden[:, chan] = hidden
            for index, value in enumerate((i_gate, f_gate, o_gate, cand, squash)):
                gates[index, :, chan] = value

        for c in range(2):
            chan, lanes = slice(c * half, (c + 1) * half), half_lanes[c]
            if t == 0:
                finish(sx, wx, c)
                whole = sh.at[1, own2, lanes]
                ends = sh.at[1, 2 * cols:3 * cols, lanes], sh.at[1, n + cols:n + 2 * cols, lanes]
            else:
                pl.when(base)(lambda c=c: finish(sh, wh, c))
                pl.when(inner)(lambda c=c: finish(sx, wx, c))
                whole = top_hidden.at[:, chan]
                ends = top_hidden.at[0:cols, chan], top_hidden.at[n - cols:n, chan]
            edges(
                lambda ends=ends, lanes=lanes, c=c: (
                    ends, at_rows(sx, t, near, lanes), sx_s.at[t, c], sx_r.at[t, c]
                ),
                z_up, not_roof,
            )
            send(
                not_roof,
                lambda whole=whole, lanes=lanes, c=c: remote(
                    whole, sx.at[t, own2, lanes], sx_s.at[t, c, 2], sx_r.at[t, c, 2], (z_up, s, k)
                ),
            )
            if t == 0:
                send_edges(ends, at_rows(sh, 1, near, lanes), sh_s.at[c], sh_r.at[1, c], z, None)
        if t == 0:
            ends = sh.at[1, 3 * cols:4 * cols, centre], sh.at[1, n:n + cols, centre]
            send_edges(ends, at_rows(sh, 1, far, centre), sh_fs, sh_f.at[1], z, None)
        else:
            ends = beyond(top_hidden)
        last = ends
        edges(
            lambda: (last, at_rows(sx, t, far, centre), sx_fs.at[t], sx_f.at[t]), z_up, not_roof
        )
        for c in range(2):
            chan = slice(c * half, (c + 1) * half)
            save(
                t, ((own1, slice(0, n)),),
                tuple(gates[index, :, chan] for index in range(5)), cells[t, own1, chan], chan,
            )

    def beside_rows(t):
        if t == 0:
            narrow_here(cells.at[0], c_r)
        far_here(sh, t, sh_f.at[t])
        far_here(sx, t, sx_f.at[t])
        for c in range(2):
            chan = slice(c * half, (c + 1) * half)
            old = jnp.concatenate([cells[t, above1, chan], cells[t, below1, chan]], axis=0)
            i_gate, f_gate, o_gate, cand, new, squash = activate(conv_beside(t, c) + bias_of(c), old)
            if t == 0:
                cells[1, above1, chan] = new[0:cols]
                cells[1, below1, chan] = new[cols:]
            save(
                t, ((above1, slice(0, cols)), (below1, slice(cols, 2 * cols))),
                (i_gate, f_gate, o_gate, cand, squash), old, chan,
            )

    def add_all(buffer, weights, offsets):
        for c in range(2):
            preact[:, c * gate_half:(c + 1) * gate_half] += conv_all(buffer, 1, weights, c, offsets)

    def all_rows_h():
        near_here(sh, 1, sh_r.at[1], half_lanes)
        for c in range(2):
            preact[:, c * gate_half:(c + 1) * gate_half] = conv_all(sh, 1, wh, c, (1,)) + bias_of(c)
        far_here(sh, 1, sh_f.at[1])
        add_all(sh, wh, (0, 2))

    def all_rows_x():
        x_here(1)
        near_here(sx, 1, sx_r.at[1], half_lanes)
        add_all(sx, wx, (1,))
        far_here(sx, 1, sx_f.at[1])
        for c in range(2):
            chan = slice(c * half, (c + 1) * half)
            now = preact[:, c * gate_half:(c + 1) * gate_half] + conv_all(sx, 1, wx, c, (0, 2))
            old = cells[1, :, chan]
            i_gate, f_gate, o_gate, cand, new, squash = activate(now, old)
            save(
                1, ((slice(0, n + 2 * cols), slice(0, n + 2 * cols)),),
                (i_gate, f_gate, o_gate, cand, squash), old, chan,
            )

    own_hidden.wait()
    spread(sh, 0, own2, hid)
    pl.when(z < 2)(lambda: weights_here(1))
    own_rows(0)
    send_tile(0, 0, inner)
    spread(sh, 1, own2, hid)

    pl.when(not_roof)(lambda: own_rows(1))
    pl.when(not_roof)(pack_factors)
    send_tile(0, 1, base)
    send_tile(0, 0, base)
    send_tile(1, 1, not_roof)
    send_tile(1, 0, not_roof)
    send_factors(1, not_roof)
    send_factors(0, early)

    @pl.when(not_roof)
    def _():
        beside_rows(0)
        beside_rows(1)

    @pl.when(roof)
    def _():
        beside_rows(0)
        all_rows_h()

    send_tile(1, 1, roof)
    pl.when(roof)(all_rows_x)

    def blank(outside):
        coef[:, :, outside, :] = jnp.zeros((2, 6, cols, hid), F32)

    pl.when(top)(lambda: blank(above1))
    pl.when(bottom)(lambda: blank(below1))

    pl.when(z < 2)(turn_all_weights)
    pl.when(z < 2)(turn_patches)

    def back_conv(t, weights):
        total = None
        for a in range(3):
            term = dot(sg[t, cols * (2 - a):cols * (2 - a) + n, :], weights[a])
            total = term if total is None else total + term
        return total.astype(BF16)

    def gate_grads(t):
        for c in range(2):
            chan = slice(c * half, (c + 1) * half)
            grad_h = gin[t, :, chan].astype(F32)
            if t == 0:
                grad_h = grad_h + ghid[:, chan].astype(F32)
            grad_c = grad_h * coef[t, 0, :, chan]
            if t == 0:
                grad_c = grad_c + carry[:, chan]
            for g, value in enumerate((
                grad_c * coef[t, 1, :, chan],
                grad_c * coef[t, 2, :, chan],
                grad_h * coef[t, 3, :, chan],
                grad_c * coef[t, 4, :, chan],
            )):
                at = 4 * hid + c * gate_half + g * half
                sg[t, :, at:at + half] = value.astype(BF16)
            if t == 1:
                carry[:, chan] = grad_c * coef[t, 5, :, chan]

    def first_conv(t, weights):
        total = None
        for b in (1, 0, 2):
            lanes = slice(b * 4 * hid, (b + 1) * 4 * hid)
            if b == 0:
                spread(sg, t, slice(0, 2 * cols + n), 4 * hid)
            for a in range(3):
                low = cols * (2 - a)
                term = dot(sg[t, low:low + n, lanes], weights[a, lanes, :])
                total = term if total is None else total + term
        return total.astype(BF16)

    def send_input_grad(t, pred):
        send_edges(outer(gx_out.at[t], cols), narrow(gin.at[t]), gx_s.at[t], gx_r.at[t], z - 1, pred)
        send(
            pred,
            lambda: remote(gx_out.at[t], gin.at[t, own1], gx_s.at[t, 2], gx_r.at[t, 2], (z - 1, s, k)),
        )

    arrived(gin.at[1, own1], gx_r.at[1, 2])
    send_vec(0, base)
    narrow_here(gin.at[1], gx_r.at[1])

    @pl.when(inner)
    def _():
        gate_grads(1)
        gx_out[1] = first_conv(1, wxt)

    send_input_grad(1, inner)

    @pl.when(inner)
    def _():
        ghid[own1] = back_conv(1, wht)

    @pl.when(base)
    def _():
        gate_grads(1)
        ghid[own1] = first_conv(1, wht)

    send_edges((ghid.at[cols:2 * cols], ghid.at[n:n + cols]), narrow(ghid), gh_s, gh_r, z, inner)
    send_vec(0, inner & not_roof)
    send_vec(2, early)
    send_tile(1, 0, roof)

    pl.when(inner)(lambda: arrived(gin.at[0, own1], gx_r.at[0, 2]))
    send_vec(1, z == 1)

    @pl.when(inner)
    def _():
        narrow_here(gin.at[0], gx_r.at[0])
        narrow_here(ghid, gh_r)
        gate_grads(0)
        gx_out[0] = first_conv(0, wxt)

    send_down()
    send_input_grad(0, z >= 2)
    send_grads(1, 0, roof)
    send_grads(1, 1, roof)
    send_grads(0, 0, z >= 2)
    send_grads(0, 1, z >= 2)

    pl.when(z >= 2)(turn_patches)

    def grads_here(t, p, lanes):
        arrived(grads_all.at[t, :, lanes], ga_r.at[t, p])

    def vec_here(index):
        arrived(vec_all.at[index], ve_r.at[index])

    def factors_here(t):
        arrived(packed_all.at[t], co_r.at[t])

    def factor(t, g):
        return packed_all[t, :, g * half:(g + 1) * half].astype(F32)

    def put(t, g, value):
        grads_all[t, :, g * half:(g + 1) * half] = (factor(t, g) * value).astype(BF16)

    pl.when(early)(lambda: factors_here(0))

    @pl.when(not_roof)
    def _():
        factors_here(1)
        vec_here(0)
        for g in range(4):
            put(1, g, vec_all[0].astype(F32))

    @pl.when(roof)
    def _():
        grads_here(1, 0, pairs[0])
        grads_here(1, 1, pairs[1])

    for j in range(LINE):
        acc[j] = dot(turned[1, j], grads_all[1])
    for p, lanes in enumerate(pairs):
        @pl.when(early)
        def _():
            if p == 0:
                vec_here(2)
                vec_here(1)
            grad_h = vec_all[1].astype(F32) + vec_all[2].astype(F32)
            grad_c = vec_all[0].astype(F32) * factor(1, 4) + grad_h * factor(0, 4)
            put(0, 2 * p, grad_h if p else grad_c)
            put(0, 2 * p + 1, grad_c)

        pl.when(z >= 2)(lambda: grads_here(0, p, lanes))
        for d in (2, 1, 3, 0):
            j = (me + d) % LINE
            leaving[d, :, lanes] = (
                acc[j, :, lanes] + dot(turned[0, j], grads_all[0, :, lanes])
            ).astype(BF16)
            chip = jnp.where(k == 0, j * LINE + x, y * LINE + j)
            for q in range(2):
                src, dst = leaving.at[d, q * rows:(q + 1) * rows, lanes], landed.at[k, me, :, lanes]
                copy = functools.partial(
                    remote, src, dst, rv_s.at[p, min(d, 1)], rv_r.at[p], (z, chip, q)
                )
                if d == 0:
                    pl.when(k == q)(
                        lambda: pltpu.make_async_copy(src, dst, rv_r.at[p]).start()
                    )
                    pl.when(k != q)(lambda: copy().start())
                else:
                    copy().start()
    for wait in pending:
        wait()
    def final(p):
        wide = slice(2 * p * hid, 2 * (p + 1) * hid)
        return pltpu.make_async_copy(result.at[:, wide], out.at[:, wide], out_sem.at[p])

    for p, lanes in enumerate(pairs):
        arrived(landed.at[:, :, :, lanes], rv_r.at[p])
        for c in range(2):
            for g in (2 * p, 2 * p + 1):
                total = landed[c, 0, :, g * half:(g + 1) * half].astype(F32)
                for i in range(1, LINE):
                    total = total + landed[c, i, :, g * half:(g + 1) * half].astype(F32)
                result[:, g * hid + c * half:g * hid + (c + 1) * half] = total
        final(p).start()
    for p, lanes in enumerate(pairs):
        for ref, sem in ((leaving.at[0, 0:rows, lanes], rv_s.at[p, 0]), (leaving.at[1:4, :, lanes], rv_s.at[p, 1])):
            remote(ref, ref, sem, sem, (z, s, 1 - k)).wait_send()
        final(p).wait()


def on_device(frames, cotangent, first_hidden, first_cell, gate_bias, gate_weight):
    steps, _, tile_rows, cols, hid = frames.shape
    n = tile_rows * cols
    pad = n + 2 * cols
    half = hid // 2
    gates = 4 * hid
    share = 18 * hid // (lax.axis_size("space") * lax.axis_size("batch"))
    block = 2 * share
    vmem = pl.BlockSpec(memory_space=pltpu.VMEM)
    anywhere = pl.BlockSpec(memory_space=pl.ANY)
    dma = pltpu.SemaphoreType.DMA
    scratch = [
        pltpu.VMEM((2, 3, 3, hid, gates // 2), BF16),
        pltpu.VMEM((2, 3, 3, hid, gates // 2), BF16),
        pltpu.VMEM((3, 3 * gates, hid), BF16),
        pltpu.VMEM((3, 3 * gates, hid), BF16),
        pltpu.VMEM((steps, pad + 2 * cols, 3 * hid), BF16),
        pltpu.VMEM((steps, pad + 2 * cols, 3 * hid), BF16),
        pltpu.VMEM((steps, pad, 3 * gates), BF16),
        pltpu.VMEM((n, hid), BF16),
        pltpu.VMEM((pad, gates), F32),
        pltpu.VMEM((5, n, hid), F32),
        pltpu.VMEM((steps, pad, hid), F32),
        pltpu.VMEM((pad, hid), F32),
        pltpu.VMEM((steps, 6, pad, hid), F32),
        pltpu.VMEM((steps, pad, hid), BF16),
        pltpu.VMEM((steps, n, hid), BF16),
        pltpu.VMEM((pad, hid), BF16),
        pltpu.VMEM((steps, 2, 2 * LINE, pad, hid), BF16),
        pltpu.VMEM((18 * hid, n), BF16),
        pltpu.VMEM((steps, LINE, block, 2 * LINE * n), BF16),
        pltpu.VMEM((steps, 2 * LINE * n, gates // 2), BF16),
        pltpu.VMEM((steps, n, 5 * hid), BF16),
        pltpu.VMEM((steps, 2 * LINE * n, 5 * half), BF16),
        pltpu.VMEM((3, 2 * LINE * n, half), BF16),
        pltpu.VMEM((LINE, block, gates // 2), F32),
        pltpu.VMEM((LINE, block, gates // 2), BF16),
        pltpu.VMEM((2, LINE, share, gates // 2), BF16),
        pltpu.VMEM((share, gates), F32),
        dma((2, 2, 4)), dma((2,)),
        dma((steps, 2, 3)), dma((steps, 2)), dma((steps, 2, 2)), dma((steps, 2)),
        dma((2,)), dma((steps, 3)), dma((2,)),
        dma((steps, 2)), dma((steps, 2)), dma((steps,)), dma((3,)), dma((2,)),
        dma((steps, 2, 2)), dma((steps, 2)), dma((2,)), dma((2,)), dma((2,)), dma((steps, 2)),
        dma((steps, 2, 3)), dma((steps, 2)), dma((2, 2)), dma((2,)), dma((steps, 3)), dma((2,)),
        dma((steps, 2)), dma((steps, 2)), dma((steps,)), dma((3,)), dma((1,)), dma((2, 2)), dma((2,)),
    ]
    result = pl.pallas_call(
        kernel,
        out_shape=jax.ShapeDtypeStruct((share, gates), F32),
        in_specs=[anywhere] * 4 + [vmem, anywhere],
        out_specs=anywhere,
        scratch_shapes=scratch,
        compiler_params=pltpu.CompilerParams(
            collective_id=0, has_side_effects=True, vmem_limit_bytes=56 * 2**20
        ),
    )(
        frames.reshape(steps, n, hid),
        cotangent.reshape(steps, n, hid),
        first_hidden.reshape(n, hid),
        first_cell.reshape(n, hid),
        gate_bias,
        gate_weight.reshape(3, 3, 2 * hid, gates),
    )
    return result[None]


def solution(mesh):
    return jax.shard_map(
        on_device,
        mesh=mesh,
        in_specs=(
            P(None, "batch", "space", None, None),
            P(None, "batch", "space", None, None),
            P("section", "batch", "space", None, None),
            P("section", "batch", "space", None, None),
            P("section", None),
            P("section", None, None),
        ),
        out_specs=P("section", ("space", "batch"), None),
        check_vma=False,
    )
```

```python
import functools

import jax
import jax.numpy as jnp
from jax import lax
from jax.experimental import pallas as pl
from jax.experimental.pallas import tpu as pltpu
from jax.sharding import PartitionSpec as P

F32 = jnp.float32
BF16 = jnp.bfloat16
MESH = pl.DeviceIdType.MESH
LINE = 4


def dot(left, right):
    return jnp.dot(left, right, preferred_element_type=F32)


def kernel(
    frames, cotangent, first_hidden, first_cell, bias, weight, out,
    wx, wh, wxt, wht, sx, sh, sg, top_hidden, preact, gates, cells, carry, coef, gin, gx_out, ghid,
    tiles_all, flipped, turned, grads_all, packed, packed_all, vec_all, acc, leaving, landed, result,
    w_sem, in_sem, sx_r, sx_f, sh_r, sh_f, c_r, gx_r, gh_r, ti_r, ga_r, co_r, ve_r, rv_r,
    fr_s, fr_f, fh_s, fh_f, fc_s, ct_s, sx_s, sx_fs, sh_s, sh_fs, gx_s, gh_s, ti_s, ga_s, co_s, ve_s, vd_s, rv_s, out_sem,
):
    z, s, k = lax.axis_index("section"), lax.axis_index("space"), lax.axis_index("batch")
    y, x = s // LINE, s % LINE
    sections, tiles = lax.axis_size("section"), lax.axis_size("space")
    cols = 32
    n = first_cell.shape[0]
    hid = first_cell.shape[1]
    half = hid // 2
    gate_half = 4 * half
    own2, above2, below2 = slice(2 * cols, 2 * cols + n), slice(0, 2 * cols), slice(2 * cols + n, 4 * cols + n)
    near = slice(cols, 2 * cols), slice(2 * cols + n, 3 * cols + n)
    far = slice(0, cols), slice(3 * cols + n, 4 * cols + n)
    own1, above1, below1 = slice(cols, cols + n), slice(0, cols), slice(cols + n, 2 * cols + n)
    centre = slice(hid, 2 * hid)
    top, bottom, base, roof = s == 0, s == tiles - 1, z == 0, z == sections - 1
    inner = jnp.logical_not(base)
    pending = []

    def send(pred, make):
        if pred is None:
            make().start()
            pending.append(lambda: make().wait_send())
        else:
            ask = pred if callable(pred) else lambda: pred
            pl.when(ask())(lambda: make().start())
            pending.append(lambda: pl.when(ask())(lambda: make().wait_send()))

    def remote(src, dst, send_sem, recv_sem, device):
        return pltpu.make_async_remote_copy(
            src_ref=src, dst_ref=dst, send_sem=send_sem, recv_sem=recv_sem,
            device_id=device, device_id_type=MESH,
        )

    def arrived(dst, recv_sem):
        remote(dst, dst, recv_sem, recv_sem, (z, s, 1 - k)).wait_recv()

    loads = {}
    for part, buffer in ((0, wx), (1, wh)):
        for c in range(2):
            for g in range(4):
                loads[part, c, g] = pltpu.make_async_copy(
                    weight.at[:, :, part * hid:(part + 1) * hid, pl.ds(g * hid + c * half, half)],
                    buffer.at[c, :, :, :, g * half:(g + 1) * half],
                    w_sem.at[part, c, g],
                )

    def weights_here(part):
        for c in range(2):
            for g in range(4):
                loads[part, c, g].wait()

    barrier = pltpu.get_barrier_semaphore()

    def greet(partners):
        for pred, device in partners:
            call = functools.partial(
                pl.semaphore_signal, barrier, inc=1, device_id=device, device_id_type=MESH
            )
            if pred is None:
                call()
            else:
                pl.when(pred)(call)

    def count(partners):
        total = 0
        for pred, _ in partners:
            total = total + (1 if pred is None else jnp.where(pred, 1, 0))
        return total

    plane = [(jnp.logical_not(top), (z, s - 1, k)), (jnp.logical_not(bottom), (z, s + 1, k))]
    plane.append((None, (z, s, 1 - k)))
    for d in range(1, LINE):
        for core in range(2):
            plane.append((None, (z, y * LINE + (x + d) % LINE, core)))
            plane.append((None, (z, ((y + d) % LINE) * LINE + x, core)))

    def section_at(step, ok):
        return [
            (ok, (z + step, s, k)),
            (ok & (s > 0), (z + step, s - 1, k)),
            (ok & (s < tiles - 1), (z + step, s + 1, k)),
        ]

    below, above = section_at(-1, z > 0), section_at(1, z < sections - 1)
    group = [
        (base, (z + 1, jnp.where(k == 0, y * LINE + j, j * LINE + x), core))
        for j in range(LINE) for core in range(2)
    ]
    greet(plane)

    half_lanes = [slice(hid + c * half, hid + (c + 1) * half) for c in range(2)]
    own_hidden = pltpu.make_async_copy(first_hidden, sh.at[0, own2, centre], in_sem.at[0])
    own_cell = pltpu.make_async_copy(first_cell, cells.at[0, own1], in_sem.at[1])
    own_hidden.start()

    @pl.when(base)
    def _():
        for t in range(2):
            for c in range(2):
                pltpu.make_async_copy(
                    frames.at[t, :, pl.ds(c * half, half)], sx.at[t, own2, half_lanes[c]], sx_r.at[t, c, 2]
                ).start()

    own_cell.start()

    @pl.when(roof)
    def _():
        for t in range(2):
            pltpu.make_async_copy(cotangent.at[t], gin.at[t, own1], gx_r.at[t, 2]).start()

    for part in (1, 0):
        for c in range(2):
            for g in range(4):
                loads[part, c, g].start()

    def clear(wide, narrow):
        for t in range(2):
            sx[t, wide, :] = jnp.zeros((2 * cols, 3 * hid), BF16)
            sh[t, wide, :] = jnp.zeros((2 * cols, 3 * hid), BF16)
            gin[t, narrow] = jnp.zeros((cols, hid), BF16)
        cells[0, narrow] = jnp.zeros((cols, hid), F32)
        ghid[narrow] = jnp.zeros((cols, hid), BF16)

    pl.when(top)(lambda: clear(above2, above1))
    pl.when(bottom)(lambda: clear(below2, below1))

    pl.semaphore_wait(
        barrier, count(plane) + count(below) + jnp.where(z == 1, len(group), 0)
    )

    def send_edges(src, dst, send_sems, recv_sems, section, pred):
        edges(lambda: (src, dst, send_sems, recv_sems), section, pred)

    def edges(parts, section, pred):
        def up():
            return s > 0 if pred is None else (s > 0) & pred

        def down():
            return s < tiles - 1 if pred is None else (s < tiles - 1) & pred

        def make(end, device):
            src, dst, send_sems, recv_sems = parts()
            return remote(src[end], dst[1 - end], send_sems.at[end], recv_sems.at[1 - end], device)

        send(up, lambda: make(0, (section, s - 1, k)))
        send(down, lambda: make(1, (section, s + 1, k)))

    def outer(ref, width):
        return ref.at[0:width], ref.at[n - width:n]

    def beyond(ref):
        return ref.at[cols:2 * cols], ref.at[n - 2 * cols:n - cols]

    def narrow(ref):
        return ref.at[above1], ref.at[below1]

    def at_rows(buffer, t, rows, lanes):
        return buffer.at[t, rows[0], lanes], buffer.at[t, rows[1], lanes]

    def halves(ref, c):
        return ref.at[0:cols, pl.ds(c * half, half)], ref.at[n - cols:n, pl.ds(c * half, half)]

    send_edges(outer(first_hidden, cols), at_rows(sh, 0, near, centre), fh_s, sh_r.at[0, 0], z, None)

    def send_frames(t):
        for c in range(2):
            send_edges(
                halves(frames.at[t], c), at_rows(sx, t, near, half_lanes[c]),
                fr_s.at[t, c], sx_r.at[t, c], z, base,
            )

    send_frames(0)
    greet(above)
    greet(group)
    greet(below)
    send_edges(beyond(first_hidden), at_rows(sh, 0, far, centre), fh_f, sh_f.at[0], z, None)
    send_edges(outer(first_cell, cols), narrow(cells.at[0]), fc_s, c_r, z, None)
    send_edges(beyond(frames.at[0]), at_rows(sx, 0, far, centre), fr_f.at[0], sx_f.at[0], z, base)
    send_frames(1)
    send_edges(beyond(frames.at[1]), at_rows(sx, 1, far, centre), fr_f.at[1], sx_f.at[1], z, base)
    for t in range(2):
        send_edges(outer(cotangent.at[t], cols), narrow(gin.at[t]), ct_s.at[t], gx_r.at[t], z, roof)

    def spread_value(value, width):
        count = value.shape[0]
        column = lax.broadcasted_iota(jnp.int32, (count, width), 0) % cols
        left = jnp.where(column == 0, 0.0, pltpu.roll(value, 1, 0)).astype(BF16)
        right = jnp.where(column == cols - 1, 0.0, pltpu.roll(value, count - 1, 0)).astype(BF16)
        return left, right

    def spread(buffer, t, rows, width):
        left, right = spread_value(buffer[t, rows, width:2 * width].astype(F32), width)
        buffer[t, rows, 0:width] = left
        buffer[t, rows, 2 * width:3 * width] = right

    def when_edges(first, second):
        pl.when(jnp.logical_not(top))(first)
        pl.when(jnp.logical_not(bottom))(second)

    def near_here(buffer, t, recv_sems, lanes):
        def here(index):
            for c, part in enumerate(lanes):
                arrived(buffer.at[t, near[index], part], recv_sems.at[c, index])
            spread(buffer, t, near[index], hid)

        when_edges(lambda: here(0), lambda: here(1))

    def far_here(buffer, t, recv_sems):
        def here(index):
            arrived(buffer.at[t, far[index], centre], recv_sems.at[index])
            spread(buffer, t, far[index], hid)

        when_edges(lambda: here(0), lambda: here(1))

    def narrow_here(ref, recv_sems):
        when_edges(
            lambda: arrived(ref.at[above1], recv_sems.at[0]),
            lambda: arrived(ref.at[below1], recv_sems.at[1]),
        )

    def conv(buffer, t, weights, c, offsets):
        total = None
        for a in offsets:
            term = dot(
                buffer[t, cols * (a + 1):cols * (a + 1) + n, :],
                weights[c, a].reshape(3 * hid, gate_half),
            )
            total = term if total is None else total + term
        return total

    def conv_all(buffer, t, weights, c, offsets):
        total = None
        for a in offsets:
            term = dot(
                buffer[t, cols * a:cols * (a + 2) + n, :],
                weights[c, a].reshape(3 * hid, gate_half),
            )
            total = term if total is None else total + term
        return total

    def conv_beside(t, c):
        total = None
        for buffer, weights in ((sh, wh), (sx, wx)):
            for a in range(3):
                low = cols * (a + 1) + n
                cells_in = jnp.concatenate(
                    [buffer[t, cols * a:cols * (a + 1), :], buffer[t, low:low + cols, :]], axis=0
                )
                term = dot(cells_in, weights[c, a].reshape(3 * hid, gate_half))
                total = term if total is None else total + term
        return total

    def bias_of(c):
        return jnp.concatenate(
            [bias[0:1, g * hid + c * half:g * hid + (c + 1) * half] for g in range(4)], axis=1
        )

    def activate(now, old):
        i_gate = jax.nn.sigmoid(now[:, 0:half])
        f_gate = jax.nn.sigmoid(now[:, half:2 * half])
        o_gate = jax.nn.sigmoid(now[:, 2 * half:3 * half])
        cand = jnp.tanh(now[:, 3 * half:])
        new = f_gate * old + i_gate * cand
        return i_gate, f_gate, o_gate, cand, new, jnp.tanh(new)

    def factors(i_gate, f_gate, o_gate, cand, squash, old):
        return (
            o_gate * (1.0 - squash * squash),
            cand * i_gate * (1.0 - i_gate),
            old * f_gate * (1.0 - f_gate),
            squash * o_gate * (1.0 - o_gate),
            i_gate * (1.0 - cand * cand),
            f_gate,
        )

    def turn_weights(source, target):
        def one(a, carried):
            for b in range(3):
                for c in range(2):
                    start = (2 - b) * 4 * hid + c * gate_half
                    target[a, start:start + gate_half, :] = source[c, a, b].T
            return carried

        lax.fori_loop(0, 3, one, 0)

    def turn_all_weights():
        turn_weights(wh, wht)
        pl.when(inner)(lambda: turn_weights(wx, wxt))

    def spread_to_group(pred, view, seven, send_sem, recv_sem):
        def go():
            for d in (2, 1, 3, 0):
                for c in range(2):
                    there = ((x if c == 0 else y) + d) % LINE
                    chip = y * LINE + there if c == 0 else there * LINE + x
                    src, dst = view(c, 2 * (x if c == 0 else y) + k)
                    copy = functools.partial(remote, src, dst, send_sem(), recv_sem(), (z, chip, c))
                    if d == 0:
                        pl.when(k == c)(lambda: pltpu.make_async_copy(src, dst, recv_sem()).start())
                        pl.when(k != c)(lambda: copy().start())
                    else:
                        copy().start()

        def done():
            remote(seven(), seven(), send_sem(), recv_sem(), (z, s, 1 - k)).wait_send()

        pl.when(pred)(go)
        pending.append(lambda: pl.when(pred)(done))

    def rows_of(slot):
        return pl.ds(pl.multiple_of(slot * n, n), n)

    most = slice(0, 7 * n)

    def send_tile(t, part, pred):
        spread_to_group(
            pred,
            lambda c, slot: (
                (sh if part else sx).at[t, cols:3 * cols + n, centre], tiles_all.at[t, part, slot]
            ),
            lambda: tiles_all.at[t, part, 0:7],
            lambda: ti_s.at[t, part], lambda: ti_r.at[t, part],
        )

    pairs = [slice(p * 2 * half, (p + 1) * 2 * half) for p in range(2)]

    def send_grads(t, p, pred):
        lanes = pairs[p]

        def view(c, slot):
            at = 4 * hid + c * gate_half
            src = sg.at[t, own1, at + lanes.start:at + lanes.stop]
            return src, grads_all.at[t, rows_of(slot), lanes]

        spread_to_group(
            pred, view, lambda: grads_all.at[t, most, lanes],
            lambda: ga_s.at[t, p], lambda: ga_r.at[t, p],
        )

    early = z < 2

    def send_factors(t):
        def view(c, slot):
            src = packed.at[t, :, c * 5 * half:(c + 1) * 5 * half]
            return src, packed_all.at[t, rows_of(slot), :]

        spread_to_group(
            early, view, lambda: packed_all.at[t, most], lambda: co_s.at[t], lambda: co_r.at[t]
        )

    def pack_factors():
        for c in range(2):
            chan = slice(c * half, (c + 1) * half)
            for t in range(2):
                first = coef[t, 0, own1, chan]
                for g in range(5):
                    if g == 4:
                        value = first * coef[t, 5, own1, chan] if t == 1 else first
                    else:
                        value = coef[t, 1 + g, own1, chan]
                        if t == 1 and g != 2:
                            value = value * first
                    at = (c * 5 + g) * half
                    packed[t, :, at:at + half] = value.astype(BF16)

    def send_vec(index, pred):
        def view(c, slot):
            chan = slice(c * half, (c + 1) * half)
            src = ghid.at[own1, chan] if index == 2 else gin.at[1 - index, own1, chan]
            return src, vec_all.at[index, rows_of(slot), :]

        spread_to_group(
            pred, view, lambda: vec_all.at[index, most], lambda: ve_s.at[index], lambda: ve_r.at[index]
        )

    def send_down():
        def go():
            for d in (2, 1, 3, 0):
                for c in range(2):
                    there = ((x if c == 0 else y) + d) % LINE
                    chip = y * LINE + there if c == 0 else there * LINE + x
                    remote(
                        gx_out.at[0, :, c * half:(c + 1) * half],
                        vec_all.at[1, rows_of(2 * (x if c == 0 else y) + k), :],
                        vd_s.at[0], ve_r.at[1], (z - 1, chip, c),
                    ).start()

        def done():
            remote(vec_all.at[1], vec_all.at[1], vd_s.at[0], ve_r.at[1], (z, s, 1 - k)).wait_send()

        pl.when(z == 1)(go)
        pending.append(lambda: pl.when(z == 1)(done))

    rows = out.shape[0]
    block = 2 * rows
    me = jnp.where(k == 0, y, x)

    def turn_patches():
        for t in range(2):
            for part in range(2):
                arrived(tiles_all.at[t, part], ti_r.at[t, part])

            def one(slot, carried):
                for part in range(2):
                    tile = tiles_all[t, part, slot]
                    left, right = spread_value(tile.astype(F32), hid)
                    for b, moved in enumerate((left, tile, right)):
                        for a in range(3):
                            at = (a * 3 + b) * 2 * hid + part * hid
                            flipped[at:at + hid, :] = moved[cols * a:cols * a + n, :].T
                for j in range(LINE):
                    chip = jnp.where(k == 0, j * LINE + x, y * LINE + j)
                    turned[t, j, :, pl.ds(pl.multiple_of(slot * n, n), n)] = flipped[
                        pl.ds(pl.multiple_of(chip * block, 32), block), :
                    ]
                return carried

            lax.fori_loop(0, 2 * LINE, one, 0)

    @pl.when(z >= 2)
    def _():
        weights_here(1)
        weights_here(0)
        turn_all_weights()

    not_roof = jnp.logical_not(roof)
    z_up = z + 1

    def save(t, into, values, old, chan):
        i_gate, f_gate, o_gate, cand, squash = values
        for index, value in enumerate(factors(i_gate, f_gate, o_gate, cand, squash, old)):
            for cells_to, cells_from in into:
                coef[t, index, cells_to, chan] = value[cells_from]

    def x_here(t):
        for c in range(2):
            arrived(sx.at[t, own2, half_lanes[c]], sx_r.at[t, c, 2])
        spread(sx, t, own2, hid)

    def add(c, term):
        preact[0:n, c * gate_half:(c + 1) * gate_half] += term

    def own_rows(t):
        part_sums = [conv(sh, t, wh, c, (1,)) + bias_of(c) for c in range(2)]
        for c in range(2):
            preact[0:n, c * gate_half:(c + 1) * gate_half] = part_sums[c]

        def x_middle():
            x_here(t)
            for c in range(2):
                add(c, conv(sx, t, wx, c, (1,)))

        def x_edges():
            near_here(sx, t, sx_r.at[t], half_lanes)

        def h_edges():
            near_here(sh, t, sh_r.at[t], (centre,))

        def h_outer():
            for c in range(2):
                add(c, conv(sh, t, wh, c, (0, 2)))

        @pl.when(base)
        def _():
            if t == 0:
                weights_here(0)
            x_middle()
            if t == 1:
                x_edges()
                for c in range(2):
                    add(c, conv(sx, t, wx, c, (0, 2)))
                h_edges()

        if t == 0:
            h_edges()
            h_outer()
            send_tile(0, 1, inner)
            pl.when(z == 1)(lambda: weights_here(0))

        @pl.when(inner)
        def _():
            if t == 1:
                h_edges()
                h_outer()
            x_middle()
            if t == 1:
                x_edges()

        if t == 0:
            x_edges()
            own_cell.wait()
            pl.when(not_roof)(lambda: pl.semaphore_wait(barrier, count(above)))

        def finish(buffer, weights, c):
            chan, lanes = slice(c * half, (c + 1) * half), half_lanes[c]
            now = preact[0:n, c * gate_half:(c + 1) * gate_half] + conv(buffer, t, weights, c, (0, 2))
            i_gate, f_gate, o_gate, cand, new, squash = activate(now, cells[t, own1, chan])
            hidden = (o_gate * squash).astype(BF16)
            if t == 0:
                sh[1, own2, lanes] = hidden
                cells[1, own1, chan] = new
            else:
                top_hidden[:, chan] = hidden
            for index, value in enumerate((i_gate, f_gate, o_gate, cand, squash)):
                gates[index, :, chan] = value

        for c in range(2):
            chan, lanes = slice(c * half, (c + 1) * half), half_lanes[c]
            if t == 0:
                finish(sx, wx, c)
                whole = sh.at[1, own2, lanes]
                ends = sh.at[1, 2 * cols:3 * cols, lanes], sh.at[1, n + cols:n + 2 * cols, lanes]
            else:
                pl.when(base)(lambda c=c: finish(sh, wh, c))
                pl.when(inner)(lambda c=c: finish(sx, wx, c))
                whole = top_hidden.at[:, chan]
                ends = top_hidden.at[0:cols, chan], top_hidden.at[n - cols:n, chan]
            edges(
                lambda ends=ends, lanes=lanes, c=c: (
                    ends, at_rows(sx, t, near, lanes), sx_s.at[t, c], sx_r.at[t, c]
                ),
                z_up, not_roof,
            )
            send(
                not_roof,
                lambda whole=whole, lanes=lanes, c=c: remote(
                    whole, sx.at[t, own2, lanes], sx_s.at[t, c, 2], sx_r.at[t, c, 2], (z_up, s, k)
                ),
            )
        if t == 0:
            ends = sh.at[1, 2 * cols:3 * cols, centre], sh.at[1, n + cols:n + 2 * cols, centre]
            send_edges(ends, at_rows(sh, 1, near, centre), sh_s.at[0], sh_r.at[1, 0], z, None)
            ends = sh.at[1, 3 * cols:4 * cols, centre], sh.at[1, n:n + cols, centre]
            send_edges(ends, at_rows(sh, 1, far, centre), sh_fs, sh_f.at[1], z, None)
        else:
            ends = beyond(top_hidden)
        last = ends
        edges(
            lambda: (last, at_rows(sx, t, far, centre), sx_fs.at[t], sx_f.at[t]), z_up, not_roof
        )
        for c in range(2):
            chan = slice(c * half, (c + 1) * half)
            save(
                t, ((own1, slice(0, n)),),
                tuple(gates[index, :, chan] for index in range(5)), cells[t, own1, chan], chan,
            )

    def beside_rows(t):
        if t == 0:
            narrow_here(cells.at[0], c_r)
        far_here(sh, t, sh_f.at[t])
        far_here(sx, t, sx_f.at[t])
        for c in range(2):
            chan = slice(c * half, (c + 1) * half)
            old = jnp.concatenate([cells[t, above1, chan], cells[t, below1, chan]], axis=0)
            i_gate, f_gate, o_gate, cand, new, squash = activate(conv_beside(t, c) + bias_of(c), old)
            if t == 0:
                cells[1, above1, chan] = new[0:cols]
                cells[1, below1, chan] = new[cols:]
            save(
                t, ((above1, slice(0, cols)), (below1, slice(cols, 2 * cols))),
                (i_gate, f_gate, o_gate, cand, squash), old, chan,
            )

    def add_all(buffer, weights, offsets):
        for c in range(2):
            preact[:, c * gate_half:(c + 1) * gate_half] += conv_all(buffer, 1, weights, c, offsets)

    def all_rows_h():
        near_here(sh, 1, sh_r.at[1], (centre,))
        for c in range(2):
            preact[:, c * gate_half:(c + 1) * gate_half] = conv_all(sh, 1, wh, c, (1,)) + bias_of(c)
        far_here(sh, 1, sh_f.at[1])
        add_all(sh, wh, (0, 2))

    def all_rows_x():
        x_here(1)
        near_here(sx, 1, sx_r.at[1], half_lanes)
        add_all(sx, wx, (1,))
        far_here(sx, 1, sx_f.at[1])
        for c in range(2):
            chan = slice(c * half, (c + 1) * half)
            now = preact[:, c * gate_half:(c + 1) * gate_half] + conv_all(sx, 1, wx, c, (0, 2))
            old = cells[1, :, chan]
            i_gate, f_gate, o_gate, cand, new, squash = activate(now, old)
            save(
                1, ((slice(0, n + 2 * cols), slice(0, n + 2 * cols)),),
                (i_gate, f_gate, o_gate, cand, squash), old, chan,
            )

    own_hidden.wait()
    spread(sh, 0, own2, hid)
    pl.when(z < 2)(lambda: weights_here(1))
    own_rows(0)
    send_tile(0, 0, inner)
    spread(sh, 1, own2, hid)

    pl.when(not_roof)(lambda: own_rows(1))
    pl.when(early)(pack_factors)
    send_tile(0, 1, base)
    send_tile(0, 0, base)
    send_tile(1, 1, not_roof)
    send_tile(1, 0, not_roof)
    send_factors(1)
    send_factors(0)

    @pl.when(not_roof)
    def _():
        beside_rows(0)
        beside_rows(1)

    @pl.when(roof)
    def _():
        beside_rows(0)
        all_rows_h()

    send_tile(1, 1, roof)
    pl.when(roof)(all_rows_x)

    def blank(outside):
        coef[:, :, outside, :] = jnp.zeros((2, 6, cols, hid), F32)

    pl.when(top)(lambda: blank(above1))
    pl.when(bottom)(lambda: blank(below1))

    pl.when(z < 2)(turn_all_weights)
    pl.when(z < 2)(turn_patches)

    def back_conv(t, weights):
        total = None
        for a in range(3):
            term = dot(sg[t, cols * (2 - a):cols * (2 - a) + n, :], weights[a])
            total = term if total is None else total + term
        return total.astype(BF16)

    def gate_grads(t):
        for c in range(2):
            chan = slice(c * half, (c + 1) * half)
            grad_h = gin[t, :, chan].astype(F32)
            if t == 0:
                grad_h = grad_h + ghid[:, chan].astype(F32)
            grad_c = grad_h * coef[t, 0, :, chan]
            if t == 0:
                grad_c = grad_c + carry[:, chan]
            for g, value in enumerate((
                grad_c * coef[t, 1, :, chan],
                grad_c * coef[t, 2, :, chan],
                grad_h * coef[t, 3, :, chan],
                grad_c * coef[t, 4, :, chan],
            )):
                at = 4 * hid + c * gate_half + g * half
                sg[t, :, at:at + half] = value.astype(BF16)
            if t == 1:
                carry[:, chan] = grad_c * coef[t, 5, :, chan]

    def first_conv(t, weights):
        total = None
        for b in (1, 0, 2):
            lanes = slice(b * 4 * hid, (b + 1) * 4 * hid)
            if b == 0:
                spread(sg, t, slice(0, 2 * cols + n), 4 * hid)
            for a in range(3):
                low = cols * (2 - a)
                term = dot(sg[t, low:low + n, lanes], weights[a, lanes, :])
                total = term if total is None else total + term
        return total.astype(BF16)

    def send_input_grad(t, pred):
        send_edges(outer(gx_out.at[t], cols), narrow(gin.at[t]), gx_s.at[t], gx_r.at[t], z - 1, pred)
        send(
            pred,
            lambda: remote(gx_out.at[t], gin.at[t, own1], gx_s.at[t, 2], gx_r.at[t, 2], (z - 1, s, k)),
        )

    arrived(gin.at[1, own1], gx_r.at[1, 2])
    send_vec(0, base)
    narrow_here(gin.at[1], gx_r.at[1])

    @pl.when(inner)
    def _():
        gate_grads(1)
        gx_out[1] = first_conv(1, wxt)

    send_input_grad(1, inner)

    @pl.when(inner)
    def _():
        ghid[own1] = back_conv(1, wht)

    @pl.when(base)
    def _():
        gate_grads(1)
        ghid[own1] = first_conv(1, wht)

    send_edges((ghid.at[cols:2 * cols], ghid.at[n:n + cols]), narrow(ghid), gh_s, gh_r, z, inner)
    send_vec(0, z == 1)
    send_vec(2, early)
    send_tile(1, 0, roof)
    send_grads(1, 0, z == 2)

    pl.when(inner)(lambda: arrived(gin.at[0, own1], gx_r.at[0, 2]))

    @pl.when(inner)
    def _():
        narrow_here(gin.at[0], gx_r.at[0])
        narrow_here(ghid, gh_r)
        gate_grads(0)
        gx_out[0] = first_conv(0, wxt)

    send_down()
    send_vec(1, z == 1)
    send_input_grad(0, z >= 2)
    send_grads(1, 0, roof)
    send_grads(1, 1, z >= 2)
    send_grads(0, 0, z >= 2)
    send_grads(0, 1, z >= 2)

    pl.when(z >= 2)(turn_patches)

    def grads_here(t, p, lanes):
        arrived(grads_all.at[t, :, lanes], ga_r.at[t, p])

    def vec_here(index):
        arrived(vec_all.at[index], ve_r.at[index])

    def factors_here(t):
        arrived(packed_all.at[t], co_r.at[t])

    def factor(t, g):
        return packed_all[t, :, g * half:(g + 1) * half].astype(F32)

    def put(t, g, value):
        grads_all[t, :, g * half:(g + 1) * half] = (factor(t, g) * value).astype(BF16)

    @pl.when(early)
    def _():
        factors_here(1)
        factors_here(0)
        vec_here(0)
        for g in range(4):
            put(1, g, vec_all[0].astype(F32))

    @pl.when(z >= 2)
    def _():
        grads_here(1, 0, pairs[0])
        grads_here(1, 1, pairs[1])

    for j in range(LINE):
        acc[j] = dot(turned[1, j], grads_all[1])
    for p, lanes in enumerate(pairs):
        @pl.when(early)
        def _():
            if p == 0:
                vec_here(2)
                vec_here(1)
            grad_h = vec_all[1].astype(F32) + vec_all[2].astype(F32)
            grad_c = vec_all[0].astype(F32) * factor(1, 4) + grad_h * factor(0, 4)
            put(0, 2 * p, grad_h if p else grad_c)
            put(0, 2 * p + 1, grad_c)

        pl.when(z >= 2)(lambda: grads_here(0, p, lanes))
        for d in (2, 1, 3, 0):
            j = (me + d) % LINE
            leaving[d, :, lanes] = (
                acc[j, :, lanes] + dot(turned[0, j], grads_all[0, :, lanes])
            ).astype(BF16)
            chip = jnp.where(k == 0, j * LINE + x, y * LINE + j)
            for q in range(2):
                src, dst = leaving.at[d, q * rows:(q + 1) * rows, lanes], landed.at[k, me, :, lanes]
                copy = functools.partial(
                    remote, src, dst, rv_s.at[p, min(d, 1)], rv_r.at[p], (z, chip, q)
                )
                if d == 0:
                    pl.when(k == q)(
                        lambda: pltpu.make_async_copy(src, dst, rv_r.at[p]).start()
                    )
                    pl.when(k != q)(lambda: copy().start())
                else:
                    copy().start()
    for wait in pending:
        wait()
    def final(p):
        wide = slice(2 * p * hid, 2 * (p + 1) * hid)
        return pltpu.make_async_copy(result.at[:, wide], out.at[:, wide], out_sem.at[p])

    for p, lanes in enumerate(pairs):
        arrived(landed.at[:, :, :, lanes], rv_r.at[p])
        for c in range(2):
            for g in (2 * p, 2 * p + 1):
                total = landed[c, 0, :, g * half:(g + 1) * half].astype(F32)
                for i in range(1, LINE):
                    total = total + landed[c, i, :, g * half:(g + 1) * half].astype(F32)
                result[:, g * hid + c * half:g * hid + (c + 1) * half] = total
        final(p).start()
    for p, lanes in enumerate(pairs):
        for ref, sem in ((leaving.at[0, 0:rows, lanes], rv_s.at[p, 0]), (leaving.at[1:4, :, lanes], rv_s.at[p, 1])):
            remote(ref, ref, sem, sem, (z, s, 1 - k)).wait_send()
        final(p).wait()


def on_device(frames, cotangent, first_hidden, first_cell, gate_bias, gate_weight):
    steps, _, tile_rows, cols, hid = frames.shape
    n = tile_rows * cols
    pad = n + 2 * cols
    half = hid // 2
    gates = 4 * hid
    share = 18 * hid // (lax.axis_size("space") * lax.axis_size("batch"))
    block = 2 * share
    vmem = pl.BlockSpec(memory_space=pltpu.VMEM)
    anywhere = pl.BlockSpec(memory_space=pl.ANY)
    dma = pltpu.SemaphoreType.DMA
    scratch = [
        pltpu.VMEM((2, 3, 3, hid, gates // 2), BF16),
        pltpu.VMEM((2, 3, 3, hid, gates // 2), BF16),
        pltpu.VMEM((3, 3 * gates, hid), BF16),
        pltpu.VMEM((3, 3 * gates, hid), BF16),
        pltpu.VMEM((steps, pad + 2 * cols, 3 * hid), BF16),
        pltpu.VMEM((steps, pad + 2 * cols, 3 * hid), BF16),
        pltpu.VMEM((steps, pad, 3 * gates), BF16),
        pltpu.VMEM((n, hid), BF16),
        pltpu.VMEM((pad, gates), F32),
        pltpu.VMEM((5, n, hid), F32),
        pltpu.VMEM((steps, pad, hid), F32),
        pltpu.VMEM((pad, hid), F32),
        pltpu.VMEM((steps, 6, pad, hid), F32),
        pltpu.VMEM((steps, pad, hid), BF16),
        pltpu.VMEM((steps, n, hid), BF16),
        pltpu.VMEM((pad, hid), BF16),
        pltpu.VMEM((steps, 2, 2 * LINE, pad, hid), BF16),
        pltpu.VMEM((18 * hid, n), BF16),
        pltpu.VMEM((steps, LINE, block, 2 * LINE * n), BF16),
        pltpu.VMEM((steps, 2 * LINE * n, gates // 2), BF16),
        pltpu.VMEM((steps, n, 5 * hid), BF16),
        pltpu.VMEM((steps, 2 * LINE * n, 5 * half), BF16),
        pltpu.VMEM((3, 2 * LINE * n, half), BF16),
        pltpu.VMEM((LINE, block, gates // 2), F32),
        pltpu.VMEM((LINE, block, gates // 2), BF16),
        pltpu.VMEM((2, LINE, share, gates // 2), BF16),
        pltpu.VMEM((share, gates), F32),
        dma((2, 2, 4)), dma((2,)),
        dma((steps, 2, 3)), dma((steps, 2)), dma((steps, 2, 2)), dma((steps, 2)),
        dma((2,)), dma((steps, 3)), dma((2,)),
        dma((steps, 2)), dma((steps, 2)), dma((steps,)), dma((3,)), dma((2,)),
        dma((steps, 2, 2)), dma((steps, 2)), dma((2,)), dma((2,)), dma((2,)), dma((steps, 2)),
        dma((steps, 2, 3)), dma((steps, 2)), dma((2, 2)), dma((2,)), dma((steps, 3)), dma((2,)),
        dma((steps, 2)), dma((steps, 2)), dma((steps,)), dma((3,)), dma((1,)), dma((2, 2)), dma((2,)),
    ]
    result = pl.pallas_call(
        kernel,
        out_shape=jax.ShapeDtypeStruct((share, gates), F32),
        in_specs=[anywhere] * 4 + [vmem, anywhere],
        out_specs=anywhere,
        scratch_shapes=scratch,
        compiler_params=pltpu.CompilerParams(
            collective_id=0, has_side_effects=True, vmem_limit_bytes=56 * 2**20
        ),
    )(
        frames.reshape(steps, n, hid),
        cotangent.reshape(steps, n, hid),
        first_hidden.reshape(n, hid),
        first_cell.reshape(n, hid),
        gate_bias,
        gate_weight.reshape(3, 3, 2 * hid, gates),
    )
    return result[None]


def solution(mesh):
    return jax.shard_map(
        on_device,
        mesh=mesh,
        in_specs=(
            P(None, "batch", "space", None, None),
            P(None, "batch", "space", None, None),
            P("section", "batch", "space", None, None),
            P("section", "batch", "space", None, None),
            P("section", None),
            P("section", None, None),
        ),
        out_specs=P("section", ("space", "batch"), None),
        check_vma=False,
    )
```
